32 devices in a mesh: seq: 8 (over y, x, core), tp: 2 (over z_hi), img: 2 (over z_lo).
Axes of the slice: x: 2, y: 2, z: 4 (z_hi: 2, z_lo: 2; z = z_hi * 2 + z_lo), core: 2. Of those that a mesh axis runs over, the one named last changes fastest.
Arguments:
- text: bfloat16 [2, 1024, 2048], P('img', 'seq'), may hold values from -6 to 6
- segment: int32 [2, 1024], P('img'), may hold values from 0 to 2, as said below
- features: bfloat16 [2, 16, 256, 1024], P('img', 'seq'), may hold values from -6 to 6
- image_count: int32 [2, 8], P('img'), may hold values from 1 to 2, as said below
- image_slot: int32 [2, 16], P('img'), may hold values from 0 to 15, as said below
- cotangent: bfloat16 [2, 1024, 2048], P('img', 'seq'), may hold values from -6 to 6
- input_gain: bfloat16 [2048], replicated, may hold values from 0.5 to 1.5
- input_shift: bfloat16 [2048], replicated, may hold values from -1.796875 to 1.796875
- query_weight: bfloat16 [2048, 2048], P(('seq', 'img'), 'tp'), may hold values from -0.125 to 0.125
- key_weight: bfloat16 [2048, 2048], P(('seq', 'img'), 'tp'), may hold values from -0.125 to 0.125
- value_weight: bfloat16 [2048, 2048], P(('seq', 'img'), 'tp'), may hold values from -0.125 to 0.125
- inner_gain: bfloat16 [2048], P('tp'), may hold values from 0.5 to 1.5
- inner_shift: bfloat16 [2048], P('tp'), may hold values from -1.796875 to 1.796875
- out_weight: bfloat16 [2048, 2048], P('tp', ('seq', 'img')), may hold values from -0.125 to 0.125
- middle_gain: bfloat16 [2048], replicated, may hold values from 0.5 to 1.5
- middle_shift: bfloat16 [2048], replicated, may hold values from -1.796875 to 1.796875
- up_weight: bfloat16 [2048, 8192], P(('seq', 'img'), 'tp'), may hold values from -0.125 to 0.125
- up_bias: bfloat16 [8192], P('tp'), may hold values from -1.796875 to 1.796875
- hidden_gain: bfloat16 [8192], P('tp'), may hold values from 0.5 to 1.5
- hidden_shift: bfloat16 [8192], P('tp'), may hold values from -1.796875 to 1.796875
- down_weight: bfloat16 [8192, 2048], P('tp', ('seq', 'img')), may hold values from -0.0625 to 0.0625
- latents: bfloat16 [64, 2048], P(None, ('seq', 'img')), may hold values from -6 to 6
- resample_query: bfloat16 [2048, 2048], P(('seq', 'img'), 'tp'), may hold values from -0.125 to 0.125
- resample_key: bfloat16 [1024, 2048], P(('seq', 'img'), 'tp'), may hold values from -0.1875 to 0.1875
- resample_value: bfloat16 [1024, 2048], P(('seq', 'img'), 'tp'), may hold values from -0.1875 to 0.1875
- resample_out: bfloat16 [2048, 2048], P('tp', ('seq', 'img')), may hold values from -1 to 1
Outputs:
- result: bfloat16 [2, 1024, 2048], P('img', 'seq')
- text_grad: float32 [2, 1024, 2048], P('img', 'seq')
- input_gain_grad: float32 [2048], replicated
- input_shift_grad: float32 [2048], replicated
- query_grad: float32 [2048, 2048], P(('seq', 'img'), 'tp')
- key_grad: float32 [2048, 2048], P(('seq', 'img'), 'tp')
- value_grad: float32 [2048, 2048], P(('seq', 'img'), 'tp')
- inner_gain_grad: float32 [2048], P('tp')
- inner_shift_grad: float32 [2048], P('tp')
- out_grad: float32 [2048, 2048], P('tp', ('seq', 'img'))
- middle_gain_grad: float32 [2048], replicated
- middle_shift_grad: float32 [2048], replicated
- up_grad: float32 [2048, 8192], P(('seq', 'img'), 'tp')
- up_bias_grad: float32 [8192], P('tp')
- hidden_gain_grad: float32 [8192], P('tp')
- hidden_shift_grad: float32 [8192], P('tp')
- down_grad: float32 [8192, 2048], P('tp', ('seq', 'img'))
- latents_grad: float32 [64, 2048], P(None, ('seq', 'img'))
- resample_query_grad: float32 [2048, 2048], P(('seq', 'img'), 'tp')
- resample_key_grad: float32 [1024, 2048], P(('seq', 'img'), 'tp')
- resample_value_grad: float32 [1024, 2048], P(('seq', 'img'), 'tp')
- resample_out_grad: float32 [2048, 2048], P('tp', ('seq', 'img'))
The draws below stay inside these ranges and needn't reach their ends.
Inputs may be any that keep to these rules, and one draw needn't show every extreme that they name: `segment`: token block b (rows 64 b to 64 b + 63) of a group belongs to sequence b mod 1; sequence s holds the documents 3 s, 3 s + 1 and 3 s + 2 in the order of its rows, each one or more rows, and the middle one has rows on every index of seq. `image_count`: some index of seq in each group holds 2 live slots and some holds one. `image_slot`: values are distinct within a group; only the live slots fill their block.
All inputs are finite; a program needn't handle non-finite values.
Results may differ from the reference program's by a relative error of at most 0.025.
Values may be sent and summed in bfloat16 or wider, within the bound.
A program may use at most 256 MiB of HBM per device.

```python
import jax
import jax.numpy as jnp
from jax import lax

D = 2048
HEADS = 32
HEAD = 64
FF = 8192
CD = 1024
PATCH = 256
LAT = 64
SEQ_MAX = 2048
IMG_DEV = 2
TOKG = 1024
DOCS = 3
IMAGES = 16
N_SEQ = 8
N_IMG = 2


def draw_segment(key, part):
    key = jax.random.fold_in(key, 11)
    keys = jax.random.split(key, 2)
    seq_len = min(SEQ_MAX, TOKG)
    seq_count = TOKG // seq_len
    reach = seq_len // N_SEQ
    head_edge = jax.random.randint(keys[0], (N_IMG, seq_count), 1, reach)
    tail_edge = seq_len - jax.random.randint(keys[1], (N_IMG, seq_count), 1, reach)
    rows = jnp.arange(TOKG, dtype=jnp.int32)
    block = rows // LAT
    which = block % seq_count
    place = block // seq_count * LAT + rows % LAT
    head_row = head_edge[:, which]
    tail_row = tail_edge[:, which]
    numbers = which[None, :] * 3 + (place[None, :] >= head_row).astype(jnp.int32) + (place[None, :] >= tail_row).astype(jnp.int32)
    return numbers.astype(jnp.int32)


def draw_image_count(key, part):
    key = jax.random.fold_in(key, 12)
    keys = jax.random.split(key, 3)
    raw_draw = jax.random.randint(keys[0], (N_IMG, N_SEQ), 0, 10)
    counts = jnp.where(raw_draw >= 7, IMG_DEV, 1)
    busiest = jax.random.randint(keys[1], (N_IMG,), 0, N_SEQ)
    quietest = (busiest + 1 + jax.random.randint(keys[2], (N_IMG,), 0, N_SEQ - 1)) % N_SEQ
    ranks = jnp.arange(N_SEQ, dtype=jnp.int32)[None, :]
    counts = jnp.where(ranks == busiest[:, None], IMG_DEV, counts)
    counts = jnp.where(ranks == quietest[:, None], 1, counts)
    return counts.astype(jnp.int32)


def draw_image_slot(key, part):
    key = jax.random.fold_in(key, 13)
    keys = jax.random.split(key, N_IMG)
    chosen = jax.vmap(lambda group_key: jax.random.permutation(group_key, TOKG // LAT)[:IMAGES])(keys)
    return chosen.astype(jnp.int32)


def level_of(own_key, dims, shards, low, largest):
    level, own = 1.0, jax.random.fold_in(own_key, 6)
    for dim, parts in shards:
        draws = jnp.exp(jax.random.uniform(jax.random.fold_in(own, dim), (parts,), jnp.float32, low / len(shards), largest / len(shards)))
        level = level * jnp.repeat(draws, dims[dim] // parts).reshape([-1 if axis == dim else 1 for axis in range(len(dims))])
    return level


def bell_draw(own_key, dims, deviation, limit, cuts=(), kind=jnp.bfloat16):
    drawn = jax.random.normal(own_key, dims, jnp.float32) * deviation
    if len(cuts) > 0:
        drawn = level_of(own_key, dims, cuts, -0.22, 0.18) * drawn
    return jnp.clip(drawn, min=-limit, max=limit).astype(kind)


def setup_inputs(seed: int = 0) -> dict:
    key_of = jax.random.split(jax.random.key(seed), 27)
    return {
        "text": bell_draw(key_of[0], (N_IMG, TOKG, D), 1.0, 6.0, ((0, 2), (1, 8))),
        "segment": draw_segment(jax.random.fold_in(key_of[26], 71), 0),
        "features": bell_draw(key_of[2], (N_IMG, IMAGES, PATCH, CD), 1.0, 6.0, ((0, 2), (1, 8))),
        "image_count": draw_image_count(jax.random.fold_in(key_of[26], 71), 0),
        "image_slot": draw_image_slot(jax.random.fold_in(key_of[26], 71), 0),
        "cotangent": bell_draw(key_of[5], (N_IMG, TOKG, D), 1.0, 6.0, ((0, 2), (1, 8))),
        "input_gain": jnp.clip(1.0 + 0.1 * jax.random.normal(key_of[6], (D,), jnp.float32), 0.5, 1.5).astype(jnp.bfloat16),
        "input_shift": bell_draw(key_of[7], (D,), 0.3, 1.796875),
        "query_weight": bell_draw(key_of[8], (D, D), D ** -0.5, 0.125, ((0, 16), (1, 2))),
        "key_weight": bell_draw(key_of[9], (D, D), D ** -0.5, 0.125, ((0, 16), (1, 2))),
        "value_weight": bell_draw(key_of[10], (D, D), D ** -0.5, 0.125, ((0, 16), (1, 2))),
        "inner_gain": jnp.clip(1.0 + 0.1 * jax.random.normal(key_of[11], (D,), jnp.float32), 0.5, 1.5).astype(jnp.bfloat16),
        "inner_shift": bell_draw(key_of[12], (D,), 0.3, 1.796875, ((0, 2),)),
        "out_weight": bell_draw(key_of[13], (D, D), D ** -0.5, 0.125, ((0, 2), (1, 16))),
        "middle_gain": jnp.clip(1.0 + 0.1 * jax.random.normal(key_of[14], (D,), jnp.float32), 0.5, 1.5).astype(jnp.bfloat16),
        "middle_shift": bell_draw(key_of[15], (D,), 0.3, 1.796875),
        "up_weight": bell_draw(key_of[16], (D, FF), D ** -0.5, 0.125, ((0, 16), (1, 2))),
        "up_bias": bell_draw(key_of[17], (FF,), 0.3, 1.796875, ((0, 2),)),
        "hidden_gain": jnp.clip(1.0 + 0.1 * jax.random.normal(key_of[18], (FF,), jnp.float32), 0.5, 1.5).astype(jnp.bfloat16),
        "hidden_shift": bell_draw(key_of[19], (FF,), 0.3, 1.796875, ((0, 2),)),
        "down_weight": bell_draw(key_of[20], (FF, D), FF ** -0.5, 0.0625, ((0, 2), (1, 16))),
        "latents": bell_draw(key_of[21], (LAT, D), 1.0, 6.0, ((1, 16),)),
        "resample_query": bell_draw(key_of[22], (D, D), D ** -0.5, 0.125, ((0, 16), (1, 2))),
        "resample_key": bell_draw(key_of[23], (CD, D), CD ** -0.5, 0.1875, ((0, 16), (1, 2))),
        "resample_value": bell_draw(key_of[24], (CD, D), CD ** -0.5, 0.1875, ((0, 16), (1, 2))),
        "resample_out": bell_draw(key_of[25], (D, D), (D // 64) ** -0.5, 1.0, ((0, 2), (1, 16))),
    }


@jax.custom_vjp
def low(v):
    return lax.optimization_barrier(v.astype(jnp.bfloat16)).astype(jnp.float32)

@jax.custom_vjp
def low_back(v):
    return v

def low_keep(v):
    return (low(v), None)

def low_pass(kept, grad):
    return (grad,)

def back_keep(v):
    return (v, None)

def back_low(kept, grad):
    return (low(grad),)
low.defvjp(low_keep, low_pass)
low_back.defvjp(back_keep, back_low)
EPSILON = 1e-05
HIGHEST_PRECISION = lax.Precision.HIGHEST

def matmul(left, right):
    return jnp.matmul(left, right, precision=HIGHEST_PRECISION)

def layer_norm(inputs, norm_gain, norm_shift):
    center = inputs - lax.optimization_barrier(jnp.mean(inputs, -1, keepdims=True))
    spread = lax.optimization_barrier(jnp.mean(center * center, -1, keepdims=True))
    return center * lax.rsqrt(spread + EPSILON) * norm_gain + norm_shift

def xpos_factors(position, half_size):
    ladder = jnp.arange(half_size, dtype=jnp.float32)
    frequency = jnp.exp(ladder * (-2.0 * jnp.log(10000.0) / (2.0 * half_size)))
    decay_base = (ladder / half_size + 0.4) / 1.4
    angles = position[:, None] * frequency[None, :]
    growth = jnp.exp(position[:, None] / 512.0 * jnp.log(decay_base)[None, :])
    return (jnp.cos(angles)[:, None, :], jnp.sin(angles)[:, None, :], growth[:, None, :])

def rotate(inputs, cosine, sine_table, factor):
    half_size = inputs.shape[-1] // 2
    first_half = inputs[..., :half_size]
    second_half = inputs[..., half_size:]
    turned = jnp.concatenate([first_half * cosine - second_half * sine_table, first_half * sine_table + second_half * cosine], -1)
    return turned * jnp.concatenate([factor, factor], -1)

def doc_positions(segment_row):
    marks = (segment_row[:, None] == jnp.arange(DOCS, dtype=jnp.int32)[None, :]).astype(jnp.int32)
    earlier_rows = (jnp.cumsum(marks, 0) - marks).astype(jnp.int32)
    return lax.optimization_barrier(jnp.sum(earlier_rows * marks, 1)).astype(jnp.int32)

def attend(query, key_rows, value_rows, segment_row):
    total_rows = query.shape[0]
    block_size = min(512, total_rows)
    positions_all = jnp.arange(total_rows, dtype=jnp.int32)
    score_scale = HEAD ** (-0.5)

    def one_block(number):
        first_row = (number * block_size).astype(jnp.int32)
        block_query = lax.dynamic_slice_in_dim(query, first_row, block_size, 0)
        row_index = lax.dynamic_slice_in_dim(positions_all, first_row, block_size, 0)
        row_segment = lax.dynamic_slice_in_dim(segment_row, first_row, block_size, 0)
        scores = low_back(jnp.einsum('qhd,khd->hqk', block_query, key_rows, precision=HIGHEST_PRECISION) * score_scale)
        allowed = (positions_all[None, :] <= row_index[:, None]) & (segment_row[None, :] == row_segment[:, None])
        scores = jnp.where(allowed[None], scores, -1e+30)
        weights = jax.nn.softmax(scores, -1)
        return jnp.einsum('hqk,khd->qhd', low(weights), value_rows, precision=HIGHEST_PRECISION)
    outputs = lax.map(jax.checkpoint(one_block), jnp.arange(total_rows // block_size, dtype=jnp.int32))
    return outputs.reshape(query.shape)

def resample(sample_params, pictures):
    latent_rows, resample_query, resample_key, resample_value, resample_out = sample_params
    image_total = pictures.shape[0]
    score_scale = HEAD ** (-0.5)
    probe = low(matmul(latent_rows, resample_query)).reshape(LAT, HEADS, HEAD)
    image_keys = low(low_back(matmul(pictures, resample_key))).reshape(image_total, PATCH, HEADS, HEAD)
    image_values = low(low_back(matmul(pictures, resample_value))).reshape(image_total, PATCH, HEADS, HEAD)
    scores = low_back(jnp.einsum('qhd,iphd->ihqp', probe, image_keys, precision=HIGHEST_PRECISION) * score_scale)
    weights = jax.nn.softmax(scores, -1)
    mixed = low(low_back(jnp.einsum('ihqp,iphd->iqhd', low(weights), image_values, precision=HIGHEST_PRECISION)))
    embed = matmul(mixed.reshape(image_total, LAT, D), resample_out)
    return low_back(low(embed))

def text_layer(text_params, mixed_in, segment_row, position):
    input_gain, input_shift, query_weight, key_weight, value_weight, inner_gain, inner_shift, out_weight, middle_gain, middle_shift, up_weight, up_bias, hidden_gain, hidden_shift, down_weight = text_params
    normed = low(layer_norm(mixed_in, input_gain, input_shift))
    query_lin = low_back(matmul(normed, query_weight)).reshape(-1, HEADS, HEAD)
    key_lin = low_back(matmul(normed, key_weight)).reshape(-1, HEADS, HEAD)
    value_lin = low_back(matmul(normed, value_weight)).reshape(-1, HEADS, HEAD)
    cosine, sine_table, growth = xpos_factors(position, HEAD // 2)
    query = low(rotate(query_lin, cosine, sine_table, growth))
    key_rows = low(rotate(key_lin, cosine, sine_table, 1.0 / growth))
    value_rows = low(value_lin)
    attended = low_back(attend(query, key_rows, value_rows, segment_row)).reshape(-1, D)
    inner = low(layer_norm(attended, inner_gain, inner_shift))
    branch = low_back(matmul(inner, out_weight))
    middle = mixed_in + branch
    lifted = low(layer_norm(middle, middle_gain, middle_shift))
    hidden_pre = low_back(matmul(lifted, up_weight) + up_bias)
    activated = jax.nn.gelu(hidden_pre, approximate=False)
    settled = low(layer_norm(activated, hidden_gain, hidden_shift))
    return middle + matmul(settled, down_weight)

def reference(text, segment, features, image_count, image_slot, cotangent, input_gain, input_shift, query_weight, key_weight, value_weight, inner_gain, inner_shift, out_weight, middle_gain, middle_shift, up_weight, up_bias, hidden_gain, hidden_shift, down_weight, latents, resample_query, resample_key, resample_value, resample_out):
    weight_list = tuple((item.astype(jnp.float32) for item in (input_gain, input_shift, query_weight, key_weight, value_weight, inner_gain, inner_shift, out_weight, middle_gain, middle_shift, up_weight, up_bias, hidden_gain, hidden_shift, down_weight, latents, resample_query, resample_key, resample_value, resample_out)))
    block_count = TOKG // LAT
    slot_range = jnp.arange(IMAGES, dtype=jnp.int32)
    outputs = []
    text_grads = []
    summed = None
    for group_index in range(N_IMG):
        segment_row = segment[group_index].astype(jnp.int32)
        position = doc_positions(segment_row).astype(jnp.float32)
        live = slot_range % IMG_DEV < jnp.repeat(image_count[group_index], IMG_DEV)
        owner = ((image_slot[group_index][None, :] == jnp.arange(block_count, dtype=jnp.int32)[:, None]) & live[None, :]).astype(jnp.float32)
        taken = lax.optimization_barrier(jnp.sum(owner, 1)) > 0.5
        pictures = features[group_index].astype(jnp.float32)

        def forward(text_rows, *params):
            embed = resample(params[15:], pictures)
            placed = jnp.einsum('bi,ild->bld', owner, embed, precision=HIGHEST_PRECISION)
            mixed_in = jnp.where(taken[:, None, None], placed, text_rows.reshape(block_count, LAT, D)).reshape(TOKG, D)
            return text_layer(params[:15], mixed_in, segment_row, position)
        output, pullback = jax.vjp(forward, text[group_index].astype(jnp.float32), *weight_list)
        grads = pullback(cotangent[group_index].astype(jnp.float32))
        outputs.append(output.astype(jnp.bfloat16))
        text_grads.append(grads[0])
        if summed is None:
            summed = grads[1:]
        else:
            summed = tuple((left + right for left, right in zip(summed, grads[1:])))
    return (jnp.stack(outputs), jnp.stack(text_grads), summed[0], summed[1], summed[2], summed[3], summed[4], summed[5], summed[6], summed[7], summed[8], summed[9], summed[10], summed[11], summed[12], summed[13], summed[14], summed[15], summed[16], summed[17], summed[18], summed[19])
```

```python
import functools

import jax
import jax.numpy as jnp
from jax import lax
from jax.experimental import pallas as pl
from jax.experimental.pallas import tpu as pltpu
from jax.sharding import PartitionSpec as P

SEQ, TP, IMG = "seq", "tp", "img"
HEAD = 64
FF = 8192
PATCH = 256
LAT = 64
SEQ_MAX = 2048
IMG_DEV = 2


EPSILON = 1e-05
HIGHEST_PRECISION = lax.Precision.HIGHEST


def shortened(x):

    def short(part):
        return part.astype(jnp.bfloat16) if part.dtype == jnp.float32 else part

    return jax.tree.map(short, x)


def xpos_factors(position, half_size):
    ladder = jnp.arange(half_size, dtype=jnp.float32)
    frequency = jnp.exp(ladder * (-2.0 * jnp.log(10000.0) / (2.0 * half_size)))
    decay_base = (ladder / half_size + 0.4) / 1.4
    angles = position[:, None] * frequency[None, :]
    growth = jnp.exp(position[:, None] / 512.0 * jnp.log(decay_base)[None, :])
    return (jnp.cos(angles)[:, None, :], jnp.sin(angles)[:, None, :], growth[:, None, :])


def rotate(inputs, cosine, sine_table, factor):
    half_size = inputs.shape[-1] // 2
    first_half = inputs[..., :half_size]
    second_half = inputs[..., half_size:]
    turned = jnp.concatenate(
        [
            first_half * cosine - second_half * sine_table,
            first_half * sine_table + second_half * cosine,
        ],
        -1,
    )
    return turned * jnp.concatenate([factor, factor], -1)


def rotate_back(gradient, cosine, sine_table, factor):
    half_size = gradient.shape[-1] // 2
    scaled = gradient * jnp.concatenate([factor, factor], -1)
    first_half = scaled[..., :half_size]
    second_half = scaled[..., half_size:]
    return jnp.concatenate(
        [
            first_half * cosine + second_half * sine_table,
            second_half * cosine - first_half * sine_table,
        ],
        -1,
    )


def tp_total(inputs):
    return jax.tree.map(lambda part: part.astype(jnp.float32), lax.psum(shortened(inputs), TP))


def full_norm(inputs, norm_gain, norm_shift):
    center = inputs - jnp.mean(inputs, -1, keepdims=True)
    spread = jnp.mean(center * center, -1, keepdims=True)
    factor = lax.rsqrt(spread + EPSILON)
    normal = center * factor
    return (normal * norm_gain + norm_shift, normal, factor)


def full_back(gradient, normal, factor, norm_gain):
    scaled = gradient * norm_gain
    return factor * (
        scaled
        - jnp.mean(scaled, -1, keepdims=True)
        - normal * jnp.mean(scaled * normal, -1, keepdims=True)
    )


def split_norm(inputs, norm_gain, norm_shift, full_width):
    totals = tp_total(
        (jnp.sum(inputs, -1, keepdims=True), jnp.sum(inputs * inputs, -1, keepdims=True))
    )
    average = totals[0] / full_width
    spread = totals[1] / full_width - average * average
    factor = lax.rsqrt(spread + EPSILON)
    normal = (inputs - average) * factor
    return (normal * norm_gain + norm_shift, normal, factor)


def split_back(gradient, normal, factor, norm_gain, full_width):
    scaled = gradient * norm_gain
    totals = tp_total(
        (jnp.sum(scaled, -1, keepdims=True), jnp.sum(scaled * normal, -1, keepdims=True))
    )
    return factor * (scaled - totals[0] / full_width - normal * (totals[1] / full_width))


def attend_piece(
    running, query_rot, key_piece, value_piece, row_index, row_segment, segment_all, score_scale
):
    heads_local = query_rot.shape[1]
    amount = key_piece.shape[0]
    block_size = 1024

    def step(state_in, number):
        first_row = number * block_size
        key_block = lax.dynamic_slice_in_dim(key_piece, first_row, block_size, 0).reshape(
            block_size, heads_local, -1
        )
        value_block = lax.dynamic_slice_in_dim(value_piece, first_row, block_size, 0).reshape(
            block_size, heads_local, -1
        )
        key_index = first_row + jnp.arange(block_size, dtype=jnp.int32)
        key_segment = lax.dynamic_slice_in_dim(segment_all, first_row, block_size, 0)
        scores = (
            jnp.einsum("qhd,khd->hqk", query_rot, key_block, preferred_element_type=jnp.float32)
            * score_scale
        )
        allowed = (key_index[None, :] <= row_index[:, None]) & (
            key_segment[None, :] == row_segment[:, None]
        )
        scores = jnp.where(allowed[None], scores, -1e30)
        best_old, total_old, accum_old = state_in
        best_new = jnp.maximum(best_old, jnp.max(scores, -1))
        weights = jnp.where(allowed[None], jnp.exp(scores - best_new[..., None]), 0.0)
        shrink = jnp.exp(best_old - best_new)
        total_new = total_old * shrink + jnp.sum(weights, -1)
        added = jnp.einsum(
            "hqk,khd->qhd",
            weights.astype(jnp.bfloat16),
            value_block,
            preferred_element_type=jnp.float32,
        )
        accum_new = accum_old * shrink.T[:, :, None] + added
        return ((best_new, total_new, accum_new), None)

    return lax.scan(step, running, jnp.arange(amount // block_size, dtype=jnp.int32))[0]


def attend_back(
    query_rot,
    key_all,
    value_all,
    grad_attended,
    log_total,
    delta,
    row_index,
    row_segment,
    segment_all,
    score_scale,
):
    heads_local = query_rot.shape[1]
    amount = key_all.shape[0]
    block_size = 1024

    def step(dquery, number):
        first_row = number * block_size
        key_block = lax.dynamic_slice_in_dim(key_all, first_row, block_size, 0).reshape(
            block_size, heads_local, -1
        )
        value_block = lax.dynamic_slice_in_dim(value_all, first_row, block_size, 0).reshape(
            block_size, heads_local, -1
        )
        key_index = first_row + jnp.arange(block_size, dtype=jnp.int32)
        key_segment = lax.dynamic_slice_in_dim(segment_all, first_row, block_size, 0)
        scores = (
            jnp.einsum("qhd,khd->hqk", query_rot, key_block, preferred_element_type=jnp.float32)
            * score_scale
        )
        allowed = (key_index[None, :] <= row_index[:, None]) & (
            key_segment[None, :] == row_segment[:, None]
        )
        weights = jnp.where(
            allowed[None],
            jnp.exp(jnp.where(allowed[None], scores, -1e30) - log_total[..., None]),
            0.0,
        )
        dweights = jnp.einsum(
            "qhd,khd->hqk", grad_attended, value_block, preferred_element_type=jnp.float32
        )
        dscores = (weights * (dweights - delta[..., None])).astype(jnp.bfloat16)
        dquery = (
            dquery
            + jnp.einsum("hqk,khd->qhd", dscores, key_block, preferred_element_type=jnp.float32)
            * score_scale
        )
        dkeys = (
            jnp.einsum("hqk,qhd->khd", dscores, query_rot, preferred_element_type=jnp.float32)
            * score_scale
        )
        dvalues = jnp.einsum(
            "hqk,qhd->khd",
            weights.astype(jnp.bfloat16),
            grad_attended,
            preferred_element_type=jnp.float32,
        )
        return (dquery, (dkeys, dvalues))

    start_grad = jnp.zeros(query_rot.shape, jnp.float32)
    dquery, outputs = lax.scan(step, start_grad, jnp.arange(amount // block_size, dtype=jnp.int32))
    return (dquery, outputs[0].reshape(amount, -1), outputs[1].reshape(amount, -1))


def on_device(
    text,
    segment,
    features,
    image_count,
    image_slot,
    cotangent,
    input_gain,
    input_shift,
    query_weight,
    key_weight,
    value_weight,
    inner_gain,
    inner_shift,
    out_weight,
    middle_gain,
    middle_shift,
    up_weight,
    up_bias,
    hidden_gain,
    hidden_shift,
    down_weight,
    latents,
    resample_query,
    resample_key,
    resample_value,
    resample_out,
):
    row_count = text.shape[1]
    model_width = text.shape[2]
    group_rows = segment.shape[1]
    seq_rank = lax.axis_index(SEQ)
    gathered_in = (
        lax.all_gather(query_weight, (SEQ, IMG), axis=0, tiled=True),
        lax.all_gather(key_weight, (SEQ, IMG), axis=0, tiled=True),
        lax.all_gather(value_weight, (SEQ, IMG), axis=0, tiled=True),
        lax.all_gather(up_weight, (SEQ, IMG), axis=0, tiled=True),
        lax.all_gather(resample_query, (SEQ, IMG), axis=0, tiled=True),
        lax.all_gather(resample_key, (SEQ, IMG), axis=0, tiled=True),
        lax.all_gather(resample_value, (SEQ, IMG), axis=0, tiled=True),
    )
    query_full, key_full, value_full, up_full, probe_full, image_key_full, image_value_full = (
        gathered_in
    )
    gathered_out = (
        lax.all_gather(out_weight, (SEQ, IMG), axis=1, tiled=True),
        lax.all_gather(down_weight, (SEQ, IMG), axis=1, tiled=True),
        lax.all_gather(resample_out, (SEQ, IMG), axis=1, tiled=True),
        lax.all_gather(latents, (SEQ, IMG), axis=1, tiled=True),
    )
    out_full, down_full, image_out_full, latent_full = gathered_out
    half_width = query_full.shape[1]
    heads_local = half_width // HEAD
    score_scale = HEAD ** (-0.5)
    gelu_exact = functools.partial(jax.nn.gelu, approximate=False)
    image_slots = features.shape[1]
    pictures = features[0].reshape(image_slots * PATCH, features.shape[3])
    probe = (
        jnp.dot(latent_full, probe_full, preferred_element_type=jnp.float32)
        .astype(jnp.bfloat16)
        .reshape(LAT, heads_local, HEAD)
    )
    image_keys = (
        jnp.dot(pictures, image_key_full, preferred_element_type=jnp.float32)
        .astype(jnp.bfloat16)
        .reshape(image_slots, PATCH, heads_local, HEAD)
    )
    image_values = (
        jnp.dot(pictures, image_value_full, preferred_element_type=jnp.float32)
        .astype(jnp.bfloat16)
        .reshape(image_slots, PATCH, heads_local, HEAD)
    )
    image_scores = (
        jnp.einsum("qhd,iphd->ihqp", probe, image_keys, preferred_element_type=jnp.float32)
        * score_scale
    )
    image_probs = jax.nn.softmax(image_scores, -1)
    image_mixed = jnp.einsum(
        "ihqp,iphd->iqhd",
        image_probs.astype(jnp.bfloat16),
        image_values,
        preferred_element_type=jnp.float32,
    )
    image_mixed = image_mixed.astype(jnp.bfloat16).reshape(image_slots * LAT, half_width)
    embed = tp_total(jnp.dot(image_mixed, image_out_full, preferred_element_type=jnp.float32))
    embed = embed.astype(jnp.bfloat16).reshape(image_slots, LAT, model_width)
    image_total = image_slot.shape[1]
    slot_range = jnp.arange(image_total, dtype=jnp.int32)
    live = slot_range % IMG_DEV < jnp.repeat(image_count[0], IMG_DEV)
    block_local = row_count // LAT
    block_count = group_rows // LAT
    block_ids = seq_rank * block_local + jnp.arange(block_local, dtype=jnp.int32)
    owner = ((image_slot[0][None, :] == block_ids[:, None]) & live[None, :]).astype(jnp.float32)
    owner_low = owner.astype(jnp.bfloat16)
    taken = jnp.sum(owner, 1) > 0.5
    chosen = owner_low
    placed = jnp.einsum(
        "bi,ild->bld",
        chosen,
        lax.all_gather(embed, SEQ, axis=0, tiled=True),
        preferred_element_type=jnp.float32,
    )
    text_blocks = text[0].astype(jnp.float32).reshape(block_local, LAT, model_width)
    mixed_in = jnp.where(taken[:, None, None], placed, text_blocks).reshape(row_count, model_width)
    segment_all = segment[0]
    docs_count = 3 * (group_rows // min(SEQ_MAX, group_rows))
    marks = (segment_all[:, None] == jnp.arange(docs_count, dtype=jnp.int32)[None, :]).astype(
        jnp.int32
    )
    earlier_rows = jnp.cumsum(marks, 0) - marks
    position_all = jnp.sum(earlier_rows * marks, 1)
    first_local = seq_rank * row_count
    row_index = first_local + jnp.arange(row_count, dtype=jnp.int32)
    row_segment = lax.dynamic_slice_in_dim(segment_all, first_local, row_count, 0)
    position = lax.dynamic_slice_in_dim(position_all, first_local, row_count, 0).astype(jnp.float32)
    cosine, sine_table, growth = xpos_factors(position, HEAD // 2)
    input_out, input_hat, input_factor = full_norm(
        mixed_in, input_gain.astype(jnp.float32), input_shift.astype(jnp.float32)
    )
    normed = input_out.astype(jnp.bfloat16)
    query_lin = jnp.dot(normed, query_full, preferred_element_type=jnp.float32).reshape(
        row_count, heads_local, HEAD
    )
    key_lin = jnp.dot(normed, key_full, preferred_element_type=jnp.float32).reshape(
        row_count, heads_local, HEAD
    )
    value_lin = jnp.dot(normed, value_full, preferred_element_type=jnp.float32)
    query_rot = rotate(query_lin, cosine, sine_table, growth).astype(jnp.bfloat16)
    keys_rot = (
        rotate(key_lin, cosine, sine_table, 1.0 / growth)
        .astype(jnp.bfloat16)
        .reshape(row_count, half_width)
    )
    values_low = value_lin.astype(jnp.bfloat16)
    start_state = (
        jnp.full((heads_local, row_count), -1e30, jnp.float32),
        jnp.zeros((heads_local, row_count), jnp.float32),
        jnp.zeros((row_count, heads_local, HEAD), jnp.float32),
    )
    best, weight_total, accum = attend_piece(
        start_state,
        query_rot,
        lax.all_gather(keys_rot, SEQ, axis=0, tiled=True),
        lax.all_gather(values_low, SEQ, axis=0, tiled=True),
        row_index,
        row_segment,
        segment_all,
        score_scale,
    )
    attended = accum / weight_total.T[:, :, None]
    log_total = best + jnp.log(weight_total)
    inner_out, inner_hat, inner_factor = split_norm(
        attended.reshape(row_count, half_width),
        inner_gain.astype(jnp.float32),
        inner_shift.astype(jnp.float32),
        model_width,
    )
    inner_low = inner_out.astype(jnp.bfloat16)
    middle = mixed_in + tp_total(jnp.dot(inner_low, out_full, preferred_element_type=jnp.float32))
    lifted_out, lifted_hat, lifted_factor = full_norm(
        middle, middle_gain.astype(jnp.float32), middle_shift.astype(jnp.float32)
    )
    lifted = lifted_out.astype(jnp.bfloat16)
    hidden_pre = jnp.dot(lifted, up_full, preferred_element_type=jnp.float32) + up_bias.astype(
        jnp.float32
    )
    activated, gelu_pull = jax.vjp(gelu_exact, hidden_pre)
    settled_out, settled_hat, settled_factor = split_norm(
        activated, hidden_gain.astype(jnp.float32), hidden_shift.astype(jnp.float32), FF
    )
    settled = settled_out.astype(jnp.bfloat16)
    final_rows = middle + tp_total(jnp.dot(settled, down_full, preferred_element_type=jnp.float32))
    result = final_rows.astype(jnp.bfloat16).reshape(1, row_count, model_width)
    grad_low = cotangent[0]
    grad_rows = grad_low.astype(jnp.float32)
    down_grad = jnp.dot(settled.T, grad_low, preferred_element_type=jnp.float32)
    d_settled = jnp.dot(grad_low, down_full.T, preferred_element_type=jnp.float32)
    hidden_gain_grad = jnp.sum(d_settled * settled_hat, 0)
    hidden_shift_grad = jnp.sum(d_settled, 0)
    d_activated = split_back(
        d_settled, settled_hat, settled_factor, hidden_gain.astype(jnp.float32), FF
    )
    d_hidden = gelu_pull(d_activated)[0].astype(jnp.bfloat16)
    up_bias_grad = jnp.sum(d_hidden.astype(jnp.float32), 0)
    up_grad = jnp.dot(lifted.T, d_hidden, preferred_element_type=jnp.float32)
    d_lifted = tp_total(jnp.dot(d_hidden, up_full.T, preferred_element_type=jnp.float32))
    middle_gain_grad = jnp.sum(d_lifted * lifted_hat, 0)
    middle_shift_grad = jnp.sum(d_lifted, 0)
    d_middle = grad_rows + full_back(
        d_lifted, lifted_hat, lifted_factor, middle_gain.astype(jnp.float32)
    )
    d_branch = d_middle.astype(jnp.bfloat16)
    out_grad = jnp.dot(inner_low.T, d_branch, preferred_element_type=jnp.float32)
    d_inner = jnp.dot(d_branch, out_full.T, preferred_element_type=jnp.float32)
    inner_gain_grad = jnp.sum(d_inner * inner_hat, 0)
    inner_shift_grad = jnp.sum(d_inner, 0)
    d_attended = split_back(
        d_inner, inner_hat, inner_factor, inner_gain.astype(jnp.float32), model_width
    )
    d_attended = d_attended.astype(jnp.bfloat16).reshape(row_count, heads_local, HEAD)
    delta = jnp.sum(d_attended.astype(jnp.float32) * attended, -1).T
    key_back, value_back = (
        lax.all_gather(keys_rot, SEQ, axis=0, tiled=True),
        lax.all_gather(values_low, SEQ, axis=0, tiled=True),
    )
    d_query_rot, d_key_term, d_value_term = attend_back(
        query_rot,
        key_back,
        value_back,
        d_attended,
        log_total,
        delta,
        row_index,
        row_segment,
        segment_all,
        score_scale,
    )
    d_key_sum, d_value_sum = (
        lax.psum_scatter(
            d_key_term.astype(jnp.bfloat16), SEQ, scatter_dimension=0, tiled=True
        ).astype(jnp.float32),
        lax.psum_scatter(
            d_value_term.astype(jnp.bfloat16), SEQ, scatter_dimension=0, tiled=True
        ).astype(jnp.float32),
    )
    d_query_lin = (
        rotate_back(d_query_rot, cosine, sine_table, growth)
        .astype(jnp.bfloat16)
        .reshape(row_count, half_width)
    )
    d_key_lin = (
        rotate_back(
            d_key_sum.reshape(row_count, heads_local, HEAD), cosine, sine_table, 1.0 / growth
        )
        .astype(jnp.bfloat16)
        .reshape(row_count, half_width)
    )
    d_value_lin = d_value_sum.astype(jnp.bfloat16)
    query_grad = jnp.dot(normed.T, d_query_lin, preferred_element_type=jnp.float32)
    key_grad = jnp.dot(normed.T, d_key_lin, preferred_element_type=jnp.float32)
    value_grad = jnp.dot(normed.T, d_value_lin, preferred_element_type=jnp.float32)
    d_normed_part = (
        jnp.dot(d_query_lin, query_full.T, preferred_element_type=jnp.float32)
        + jnp.dot(d_key_lin, key_full.T, preferred_element_type=jnp.float32)
        + jnp.dot(d_value_lin, value_full.T, preferred_element_type=jnp.float32)
    )
    d_normed = tp_total(d_normed_part)
    input_gain_grad = jnp.sum(d_normed * input_hat, 0)
    input_shift_grad = jnp.sum(d_normed, 0)
    d_mixed = d_middle + full_back(
        d_normed, input_hat, input_factor, input_gain.astype(jnp.float32)
    )
    d_blocks = d_mixed.reshape(block_local, LAT, model_width)
    text_grad = jnp.where(taken[:, None, None], 0.0, d_blocks).reshape(1, row_count, model_width)
    my_target = lax.dynamic_slice_in_dim(image_slot[0], seq_rank * image_slots, image_slots, 0)
    my_live = lax.dynamic_slice_in_dim(live, seq_rank * image_slots, image_slots, 0)
    owner_mine = (
        (jnp.arange(block_count, dtype=jnp.int32)[:, None] == my_target[None, :]) & my_live[None, :]
    ).astype(jnp.bfloat16)
    chosen = owner_mine
    d_embed = jnp.einsum(
        "bi,bld->ild",
        chosen,
        lax.all_gather(d_blocks.astype(jnp.bfloat16), SEQ, axis=0, tiled=True),
        preferred_element_type=jnp.float32,
    )
    d_embed_low = d_embed.astype(jnp.bfloat16).reshape(image_slots * LAT, model_width)
    resample_out_grad = jnp.dot(image_mixed.T, d_embed_low, preferred_element_type=jnp.float32)
    d_image_mixed = jnp.dot(d_embed_low, image_out_full.T, preferred_element_type=jnp.float32)
    d_image_mixed = d_image_mixed.astype(jnp.bfloat16).reshape(image_slots, LAT, heads_local, HEAD)
    d_image_probs = jnp.einsum(
        "iqhd,iphd->ihqp", d_image_mixed, image_values, preferred_element_type=jnp.float32
    )
    d_image_scores = image_probs * (
        d_image_probs - jnp.sum(image_probs * d_image_probs, -1, keepdims=True)
    )
    d_image_scores = d_image_scores.astype(jnp.bfloat16)
    d_probe = (
        jnp.einsum("ihqp,iphd->qhd", d_image_scores, image_keys, preferred_element_type=jnp.float32)
        * score_scale
    )
    d_image_keys = (
        jnp.einsum("ihqp,qhd->iphd", d_image_scores, probe, preferred_element_type=jnp.float32)
        * score_scale
    ).astype(jnp.bfloat16)
    d_image_values = jnp.einsum(
        "ihqp,iqhd->iphd",
        image_probs.astype(jnp.bfloat16),
        d_image_mixed,
        preferred_element_type=jnp.float32,
    ).astype(jnp.bfloat16)
    resample_key_grad = jnp.dot(
        pictures.T,
        d_image_keys.reshape(image_slots * PATCH, half_width),
        preferred_element_type=jnp.float32,
    )
    resample_value_grad = jnp.dot(
        pictures.T,
        d_image_values.reshape(image_slots * PATCH, half_width),
        preferred_element_type=jnp.float32,
    )
    d_probe_flat = d_probe.reshape(LAT, half_width)
    resample_query_grad = jnp.dot(
        latent_full.astype(jnp.float32).T, d_probe_flat, precision=HIGHEST_PRECISION
    )
    latent_grad = tp_total(
        jnp.dot(d_probe_flat, probe_full.astype(jnp.float32).T, precision=HIGHEST_PRECISION)
    )
    summed_in = (
        lax.psum_scatter(query_grad, (SEQ, IMG), scatter_dimension=0, tiled=True),
        lax.psum_scatter(key_grad, (SEQ, IMG), scatter_dimension=0, tiled=True),
        lax.psum_scatter(value_grad, (SEQ, IMG), scatter_dimension=0, tiled=True),
        lax.psum_scatter(up_grad, (SEQ, IMG), scatter_dimension=0, tiled=True),
        lax.psum_scatter(resample_query_grad, (SEQ, IMG), scatter_dimension=0, tiled=True),
        lax.psum_scatter(resample_key_grad, (SEQ, IMG), scatter_dimension=0, tiled=True),
        lax.psum_scatter(resample_value_grad, (SEQ, IMG), scatter_dimension=0, tiled=True),
    )
    summed_out = (
        lax.psum_scatter(out_grad, (SEQ, IMG), scatter_dimension=1, tiled=True),
        lax.psum_scatter(down_grad, (SEQ, IMG), scatter_dimension=1, tiled=True),
        lax.psum_scatter(resample_out_grad, (SEQ, IMG), scatter_dimension=1, tiled=True),
        lax.psum_scatter(latent_grad, (SEQ, IMG), scatter_dimension=1, tiled=True),
    )
    summed_small = lax.psum(
        (
            input_gain_grad,
            input_shift_grad,
            inner_gain_grad,
            inner_shift_grad,
            middle_gain_grad,
            middle_shift_grad,
            up_bias_grad,
            hidden_gain_grad,
            hidden_shift_grad,
        ),
        (SEQ, IMG),
    )
    return (
        result,
        text_grad,
        summed_small[0],
        summed_small[1],
        summed_in[0],
        summed_in[1],
        summed_in[2],
        summed_small[2],
        summed_small[3],
        summed_out[0],
        summed_small[4],
        summed_small[5],
        summed_in[3],
        summed_small[6],
        summed_small[7],
        summed_small[8],
        summed_out[1],
        summed_out[3],
        summed_in[4],
        summed_in[5],
        summed_in[6],
        summed_out[2],
    )


MESH_IDS = pl.DeviceIdType.MESH
ANYWHERE = pl.BlockSpec(memory_space=pl.ANY)
ON_CHIP = pl.BlockSpec(memory_space=pltpu.VMEM)
LANES = 128
PLANE = 8
VMEM_BYTES = 60 * 1024 * 1024
PIECES = 4
FRONT, BACK, ALL, ROWS, INWARD, OUTWARD = range(6)


def narrow_heads(mesh):
    return mesh.shape[SEQ] != PLANE or mesh.shape[IMG] != 2 or mesh.shape[TP] != 2


def flipped(number, bit):
    step = 2**bit
    return number + step - 2 * step * ((number // step) % 2)


class Places:
    def __init__(self):
        self.seq, self.tp, self.img = (lax.axis_index(name) for name in (SEQ, TP, IMG))
        self.s_core, self.s_x, self.s_y = (flipped(self.seq, bit) for bit in range(3))
        self.s_xy = flipped(self.s_x, 2)
        self.core, self.x, self.y = (self.at(seq) for seq in (self.s_core, self.s_x, self.s_y))
        self.tp_peer = (self.seq, 1 - self.tp, self.img)
        self.img_peer = (self.seq, self.tp, 1 - self.img)

    def at(self, seq):
        return (seq, self.tp, self.img)


def greet(peers):
    barrier = pltpu.get_barrier_semaphore()
    for peer in peers:
        pl.semaphore_signal(barrier, inc=1, device_id=peer, device_id_type=MESH_IDS)
    pl.semaphore_wait(barrier, len(peers))


def remote(src, dst, send, recv, peer):
    return pltpu.make_async_remote_copy(
        src_ref=src, dst_ref=dst, send_sem=send, recv_sem=recv, device_id=peer, device_id_type=MESH_IDS
    )


def rows_at(ref, first, count):
    return ref.at[pl.ds(pl.multiple_of(first, 16), count)]


class Spread:
    def __init__(self, here, out, block, first, count, send, recv):
        self.here, self.out, self.block = here, out, block
        self.first, self.count, self.send, self.recv = first, count, send, recv
        self.half = count // 2
        self.sent = []

    def part(self, seq, which):
        first = seq * self.block + self.first
        if which == ALL:
            return rows_at(self.out, first, self.count)
        return rows_at(self.out, first + (self.half if which == BACK else 0), self.half)

    def copy(self, src, dst, slot, peer):
        return remote(src, dst, self.send.at[slot], self.recv.at[slot], peer)

    def go(self, src, dst, slot, peer):
        made = self.copy(src, dst, slot, peer)
        made.start()
        self.sent.append(made)

    def own(self, src, src_first):
        here, seq = self.here, self.here.seq

        def own_part(which):
            if which == ALL:
                return rows_at(src, src_first, self.count)
            return rows_at(src, src_first + (self.half if which == BACK else 0), self.half)

        self.go(own_part(FRONT), self.part(seq, FRONT), 0, here.x)
        self.go(own_part(BACK), self.part(seq, BACK), 1, here.y)
        self.go(own_part(BACK), self.part(seq, BACK), 2, here.x)
        self.go(own_part(FRONT), self.part(seq, FRONT), 3, here.y)
        self.go(own_part(ALL), self.part(seq, ALL), 4, here.core)

    def arrived(self, slot, seq, which):
        target = self.part(seq, which)
        self.copy(target, target, slot, self.here.core).wait_recv()

    def forward(self):
        here = self.here
        self.arrived(0, here.s_x, FRONT)
        self.go(self.part(here.s_x, FRONT), self.part(here.s_x, FRONT), 5, here.y)
        self.arrived(1, here.s_y, BACK)
        self.go(self.part(here.s_y, BACK), self.part(here.s_y, BACK), 6, here.x)
        self.arrived(2, here.s_x, BACK)
        self.go(self.part(here.s_x, ALL), self.part(here.s_x, ALL), 7, here.core)
        self.arrived(3, here.s_y, FRONT)
        self.go(self.part(here.s_y, ALL), self.part(here.s_y, ALL), 8, here.core)

    def corner(self):
        here = self.here
        self.arrived(5, here.s_xy, FRONT)
        self.arrived(6, here.s_xy, BACK)
        self.go(self.part(here.s_xy, ALL), self.part(here.s_xy, ALL), 9, here.core)

    def finish(self):
        core = self.here.s_core
        self.arrived(4, core, ALL)
        self.arrived(7, flipped(core, 1), ALL)
        self.arrived(8, flipped(core, 2), ALL)
        self.arrived(9, flipped(flipped(core, 1), 2), ALL)
        for made in self.sent:
            made.wait_send()


def wavefront(stages, count, waiting=()):
    waiting = list(waiting)
    ticks = count + max(lag for lag, _ in stages)
    share = -(-len(waiting) // max(ticks - 2, 1))
    for tick in range(ticks):
        for lag, stage in reversed(stages):
            piece = tick - lag
            if 0 <= piece < count:
                stage(piece)
        for launch in waiting[:share]:
            launch()
        del waiting[:share]


def weight_blocks(weight, side):
    if side == INWARD:
        return (weight.shape[0], weight.shape[1] // PLANE)
    return (weight.shape[0] // PLANE, weight.shape[1])


def intake(gathered, weights, sides, cid):
    n_rows, n_weights = len(gathered), len(weights)
    pieces = PIECES

    def kernel(*refs):
        row_refs, weight_refs = refs[:n_rows], refs[n_rows : n_rows + n_weights]
        refs = refs[n_rows + n_weights :]
        row_outs, weight_outs = refs[:n_rows], refs[n_rows : n_rows + n_weights]
        local, send, recv, w_local, w_send, w_recv, z_send, z_recv = refs[n_rows + n_weights :]
        here = Places()
        seq, tp, img = here.seq, here.tp, here.img
        others = [lax.rem(seq + step, PLANE) for step in range(1, PLANE)]
        greet([(other, tp, img) for other in others] + [here.img_peer])

        def slot_of(out, side, shape, from_seq, from_img):
            number = from_seq * 2 + from_img
            if side == INWARD:
                return out.at[pl.ds(pl.multiple_of(number * shape[0], shape[0]), shape[0])]
            return out.at[:, pl.ds(pl.multiple_of(number * shape[1], shape[1]), shape[1])]

        def block_of(weight, side, shape, to_seq):
            if side == INWARD:
                return weight.at[:, pl.ds(pl.multiple_of(to_seq * shape[1], shape[1]), shape[1])]
            return weight.at[pl.ds(pl.multiple_of(to_seq * shape[0], shape[0]), shape[0])]

        flights, own_copies = [], []

        def begin(index):
            weight, out, side = weight_refs[index], weight_outs[index], sides[index]
            shape = weight_blocks(weight, side)
            mine = pltpu.make_async_copy(
                block_of(weight, side, shape, seq), slot_of(out, side, shape, seq, img), w_local.at[index]
            )
            mine.start()
            crossing = remote(
                block_of(weight, side, shape, seq),
                slot_of(out, side, shape, seq, img),
                z_send.at[index, 0],
                z_recv.at[index, 0],
                here.img_peer,
            )
            crossing.start()
            own_copies.append(mine)
            flights.append(crossing)
            for step, other in enumerate(others, 1):
                made = remote(
                    block_of(weight, side, shape, other),
                    slot_of(out, side, shape, seq, img),
                    w_send.at[index, step],
                    w_recv.at[index, step],
                    here.at(other),
                )
                made.start()
                flights.append(made)

        spreads = []
        for number, (rows, out) in enumerate(zip(row_refs, row_outs)):
            block = rows.shape[0]
            count = block // pieces
            keep = pltpu.make_async_copy(rows, rows_at(out, seq * block, block), local.at[number])
            keep.start()
            own_copies.append(keep)
            for piece in range(pieces):
                at = number * pieces + piece
                spreads.append(
                    (Spread(here, out, block, piece * count, count, send.at[at], recv.at[at]), rows, piece * count)
                )

        def cross(piece):
            for index in range(piece, n_weights, len(spreads)):
                weight, out, side = weight_refs[index], weight_outs[index], sides[index]
                shape = weight_blocks(weight, side)
                for step in range(1, PLANE):
                    source = lax.rem(seq + PLANE - step, PLANE)
                    landed = slot_of(out, side, shape, source, img)
                    remote(landed, landed, w_send.at[index, step], w_recv.at[index, step], here.core).wait_recv()
                    crossing = remote(
                        landed, landed, z_send.at[index, step], z_recv.at[index, step], here.img_peer
                    )
                    crossing.start()
                    flights.append(crossing)

        def own_rows(piece):
            for index in range(piece, n_weights, len(spreads)):
                begin(index)
            spreads[piece][0].own(spreads[piece][1], spreads[piece][2])

        wavefront(
            [
                (0, own_rows),
                (2, lambda piece: spreads[piece][0].forward()),
                (3, lambda piece: cross(piece)),
                (4, lambda piece: spreads[piece][0].corner()),
            ],
            len(spreads),
        )
        for index, (weight, out, side) in enumerate(zip(weight_refs, weight_outs, sides)):
            shape = weight_blocks(weight, side)
            for step in range(PLANE):
                source = lax.rem(seq + PLANE - step, PLANE)
                landed = slot_of(out, side, shape, source, 1 - img)
                remote(landed, landed, z_send.at[index, step], z_recv.at[index, step], here.core).wait_recv()
        for spread, _, _ in spreads:
            spread.finish()
        for made in flights:
            made.wait_send()
        for made in own_copies:
            made.wait()

    def whole(weight, side):
        shape = weight_blocks(weight, side)
        if side == INWARD:
            return jax.ShapeDtypeStruct((2 * PLANE * shape[0], shape[1]), weight.dtype)
        return jax.ShapeDtypeStruct((shape[0], 2 * PLANE * shape[1]), weight.dtype)

    dma = pltpu.SemaphoreType.DMA
    outs = [jax.ShapeDtypeStruct((PLANE * rows.shape[0], rows.shape[1]), rows.dtype) for rows in gathered]
    outs += [whole(weight, side) for weight, side in zip(weights, sides)]
    made = pl.pallas_call(
        kernel,
        out_shape=tuple(outs),
        in_specs=[ANYWHERE] * (n_rows + n_weights),
        out_specs=tuple([ANYWHERE] * len(outs)),
        scratch_shapes=[
            dma((n_rows,)),
            dma((n_rows * pieces, 10)),
            dma((n_rows * pieces, 10)),
            dma((n_weights,)),
            dma((n_weights, PLANE)),
            dma((n_weights, PLANE)),
            dma((n_weights, PLANE)),
            dma((n_weights, PLANE)),
        ],
        compiler_params=pltpu.CompilerParams(
            collective_id=cid, has_side_effects=True, vmem_limit_bytes=VMEM_BYTES
        ),
    )(*gathered, *weights)
    return made[:n_rows], made[n_rows:]


class Rider:
    inputs, out_shapes, scratch = (), (), ()

    def bind(self, here, ins, outs, scratch):
        self.here, self.ins, self.outs, self.held = here, ins, outs, scratch
        self.sent, self.kept, self.due, self.launches = [], [], [], []

    def keep(self, src, dst, sem):
        made = pltpu.make_async_copy(src, dst, sem)
        self.launches.append(made.start)
        self.kept.append(made)

    def send(self, src, dst, send, recv, peer):
        made = remote(src, dst, send, recv, peer)
        self.launches.append(made.start)
        self.sent.append(made)

    def finish(self):
        for dst, send, recv in self.due:
            remote(dst, dst, send, recv, self.here.core).wait_recv()
        for made in self.sent:
            made.wait_send()
        for made in self.kept:
            made.wait()


class PlaneWeights(Rider):
    def __init__(self, weights, sides):
        self.inputs, self.sides = weights, sides
        self.blocks = [weight_blocks(weight, side) for weight, side in zip(weights, sides)]
        self.out_shapes = [
            jax.ShapeDtypeStruct((PLANE,) + block, weight.dtype) for block, weight in zip(self.blocks, weights)
        ]
        dma = pltpu.SemaphoreType.DMA
        self.scratch = [dma((len(weights), PLANE)), dma((len(weights), PLANE))]

    def peers(self, here):
        return [here.at(lax.rem(here.seq + step, PLANE)) for step in range(1, PLANE)]

    def start(self):
        here, (send, recv) = self.here, self.held
        for index, (weight, out, side, block) in enumerate(zip(self.ins, self.outs, self.sides, self.blocks)):
            for step in range(PLANE):
                target = lax.rem(here.seq + step, PLANE)
                source = lax.rem(here.seq + PLANE - step, PLANE)
                if side == INWARD:
                    part = weight.at[:, pl.ds(pl.multiple_of(target * block[1], block[1]), block[1])]
                else:
                    part = weight.at[pl.ds(pl.multiple_of(target * block[0], block[0]), block[0])]
                if step == 0:
                    self.keep(part, out.at[here.seq], recv.at[index, 0])
                else:
                    self.send(part, out.at[here.seq], send.at[index, step], recv.at[index, step], here.at(target))
                    self.due.append((out.at[source], send.at[index, step], recv.at[index, step]))


class CrossWeights(Rider):
    def __init__(self, blocks, sides):
        self.inputs, self.sides = blocks, sides
        self.out_shapes = []
        for block, side in zip(blocks, sides):
            count, rows, columns = block.shape
            shape = (count, 2, rows, columns) if side == INWARD else (rows, count * 2 * columns)
            self.out_shapes.append(jax.ShapeDtypeStruct(shape, block.dtype))
        dma = pltpu.SemaphoreType.DMA
        self.scratch = [dma((len(blocks), PLANE)), dma((len(blocks), PLANE)), dma((len(blocks), PLANE))]

    def peers(self, here):
        return [here.img_peer]

    def start(self):
        here, (send, recv, local) = self.here, self.held
        for index, (block, out, side) in enumerate(zip(self.ins, self.outs, self.sides)):
            width = block.shape[2]
            for seq in range(PLANE):

                def place(img, seq=seq, width=width, out=out, side=side):
                    if side == INWARD:
                        return out.at[seq, img]
                    return out.at[:, pl.ds(pl.multiple_of((seq * 2 + img) * width, width), width)]

                self.send(
                    block.at[seq], place(here.img), send.at[index, seq], recv.at[index, seq], here.img_peer
                )
                self.keep(block.at[seq], place(here.img), local.at[index, seq])
                self.due.append((place(1 - here.img), send.at[index, seq], recv.at[index, seq]))


class CrossGrads(Rider):
    def __init__(self, grads, sides):
        self.inputs, self.sides = grads, sides
        self.out_shapes = []
        for grad, side in zip(grads, sides):
            if side == INWARD:
                shape = (grad.shape[0], grad.shape[2], grad.shape[3])
            else:
                shape = (PLANE, grad.shape[0], grad.shape[1] // (2 * PLANE))
            self.out_shapes.append(jax.ShapeDtypeStruct(shape, grad.dtype))
        dma = pltpu.SemaphoreType.DMA
        self.scratch = [dma((len(grads), PLANE)), dma((len(grads), PLANE))]

    def peers(self, here):
        return [here.img_peer]

    def start(self):
        here, (send, recv) = self.here, self.held
        for index, (grad, out, side) in enumerate(zip(self.ins, self.outs, self.sides)):
            width = out.shape[2]
            for seq in range(PLANE):
                if side == INWARD:
                    part = grad.at[seq, 1 - here.img]
                else:
                    part = grad.at[:, pl.ds(pl.multiple_of((seq * 2 + 1 - here.img) * width, width), width)]
                self.send(part, out.at[seq], send.at[index, seq], recv.at[index, seq], here.img_peer)
                self.due.append((out.at[seq], send.at[index, seq], recv.at[index, seq]))


class Stream:
    def __init__(self, left, right, across, row_inputs, row_kinds, row_outs, row_function, gather):
        self.inputs = [left, right] + list(row_inputs)
        self.across, self.row_kinds, self.row_outs = across, row_kinds, row_outs
        self.row_function, self.gather = row_function, gather
        rows_all = left.shape[0]
        width = right.shape[0] if across else right.shape[1]
        self.width, self.block, self.pieces = width, rows_all // PLANE, PIECES
        self.count = self.block // self.pieces
        self.half = self.count // 2
        low_type = jnp.bfloat16
        self.out_shapes = [shape for shape, _ in row_outs]
        if gather:
            self.out_shapes.append(jax.ShapeDtypeStruct((rows_all, width), low_type))
        dma = pltpu.SemaphoreType.DMA
        block, pieces, count, half = self.block, self.pieces, self.count, self.half
        self.scratch = [
            pltpu.VMEM((4, block, width), low_type),
            pltpu.VMEM((4, block, width), low_type),
            pltpu.VMEM((4, block, width), jnp.float32),
            pltpu.VMEM((pieces, half, width), low_type),
            pltpu.VMEM((pieces, half, width), low_type),
            pltpu.VMEM((pieces, count, width), low_type),
            pltpu.VMEM((pieces, count, width), low_type),
            pltpu.VMEM((pieces, count, width), low_type),
            pltpu.VMEM((pieces, count, width), low_type),
            pltpu.VMEM((block, width), low_type),
            dma((4,)),
            dma((4,)),
            dma((pieces, 7)),
            dma((pieces, 7)),
            dma((pieces, 10)),
            dma((pieces, 10)),
            dma((pieces,)),
        ]

    def out_specs(self):
        return [ON_CHIP] * len(self.row_outs) + [ANYWHERE] * (len(self.out_shapes) - len(self.row_outs))

    def peers(self, here):
        return [here.core, here.x, here.y, here.tp_peer]

    def bind(self, here, ins, outs, scratch):
        self.here = here
        self.left, self.right, self.ins = ins[0], ins[1], ins[2:]
        self.outs = outs
        (self.away, self.core_in, self.near, self.from_xd, self.from_yd, self.from_x, self.from_y) = scratch[:7]
        (self.mine, self.theirs, self.low, self.c_send, self.c_recv) = scratch[7:12]
        (self.send, self.recv, self.g_send, self.g_recv, self.l_sem) = scratch[12:]
        self.sent, self.spreads, self.core_copies = [], [], {}

    def chunk(self, base, kind):
        if kind in (1, 3):
            base = flipped(base, 1)
        if kind in (2, 3):
            base = flipped(base, 2)
        return base

    def product(self, seq, target, low_type):
        first = pl.multiple_of(seq * self.block, self.block)
        rows = self.left[pl.ds(first, self.block), :]
        step = min(512, self.width)
        for column in range(0, self.width, step):
            if self.across:
                part = lax.dot_general(
                    rows,
                    self.right[column : column + step, :],
                    (((1,), (1,)), ((), ())),
                    preferred_element_type=jnp.float32,
                )
            else:
                part = jnp.dot(
                    rows, self.right[:, column : column + step], preferred_element_type=jnp.float32
                )
            target[:, column : column + step] = part.astype(low_type)

    def begin(self):
        here = self.here
        for kind in (3, 1, 2, 0):
            self.product(self.chunk(here.s_core, kind), self.away.at[kind], jnp.bfloat16)
            made = remote(
                self.away.at[kind], self.core_in.at[kind], self.c_send.at[kind], self.c_recv.at[kind], here.core
            )
            made.start()
            self.core_copies[kind] = made
            self.product(self.chunk(here.seq, kind), self.near.at[kind], jnp.float32)

    def go(self, src, dst, piece, slot, peer):
        made = remote(src, dst, self.send.at[piece, slot], self.recv.at[piece, slot], peer)
        made.start()
        self.sent.append(made)

    def landed(self, dst, piece, slot):
        remote(dst, dst, self.send.at[piece, slot], self.recv.at[piece, slot], self.here.core).wait_recv()

    def held(self, kind, piece, which=ALL):
        first, rows = piece * self.count, self.count
        if which != ALL:
            first, rows = first + (self.half if which == BACK else 0), self.half
        return self.core_in.at[kind, pl.ds(first, rows)]

    def folded(self, kind, piece):
        if piece == 0:
            self.core_copies[kind].wait_recv()
        near = self.near[kind, pl.ds(piece * self.count, self.count), :]
        return self.held(kind, piece)[...].astype(jnp.float32) + near

    def first_sends(self, piece):
        here, half = self.here, self.half
        self.held(3, piece)[...] = self.folded(3, piece).astype(jnp.bfloat16)
        self.go(self.held(3, piece, FRONT), self.from_xd.at[piece], piece, 0, here.x)
        self.go(self.held(3, piece, BACK), self.from_yd.at[piece], piece, 1, here.y)
        self.held(1, piece)[...] = self.folded(1, piece).astype(jnp.bfloat16)
        self.go(self.held(1, piece, FRONT), self.from_x.at[piece, pl.ds(0, half)], piece, 2, here.x)
        self.held(2, piece)[...] = self.folded(2, piece).astype(jnp.bfloat16)
        self.go(self.held(2, piece, BACK), self.from_y.at[piece, pl.ds(half, half)], piece, 3, here.y)

    def second_sends(self, piece):
        here, half = self.here, self.half
        self.landed(self.from_xd.at[piece], piece, 0)
        at = self.held(2, piece, FRONT)
        at[...] = (at[...].astype(jnp.float32) + self.from_xd[piece].astype(jnp.float32)).astype(jnp.bfloat16)
        self.go(at, self.from_y.at[piece, pl.ds(0, half)], piece, 4, here.y)
        self.landed(self.from_yd.at[piece], piece, 1)
        at = self.held(1, piece, BACK)
        at[...] = (at[...].astype(jnp.float32) + self.from_yd[piece].astype(jnp.float32)).astype(jnp.bfloat16)
        self.go(at, self.from_x.at[piece, pl.ds(half, half)], piece, 5, here.x)

    def plane_sum(self, piece):
        half = self.half
        self.landed(self.from_x.at[piece, pl.ds(0, half)], piece, 2)
        self.landed(self.from_y.at[piece, pl.ds(half, half)], piece, 3)
        self.landed(self.from_y.at[piece, pl.ds(0, half)], piece, 4)
        self.landed(self.from_x.at[piece, pl.ds(half, half)], piece, 5)
        total = self.folded(0, piece)
        total = total + self.from_x[piece].astype(jnp.float32) + self.from_y[piece].astype(jnp.float32)
        self.mine[piece] = total.astype(jnp.bfloat16)
        self.go(self.mine.at[piece], self.theirs.at[piece], piece, 6, self.here.tp_peer)

    def rows_done(self, piece):
        here = self.here
        self.landed(self.theirs.at[piece], piece, 6)
        total = self.mine[piece].astype(jnp.float32) + self.theirs[piece].astype(jnp.float32)
        rows = pl.ds(piece * self.count, self.count)
        views = [ref.at[rows] if kind == ROWS else ref for ref, kind in zip(self.ins, self.row_kinds)]
        out_views = [ref.at[rows] if kind == ROWS else ref for ref, (_, kind) in zip(self.outs, self.row_outs)]
        given = self.row_function(total, piece, views, out_views)
        if self.gather:
            out = self.outs[-1]
            self.low[rows, :] = given
            first = pl.multiple_of(here.seq * self.block + piece * self.count, 16)
            keep = pltpu.make_async_copy(self.low.at[rows], out.at[pl.ds(first, self.count)], self.l_sem.at[piece])
            keep.start()
            spread = Spread(
                here, out, self.block, piece * self.count, self.count, self.g_send.at[piece], self.g_recv.at[piece]
            )
            spread.own(self.low, piece * self.count)
            self.spreads.append((spread, keep))

    def stages(self):
        stages = [(0, self.first_sends), (1, self.second_sends), (2, self.plane_sum), (4, self.rows_done)]
        if self.gather:
            stages.append((5, lambda piece: self.spreads[piece][0].forward()))
            stages.append((6, lambda piece: self.spreads[piece][0].corner()))
        return stages

    def finish(self):
        for spread, keep in self.spreads:
            spread.finish()
            keep.wait()
        for made in self.sent:
            made.wait_send()
        for made in self.core_copies.values():
            made.wait_send()


def exchange(streams, riders, cid):
    parts = list(streams) + list(riders)

    def kernel(*refs):
        here = Places()
        refs = list(refs)

        def take(count):
            taken = refs[:count]
            del refs[:count]
            return taken

        ins = [take(len(part.inputs)) for part in parts]
        outs = [take(len(part.out_shapes)) for part in parts]
        for part, part_ins, part_outs in zip(parts, ins, outs):
            part.bind(here, part_ins, part_outs, take(len(part.scratch)))
        wide_riders = [rider for rider in riders if len(rider.peers(here)) > 1]
        peers = [here.tp_peer]
        if any(not isinstance(rider, PlaneWeights) for rider in riders):
            peers.append(here.img_peer)
        if wide_riders:
            peers += wide_riders[0].peers(here)
        else:
            peers += [here.core, here.x, here.y]
        greet(peers)
        streams[0].begin()
        for rider in riders:
            rider.start()
        for stream in streams[1:]:
            stream.begin()
        stages = []
        for stream in reversed(streams):
            stages += stream.stages()
        wavefront(stages, PIECES, [launch for rider in riders for launch in rider.launches])
        for part in parts:
            part.finish()

    out_shapes = [shape for part in parts for shape in part.out_shapes]
    in_specs = [ON_CHIP] * sum(len(stream.inputs) for stream in streams)
    in_specs += [ANYWHERE] * sum(len(rider.inputs) for rider in riders)
    out_specs = [spec for stream in streams for spec in stream.out_specs()]
    out_specs += [ANYWHERE] * sum(len(rider.out_shapes) for rider in riders)
    made = pl.pallas_call(
        kernel,
        out_shape=tuple(out_shapes),
        in_specs=in_specs,
        out_specs=tuple(out_specs),
        scratch_shapes=[item for part in parts for item in part.scratch],
        compiler_params=pltpu.CompilerParams(
            collective_id=cid, has_side_effects=True, vmem_limit_bytes=VMEM_BYTES
        ),
    )(*[value for part in parts for value in part.inputs])
    made = list(made)
    split = []
    for part in parts:
        split.append(made[: len(part.out_shapes)])
        del made[: len(part.out_shapes)]
    return split


def finale(pairs, late, sides, late_sides, small, latents_t, query_rows, cid):
    n, n_late = len(sides), len(late_sides)
    all_sides = list(sides) + list(late_sides)
    grads = [grad for grad, _ in pairs] + list(late)

    def block_shape(grad, side):
        if side == INWARD:
            return (grad.shape[2], grad.shape[3])
        return (grad.shape[0], grad.shape[1] // (2 * PLANE))

    blocks = [block_shape(grad, side) for grad, side in zip(grads, all_sides)]
    total = n + n_late

    def kernel(*refs):
        refs = list(refs)

        def take(count):
            taken = refs[:count]
            del refs[:count]
            return taken

        grad_refs = take(total)
        theirs = take(n)
        small_ref, latents_ref, query_ref = take(3)
        out_refs = take(total)
        sums_out, query_out, latent_out = take(3)
        late_theirs = take(n_late)
        summed = take(total)
        small_theirs, small_mine, small_all, lat_mine, lat_theirs = take(5)
        z_send, z_recv, send, recv, local, s_send, s_recv = take(7)
        here = Places()
        seq, img = here.seq, here.img
        ring = [here.at(lax.rem(seq + step, PLANE)) for step in range(1, PLANE)]
        greet(ring + [here.img_peer, here.tp_peer])
        theirs = theirs + late_theirs

        def part_of(index, to_seq, to_img):
            ref, block = grad_refs[index], blocks[index]
            if all_sides[index] == INWARD:
                return ref.at[to_seq, to_img]
            return ref.at[:, pl.ds(pl.multiple_of((to_seq * 2 + to_img) * block[1], block[1]), block[1])]

        def slot_of(index, from_seq):
            ref, block = out_refs[index], blocks[index]
            if all_sides[index] == INWARD:
                return ref.at[:, pl.ds(pl.multiple_of(from_seq * block[1], block[1]), block[1])]
            return ref.at[pl.ds(pl.multiple_of(from_seq * block[0], block[0]), block[0])]

        waits, crossings = [], {}
        small_cross = remote(small_ref, small_theirs, s_send.at[0], s_recv.at[0], here.img_peer)
        small_cross.start()
        for index in range(n, total):
            for step in range(PLANE):
                target = lax.rem(seq + step, PLANE)
                made = remote(
                    part_of(index, target, 1 - img),
                    theirs[index].at[target],
                    z_send.at[index - n, step],
                    z_recv.at[index - n, step],
                    here.img_peer,
                )
                made.start()
                crossings[index, step] = made

        def deliver(index):
            for step in range(PLANE):
                target = lax.rem(seq + step, PLANE)
                if index >= n:
                    crossings[index, step].wait_recv()
                mine = part_of(index, target, img)[...].astype(jnp.float32)
                summed[index][target] = (mine + theirs[index][target].astype(jnp.float32)).astype(jnp.bfloat16)
                if step == 0:
                    made = pltpu.make_async_copy(summed[index].at[target], slot_of(index, seq), local.at[index])
                    made.start()
                    waits.append(made.wait)
                    continue
                made = remote(
                    summed[index].at[target],
                    slot_of(index, seq),
                    send.at[index, step],
                    recv.at[index, step],
                    here.at(target),
                )
                made.start()
                waits.append(made.wait_send)

        deliver(0)
        small_cross.wait()
        small_mine[...] = small_ref[...] + small_theirs[...]
        small_all[seq] = small_mine[...]
        small_copies = []
        for step, peer in enumerate(ring, 1):
            made = remote(small_mine, small_all.at[seq], s_send.at[step], s_recv.at[step], peer)
            made.start()
            small_copies.append(made)
        for index in range(1, total):
            deliver(index)
        for made in small_copies:
            made.wait()
        sums_out[...] = small_all[...]
        rows = latents_ref.shape[1]
        latent_part = jnp.zeros(lat_mine.shape, jnp.float32)
        columns = small_all.shape[2]
        for source in range(PLANE):
            probe = small_all[source, :rows, :]
            at = slice(source * columns, (source + 1) * columns)
            query_out[:, at] = jnp.dot(
                latents_ref[...], probe, precision=HIGHEST_PRECISION, preferred_element_type=jnp.float32
            )
            latent_part += lax.dot_general(
                probe,
                query_ref[:, at],
                (((1,), (1,)), ((), ())),
                precision=HIGHEST_PRECISION,
                preferred_element_type=jnp.float32,
            )
        lat_mine[...] = latent_part
        last = remote(lat_mine, lat_theirs, s_send.at[PLANE], s_recv.at[PLANE], here.tp_peer)
        last.start()
        last.wait()
        latent_out[...] = lat_mine[...] + lat_theirs[...]
        for index in range(total):
            for step in range(1, PLANE):
                source = lax.rem(seq + PLANE - step, PLANE)
                at = slot_of(index, source)
                remote(at, at, send.at[index, step], recv.at[index, step], here.core).wait_recv()
        for wait in waits:
            wait()
        for made in crossings.values():
            made.wait_send()

    dma, low_type, f32 = pltpu.SemaphoreType.DMA, jnp.bfloat16, jnp.float32
    outs = []
    for block, side in zip(blocks, all_sides):
        shape = (block[0], PLANE * block[1]) if side == INWARD else (PLANE * block[0], block[1])
        outs.append(jax.ShapeDtypeStruct(shape, low_type))
    small_shapes = [
        jax.ShapeDtypeStruct((PLANE,) + small.shape, f32),
        jax.ShapeDtypeStruct(query_rows.shape, f32),
        jax.ShapeDtypeStruct((latents_t.shape[1], latents_t.shape[0]), f32),
    ]
    made = pl.pallas_call(
        kernel,
        out_shape=tuple(outs + small_shapes),
        in_specs=[ON_CHIP] * (total + n + 3),
        out_specs=tuple([ANYWHERE] * total + [ON_CHIP] * 3),
        scratch_shapes=[pltpu.VMEM((PLANE,) + block, low_type) for block in blocks[n:]]
        + [pltpu.VMEM((PLANE,) + block, low_type) for block in blocks]
        + [
            pltpu.VMEM(small.shape, f32),
            pltpu.VMEM(small.shape, f32),
            pltpu.VMEM((PLANE,) + small.shape, f32),
            pltpu.VMEM((latents_t.shape[1], latents_t.shape[0]), f32),
            pltpu.VMEM((latents_t.shape[1], latents_t.shape[0]), f32),
            dma((n_late, PLANE)),
            dma((n_late, PLANE)),
            dma((total, PLANE)),
            dma((total, PLANE)),
            dma((total,)),
            dma((PLANE + 1,)),
            dma((PLANE + 1,)),
        ],
        compiler_params=pltpu.CompilerParams(
            collective_id=cid, has_side_effects=True, vmem_limit_bytes=VMEM_BYTES
        ),
    )(*grads, *[given for _, given in pairs], small, latents_t, query_rows)
    return made[:total], made[total:]


def widened(arrays):
    def kernel(*refs):
        for src, dst in zip(refs[: len(arrays)], refs[len(arrays) :]):
            dst[...] = src[...].astype(jnp.float32)

    return pl.pallas_call(
        kernel,
        out_shape=tuple(jax.ShapeDtypeStruct(array.shape, jnp.float32) for array in arrays),
        in_specs=[ON_CHIP] * len(arrays),
        out_specs=tuple([ON_CHIP] * len(arrays)),
        compiler_params=pltpu.CompilerParams(vmem_limit_bytes=VMEM_BYTES),
    )(*arrays)


def small_total(values, cid):
    def kernel(in_ref, out_ref, plane, mine, theirs, send, recv):
        here = Places()
        seq, tp, img = here.seq, here.tp, here.img
        peers = [(lax.rem(seq + step, PLANE), tp, img) for step in range(1, PLANE)]
        greet(peers + [here.tp_peer])
        made = []
        for step, peer in enumerate(peers):
            copy = remote(in_ref, plane.at[step], send.at[step], recv.at[step], peer)
            copy.start()
            made.append(copy)
        total = in_ref[...]
        for step, copy in enumerate(made):
            copy.wait_recv()
            total = total + plane[step]
        mine[...] = total
        last = remote(mine, theirs, send.at[PLANE - 1], recv.at[PLANE - 1], here.tp_peer)
        last.start()
        last.wait()
        out_ref[...] = mine[...] + theirs[...]
        for copy in made:
            copy.wait_send()

    dma = pltpu.SemaphoreType.DMA
    return pl.pallas_call(
        kernel,
        out_shape=jax.ShapeDtypeStruct(values.shape, values.dtype),
        in_specs=[ON_CHIP],
        out_specs=ON_CHIP,
        scratch_shapes=[
            pltpu.VMEM((PLANE - 1,) + values.shape, values.dtype),
            pltpu.VMEM(values.shape, values.dtype),
            pltpu.VMEM(values.shape, values.dtype),
            dma((PLANE,)),
            dma((PLANE,)),
        ],
        compiler_params=pltpu.CompilerParams(collective_id=cid, has_side_effects=True),
    )(values)


def small_gather(values, cid):
    def kernel(in_ref, out_ref, send, recv):
        here = Places()
        seq, tp, img = here.seq, here.tp, here.img
        peers = []
        for step in range(2 * PLANE):
            if step == 0:
                continue
            peers.append((lax.rem(seq + step // 2, PLANE), tp, lax.rem(img + step % 2, 2)))
        greet(peers)
        out_ref[seq, img] = in_ref[...]
        made = []
        for step, peer in enumerate(peers):
            copy = remote(in_ref, out_ref.at[seq, img], send.at[step], recv.at[step], peer)
            copy.start()
            made.append(copy)
        for copy in made:
            copy.wait()

    dma = pltpu.SemaphoreType.DMA
    return pl.pallas_call(
        kernel,
        out_shape=jax.ShapeDtypeStruct((PLANE, 2) + values.shape, values.dtype),
        in_specs=[ON_CHIP],
        out_specs=ON_CHIP,
        scratch_shapes=[dma((2 * PLANE - 1,)), dma((2 * PLANE - 1,))],
        compiler_params=pltpu.CompilerParams(
            collective_id=cid, has_side_effects=True, vmem_limit_bytes=VMEM_BYTES
        ),
    )(values)


def norm_rows(rows, gain, shift):
    center = rows - jnp.mean(rows, -1, keepdims=True)
    factor = lax.rsqrt(jnp.mean(center * center, -1, keepdims=True) + EPSILON)
    normal = center * factor
    return (normal * gain + shift, normal, factor)


def dot32(left, right):
    return jnp.dot(left, right, preferred_element_type=jnp.float32)


def on_plane(
    text,
    segment,
    features,
    image_count,
    image_slot,
    cotangent,
    input_gain,
    input_shift,
    query_weight,
    key_weight,
    value_weight,
    inner_gain,
    inner_shift,
    out_weight,
    middle_gain,
    middle_shift,
    up_weight,
    up_bias,
    hidden_gain,
    hidden_shift,
    down_weight,
    latents,
    resample_query,
    resample_key,
    resample_value,
    resample_out,
):
    f32, low = jnp.float32, jnp.bfloat16
    row_count, model_width = text.shape[1], text.shape[2]
    group_rows = segment.shape[1]
    seq_rank = lax.axis_index(SEQ)
    image_slots = features.shape[1]
    image_total = image_slot.shape[1]
    half_width = query_weight.shape[1]
    own_width = half_width // PLANE
    own_heads = own_width // HEAD
    score_scale = HEAD ** (-0.5)

    rows, own = intake(
        (features[0].reshape(image_slots * PATCH, features.shape[3]),),
        (
            resample_key,
            resample_value,
            resample_query,
            resample_out,
            query_weight,
            key_weight,
            value_weight,
            out_weight,
        ),
        (INWARD, INWARD, INWARD, OUTWARD, INWARD, INWARD, INWARD, OUTWARD),
        1,
    )
    (pictures,) = rows
    image_key_own, image_value_own, probe_own, image_out_own, query_own, key_own, value_own, out_own = own
    qkv_own = jnp.concatenate([query_own, key_own, value_own], 1)
    latent_all = small_gather(latents, 2).transpose(2, 0, 1, 3).reshape(LAT, model_width)

    probe = dot32(latent_all, probe_own).astype(low).reshape(LAT, own_heads, HEAD)
    image_keys = dot32(pictures, image_key_own).astype(low).reshape(image_total, PATCH, own_heads, HEAD)
    image_values = dot32(pictures, image_value_own).astype(low).reshape(image_total, PATCH, own_heads, HEAD)
    image_scores = (
        jnp.einsum("qhd,iphd->ihqp", probe, image_keys, preferred_element_type=f32) * score_scale
    )
    image_probs = jax.nn.softmax(image_scores, -1)
    image_mixed = jnp.einsum(
        "ihqp,iphd->iqhd", image_probs.astype(low), image_values, preferred_element_type=f32
    )
    image_mixed = image_mixed.astype(low).reshape(image_total, LAT * own_width)

    slot_range = jnp.arange(image_total, dtype=jnp.int32)
    live = slot_range % IMG_DEV < jnp.repeat(image_count[0], IMG_DEV)
    block_count = group_rows // LAT
    owner = (
        (image_slot[0][None, :] == jnp.arange(block_count, dtype=jnp.int32)[:, None]) & live[None, :]
    ).astype(low)
    mixed_placed = dot32(owner, image_mixed).astype(low).reshape(group_rows, own_width)
    taken = jnp.repeat((jnp.sum(owner.astype(f32), 1) > 0.5).astype(f32), LAT)[:, None]
    taken_own = lax.dynamic_slice_in_dim(taken, seq_rank * row_count, row_count, 0)

    def wide(vector):
        return vector.astype(f32)[None, :]

    def own_part(vector):
        width = vector.shape[0] // PLANE
        return lax.dynamic_slice_in_dim(vector, seq_rank * width, width, 0)

    def begin(total, piece, views, outs):
        text_view, taken_view, gain, shift = views
        embed = total.astype(jnp.bfloat16).astype(jnp.float32)
        mixed = jnp.where(taken_view[...] > 0.5, embed, text_view[...].astype(jnp.float32))
        outs[0][...] = mixed
        return norm_rows(mixed, gain[...], shift[...])[0].astype(jnp.bfloat16)

    rows_wide = jax.ShapeDtypeStruct((row_count, model_width), f32)
    (mixed_in, normed), hidden_blocks = exchange(
        [
            Stream(
                mixed_placed,
                image_out_own,
                False,
                (text[0], taken_own, wide(input_gain), wide(input_shift)),
                (ROWS, ROWS, ALL, ALL),
                ((rows_wide, ROWS),),
                begin,
                True,
            )
        ],
        [PlaneWeights((up_weight, down_weight), (INWARD, OUTWARD))],
        3,
    )

    segment_all = segment[0]
    docs_count = 3 * (group_rows // min(SEQ_MAX, group_rows))
    marks = (segment_all[:, None] == jnp.arange(docs_count, dtype=jnp.int32)[None, :]).astype(jnp.int32)
    earlier_rows = jnp.cumsum(marks, 0) - marks
    position = jnp.sum(earlier_rows * marks, 1).astype(f32)
    cosine, sine_table, growth = xpos_factors(position, HEAD // 2)
    row_index = jnp.arange(group_rows, dtype=jnp.int32)
    allowed = (row_index[None, :] <= row_index[:, None]) & (segment_all[None, :] == segment_all[:, None])

    cot_late, _ = lax.optimization_barrier((cotangent[0], normed))
    cot_all = lax.all_gather(cot_late, SEQ, axis=0, tiled=True)
    lin = dot32(normed, qkv_own)
    query_rot = rotate(
        lin[:, :own_width].reshape(group_rows, own_heads, HEAD), cosine, sine_table, growth
    ).astype(low)
    keys_rot = rotate(
        lin[:, own_width : 2 * own_width].reshape(group_rows, own_heads, HEAD), cosine, sine_table, 1.0 / growth
    ).astype(low)
    values = lin[:, 2 * own_width :].astype(low).reshape(group_rows, own_heads, HEAD)
    scores = jnp.einsum("qhd,khd->hqk", query_rot, keys_rot, preferred_element_type=f32) * score_scale
    probs = jax.nn.softmax(jnp.where(allowed[None], scores, -1e30), -1)
    attended = jnp.einsum("hqk,khd->qhd", probs.astype(low), values, preferred_element_type=f32)
    attended = attended.reshape(group_rows, own_width)

    def split_stats(parts, cid):
        total = small_total(jnp.stack(parts), cid)
        return [total[number][:, None] for number in range(len(parts))]

    inner_sum, inner_square = split_stats((jnp.sum(attended, 1), jnp.sum(attended * attended, 1)), 4)
    average = inner_sum / model_width
    inner_factor = lax.rsqrt(inner_square / model_width - average * average + EPSILON)
    inner_hat = (attended - average) * inner_factor
    inner_gain_own = wide(own_part(inner_gain))
    inner_low = (inner_hat * inner_gain_own + wide(own_part(inner_shift))).astype(low)

    def middle_step(total, piece, views, outs):
        mixed_view, gain, shift = views
        middle = mixed_view[...] + total
        outs[0][...] = middle
        return norm_rows(middle, gain[...], shift[...])[0].astype(jnp.bfloat16)

    (middle, lifted), hidden_own = exchange(
        [
            Stream(
                inner_low,
                out_own,
                False,
                (mixed_in, wide(middle_gain), wide(middle_shift)),
                (ROWS, ALL, ALL),
                ((rows_wide, ROWS),),
                middle_step,
                True,
            )
        ],
        [CrossWeights(hidden_blocks, (INWARD, OUTWARD))],
        5,
    )
    up_own, down_own = hidden_own[0].reshape(model_width, -1), hidden_own[1]
    own_hidden = up_own.shape[1]

    hidden_pre = dot32(lifted, up_own) + wide(own_part(up_bias))
    activated, gelu_pull = jax.vjp(functools.partial(jax.nn.gelu, approximate=False), hidden_pre)
    d_settled = dot32(cot_all, down_own.T)
    hidden_gain_own = wide(own_part(hidden_gain))
    scaled = d_settled * hidden_gain_own
    sum_act, sum_square, sum_scaled, sum_cross = split_stats(
        (
            jnp.sum(activated, 1),
            jnp.sum(activated * activated, 1),
            jnp.sum(scaled, 1),
            jnp.sum(scaled * activated, 1),
        ),
        6,
    )
    average = sum_act / FF
    hidden_factor = lax.rsqrt(sum_square / FF - average * average + EPSILON)
    settled_hat = (activated - average) * hidden_factor
    settled = (settled_hat * hidden_gain_own + wide(own_part(hidden_shift))).astype(low)
    mean_scaled = sum_scaled / FF
    mean_cross = hidden_factor * (sum_cross / FF - average * mean_scaled)
    d_activated = hidden_factor * (scaled - mean_scaled - settled_hat * mean_cross)
    d_hidden = gelu_pull(d_activated)[0].astype(low)
    hidden_gain_grad = jnp.sum(d_settled * settled_hat, 0)
    hidden_shift_grad = jnp.sum(d_settled, 0)
    up_bias_grad = jnp.sum(d_hidden.astype(f32), 0)
    down_grad = dot32(settled.T, cot_all).astype(low)
    up_grad = dot32(lifted.T, d_hidden).astype(low)

    def blocks_in(grad):
        return grad.reshape(PLANE, 2, -1, grad.shape[1])

    def last_step(total, piece, views, outs):
        outs[0][...] = (views[0][...] + total).astype(jnp.bfloat16)

    vector_out = jax.ShapeDtypeStruct((1, model_width), f32)

    def norm_back_step(total, piece, views, outs):
        rows_view, carried_view, gain = views
        rows_in = rows_view[...]
        center = rows_in - jnp.mean(rows_in, -1, keepdims=True)
        factor = lax.rsqrt(jnp.mean(center * center, -1, keepdims=True) + EPSILON)
        normal = center * factor
        grad = carried_view[...].astype(jnp.float32) + full_back(total, normal, factor, gain[...])
        outs[0][...] = grad
        if piece == 0:
            outs[1][...] = jnp.zeros_like(outs[1])
            outs[2][...] = jnp.zeros_like(outs[2])
        outs[1][...] += jnp.sum(total * normal, 0, keepdims=True)
        outs[2][...] += jnp.sum(total, 0, keepdims=True)
        return grad.astype(jnp.bfloat16)

    hidden_grads = (blocks_in(up_grad), down_grad)
    (d_middle, middle_gain_grad, middle_shift_grad, d_branch), hidden_theirs = exchange(
        [
            Stream(
                d_hidden,
                up_own,
                True,
                (middle, cotangent[0], wide(middle_gain)),
                (ROWS, ROWS, ALL),
                ((rows_wide, ROWS), (vector_out, ALL), (vector_out, ALL)),
                norm_back_step,
                True,
            )
        ],
        [CrossGrads(hidden_grads, (INWARD, OUTWARD))],
        8,
    )

    out_grad = dot32(inner_low.T, d_branch).astype(low)
    d_inner = dot32(d_branch, out_own.T)
    inner_gain_grad = jnp.sum(d_inner * inner_hat, 0)
    inner_shift_grad = jnp.sum(d_inner, 0)
    scaled = d_inner * inner_gain_own
    sum_scaled, sum_cross = split_stats((jnp.sum(scaled, 1), jnp.sum(scaled * inner_hat, 1)), 9)
    d_attended = inner_factor * (scaled - sum_scaled / model_width - inner_hat * (sum_cross / model_width))
    d_attended = d_attended.astype(low).reshape(group_rows, own_heads, HEAD)
    delta = jnp.sum(d_attended.astype(f32) * attended.reshape(group_rows, own_heads, HEAD), -1).T
    d_probs = jnp.einsum("qhd,khd->hqk", d_attended, values, preferred_element_type=f32)
    d_scores = (probs * (d_probs - delta[..., None])).astype(low)
    d_query = jnp.einsum("hqk,khd->qhd", d_scores, keys_rot, preferred_element_type=f32) * score_scale
    d_key = jnp.einsum("hqk,qhd->khd", d_scores, query_rot, preferred_element_type=f32) * score_scale
    d_value = jnp.einsum("hqk,qhd->khd", probs.astype(low), d_attended, preferred_element_type=f32)
    d_lin = jnp.concatenate(
        [
            rotate_back(d_query, cosine, sine_table, growth).astype(low).reshape(group_rows, own_width),
            rotate_back(d_key, cosine, sine_table, 1.0 / growth).astype(low).reshape(group_rows, own_width),
            d_value.astype(low).reshape(group_rows, own_width),
        ],
        1,
    )
    lin_grad = dot32(normed.T, d_lin).astype(low)
    layer_grads = (
        blocks_in(lin_grad[:, :own_width]),
        blocks_in(lin_grad[:, own_width : 2 * own_width]),
        blocks_in(lin_grad[:, 2 * own_width :]),
        out_grad,
    )
    layer_sides = (INWARD, INWARD, INWARD, OUTWARD)
    (d_mixed, input_gain_grad, input_shift_grad, d_rows), (result,), layer_theirs = exchange(
        [
            Stream(
                d_lin,
                qkv_own,
                True,
                (mixed_in, d_middle, wide(input_gain)),
                (ROWS, ROWS, ALL),
                ((rows_wide, ROWS), (vector_out, ALL), (vector_out, ALL)),
                norm_back_step,
                True,
            ),
            Stream(
                settled,
                down_own,
                False,
                (middle,),
                (ROWS,),
                ((jax.ShapeDtypeStruct((row_count, model_width), low), ROWS),),
                last_step,
                False,
            ),
        ],
        [CrossGrads(layer_grads, layer_sides)],
        10,
    )
    text_grad = jnp.where(taken_own > 0.5, 0.0, d_mixed)

    image_out_grad = dot32(mixed_placed.T, d_rows).astype(low)
    d_mixed_rows = dot32(d_rows, image_out_own.T).astype(low)
    d_image_mixed = dot32(owner.T, d_mixed_rows.reshape(block_count, LAT * own_width)).astype(low)
    d_image_mixed = d_image_mixed.reshape(image_total, LAT, own_heads, HEAD)
    d_image_probs = jnp.einsum("iqhd,iphd->ihqp", d_image_mixed, image_values, preferred_element_type=f32)
    d_image_scores = image_probs * (
        d_image_probs - jnp.sum(image_probs * d_image_probs, -1, keepdims=True)
    )
    d_image_scores = d_image_scores.astype(low)
    d_probe = jnp.einsum("ihqp,iphd->qhd", d_image_scores, image_keys, preferred_element_type=f32) * score_scale
    d_image_keys = (
        jnp.einsum("ihqp,qhd->iphd", d_image_scores, probe, preferred_element_type=f32) * score_scale
    ).astype(low)
    d_image_values = jnp.einsum(
        "ihqp,iqhd->iphd", image_probs.astype(low), d_image_mixed, preferred_element_type=f32
    ).astype(low)
    picture_rows = image_total * PATCH
    image_grad = dot32(
        pictures.T,
        jnp.concatenate(
            [d_image_keys.reshape(picture_rows, own_width), d_image_values.reshape(picture_rows, own_width)], 1
        ),
    ).astype(low)

    own_vectors = jnp.concatenate(
        [inner_gain_grad, inner_shift_grad, up_bias_grad, hidden_gain_grad, hidden_shift_grad]
    )
    row_vectors = jnp.concatenate(
        [input_gain_grad[0], input_shift_grad[0], middle_gain_grad[0], middle_shift_grad[0]]
    )
    packed = jnp.concatenate([row_vectors, own_vectors]).reshape(-1, LANES)
    spare = -packed.shape[0] % 8
    packed = jnp.concatenate([d_probe.reshape(LAT, own_width), jnp.pad(packed, ((0, spare), (0, 0)))], 0)
    image_grads = (blocks_in(image_grad[:, :own_width]), blocks_in(image_grad[:, own_width:]), image_out_grad)
    owned, (spread, resample_query_grad, latent_grad) = finale(
        list(zip(hidden_grads + layer_grads, hidden_theirs + layer_theirs)),
        image_grads,
        (INWARD, OUTWARD) + layer_sides,
        (INWARD, INWARD, OUTWARD),
        packed,
        latents.astype(f32).T,
        resample_query.astype(f32),
        12,
    )
    up_sum, down_sum, query_sum, key_sum, value_sum, out_sum, image_key_sum, image_value_sum, image_out_sum = widened(owned)
    spread = spread.reshape(PLANE, -1)
    first = LAT * own_width
    row_sums = spread[:, first : first + row_vectors.shape[0]].sum(0).reshape(4, model_width)
    own_sums = spread[:, first + row_vectors.shape[0] :]

    def joined(start, width):
        return own_sums[:, start : start + width].reshape(-1)

    inner_gain_sum = joined(0, own_width)
    inner_shift_sum = joined(own_width, own_width)
    up_bias_sum = joined(2 * own_width, own_hidden)
    hidden_gain_sum = joined(2 * own_width + own_hidden, own_hidden)
    hidden_shift_sum = joined(2 * own_width + 2 * own_hidden, own_hidden)

    return (
        result[None],
        text_grad[None],
        row_sums[0],
        row_sums[1],
        query_sum,
        key_sum,
        value_sum,
        inner_gain_sum,
        inner_shift_sum,
        out_sum,
        row_sums[2],
        row_sums[3],
        up_sum,
        up_bias_sum,
        hidden_gain_sum,
        hidden_shift_sum,
        down_sum,
        latent_grad,
        resample_query_grad,
        image_key_sum,
        image_value_sum,
        image_out_sum,
    )


def solution(mesh):
    placed = (
        P(IMG, SEQ, None),
        P(IMG, None),
        P(IMG, SEQ, None, None),
        P(IMG, None),
        P(IMG, None),
        P(IMG, SEQ, None),
        P(),
        P(),
        P((SEQ, IMG), TP),
        P((SEQ, IMG), TP),
        P((SEQ, IMG), TP),
        P(TP),
        P(TP),
        P(TP, (SEQ, IMG)),
        P(),
        P(),
        P((SEQ, IMG), TP),
        P(TP),
        P(TP),
        P(TP),
        P(TP, (SEQ, IMG)),
        P(None, (SEQ, IMG)),
        P((SEQ, IMG), TP),
        P((SEQ, IMG), TP),
        P((SEQ, IMG), TP),
        P(TP, (SEQ, IMG)),
    )
    return jax.shard_map(
        on_device if narrow_heads(mesh) else on_plane,
        mesh=mesh,
        in_specs=placed,
        out_specs=(
            P(IMG, SEQ, None),
            P(IMG, SEQ, None),
            P(),
            P(),
            P((SEQ, IMG), TP),
            P((SEQ, IMG), TP),
            P((SEQ, IMG), TP),
            P(TP),
            P(TP),
            P(TP, (SEQ, IMG)),
            P(),
            P(),
            P((SEQ, IMG), TP),
            P(TP),
            P(TP),
            P(TP),
            P(TP, (SEQ, IMG)),
            P(None, (SEQ, IMG)),
            P((SEQ, IMG), TP),
            P((SEQ, IMG), TP),
            P((SEQ, IMG), TP),
            P(TP, (SEQ, IMG)),
        ),
        check_vma=False,
    )
```

```python
import functools

import jax
import jax.numpy as jnp
from jax import lax
from jax.experimental import pallas as pl
from jax.experimental.pallas import tpu as pltpu
from jax.sharding import PartitionSpec as P

SEQ, TP, IMG = "seq", "tp", "img"
HEAD = 64
FF = 8192
PATCH = 256
LAT = 64
SEQ_MAX = 2048
IMG_DEV = 2


EPSILON = 1e-05
HIGHEST_PRECISION = lax.Precision.HIGHEST


def shortened(x):

    def short(part):
        return part.astype(jnp.bfloat16) if part.dtype == jnp.float32 else part

    return jax.tree.map(short, x)


def xpos_factors(position, half_size):
    ladder = jnp.arange(half_size, dtype=jnp.float32)
    frequency = jnp.exp(ladder * (-2.0 * jnp.log(10000.0) / (2.0 * half_size)))
    decay_base = (ladder / half_size + 0.4) / 1.4
    angles = position[:, None] * frequency[None, :]
    growth = jnp.exp(position[:, None] / 512.0 * jnp.log(decay_base)[None, :])
    return (jnp.cos(angles)[:, None, :], jnp.sin(angles)[:, None, :], growth[:, None, :])


def rotate(inputs, cosine, sine_table, factor):
    half_size = inputs.shape[-1] // 2
    first_half = inputs[..., :half_size]
    second_half = inputs[..., half_size:]
    turned = jnp.concatenate(
        [
            first_half * cosine - second_half * sine_table,
            first_half * sine_table + second_half * cosine,
        ],
        -1,
    )
    return turned * jnp.concatenate([factor, factor], -1)


def rotate_back(gradient, cosine, sine_table, factor):
    half_size = gradient.shape[-1] // 2
    scaled = gradient * jnp.concatenate([factor, factor], -1)
    first_half = scaled[..., :half_size]
    second_half = scaled[..., half_size:]
    return jnp.concatenate(
        [
            first_half * cosine + second_half * sine_table,
            second_half * cosine - first_half * sine_table,
        ],
        -1,
    )


def tp_total(inputs):
    return jax.tree.map(lambda part: part.astype(jnp.float32), lax.psum(shortened(inputs), TP))


def full_norm(inputs, norm_gain, norm_shift):
    center = inputs - jnp.mean(inputs, -1, keepdims=True)
    spread = jnp.mean(center * center, -1, keepdims=True)
    factor = lax.rsqrt(spread + EPSILON)
    normal = center * factor
    return (normal * norm_gain + norm_shift, normal, factor)


def full_back(gradient, normal, factor, norm_gain):
    scaled = gradient * norm_gain
    return factor * (
        scaled
        - jnp.mean(scaled, -1, keepdims=True)
        - normal * jnp.mean(scaled * normal, -1, keepdims=True)
    )


def split_norm(inputs, norm_gain, norm_shift, full_width):
    totals = tp_total(
        (jnp.sum(inputs, -1, keepdims=True), jnp.sum(inputs * inputs, -1, keepdims=True))
    )
    average = totals[0] / full_width
    spread = totals[1] / full_width - average * average
    factor = lax.rsqrt(spread + EPSILON)
    normal = (inputs - average) * factor
    return (normal * norm_gain + norm_shift, normal, factor)


def split_back(gradient, normal, factor, norm_gain, full_width):
    scaled = gradient * norm_gain
    totals = tp_total(
        (jnp.sum(scaled, -1, keepdims=True), jnp.sum(scaled * normal, -1, keepdims=True))
    )
    return factor * (scaled - totals[0] / full_width - normal * (totals[1] / full_width))


def attend_piece(
    running, query_rot, key_piece, value_piece, row_index, row_segment, segment_all, score_scale
):
    heads_local = query_rot.shape[1]
    amount = key_piece.shape[0]
    block_size = 1024

    def step(state_in, number):
        first_row = number * block_size
        key_block = lax.dynamic_slice_in_dim(key_piece, first_row, block_size, 0).reshape(
            block_size, heads_local, -1
        )
        value_block = lax.dynamic_slice_in_dim(value_piece, first_row, block_size, 0).reshape(
            block_size, heads_local, -1
        )
        key_index = first_row + jnp.arange(block_size, dtype=jnp.int32)
        key_segment = lax.dynamic_slice_in_dim(segment_all, first_row, block_size, 0)
        scores = (
            jnp.einsum("qhd,khd->hqk", query_rot, key_block, preferred_element_type=jnp.float32)
            * score_scale
        )
        allowed = (key_index[None, :] <= row_index[:, None]) & (
            key_segment[None, :] == row_segment[:, None]
        )
        scores = jnp.where(allowed[None], scores, -1e30)
        best_old, total_old, accum_old = state_in
        best_new = jnp.maximum(best_old, jnp.max(scores, -1))
        weights = jnp.where(allowed[None], jnp.exp(scores - best_new[..., None]), 0.0)
        shrink = jnp.exp(best_old - best_new)
        total_new = total_old * shrink + jnp.sum(weights, -1)
        added = jnp.einsum(
            "hqk,khd->qhd",
            weights.astype(jnp.bfloat16),
            value_block,
            preferred_element_type=jnp.float32,
        )
        accum_new = accum_old * shrink.T[:, :, None] + added
        return ((best_new, total_new, accum_new), None)

    return lax.scan(step, running, jnp.arange(amount // block_size, dtype=jnp.int32))[0]


def attend_back(
    query_rot,
    key_all,
    value_all,
    grad_attended,
    log_total,
    delta,
    row_index,
    row_segment,
    segment_all,
    score_scale,
):
    heads_local = query_rot.shape[1]
    amount = key_all.shape[0]
    block_size = 1024

    def step(dquery, number):
        first_row = number * block_size
        key_block = lax.dynamic_slice_in_dim(key_all, first_row, block_size, 0).reshape(
            block_size, heads_local, -1
        )
        value_block = lax.dynamic_slice_in_dim(value_all, first_row, block_size, 0).reshape(
            block_size, heads_local, -1
        )
        key_index = first_row + jnp.arange(block_size, dtype=jnp.int32)
        key_segment = lax.dynamic_slice_in_dim(segment_all, first_row, block_size, 0)
        scores = (
            jnp.einsum("qhd,khd->hqk", query_rot, key_block, preferred_element_type=jnp.float32)
            * score_scale
        )
        allowed = (key_index[None, :] <= row_index[:, None]) & (
            key_segment[None, :] == row_segment[:, None]
        )
        weights = jnp.where(
            allowed[None],
            jnp.exp(jnp.where(allowed[None], scores, -1e30) - log_total[..., None]),
            0.0,
        )
        dweights = jnp.einsum(
            "qhd,khd->hqk", grad_attended, value_block, preferred_element_type=jnp.float32
        )
        dscores = (weights * (dweights - delta[..., None])).astype(jnp.bfloat16)
        dquery = (
            dquery
            + jnp.einsum("hqk,khd->qhd", dscores, key_block, preferred_element_type=jnp.float32)
            * score_scale
        )
        dkeys = (
            jnp.einsum("hqk,qhd->khd", dscores, query_rot, preferred_element_type=jnp.float32)
            * score_scale
        )
        dvalues = jnp.einsum(
            "hqk,qhd->khd",
            weights.astype(jnp.bfloat16),
            grad_attended,
            preferred_element_type=jnp.float32,
        )
        return (dquery, (dkeys, dvalues))

    start_grad = jnp.zeros(query_rot.shape, jnp.float32)
    dquery, outputs = lax.scan(step, start_grad, jnp.arange(amount // block_size, dtype=jnp.int32))
    return (dquery, outputs[0].reshape(amount, -1), outputs[1].reshape(amount, -1))


def on_device(
    text,
    segment,
    features,
    image_count,
    image_slot,
    cotangent,
    input_gain,
    input_shift,
    query_weight,
    key_weight,
    value_weight,
    inner_gain,
    inner_shift,
    out_weight,
    middle_gain,
    middle_shift,
    up_weight,
    up_bias,
    hidden_gain,
    hidden_shift,
    down_weight,
    latents,
    resample_query,
    resample_key,
    resample_value,
    resample_out,
):
    row_count = text.shape[1]
    model_width = text.shape[2]
    group_rows = segment.shape[1]
    seq_rank = lax.axis_index(SEQ)
    gathered_in = (
        lax.all_gather(query_weight, (SEQ, IMG), axis=0, tiled=True),
        lax.all_gather(key_weight, (SEQ, IMG), axis=0, tiled=True),
        lax.all_gather(value_weight, (SEQ, IMG), axis=0, tiled=True),
        lax.all_gather(up_weight, (SEQ, IMG), axis=0, tiled=True),
        lax.all_gather(resample_query, (SEQ, IMG), axis=0, tiled=True),
        lax.all_gather(resample_key, (SEQ, IMG), axis=0, tiled=True),
        lax.all_gather(resample_value, (SEQ, IMG), axis=0, tiled=True),
    )
    query_full, key_full, value_full, up_full, probe_full, image_key_full, image_value_full = (
        gathered_in
    )
    gathered_out = (
        lax.all_gather(out_weight, (SEQ, IMG), axis=1, tiled=True),
        lax.all_gather(down_weight, (SEQ, IMG), axis=1, tiled=True),
        lax.all_gather(resample_out, (SEQ, IMG), axis=1, tiled=True),
        lax.all_gather(latents, (SEQ, IMG), axis=1, tiled=True),
    )
    out_full, down_full, image_out_full, latent_full = gathered_out
    half_width = query_full.shape[1]
    heads_local = half_width // HEAD
    score_scale = HEAD ** (-0.5)
    gelu_exact = functools.partial(jax.nn.gelu, approximate=False)
    image_slots = features.shape[1]
    pictures = features[0].reshape(image_slots * PATCH, features.shape[3])
    probe = (
        jnp.dot(latent_full, probe_full, preferred_element_type=jnp.float32)
        .astype(jnp.bfloat16)
        .reshape(LAT, heads_local, HEAD)
    )
    image_keys = (
        jnp.dot(pictures, image_key_full, preferred_element_type=jnp.float32)
        .astype(jnp.bfloat16)
        .reshape(image_slots, PATCH, heads_local, HEAD)
    )
    image_values = (
        jnp.dot(pictures, image_value_full, preferred_element_type=jnp.float32)
        .astype(jnp.bfloat16)
        .reshape(image_slots, PATCH, heads_local, HEAD)
    )
    image_scores = (
        jnp.einsum("qhd,iphd->ihqp", probe, image_keys, preferred_element_type=jnp.float32)
        * score_scale
    )
    image_probs = jax.nn.softmax(image_scores, -1)
    image_mixed = jnp.einsum(
        "ihqp,iphd->iqhd",
        image_probs.astype(jnp.bfloat16),
        image_values,
        preferred_element_type=jnp.float32,
    )
    image_mixed = image_mixed.astype(jnp.bfloat16).reshape(image_slots * LAT, half_width)
    embed = tp_total(jnp.dot(image_mixed, image_out_full, preferred_element_type=jnp.float32))
    embed = embed.astype(jnp.bfloat16).reshape(image_slots, LAT, model_width)
    image_total = image_slot.shape[1]
    slot_range = jnp.arange(image_total, dtype=jnp.int32)
    live = slot_range % IMG_DEV < jnp.repeat(image_count[0], IMG_DEV)
    block_local = row_count // LAT
    block_count = group_rows // LAT
    block_ids = seq_rank * block_local + jnp.arange(block_local, dtype=jnp.int32)
    owner = ((image_slot[0][None, :] == block_ids[:, None]) & live[None, :]).astype(jnp.float32)
    owner_low = owner.astype(jnp.bfloat16)
    taken = jnp.sum(owner, 1) > 0.5
    chosen = owner_low
    placed = jnp.einsum(
        "bi,ild->bld",
        chosen,
        lax.all_gather(embed, SEQ, axis=0, tiled=True),
        preferred_element_type=jnp.float32,
    )
    text_blocks = text[0].astype(jnp.float32).reshape(block_local, LAT, model_width)
    mixed_in = jnp.where(taken[:, None, None], placed, text_blocks).reshape(row_count, model_width)
    segment_all = segment[0]
    docs_count = 3 * (group_rows // min(SEQ_MAX, group_rows))
    marks = (segment_all[:, None] == jnp.arange(docs_count, dtype=jnp.int32)[None, :]).astype(
        jnp.int32
    )
    earlier_rows = jnp.cumsum(marks, 0) - marks
    position_all = jnp.sum(earlier_rows * marks, 1)
    first_local = seq_rank * row_count
    row_index = first_local + jnp.arange(row_count, dtype=jnp.int32)
    row_segment = lax.dynamic_slice_in_dim(segment_all, first_local, row_count, 0)
    position = lax.dynamic_slice_in_dim(position_all, first_local, row_count, 0).astype(jnp.float32)
    cosine, sine_table, growth = xpos_factors(position, HEAD // 2)
    input_out, input_hat, input_factor = full_norm(
        mixed_in, input_gain.astype(jnp.float32), input_shift.astype(jnp.float32)
    )
    normed = input_out.astype(jnp.bfloat16)
    query_lin = jnp.dot(normed, query_full, preferred_element_type=jnp.float32).reshape(
        row_count, heads_local, HEAD
    )
    key_lin = jnp.dot(normed, key_full, preferred_element_type=jnp.float32).reshape(
        row_count, heads_local, HEAD
    )
    value_lin = jnp.dot(normed, value_full, preferred_element_type=jnp.float32)
    query_rot = rotate(query_lin, cosine, sine_table, growth).astype(jnp.bfloat16)
    keys_rot = (
        rotate(key_lin, cosine, sine_table, 1.0 / growth)
        .astype(jnp.bfloat16)
        .reshape(row_count, half_width)
    )
    values_low = value_lin.astype(jnp.bfloat16)
    start_state = (
        jnp.full((heads_local, row_count), -1e30, jnp.float32),
        jnp.zeros((heads_local, row_count), jnp.float32),
        jnp.zeros((row_count, heads_local, HEAD), jnp.float32),
    )
    best, weight_total, accum = attend_piece(
        start_state,
        query_rot,
        lax.all_gather(keys_rot, SEQ, axis=0, tiled=True),
        lax.all_gather(values_low, SEQ, axis=0, tiled=True),
        row_index,
        row_segment,
        segment_all,
        score_scale,
    )
    attended = accum / weight_total.T[:, :, None]
    log_total = best + jnp.log(weight_total)
    inner_out, inner_hat, inner_factor = split_norm(
        attended.reshape(row_count, half_width),
        inner_gain.astype(jnp.float32),
        inner_shift.astype(jnp.float32),
        model_width,
    )
    inner_low = inner_out.astype(jnp.bfloat16)
    middle = mixed_in + tp_total(jnp.dot(inner_low, out_full, preferred_element_type=jnp.float32))
    lifted_out, lifted_hat, lifted_factor = full_norm(
        middle, middle_gain.astype(jnp.float32), middle_shift.astype(jnp.float32)
    )
    lifted = lifted_out.astype(jnp.bfloat16)
    hidden_pre = jnp.dot(lifted, up_full, preferred_element_type=jnp.float32) + up_bias.astype(
        jnp.float32
    )
    activated, gelu_pull = jax.vjp(gelu_exact, hidden_pre)
    settled_out, settled_hat, settled_factor = split_norm(
        activated, hidden_gain.astype(jnp.float32), hidden_shift.astype(jnp.float32), FF
    )
    settled = settled_out.astype(jnp.bfloat16)
    final_rows = middle + tp_total(jnp.dot(settled, down_full, preferred_element_type=jnp.float32))
    result = final_rows.astype(jnp.bfloat16).reshape(1, row_count, model_width)
    grad_low = cotangent[0]
    grad_rows = grad_low.astype(jnp.float32)
    down_grad = jnp.dot(settled.T, grad_low, preferred_element_type=jnp.float32)
    d_settled = jnp.dot(grad_low, down_full.T, preferred_element_type=jnp.float32)
    hidden_gain_grad = jnp.sum(d_settled * settled_hat, 0)
    hidden_shift_grad = jnp.sum(d_settled, 0)
    d_activated = split_back(
        d_settled, settled_hat, settled_factor, hidden_gain.astype(jnp.float32), FF
    )
    d_hidden = gelu_pull(d_activated)[0].astype(jnp.bfloat16)
    up_bias_grad = jnp.sum(d_hidden.astype(jnp.float32), 0)
    up_grad = jnp.dot(lifted.T, d_hidden, preferred_element_type=jnp.float32)
    d_lifted = tp_total(jnp.dot(d_hidden, up_full.T, preferred_element_type=jnp.float32))
    middle_gain_grad = jnp.sum(d_lifted * lifted_hat, 0)
    middle_shift_grad = jnp.sum(d_lifted, 0)
    d_middle = grad_rows + full_back(
        d_lifted, lifted_hat, lifted_factor, middle_gain.astype(jnp.float32)
    )
    d_branch = d_middle.astype(jnp.bfloat16)
    out_grad = jnp.dot(inner_low.T, d_branch, preferred_element_type=jnp.float32)
    d_inner = jnp.dot(d_branch, out_full.T, preferred_element_type=jnp.float32)
    inner_gain_grad = jnp.sum(d_inner * inner_hat, 0)
    inner_shift_grad = jnp.sum(d_inner, 0)
    d_attended = split_back(
        d_inner, inner_hat, inner_factor, inner_gain.astype(jnp.float32), model_width
    )
    d_attended = d_attended.astype(jnp.bfloat16).reshape(row_count, heads_local, HEAD)
    delta = jnp.sum(d_attended.astype(jnp.float32) * attended, -1).T
    key_back, value_back = (
        lax.all_gather(keys_rot, SEQ, axis=0, tiled=True),
        lax.all_gather(values_low, SEQ, axis=0, tiled=True),
    )
    d_query_rot, d_key_term, d_value_term = attend_back(
        query_rot,
        key_back,
        value_back,
        d_attended,
        log_total,
        delta,
        row_index,
        row_segment,
        segment_all,
        score_scale,
    )
    d_key_sum, d_value_sum = (
        lax.psum_scatter(
            d_key_term.astype(jnp.bfloat16), SEQ, scatter_dimension=0, tiled=True
        ).astype(jnp.float32),
        lax.psum_scatter(
            d_value_term.astype(jnp.bfloat16), SEQ, scatter_dimension=0, tiled=True
        ).astype(jnp.float32),
    )
    d_query_lin = (
        rotate_back(d_query_rot, cosine, sine_table, growth)
        .astype(jnp.bfloat16)
        .reshape(row_count, half_width)
    )
    d_key_lin = (
        rotate_back(
            d_key_sum.reshape(row_count, heads_local, HEAD), cosine, sine_table, 1.0 / growth
        )
        .astype(jnp.bfloat16)
        .reshape(row_count, half_width)
    )
    d_value_lin = d_value_sum.astype(jnp.bfloat16)
    query_grad = jnp.dot(normed.T, d_query_lin, preferred_element_type=jnp.float32)
    key_grad = jnp.dot(normed.T, d_key_lin, preferred_element_type=jnp.float32)
    value_grad = jnp.dot(normed.T, d_value_lin, preferred_element_type=jnp.float32)
    d_normed_part = (
        jnp.dot(d_query_lin, query_full.T, preferred_element_type=jnp.float32)
        + jnp.dot(d_key_lin, key_full.T, preferred_element_type=jnp.float32)
        + jnp.dot(d_value_lin, value_full.T, preferred_element_type=jnp.float32)
    )
    d_normed = tp_total(d_normed_part)
    input_gain_grad = jnp.sum(d_normed * input_hat, 0)
    input_shift_grad = jnp.sum(d_normed, 0)
    d_mixed = d_middle + full_back(
        d_normed, input_hat, input_factor, input_gain.astype(jnp.float32)
    )
    d_blocks = d_mixed.reshape(block_local, LAT, model_width)
    text_grad = jnp.where(taken[:, None, None], 0.0, d_blocks).reshape(1, row_count, model_width)
    my_target = lax.dynamic_slice_in_dim(image_slot[0], seq_rank * image_slots, image_slots, 0)
    my_live = lax.dynamic_slice_in_dim(live, seq_rank * image_slots, image_slots, 0)
    owner_mine = (
        (jnp.arange(block_count, dtype=jnp.int32)[:, None] == my_target[None, :]) & my_live[None, :]
    ).astype(jnp.bfloat16)
    chosen = owner_mine
    d_embed = jnp.einsum(
        "bi,bld->ild",
        chosen,
        lax.all_gather(d_blocks.astype(jnp.bfloat16), SEQ, axis=0, tiled=True),
        preferred_element_type=jnp.float32,
    )
    d_embed_low = d_embed.astype(jnp.bfloat16).reshape(image_slots * LAT, model_width)
    resample_out_grad = jnp.dot(image_mixed.T, d_embed_low, preferred_element_type=jnp.float32)
    d_image_mixed = jnp.dot(d_embed_low, image_out_full.T, preferred_element_type=jnp.float32)
    d_image_mixed = d_image_mixed.astype(jnp.bfloat16).reshape(image_slots, LAT, heads_local, HEAD)
    d_image_probs = jnp.einsum(
        "iqhd,iphd->ihqp", d_image_mixed, image_values, preferred_element_type=jnp.float32
    )
    d_image_scores = image_probs * (
        d_image_probs - jnp.sum(image_probs * d_image_probs, -1, keepdims=True)
    )
    d_image_scores = d_image_scores.astype(jnp.bfloat16)
    d_probe = (
        jnp.einsum("ihqp,iphd->qhd", d_image_scores, image_keys, preferred_element_type=jnp.float32)
        * score_scale
    )
    d_image_keys = (
        jnp.einsum("ihqp,qhd->iphd", d_image_scores, probe, preferred_element_type=jnp.float32)
        * score_scale
    ).astype(jnp.bfloat16)
    d_image_values = jnp.einsum(
        "ihqp,iqhd->iphd",
        image_probs.astype(jnp.bfloat16),
        d_image_mixed,
        preferred_element_type=jnp.float32,
    ).astype(jnp.bfloat16)
    resample_key_grad = jnp.dot(
        pictures.T,
        d_image_keys.reshape(image_slots * PATCH, half_width),
        preferred_element_type=jnp.float32,
    )
    resample_value_grad = jnp.dot(
        pictures.T,
        d_image_values.reshape(image_slots * PATCH, half_width),
        preferred_element_type=jnp.float32,
    )
    d_probe_flat = d_probe.reshape(LAT, half_width)
    resample_query_grad = jnp.dot(
        latent_full.astype(jnp.float32).T, d_probe_flat, precision=HIGHEST_PRECISION
    )
    latent_grad = tp_total(
        jnp.dot(d_probe_flat, probe_full.astype(jnp.float32).T, precision=HIGHEST_PRECISION)
    )
    summed_in = (
        lax.psum_scatter(query_grad, (SEQ, IMG), scatter_dimension=0, tiled=True),
        lax.psum_scatter(key_grad, (SEQ, IMG), scatter_dimension=0, tiled=True),
        lax.psum_scatter(value_grad, (SEQ, IMG), scatter_dimension=0, tiled=True),
        lax.psum_scatter(up_grad, (SEQ, IMG), scatter_dimension=0, tiled=True),
        lax.psum_scatter(resample_query_grad, (SEQ, IMG), scatter_dimension=0, tiled=True),
        lax.psum_scatter(resample_key_grad, (SEQ, IMG), scatter_dimension=0, tiled=True),
        lax.psum_scatter(resample_value_grad, (SEQ, IMG), scatter_dimension=0, tiled=True),
    )
    summed_out = (
        lax.psum_scatter(out_grad, (SEQ, IMG), scatter_dimension=1, tiled=True),
        lax.psum_scatter(down_grad, (SEQ, IMG), scatter_dimension=1, tiled=True),
        lax.psum_scatter(resample_out_grad, (SEQ, IMG), scatter_dimension=1, tiled=True),
        lax.psum_scatter(latent_grad, (SEQ, IMG), scatter_dimension=1, tiled=True),
    )
    summed_small = lax.psum(
        (
            input_gain_grad,
            input_shift_grad,
            inner_gain_grad,
            inner_shift_grad,
            middle_gain_grad,
            middle_shift_grad,
            up_bias_grad,
            hidden_gain_grad,
            hidden_shift_grad,
        ),
        (SEQ, IMG),
    )
    return (
        result,
        text_grad,
        summed_small[0],
        summed_small[1],
        summed_in[0],
        summed_in[1],
        summed_in[2],
        summed_small[2],
        summed_small[3],
        summed_out[0],
        summed_small[4],
        summed_small[5],
        summed_in[3],
        summed_small[6],
        summed_small[7],
        summed_small[8],
        summed_out[1],
        summed_out[3],
        summed_in[4],
        summed_in[5],
        summed_in[6],
        summed_out[2],
    )


MESH_IDS = pl.DeviceIdType.MESH
ANYWHERE = pl.BlockSpec(memory_space=pl.ANY)
ON_CHIP = pl.BlockSpec(memory_space=pltpu.VMEM)
LANES = 128
PLANE = 8
VMEM_BYTES = 60 * 1024 * 1024
PIECES = 4
FRONT, BACK, ALL, ROWS, INWARD, OUTWARD, SHARED = range(7)


def narrow_heads(mesh):
    return mesh.shape[SEQ] != PLANE or mesh.shape[IMG] != 2 or mesh.shape[TP] != 2


def flipped(number, bit):
    step = 2**bit
    return number + step - 2 * step * ((number // step) % 2)


class Places:
    def __init__(self):
        self.seq, self.tp, self.img = (lax.axis_index(name) for name in (SEQ, TP, IMG))
        self.s_core, self.s_x, self.s_y = (flipped(self.seq, bit) for bit in range(3))
        self.s_xy = flipped(self.s_x, 2)
        self.core, self.x, self.y = (self.at(seq) for seq in (self.s_core, self.s_x, self.s_y))
        self.tp_peer = (self.seq, 1 - self.tp, self.img)
        self.img_peer = (self.seq, self.tp, 1 - self.img)

    def at(self, seq):
        return (seq, self.tp, self.img)


def greet(peers):
    barrier = pltpu.get_barrier_semaphore()
    for peer in peers:
        pl.semaphore_signal(barrier, inc=1, device_id=peer, device_id_type=MESH_IDS)
    pl.semaphore_wait(barrier, len(peers))


def remote(src, dst, send, recv, peer):
    return pltpu.make_async_remote_copy(
        src_ref=src, dst_ref=dst, send_sem=send, recv_sem=recv, device_id=peer, device_id_type=MESH_IDS
    )


def rows_at(ref, first, count):
    return ref.at[pl.ds(pl.multiple_of(first, 16), count)]


class Spread:
    def __init__(self, here, out, block, first, count, send, recv):
        self.here, self.out, self.block = here, out, block
        self.first, self.count, self.send, self.recv = first, count, send, recv
        self.half = count // 2
        self.sent = []

    def part(self, seq, which):
        first = seq * self.block + self.first
        if which == ALL:
            return rows_at(self.out, first, self.count)
        return rows_at(self.out, first + (self.half if which == BACK else 0), self.half)

    def copy(self, src, dst, slot, peer):
        return remote(src, dst, self.send.at[slot], self.recv.at[slot], peer)

    def go(self, src, dst, slot, peer):
        made = self.copy(src, dst, slot, peer)
        made.start()
        self.sent.append(made)

    def own(self, src, src_first):
        here, seq = self.here, self.here.seq

        def own_part(which):
            if which == ALL:
                return rows_at(src, src_first, self.count)
            return rows_at(src, src_first + (self.half if which == BACK else 0), self.half)

        self.go(own_part(FRONT), self.part(seq, FRONT), 0, here.x)
        self.go(own_part(BACK), self.part(seq, BACK), 1, here.y)
        self.go(own_part(BACK), self.part(seq, BACK), 2, here.x)
        self.go(own_part(FRONT), self.part(seq, FRONT), 3, here.y)
        self.go(own_part(ALL), self.part(seq, ALL), 4, here.core)

    def arrived(self, slot, seq, which):
        target = self.part(seq, which)
        self.copy(target, target, slot, self.here.core).wait_recv()

    def forward(self):
        here = self.here
        self.arrived(0, here.s_x, FRONT)
        self.go(self.part(here.s_x, FRONT), self.part(here.s_x, FRONT), 5, here.y)
        self.arrived(1, here.s_y, BACK)
        self.go(self.part(here.s_y, BACK), self.part(here.s_y, BACK), 6, here.x)
        self.arrived(2, here.s_x, BACK)
        self.go(self.part(here.s_x, ALL), self.part(here.s_x, ALL), 7, here.core)
        self.arrived(3, here.s_y, FRONT)
        self.go(self.part(here.s_y, ALL), self.part(here.s_y, ALL), 8, here.core)

    def corner(self):
        here = self.here
        self.arrived(5, here.s_xy, FRONT)
        self.arrived(6, here.s_xy, BACK)
        self.go(self.part(here.s_xy, ALL), self.part(here.s_xy, ALL), 9, here.core)

    def finish(self):
        core = self.here.s_core
        self.arrived(4, core, ALL)
        self.arrived(7, flipped(core, 1), ALL)
        self.arrived(8, flipped(core, 2), ALL)
        self.arrived(9, flipped(flipped(core, 1), 2), ALL)
        for made in self.sent:
            made.wait_send()


def wavefront(stages, count, waiting=()):
    waiting = list(waiting)
    ticks = count + max(lag for lag, _ in stages)
    share = -(-len(waiting) // max(ticks - 2, 1))
    for tick in range(ticks):
        for lag, stage in reversed(stages):
            piece = tick - lag
            if 0 <= piece < count:
                stage(piece)
        for launch in waiting[:share]:
            launch()
        del waiting[:share]


def weight_blocks(weight, side):
    if side == SHARED:
        return weight.shape
    if side == INWARD:
        return (weight.shape[0], weight.shape[1] // PLANE)
    return (weight.shape[0] // PLANE, weight.shape[1])


def intake(gathered, weights, sides, cid):
    n_rows, n_weights = len(gathered), len(weights)
    pieces = PIECES

    def kernel(*refs):
        row_refs, weight_refs = refs[:n_rows], refs[n_rows : n_rows + n_weights]
        refs = refs[n_rows + n_weights :]
        row_outs, weight_outs = refs[:n_rows], refs[n_rows : n_rows + n_weights]
        local, send, recv, w_local, w_send, w_recv, z_send, z_recv = refs[n_rows + n_weights :]
        here = Places()
        seq, tp, img = here.seq, here.tp, here.img
        others = [lax.rem(seq + step, PLANE) for step in range(1, PLANE)]
        greet([(other, tp, img) for other in others] + [here.img_peer])

        def slot_of(out, side, shape, from_seq, from_img):
            number = from_seq * 2 + from_img
            if side == INWARD:
                return out.at[pl.ds(pl.multiple_of(number * shape[0], shape[0]), shape[0])]
            return out.at[:, pl.ds(pl.multiple_of(number * shape[1], shape[1]), shape[1])]

        def block_of(weight, side, shape, to_seq):
            if side == SHARED:
                return weight
            if side == INWARD:
                return weight.at[:, pl.ds(pl.multiple_of(to_seq * shape[1], shape[1]), shape[1])]
            return weight.at[pl.ds(pl.multiple_of(to_seq * shape[0], shape[0]), shape[0])]

        flights, own_copies = [], []

        def begin(index):
            weight, out, side = weight_refs[index], weight_outs[index], sides[index]
            shape = weight_blocks(weight, side)
            mine = pltpu.make_async_copy(
                block_of(weight, side, shape, seq), slot_of(out, side, shape, seq, img), w_local.at[index]
            )
            mine.start()
            crossing = remote(
                block_of(weight, side, shape, seq),
                slot_of(out, side, shape, seq, img),
                z_send.at[index, 0],
                z_recv.at[index, 0],
                here.img_peer,
            )
            crossing.start()
            own_copies.append(mine)
            flights.append(crossing)
            for step, other in enumerate(others, 1):
                made = remote(
                    block_of(weight, side, shape, other),
                    slot_of(out, side, shape, seq, img),
                    w_send.at[index, step],
                    w_recv.at[index, step],
                    here.at(other),
                )
                made.start()
                flights.append(made)

        spreads = []
        for number, (rows, out) in enumerate(zip(row_refs, row_outs)):
            block = rows.shape[0]
            count = block // pieces
            keep = pltpu.make_async_copy(rows, rows_at(out, seq * block, block), local.at[number])
            keep.start()
            own_copies.append(keep)
            for piece in range(pieces):
                at = number * pieces + piece
                spreads.append(
                    (Spread(here, out, block, piece * count, count, send.at[at], recv.at[at]), rows, piece * count)
                )

        def cross(piece):
            for index in range(piece, n_weights, len(spreads)):
                weight, out, side = weight_refs[index], weight_outs[index], sides[index]
                shape = weight_blocks(weight, side)
                for step in range(1, PLANE):
                    source = lax.rem(seq + PLANE - step, PLANE)
                    landed = slot_of(out, side, shape, source, img)
                    remote(landed, landed, w_send.at[index, step], w_recv.at[index, step], here.core).wait_recv()
                    crossing = remote(
                        landed, landed, z_send.at[index, step], z_recv.at[index, step], here.img_peer
                    )
                    crossing.start()
                    flights.append(crossing)

        def own_rows(piece):
            for index in range(piece, n_weights, len(spreads)):
                begin(index)
            spreads[piece][0].own(spreads[piece][1], spreads[piece][2])

        wavefront(
            [
                (0, own_rows),
                (2, lambda piece: spreads[piece][0].forward()),
                (3, lambda piece: cross(piece)),
                (4, lambda piece: spreads[piece][0].corner()),
            ],
            len(spreads),
        )
        for index, (weight, out, side) in enumerate(zip(weight_refs, weight_outs, sides)):
            shape = weight_blocks(weight, side)
            for step in range(PLANE):
                source = lax.rem(seq + PLANE - step, PLANE)
                landed = slot_of(out, side, shape, source, 1 - img)
                remote(landed, landed, z_send.at[index, step], z_recv.at[index, step], here.core).wait_recv()
        for spread, _, _ in spreads:
            spread.finish()
        for made in flights:
            made.wait_send()
        for made in own_copies:
            made.wait()

    def whole(weight, side):
        shape = weight_blocks(weight, side)
        if side == INWARD:
            return jax.ShapeDtypeStruct((2 * PLANE * shape[0], shape[1]), weight.dtype)
        return jax.ShapeDtypeStruct((shape[0], 2 * PLANE * shape[1]), weight.dtype)

    dma = pltpu.SemaphoreType.DMA
    outs = [jax.ShapeDtypeStruct((PLANE * rows.shape[0], rows.shape[1]), rows.dtype) for rows in gathered]
    outs += [whole(weight, side) for weight, side in zip(weights, sides)]
    made = pl.pallas_call(
        kernel,
        out_shape=tuple(outs),
        in_specs=[ANYWHERE] * (n_rows + n_weights),
        out_specs=tuple([ANYWHERE] * len(outs)),
        scratch_shapes=[
            dma((n_rows,)),
            dma((n_rows * pieces, 10)),
            dma((n_rows * pieces, 10)),
            dma((n_weights,)),
            dma((n_weights, PLANE)),
            dma((n_weights, PLANE)),
            dma((n_weights, PLANE)),
            dma((n_weights, PLANE)),
        ],
        compiler_params=pltpu.CompilerParams(
            collective_id=cid, has_side_effects=True, vmem_limit_bytes=VMEM_BYTES
        ),
    )(*gathered, *weights)
    return made[:n_rows], made[n_rows:]


class Rider:
    inputs, out_shapes, scratch = (), (), ()

    def bind(self, here, ins, outs, scratch):
        self.here, self.ins, self.outs, self.held = here, ins, outs, scratch
        self.sent, self.kept, self.due, self.launches = [], [], [], []

    def keep(self, src, dst, sem):
        made = pltpu.make_async_copy(src, dst, sem)
        self.launches.append(made.start)
        self.kept.append(made)

    def send(self, src, dst, send, recv, peer):
        made = remote(src, dst, send, recv, peer)
        self.launches.append(made.start)
        self.sent.append(made)

    def finish(self):
        for dst, send, recv in self.due:
            remote(dst, dst, send, recv, self.here.core).wait_recv()
        for made in self.sent:
            made.wait_send()
        for made in self.kept:
            made.wait()


class PlaneWeights(Rider):
    def __init__(self, weights, sides):
        self.inputs, self.sides = weights, sides
        self.blocks = [weight_blocks(weight, side) for weight, side in zip(weights, sides)]
        self.out_shapes = [
            jax.ShapeDtypeStruct((PLANE,) + block, weight.dtype) for block, weight in zip(self.blocks, weights)
        ]
        dma = pltpu.SemaphoreType.DMA
        self.scratch = [dma((len(weights), PLANE)), dma((len(weights), PLANE))]

    def peers(self, here):
        return [here.at(lax.rem(here.seq + step, PLANE)) for step in range(1, PLANE)]

    def start(self):
        here, (send, recv) = self.here, self.held
        for index, (weight, out, side, block) in enumerate(zip(self.ins, self.outs, self.sides, self.blocks)):
            for step in range(PLANE):
                target = lax.rem(here.seq + step, PLANE)
                source = lax.rem(here.seq + PLANE - step, PLANE)
                if side == INWARD:
                    part = weight.at[:, pl.ds(pl.multiple_of(target * block[1], block[1]), block[1])]
                else:
                    part = weight.at[pl.ds(pl.multiple_of(target * block[0], block[0]), block[0])]
                if step == 0:
                    self.keep(part, out.at[here.seq], recv.at[index, 0])
                else:
                    self.send(part, out.at[here.seq], send.at[index, step], recv.at[index, step], here.at(target))
                    self.due.append((out.at[source], send.at[index, step], recv.at[index, step]))


class CrossWeights(Rider):
    def __init__(self, blocks, sides):
        self.inputs, self.sides = blocks, sides
        self.out_shapes = []
        for block, side in zip(blocks, sides):
            count, rows, columns = block.shape
            shape = (count, 2, rows, columns) if side == INWARD else (rows, count * 2 * columns)
            self.out_shapes.append(jax.ShapeDtypeStruct(shape, block.dtype))
        dma = pltpu.SemaphoreType.DMA
        self.scratch = [dma((len(blocks), PLANE)), dma((len(blocks), PLANE)), dma((len(blocks), PLANE))]

    def peers(self, here):
        return [here.img_peer]

    def start(self):
        here, (send, recv, local) = self.here, self.held
        for index, (block, out, side) in enumerate(zip(self.ins, self.outs, self.sides)):
            width = block.shape[2]
            for seq in range(PLANE):

                def place(img, seq=seq, width=width, out=out, side=side):
                    if side == INWARD:
                        return out.at[seq, img]
                    return out.at[:, pl.ds(pl.multiple_of((seq * 2 + img) * width, width), width)]

                self.send(
                    block.at[seq], place(here.img), send.at[index, seq], recv.at[index, seq], here.img_peer
                )
                self.keep(block.at[seq], place(here.img), local.at[index, seq])
                self.due.append((place(1 - here.img), send.at[index, seq], recv.at[index, seq]))


class CrossGrads(Rider):
    def __init__(self, grads, sides):
        self.inputs, self.sides = grads, sides
        self.out_shapes = []
        for grad, side in zip(grads, sides):
            if side == INWARD:
                shape = (grad.shape[0], grad.shape[2], grad.shape[3])
            else:
                shape = (PLANE, grad.shape[0], grad.shape[1] // (2 * PLANE))
            self.out_shapes.append(jax.ShapeDtypeStruct(shape, grad.dtype))
        dma = pltpu.SemaphoreType.DMA
        self.scratch = [dma((len(grads), PLANE)), dma((len(grads), PLANE))]

    def peers(self, here):
        return [here.img_peer]

    def start(self):
        here, (send, recv) = self.here, self.held
        for index, (grad, out, side) in enumerate(zip(self.ins, self.outs, self.sides)):
            width = out.shape[2]
            for seq in range(PLANE):
                if side == INWARD:
                    part = grad.at[seq, 1 - here.img]
                else:
                    part = grad.at[:, pl.ds(pl.multiple_of((seq * 2 + 1 - here.img) * width, width), width)]
                self.send(part, out.at[seq], send.at[index, seq], recv.at[index, seq], here.img_peer)
                self.due.append((out.at[seq], send.at[index, seq], recv.at[index, seq]))


class Stream:
    def __init__(self, rows_all, left, right, across, row_inputs, row_kinds, row_outs, row_function, gather):
        self.own_left = left is not None
        self.inputs = ([left] if self.own_left else []) + [right] + list(row_inputs)
        self.across, self.row_kinds, self.row_outs = across, row_kinds, row_outs
        self.row_function, self.gather = row_function, gather
        width = right.shape[0] if across else right.shape[1]
        self.width, self.block, self.pieces = width, rows_all // PLANE, PIECES
        self.count = self.block // self.pieces
        self.half = self.count // 2
        low_type = jnp.bfloat16
        self.out_shapes = [shape for shape, _ in row_outs]
        if gather:
            self.out_shapes.append(jax.ShapeDtypeStruct((rows_all, width), low_type))
        dma = pltpu.SemaphoreType.DMA
        block, pieces, count, half = self.block, self.pieces, self.count, self.half
        self.scratch = [
            pltpu.VMEM((4, block, width), low_type),
            pltpu.VMEM((4, block, width), low_type),
            pltpu.VMEM((4, block, width), jnp.float32),
            pltpu.VMEM((pieces, half, width), low_type),
            pltpu.VMEM((pieces, half, width), low_type),
            pltpu.VMEM((pieces, count, width), low_type),
            pltpu.VMEM((pieces, count, width), low_type),
            pltpu.VMEM((pieces, count, width), low_type),
            pltpu.VMEM((pieces, count, width), low_type),
            pltpu.VMEM((block, width), low_type),
            dma((4,)),
            dma((4,)),
            dma((pieces, 7)),
            dma((pieces, 7)),
            dma((pieces, 10)),
            dma((pieces, 10)),
            dma((pieces,)),
        ]

    def out_specs(self):
        return [ON_CHIP] * len(self.row_outs) + [ANYWHERE] * (len(self.out_shapes) - len(self.row_outs))

    def peers(self, here):
        return [here.core, here.x, here.y, here.tp_peer]

    def bind(self, here, ins, outs, scratch):
        self.here = here
        if self.own_left:
            self.left, ins = ins[0], ins[1:]
        self.right, self.ins = ins[0], ins[1:]
        self.outs = outs
        (self.away, self.core_in, self.near, self.from_xd, self.from_yd, self.from_x, self.from_y) = scratch[:7]
        (self.mine, self.theirs, self.low, self.c_send, self.c_recv) = scratch[7:12]
        (self.send, self.recv, self.g_send, self.g_recv, self.l_sem) = scratch[12:]
        self.sent, self.spreads, self.core_copies = [], [], {}

    def chunk(self, base, kind):
        if kind in (1, 3):
            base = flipped(base, 1)
        if kind in (2, 3):
            base = flipped(base, 2)
        return base

    def product(self, seq, target, low_type):
        first = pl.multiple_of(seq * self.block, self.block)
        rows = self.left[pl.ds(first, self.block), :]
        step = min(512, self.width)
        for column in range(0, self.width, step):
            if self.across:
                part = lax.dot_general(
                    rows,
                    self.right[column : column + step, :],
                    (((1,), (1,)), ((), ())),
                    preferred_element_type=jnp.float32,
                )
            else:
                part = jnp.dot(
                    rows, self.right[:, column : column + step], preferred_element_type=jnp.float32
                )
            target[:, column : column + step] = part.astype(low_type)

    def begin(self):
        here = self.here
        for kind in (3, 1, 2, 0):
            self.product(self.chunk(here.s_core, kind), self.away.at[kind], jnp.bfloat16)
            made = remote(
                self.away.at[kind], self.core_in.at[kind], self.c_send.at[kind], self.c_recv.at[kind], here.core
            )
            made.start()
            self.core_copies[kind] = made
            self.product(self.chunk(here.seq, kind), self.near.at[kind], jnp.float32)

    def go(self, src, dst, piece, slot, peer):
        made = remote(src, dst, self.send.at[piece, slot], self.recv.at[piece, slot], peer)
        made.start()
        self.sent.append(made)

    def landed(self, dst, piece, slot):
        remote(dst, dst, self.send.at[piece, slot], self.recv.at[piece, slot], self.here.core).wait_recv()

    def held(self, kind, piece, which=ALL):
        first, rows = piece * self.count, self.count
        if which != ALL:
            first, rows = first + (self.half if which == BACK else 0), self.half
        return self.core_in.at[kind, pl.ds(first, rows)]

    def folded(self, kind, piece):
        if piece == 0:
            self.core_copies[kind].wait_recv()
        near = self.near[kind, pl.ds(piece * self.count, self.count), :]
        return self.held(kind, piece)[...].astype(jnp.float32) + near

    def first_sends(self, piece):
        here, half = self.here, self.half
        self.held(3, piece)[...] = self.folded(3, piece).astype(jnp.bfloat16)
        self.go(self.held(3, piece, FRONT), self.from_xd.at[piece], piece, 0, here.x)
        self.go(self.held(3, piece, BACK), self.from_yd.at[piece], piece, 1, here.y)
        self.held(1, piece)[...] = self.folded(1, piece).astype(jnp.bfloat16)
        self.go(self.held(1, piece, FRONT), self.from_x.at[piece, pl.ds(0, half)], piece, 2, here.x)
        self.held(2, piece)[...] = self.folded(2, piece).astype(jnp.bfloat16)
        self.go(self.held(2, piece, BACK), self.from_y.at[piece, pl.ds(half, half)], piece, 3, here.y)

    def second_sends(self, piece):
        here, half = self.here, self.half
        self.landed(self.from_xd.at[piece], piece, 0)
        at = self.held(2, piece, FRONT)
        at[...] = (at[...].astype(jnp.float32) + self.from_xd[piece].astype(jnp.float32)).astype(jnp.bfloat16)
        self.go(at, self.from_y.at[piece, pl.ds(0, half)], piece, 4, here.y)
        self.landed(self.from_yd.at[piece], piece, 1)
        at = self.held(1, piece, BACK)
        at[...] = (at[...].astype(jnp.float32) + self.from_yd[piece].astype(jnp.float32)).astype(jnp.bfloat16)
        self.go(at, self.from_x.at[piece, pl.ds(half, half)], piece, 5, here.x)

    def plane_sum(self, piece):
        half = self.half
        self.landed(self.from_x.at[piece, pl.ds(0, half)], piece, 2)
        self.landed(self.from_y.at[piece, pl.ds(half, half)], piece, 3)
        self.landed(self.from_y.at[piece, pl.ds(0, half)], piece, 4)
        self.landed(self.from_x.at[piece, pl.ds(half, half)], piece, 5)
        total = self.folded(0, piece)
        total = total + self.from_x[piece].astype(jnp.float32) + self.from_y[piece].astype(jnp.float32)
        self.mine[piece] = total.astype(jnp.bfloat16)
        self.go(self.mine.at[piece], self.theirs.at[piece], piece, 6, self.here.tp_peer)

    def rows_done(self, piece):
        here = self.here
        self.landed(self.theirs.at[piece], piece, 6)
        total = self.mine[piece].astype(jnp.float32) + self.theirs[piece].astype(jnp.float32)
        rows = pl.ds(piece * self.count, self.count)
        views = [ref.at[rows] if kind == ROWS else ref for ref, kind in zip(self.ins, self.row_kinds)]
        out_views = [ref.at[rows] if kind == ROWS else ref for ref, (_, kind) in zip(self.outs, self.row_outs)]
        given = self.row_function(total, piece, views, out_views)
        if self.gather:
            out = self.outs[-1]
            self.low[rows, :] = given
            first = pl.multiple_of(here.seq * self.block + piece * self.count, 16)
            keep = pltpu.make_async_copy(self.low.at[rows], out.at[pl.ds(first, self.count)], self.l_sem.at[piece])
            keep.start()
            spread = Spread(
                here, out, self.block, piece * self.count, self.count, self.g_send.at[piece], self.g_recv.at[piece]
            )
            spread.own(self.low, piece * self.count)
            self.spreads.append((spread, keep))

    def stages(self):
        stages = [(0, self.first_sends), (1, self.second_sends), (2, self.plane_sum), (4, self.rows_done)]
        if self.gather:
            stages.append((5, lambda piece: self.spreads[piece][0].forward()))
            stages.append((6, lambda piece: self.spreads[piece][0].corner()))
        return stages

    def finish(self):
        for spread, keep in self.spreads:
            spread.finish()
            keep.wait()
        for made in self.sent:
            made.wait_send()
        for made in self.core_copies.values():
            made.wait_send()


class Front(Rider):
    def total_scratch(self, count, rows):
        dma = pltpu.SemaphoreType.DMA
        return [
            pltpu.VMEM((PLANE - 1, count, rows), jnp.float32),
            pltpu.VMEM((count, rows), jnp.float32),
            pltpu.VMEM((count, rows), jnp.float32),
            pltpu.VMEM((count, rows), jnp.float32),
            dma((PLANE,)),
            dma((PLANE,)),
        ]

    def peers(self, here):
        return [here.at(lax.rem(here.seq + step, PLANE)) for step in range(1, PLANE)]

    def small_sum(self, scratch):
        here, (plane, own, mine, theirs, send, recv) = self.here, scratch
        made = []
        for step, peer in enumerate(self.peers(here)):
            copy = remote(own, plane.at[step], send.at[step], recv.at[step], peer)
            copy.start()
            made.append(copy)
        total = own[...]
        for step, copy in enumerate(made):
            copy.wait_recv()
            total = total + plane[step]
        mine[...] = total
        last = remote(mine, theirs, send.at[PLANE - 1], recv.at[PLANE - 1], here.tp_peer)
        last.start()
        last.wait()
        for copy in made:
            copy.wait_send()
        total = mine[...] + theirs[...]
        count, rows = total.shape
        return jnp.concatenate([total, jnp.zeros((8 - count, rows), jnp.float32)], 0).T


class InnerFront(Front):
    def __init__(self, attended, sums, gain, shift, full_width):
        self.inputs = [attended, sums, gain, shift]
        self.full_width = full_width
        rows, width = attended.shape
        self.out_shapes = [
            jax.ShapeDtypeStruct((rows, width), jnp.bfloat16),
            jax.ShapeDtypeStruct((rows, width), jnp.float32),
            jax.ShapeDtypeStruct((rows, width), jnp.float32),
        ]
        self.scratch = self.total_scratch(sums.shape[0], rows)

    def run(self):
        attended, sums, gain, shift = self.ins
        low, hat, factor_out = self.outs
        self.held[1][...] = sums[...]
        total = self.small_sum(self.held)
        average = total[:, 0:1] / self.full_width
        factor = lax.rsqrt(total[:, 1:2] / self.full_width - average * average + EPSILON)
        normal = (attended[...] - average) * factor
        hat[...] = normal
        factor_out[...] = jnp.broadcast_to(factor, normal.shape)
        low[...] = (normal * gain[...] + shift[...]).astype(jnp.bfloat16)
        return low


class GradFront(Front):
    def grads(self, products):
        here = self.here
        for seq in range(PLANE):
            for product in products:
                self.launches.append(functools.partial(self.part, product, seq))

    def part(self, product, seq):
        left, right, outs, side, theirs, send, recv = product
        here = self.here
        span = (left.shape[1] if side == INWARD else right.shape[1]) // PLANE
        at = slice(seq * span, (seq + 1) * span)
        contract = (((0,), (0,)), ((), ()))
        if side == INWARD:
            made = lax.dot_general(left[:, at], right[...], contract, preferred_element_type=jnp.float32)
        else:
            made = lax.dot_general(left[...], right[:, at], contract, preferred_element_type=jnp.float32)
        made = made.astype(jnp.bfloat16)
        half = span // 2
        for number, out in enumerate(outs):
            if side == INWARD:
                width = out.shape[3]
                piece = made[:, number * width : (number + 1) * width]
                out[seq, 0], out[seq, 1] = piece[:half], piece[half:]
                src = out.at[seq, 1 - here.img]
            else:
                out[:, at] = made
                src = out.at[:, pl.ds(pl.multiple_of((seq * 2 + 1 - here.img) * half, half), half)]
            copy = remote(
                src, theirs[number].at[seq], send.at[number, seq], recv.at[number, seq], here.img_peer
            )
            copy.start()
            self.sent.append(copy)
            self.due.append((theirs[number].at[seq], send.at[number, seq], recv.at[number, seq]))


def grad_shapes(model_width, rows, side):
    span = model_width // PLANE
    if side == INWARD:
        shapes = [(PLANE, 2, span // 2, rows), (PLANE, span // 2, rows)]
    else:
        shapes = [(rows, model_width), (PLANE, rows, span // 2)]
    return [jax.ShapeDtypeStruct(shape, jnp.bfloat16) for shape in shapes]


class HiddenFront(GradFront):
    def __init__(self, activated, slope, d_settled, sums, gain, shift, lifted, cotangent_all, full_width):
        self.inputs = [activated, slope, d_settled, sums, gain, shift, lifted, cotangent_all]
        self.full_width = full_width
        rows, width = activated.shape
        model_width = lifted.shape[1]
        low_shape = jax.ShapeDtypeStruct((rows, width), jnp.bfloat16)
        up, up_theirs = grad_shapes(model_width, width, INWARD)
        down, down_theirs = grad_shapes(model_width, width, OUTWARD)
        self.out_shapes = [
            low_shape,
            low_shape,
            jax.ShapeDtypeStruct((8, width), jnp.float32),
            up,
            down,
            up_theirs,
            down_theirs,
        ]
        dma = pltpu.SemaphoreType.DMA
        self.scratch = self.total_scratch(sums.shape[0], rows) + [dma((1, PLANE))] * 4

    def run(self):
        activated, slope, d_settled, sums, gain, shift, lifted, cotangent_all = self.ins
        settled, d_hidden, vectors, up, down, up_theirs, down_theirs = self.outs
        self.held[1][...] = sums[...]
        total = self.small_sum(self.held[:6]) / self.full_width
        average = total[:, 0:1]
        factor = lax.rsqrt(total[:, 1:2] - average * average + EPSILON)
        mean_scaled = total[:, 2:3]
        mean_cross = factor * (total[:, 3:4] - average * mean_scaled)
        rows = activated.shape[0]
        step = rows // PLANE
        gain_sum = shift_sum = bias_sum = 0.0
        for first in range(0, rows, step):
            at = slice(first, first + step)
            normal = (activated[at, :] - average[at]) * factor[at]
            settled[at, :] = (normal * gain[...] + shift[...]).astype(jnp.bfloat16)
            grad = d_settled[at, :]
            inner = factor[at] * (grad * gain[...] - mean_scaled[at] - normal * mean_cross[at])
            low = (slope[at, :] * inner).astype(jnp.bfloat16)
            d_hidden[at, :] = low
            gain_sum += jnp.sum(grad * normal, 0, keepdims=True)
            shift_sum += jnp.sum(grad, 0, keepdims=True)
            bias_sum += jnp.sum(low.astype(jnp.float32), 0, keepdims=True)
        vectors[...] = jnp.zeros_like(vectors)
        vectors[0:1, :], vectors[1:2, :], vectors[2:3, :] = gain_sum, shift_sum, bias_sum
        up_send, up_recv, down_send, down_recv = self.held[6:]
        self.grads(
            [
                (lifted, d_hidden, [up], INWARD, [up_theirs], up_send, up_recv),
                (settled, cotangent_all, [down], OUTWARD, [down_theirs], down_send, down_recv),
            ]
        )
        return d_hidden


class AttendFront(GradFront):
    def __init__(self, d_branch, out_part, hat, factor, gain, kept, tables, segment, normed, inner_low, full_width):
        self.inputs = [d_branch, out_part, hat, factor, gain, *kept, *tables]
        self.inputs += [segment[:, None], segment[None, :], normed, inner_low]
        self.full_width = full_width
        rows, width = hat.shape
        model_width = normed.shape[1]
        low_type, f32, dma = jnp.bfloat16, jnp.float32, pltpu.SemaphoreType.DMA
        inward, inward_theirs = grad_shapes(model_width, width, INWARD)
        out, out_theirs = grad_shapes(model_width, width, OUTWARD)
        self.out_shapes = [jax.ShapeDtypeStruct((8, width), f32)]
        self.out_shapes += [inward, inward, inward, out, inward_theirs, inward_theirs, inward_theirs, out_theirs]
        self.scratch = self.total_scratch(2, rows) + [dma((3, PLANE)), dma((3, PLANE)), dma((1, PLANE)), dma((1, PLANE))]
        self.scratch += [pltpu.VMEM((rows, width), low_type), pltpu.VMEM((rows, 3 * width), low_type)]
        self.scratch += [pltpu.VMEM((rows, width), f32)] * 4

    def run(self):
        d_branch, out_part, hat, factor, gain, attended, q_ref, k_ref, v_ref, lse = self.ins[:10]
        cos_ref, sin_ref, grow_ref, column_ref, row_ref, normed, inner_low = self.ins[10:]
        vectors, *grads = self.outs
        grad_send, grad_recv, out_send, out_recv, d_att, lin_out, d_inner, d_query, d_key, d_value = self.held[6:]
        rows_all, width = hat.shape
        f32, low_type = jnp.float32, jnp.bfloat16
        gain_sum = shift_sum = 0.0
        for first in range(0, rows_all, ATTEND_ROWS):
            at = slice(first, first + ATTEND_ROWS)
            grad = lax.dot_general(
                d_branch[at, :], out_part[...], (((1,), (1,)), ((), ())), preferred_element_type=f32
            )
            d_inner[at, :] = grad
            gain_sum += jnp.sum(grad * hat[at, :], 0, keepdims=True)
            shift_sum += jnp.sum(grad, 0, keepdims=True)
            scaled = grad * gain[...]
            sums = [jnp.sum(scaled, 1, keepdims=True), jnp.sum(scaled * hat[at, :], 1, keepdims=True)]
            self.held[1][:, at] = as_lanes(sums)[:2]
        vectors[...] = jnp.zeros_like(vectors)
        vectors[0:1, :], vectors[1:2, :] = gain_sum, shift_sum
        total = self.small_sum(self.held[:6]) / self.full_width
        d_att[...] = (
            factor[...] * (d_inner[...] * gain[...] - total[:, 0:1] - hat[...] * total[:, 1:2])
        ).astype(low_type)
        heads, scale = width // HEAD, HEAD ** (-0.5)
        for first in range(0, rows_all, ATTEND_ROWS):
            at, keys = slice(first, first + ATTEND_ROWS), first + ATTEND_ROWS
            allowed = allowed_part(column_ref, row_ref, first, ATTEND_ROWS, keys)
            for head in range(heads):
                lanes = slice(head * HEAD, (head + 1) * HEAD)
                scores = lax.dot_general(
                    q_ref[at, lanes] * scale,
                    k_ref[:keys, lanes],
                    (((1,), (1,)), ((), ())),
                    preferred_element_type=f32,
                )
                scores = jnp.where(allowed, scores, -1e30)
                probs = jnp.exp(scores - lse[at, head : head + 1])
                d_rows = d_att[at, lanes]
                d_probs = lax.dot_general(
                    d_rows, v_ref[:keys, lanes], (((1,), (1,)), ((), ())), preferred_element_type=f32
                )
                delta = jnp.sum(d_rows.astype(f32) * attended[at, lanes], -1, keepdims=True)
                d_scores = (probs * (d_probs - delta)).astype(low_type)
                d_query[at, lanes] = jnp.dot(d_scores, k_ref[:keys, lanes], preferred_element_type=f32) * scale
                key_part = (
                    lax.dot_general(
                        d_scores, q_ref[at, lanes], (((0,), (0,)), ((), ())), preferred_element_type=f32
                    )
                    * scale
                )
                value_part = lax.dot_general(
                    probs.astype(low_type), d_rows, (((0,), (0,)), ((), ())), preferred_element_type=f32
                )
                if first:
                    d_key[:first, lanes] += key_part[:first]
                    d_value[:first, lanes] += value_part[:first]
                d_key[first:keys, lanes] = key_part[first:]
                d_value[first:keys, lanes] = value_part[first:]
        for first in range(0, rows_all, ATTEND_ROWS):
            at = slice(first, first + ATTEND_ROWS)
            cosine, sine, growth = cos_ref[at, :], sin_ref[at, :], grow_ref[at, :]
            scaled = d_query[at, :] * growth
            lin_out[at, :width] = (scaled * cosine - halves_swapped(scaled) * sine).astype(low_type)
            scaled = d_key[at, :] * (1.0 / growth)
            lin_out[at, width : 2 * width] = (scaled * cosine - halves_swapped(scaled) * sine).astype(low_type)
            lin_out[at, 2 * width :] = d_value[at, :].astype(low_type)
        self.grads(
            [
                (normed, lin_out, grads[:3], INWARD, grads[4:7], grad_send, grad_recv),
                (inner_low, d_branch, grads[3:4], OUTWARD, grads[7:], out_send, out_recv),
            ]
        )
        return lin_out


def exchange(front, streams, riders, cid):
    fronts = [front] if front is not None else []
    parts = fronts + list(streams) + list(riders)

    def kernel(*refs):
        here = Places()
        refs = list(refs)

        def take(count):
            taken = refs[:count]
            del refs[:count]
            return taken

        ins = [take(len(part.inputs)) for part in parts]
        outs = [take(len(part.out_shapes)) for part in parts]
        for part, part_ins, part_outs in zip(parts, ins, outs):
            part.bind(here, part_ins, part_outs, take(len(part.scratch)))
        wide_parts = fronts + [rider for rider in riders if isinstance(rider, PlaneWeights)]
        peers = [here.tp_peer]
        if isinstance(front, GradFront) or any(not isinstance(rider, PlaneWeights) for rider in riders):
            peers.append(here.img_peer)
        if wide_parts:
            peers += wide_parts[0].peers(here)
        else:
            peers += [here.core, here.x, here.y]
        greet(peers)
        if front is not None:
            streams[0].left = front.run()
        streams[0].begin()
        for rider in riders:
            rider.start()
        for stream in streams[1:]:
            stream.begin()
        stages = []
        for stream in reversed(streams):
            stages += stream.stages()
        wavefront(stages, PIECES, [launch for part in fronts + list(riders) for launch in part.launches])
        for part in parts:
            part.finish()

    out_shapes = [shape for part in parts for shape in part.out_shapes]
    in_specs = [ON_CHIP] * sum(len(part.inputs) for part in fronts + list(streams))
    in_specs += [ANYWHERE] * sum(len(rider.inputs) for rider in riders)
    out_specs = [ON_CHIP for part in fronts for _ in part.out_shapes]
    out_specs += [spec for stream in streams for spec in stream.out_specs()]
    out_specs += [ANYWHERE] * sum(len(rider.out_shapes) for rider in riders)
    made = pl.pallas_call(
        kernel,
        out_shape=tuple(out_shapes),
        in_specs=in_specs,
        out_specs=tuple(out_specs),
        scratch_shapes=[item for part in parts for item in part.scratch],
        compiler_params=pltpu.CompilerParams(
            collective_id=cid, has_side_effects=True, vmem_limit_bytes=VMEM_BYTES
        ),
    )(*[value for part in parts for value in part.inputs])
    made = list(made)
    split = []
    for part in parts:
        split.append(made[: len(part.out_shapes)])
        del made[: len(part.out_shapes)]
    return split


def finale(pairs, late, sides, late_sides, small, latents_t, query_rows, cid):
    n, n_late = len(sides), len(late_sides)
    all_sides = list(sides) + list(late_sides)
    grads = [grad for grad, _ in pairs] + list(late)

    def block_shape(grad, side):
        if side == INWARD:
            return (grad.shape[2], grad.shape[3])
        return (grad.shape[0], grad.shape[1] // (2 * PLANE))

    blocks = [block_shape(grad, side) for grad, side in zip(grads, all_sides)]
    total = n + n_late

    def kernel(*refs):
        refs = list(refs)

        def take(count):
            taken = refs[:count]
            del refs[:count]
            return taken

        grad_refs = take(total)
        theirs = take(n)
        small_ref, latents_ref, query_ref = take(3)
        out_refs = take(total)
        sums_out, query_out, latent_out = take(3)
        late_theirs = take(n_late)
        summed = take(total)
        small_theirs, small_mine, small_all, lat_mine, lat_theirs = take(5)
        z_send, z_recv, send, recv, local, s_send, s_recv = take(7)
        here = Places()
        seq, img = here.seq, here.img
        ring = [here.at(lax.rem(seq + step, PLANE)) for step in range(1, PLANE)]
        greet(ring + [here.img_peer, here.tp_peer])
        theirs = theirs + late_theirs

        def part_of(index, to_seq, to_img):
            ref, block = grad_refs[index], blocks[index]
            if all_sides[index] == INWARD:
                return ref.at[to_seq, to_img]
            return ref.at[:, pl.ds(pl.multiple_of((to_seq * 2 + to_img) * block[1], block[1]), block[1])]

        def slot_of(index, from_seq):
            ref, block = out_refs[index], blocks[index]
            if all_sides[index] == INWARD:
                return ref.at[:, pl.ds(pl.multiple_of(from_seq * block[1], block[1]), block[1])]
            return ref.at[pl.ds(pl.multiple_of(from_seq * block[0], block[0]), block[0])]

        waits, crossings = [], {}
        small_cross = remote(small_ref, small_theirs, s_send.at[0], s_recv.at[0], here.img_peer)
        small_cross.start()
        for index in range(n, total):
            for step in range(PLANE):
                target = lax.rem(seq + step, PLANE)
                made = remote(
                    part_of(index, target, 1 - img),
                    theirs[index].at[target],
                    z_send.at[index - n, step],
                    z_recv.at[index - n, step],
                    here.img_peer,
                )
                made.start()
                crossings[index, step] = made

        def deliver(index):
            for step in range(PLANE):
                target = lax.rem(seq + step, PLANE)
                if index >= n:
                    crossings[index, step].wait_recv()
                mine = part_of(index, target, img)[...].astype(jnp.float32)
                summed[index][target] = (mine + theirs[index][target].astype(jnp.float32)).astype(jnp.bfloat16)
                if step == 0:
                    made = pltpu.make_async_copy(summed[index].at[target], slot_of(index, seq), local.at[index])
                    made.start()
                    waits.append(made.wait)
                    continue
                made = remote(
                    summed[index].at[target],
                    slot_of(index, seq),
                    send.at[index, step],
                    recv.at[index, step],
                    here.at(target),
                )
                made.start()
                waits.append(made.wait_send)

        deliver(0)
        small_cross.wait()
        small_mine[...] = small_ref[...] + small_theirs[...]
        small_all[seq] = small_mine[...]
        small_copies = []
        for step, peer in enumerate(ring, 1):
            made = remote(small_mine, small_all.at[seq], s_send.at[step], s_recv.at[step], peer)
            made.start()
            small_copies.append(made)
        for index in range(1, total):
            deliver(index)
        for made in small_copies:
            made.wait()
        sums_out[...] = small_all[...]
        rows = latents_ref.shape[1]
        latent_part = jnp.zeros(lat_mine.shape, jnp.float32)
        columns = small_all.shape[2]
        for source in range(PLANE):
            probe = small_all[source, :rows, :]
            at = slice(source * columns, (source + 1) * columns)
            query_out[:, at] = jnp.dot(
                latents_ref[...], probe, precision=HIGHEST_PRECISION, preferred_element_type=jnp.float32
            )
            latent_part += lax.dot_general(
                probe,
                query_ref[:, at],
                (((1,), (1,)), ((), ())),
                precision=HIGHEST_PRECISION,
                preferred_element_type=jnp.float32,
            )
        lat_mine[...] = latent_part
        last = remote(lat_mine, lat_theirs, s_send.at[PLANE], s_recv.at[PLANE], here.tp_peer)
        last.start()
        last.wait()
        latent_out[...] = lat_mine[...] + lat_theirs[...]
        for index in range(total):
            for step in range(1, PLANE):
                source = lax.rem(seq + PLANE - step, PLANE)
                at = slot_of(index, source)
                remote(at, at, send.at[index, step], recv.at[index, step], here.core).wait_recv()
        for wait in waits:
            wait()
        for made in crossings.values():
            made.wait_send()

    dma, low_type, f32 = pltpu.SemaphoreType.DMA, jnp.bfloat16, jnp.float32
    outs = []
    for block, side in zip(blocks, all_sides):
        shape = (block[0], PLANE * block[1]) if side == INWARD else (PLANE * block[0], block[1])
        outs.append(jax.ShapeDtypeStruct(shape, low_type))
    small_shapes = [
        jax.ShapeDtypeStruct((PLANE,) + small.shape, f32),
        jax.ShapeDtypeStruct(query_rows.shape, f32),
        jax.ShapeDtypeStruct((latents_t.shape[1], latents_t.shape[0]), f32),
    ]
    made = pl.pallas_call(
        kernel,
        out_shape=tuple(outs + small_shapes),
        in_specs=[ON_CHIP] * (total + n + 3),
        out_specs=tuple([ANYWHERE] * total + [ON_CHIP] * 3),
        scratch_shapes=[pltpu.VMEM((PLANE,) + block, low_type) for block in blocks[n:]]
        + [pltpu.VMEM((PLANE,) + block, low_type) for block in blocks]
        + [
            pltpu.VMEM(small.shape, f32),
            pltpu.VMEM(small.shape, f32),
            pltpu.VMEM((PLANE,) + small.shape, f32),
            pltpu.VMEM((latents_t.shape[1], latents_t.shape[0]), f32),
            pltpu.VMEM((latents_t.shape[1], latents_t.shape[0]), f32),
            dma((n_late, PLANE)),
            dma((n_late, PLANE)),
            dma((total, PLANE)),
            dma((total, PLANE)),
            dma((total,)),
            dma((PLANE + 1,)),
            dma((PLANE + 1,)),
        ],
        compiler_params=pltpu.CompilerParams(
            collective_id=cid, has_side_effects=True, vmem_limit_bytes=VMEM_BYTES
        ),
    )(*grads, *[given for _, given in pairs], small, latents_t, query_rows)
    return made[:total], made[total:]


def widened(arrays):
    def kernel(*refs):
        for src, dst in zip(refs[: len(arrays)], refs[len(arrays) :]):
            dst[...] = src[...].astype(jnp.float32)

    return pl.pallas_call(
        kernel,
        out_shape=tuple(jax.ShapeDtypeStruct(array.shape, jnp.float32) for array in arrays),
        in_specs=[ON_CHIP] * len(arrays),
        out_specs=tuple([ON_CHIP] * len(arrays)),
        compiler_params=pltpu.CompilerParams(vmem_limit_bytes=VMEM_BYTES),
    )(*arrays)


IMAGES_A_STEP = 4


def image_probs_of(probe, keys, scale):
    scores = lax.dot_general(
        probe * scale, keys, (((1,), (1,)), ((), ())), preferred_element_type=jnp.float32
    )
    weights = jnp.exp(scores - jnp.max(scores, -1, keepdims=True))
    return weights * (1.0 / jnp.sum(weights, -1, keepdims=True))


def image_forward(pictures, key_part, value_part, latent_all, probe_part, slots, live):
    images, width = slots.shape[0], key_part.shape[1]
    scale = HEAD ** (-0.5)
    step = IMAGES_A_STEP * PATCH

    def kernel(slots_ref, live_ref, pictures_ref, key_w, value_w, latent_ref, probe_w, keys, placed, probe, both_w):
        number = pl.program_id(0)

        @pl.when(number == 0)
        def _():
            probe[...] = jnp.dot(latent_ref[...], probe_w[...], preferred_element_type=jnp.float32).astype(
                jnp.bfloat16
            )
            both_w[:, :width] = key_w[...]
            both_w[:, width:] = value_w[...]

        keys[...] = jnp.dot(pictures_ref[...], both_w[...], preferred_element_type=jnp.float32).astype(jnp.bfloat16)
        for image in range(IMAGES_A_STEP):
            slot = number * IMAGES_A_STEP + image
            alive = (live_ref[slot] > 0).astype(jnp.float32)
            rows = slice(image * PATCH, (image + 1) * PATCH)
            mixed = []
            for first in range(0, width, HEAD):
                probs = image_probs_of(probe[:, first : first + HEAD], keys[rows, first : first + HEAD], scale)
                values = keys[rows, width + first : width + first + HEAD]
                mixed.append(jnp.dot(probs.astype(jnp.bfloat16), values, preferred_element_type=jnp.float32))
            at = pl.ds(pl.multiple_of(slots_ref[slot] * LAT, LAT), LAT)
            placed[at, :] = (jnp.concatenate(mixed, 1) * alive).astype(jnp.bfloat16)

    def whole(shape):
        return pl.BlockSpec(shape, lambda i, slots, live: (0, 0))

    return pl.pallas_call(
        kernel,
        out_shape=(
            jax.ShapeDtypeStruct((images * PATCH, 2 * width), jnp.bfloat16),
            jax.ShapeDtypeStruct((images * LAT, width), jnp.bfloat16),
            jax.ShapeDtypeStruct((LAT, width), jnp.bfloat16),
        ),
        grid_spec=pltpu.PrefetchScalarGridSpec(
            num_scalar_prefetch=2,
            grid=(images // IMAGES_A_STEP,),
            in_specs=[
                pl.BlockSpec((step, pictures.shape[1]), lambda i, slots, live: (i, 0)),
                whole(key_part.shape),
                whole(value_part.shape),
                whole(latent_all.shape),
                whole(probe_part.shape),
            ],
            out_specs=(
                pl.BlockSpec((step, 2 * width), lambda i, slots, live: (i, 0)),
                whole((images * LAT, width)),
                whole((LAT, width)),
            ),
            scratch_shapes=[pltpu.VMEM((key_part.shape[0], 2 * width), jnp.bfloat16)],
        ),
        compiler_params=pltpu.CompilerParams(vmem_limit_bytes=VMEM_BYTES),
    )(slots, live, pictures, key_part, value_part, latent_all, probe_part)


def image_backward(d_rows, pictures, keys, probe, placed, out_part, slots, live):
    images, width = slots.shape[0], probe.shape[1]
    model_width, picture_width = d_rows.shape[1], pictures.shape[1]
    scale = HEAD ** (-0.5)
    f32, low_type = jnp.float32, jnp.bfloat16
    step = IMAGES_A_STEP * PATCH
    steps = images // IMAGES_A_STEP

    def kernel(slots_ref, live_ref, d_ref, pictures_ref, keys_ref, probe_ref, placed_ref, out_w, *rest):
        key_out, value_out, out_out, probe_out, both_sum, d_mixed, d_both = rest
        number = pl.program_id(0)

        @pl.when(number == 0)
        def _():
            probe_out[...] = jnp.zeros_like(probe_out)
            d_mixed[...] = lax.dot_general(
                d_ref[...], out_w[...], (((1,), (1,)), ((), ())), preferred_element_type=f32
            ).astype(low_type)
            out_out[...] = lax.dot_general(
                placed_ref[...], d_ref[...], (((0,), (0,)), ((), ())), preferred_element_type=f32
            ).astype(low_type)

        for image in range(IMAGES_A_STEP):
            slot = number * IMAGES_A_STEP + image
            alive = (live_ref[slot] > 0).astype(low_type)
            rows = slice(image * PATCH, (image + 1) * PATCH)
            d_here = d_mixed[pl.ds(pl.multiple_of(slots_ref[slot] * LAT, LAT), LAT), :] * alive
            d_probe = []
            for first in range(0, width, HEAD):
                at = slice(first, first + HEAD)
                keys_here = keys_ref[rows, at]
                values = keys_ref[rows, width + first : width + first + HEAD]
                probs = image_probs_of(probe_ref[:, at], keys_here, scale)
                d_probs = lax.dot_general(
                    d_here[:, at], values, (((1,), (1,)), ((), ())), preferred_element_type=f32
                )
                d_scores = probs * (d_probs - jnp.sum(probs * d_probs, -1, keepdims=True))
                d_scores = d_scores.astype(low_type)
                d_probe.append(jnp.dot(d_scores, keys_here, preferred_element_type=f32) * scale)
                d_both[rows, at] = (
                    lax.dot_general(
                        d_scores, probe_ref[:, at], (((0,), (0,)), ((), ())), preferred_element_type=f32
                    )
                    * scale
                ).astype(low_type)
                d_both[rows, width + first : width + first + HEAD] = lax.dot_general(
                    probs.astype(low_type), d_here[:, at], (((0,), (0,)), ((), ())), preferred_element_type=f32
                ).astype(low_type)
            probe_out[...] += jnp.concatenate(d_probe, 1)
        part = lax.dot_general(
            pictures_ref[...], d_both[...], (((0,), (0,)), ((), ())), preferred_element_type=f32
        )

        @pl.when(number == 0)
        def _():
            both_sum[...] = part

        @pl.when(number > 0)
        def _():
            both_sum[...] += part

        @pl.when(number == steps - 1)
        def _():
            key_out[...] = both_sum[:, :width].astype(low_type)
            value_out[...] = both_sum[:, width:].astype(low_type)

    def whole(shape):
        return pl.BlockSpec(shape, lambda i, slots, live: (0, 0))

    def stepped(columns):
        return pl.BlockSpec((step, columns), lambda i, slots, live: (i, 0))

    return pl.pallas_call(
        kernel,
        out_shape=(
            jax.ShapeDtypeStruct((picture_width, width), low_type),
            jax.ShapeDtypeStruct((picture_width, width), low_type),
            jax.ShapeDtypeStruct((width, model_width), low_type),
            jax.ShapeDtypeStruct((LAT, width), f32),
        ),
        grid_spec=pltpu.PrefetchScalarGridSpec(
            num_scalar_prefetch=2,
            grid=(steps,),
            in_specs=[
                whole(d_rows.shape),
                stepped(picture_width),
                stepped(2 * width),
                whole(probe.shape),
                whole(placed.shape),
                whole(out_part.shape),
            ],
            out_specs=(
                whole((picture_width, width)),
                whole((picture_width, width)),
                whole((width, model_width)),
                whole((LAT, width)),
            ),
            scratch_shapes=[
                pltpu.VMEM((picture_width, 2 * width), f32),
                pltpu.VMEM((d_rows.shape[0], width), low_type),
                pltpu.VMEM((step, 2 * width), low_type),
            ],
        ),
        compiler_params=pltpu.CompilerParams(vmem_limit_bytes=VMEM_BYTES),
    )(slots, live, d_rows, pictures, keys, probe, placed, out_part)


def xpos_tables(position, width):
    cosine, sine, growth = (table[:, 0, :] for table in xpos_factors(position, HEAD // 2))
    repeats = width // HEAD
    return (
        jnp.tile(cosine, (1, 2 * repeats)),
        jnp.tile(jnp.concatenate([-sine, sine], 1), (1, repeats)),
        jnp.tile(growth, (1, 2 * repeats)),
    )


def halves_swapped(rows):
    width, half = rows.shape[1], HEAD // 2
    lane = lax.broadcasted_iota(jnp.int32, rows.shape, 1)
    ahead = pltpu.roll(rows, width - half, 1)
    behind = pltpu.roll(rows, half, 1)
    return jnp.where(lane % HEAD < half, ahead, behind)


def allowed_part(segment_column, segment_row, first, count, keys):
    row = first + lax.broadcasted_iota(jnp.int32, (count, keys), 0)
    column = lax.broadcasted_iota(jnp.int32, (count, keys), 1)
    same = segment_column[pl.ds(first, count), :] == segment_row[:, :keys]
    return same & (column <= row)


ATTEND_ROWS = 256


def attend_forward(normed, query_w, key_w, value_w, tables, segment):
    rows_all, width = normed.shape[0], query_w.shape[1]
    heads = width // HEAD
    scale = HEAD ** (-0.5)
    f32, low_type = jnp.float32, jnp.bfloat16

    def kernel(normed_ref, query_ref, key_ref, value_ref, cos_ref, sin_ref, grow_ref, column_ref, row_ref, *outs):
        q_out, k_out, v_out, att_out, lse_out, stat_out = outs
        for first in range(0, rows_all, ATTEND_ROWS):
            at = slice(first, first + ATTEND_ROWS)
            rows = normed_ref[at, :]
            cosine, sine, growth = cos_ref[at, :], sin_ref[at, :], grow_ref[at, :]
            lin = jnp.dot(rows, query_ref[...], preferred_element_type=f32)
            q_out[at, :] = ((lin * cosine + halves_swapped(lin) * sine) * growth).astype(low_type)
            lin = jnp.dot(rows, key_ref[...], preferred_element_type=f32)
            k_out[at, :] = ((lin * cosine + halves_swapped(lin) * sine) * (1.0 / growth)).astype(low_type)
            v_out[at, :] = jnp.dot(rows, value_ref[...], preferred_element_type=f32).astype(low_type)
        for first in range(0, rows_all, ATTEND_ROWS):
            at, keys = slice(first, first + ATTEND_ROWS), first + ATTEND_ROWS
            allowed = allowed_part(column_ref, row_ref, first, ATTEND_ROWS, keys)
            for head in range(heads):
                lanes = slice(head * HEAD, (head + 1) * HEAD)
                scores = lax.dot_general(
                    q_out[at, lanes] * scale,
                    k_out[:keys, lanes],
                    (((1,), (1,)), ((), ())),
                    preferred_element_type=f32,
                )
                scores = jnp.where(allowed, scores, -1e30)
                best = jnp.max(scores, -1, keepdims=True)
                weights = jnp.exp(scores - best)
                total = jnp.sum(weights, -1, keepdims=True)
                probs = (weights * (1.0 / total)).astype(low_type)
                att_out[at, lanes] = jnp.dot(probs, v_out[:keys, lanes], preferred_element_type=f32)
                lse_out[at, head : head + 1] = best + jnp.log(total)
        for first in range(0, rows_all, ATTEND_ROWS):
            at = slice(first, first + ATTEND_ROWS)
            rows = att_out[at, :]
            sums = [jnp.sum(rows, 1, keepdims=True), jnp.sum(rows * rows, 1, keepdims=True)]
            stat_out[:, at] = as_lanes(sums)[:2]

    return pl.pallas_call(
        kernel,
        out_shape=(
            jax.ShapeDtypeStruct((rows_all, width), low_type),
            jax.ShapeDtypeStruct((rows_all, width), low_type),
            jax.ShapeDtypeStruct((rows_all, width), low_type),
            jax.ShapeDtypeStruct((rows_all, width), f32),
            jax.ShapeDtypeStruct((rows_all, 8), f32),
            jax.ShapeDtypeStruct((2, rows_all), f32),
        ),
        in_specs=[ON_CHIP] * 9,
        out_specs=(ON_CHIP,) * 6,
        compiler_params=pltpu.CompilerParams(vmem_limit_bytes=VMEM_BYTES),
    )(normed, query_w, key_w, value_w, *tables, segment[:, None], segment[None, :])


def as_lanes(columns):
    rows = columns[0].shape[0]
    lane = lax.broadcasted_iota(jnp.int32, (rows, LANES), 1)
    joined = jnp.zeros((rows, LANES), jnp.float32)
    for number, column in enumerate(columns):
        joined = jnp.where(lane == number, column, joined)
    return joined.T[:8, :]


def hidden_forward(lifted, up_part, bias, cotangent_all, down_part, gain):
    rows_all, width = lifted.shape[0], up_part.shape[1]
    model_width = lifted.shape[1]
    step = min(256, rows_all)
    f32 = jnp.float32

    def kernel(lifted_ref, up_ref, bias_ref, cot_ref, down_ref, gain_ref, act_out, slope_out, grad_out, stat_out):
        pre = jnp.dot(lifted_ref[...], up_ref[...], preferred_element_type=f32) + bias_ref[...]
        below = 0.5 + 0.5 * lax.erf(pre * (0.5**0.5))
        activated = pre * below
        act_out[...] = activated
        slope_out[...] = below + pre * jnp.exp(-0.5 * pre * pre) * (1.0 / (2.0 * jnp.pi) ** 0.5)
        grad = lax.dot_general(
            cot_ref[...], down_ref[...], (((1,), (1,)), ((), ())), preferred_element_type=f32
        )
        grad_out[...] = grad
        scaled = grad * gain_ref[...]
        sums = [activated, activated * activated, scaled, scaled * activated]
        stat_out[...] = as_lanes([jnp.sum(part, 1, keepdims=True) for part in sums])[:4]

    def whole(shape):
        return pl.BlockSpec(shape, lambda i: (0, 0))

    def rows(columns):
        return pl.BlockSpec((step, columns), lambda i: (i, 0))

    wide_shape = jax.ShapeDtypeStruct((rows_all, width), f32)
    return pl.pallas_call(
        kernel,
        out_shape=(wide_shape, wide_shape, wide_shape, jax.ShapeDtypeStruct((4, rows_all), f32)),
        grid=(rows_all // step,),
        in_specs=[
            rows(model_width),
            whole(up_part.shape),
            whole(bias.shape),
            rows(model_width),
            whole(down_part.shape),
            whole(gain.shape),
        ],
        out_specs=(rows(width), rows(width), rows(width), pl.BlockSpec((4, step), lambda i: (0, i))),
        compiler_params=pltpu.CompilerParams(vmem_limit_bytes=VMEM_BYTES),
    )(lifted, up_part, bias, cotangent_all, down_part, gain)


def norm_rows(rows, gain, shift):
    center = rows - jnp.mean(rows, -1, keepdims=True)
    factor = lax.rsqrt(jnp.mean(center * center, -1, keepdims=True) + EPSILON)
    normal = center * factor
    return (normal * gain + shift, normal, factor)


def dot32(left, right):
    return jnp.dot(left, right, preferred_element_type=jnp.float32)


def on_plane(
    text,
    segment,
    features,
    image_count,
    image_slot,
    cotangent,
    input_gain,
    input_shift,
    query_weight,
    key_weight,
    value_weight,
    inner_gain,
    inner_shift,
    out_weight,
    middle_gain,
    middle_shift,
    up_weight,
    up_bias,
    hidden_gain,
    hidden_shift,
    down_weight,
    latents,
    resample_query,
    resample_key,
    resample_value,
    resample_out,
):
    f32, low = jnp.float32, jnp.bfloat16
    row_count, model_width = text.shape[1], text.shape[2]
    group_rows = segment.shape[1]
    seq_rank = lax.axis_index(SEQ)
    image_slots = features.shape[1]
    image_total = image_slot.shape[1]
    half_width = query_weight.shape[1]
    own_width = half_width // PLANE
    own_heads = own_width // HEAD
    score_scale = HEAD ** (-0.5)

    rows, own = intake(
        (features[0].reshape(image_slots * PATCH, features.shape[3]),),
        (
            resample_key,
            resample_value,
            resample_query,
            latents,
            resample_out,
            query_weight,
            key_weight,
            value_weight,
            out_weight,
        ),
        (INWARD, INWARD, INWARD, SHARED, OUTWARD, INWARD, INWARD, INWARD, OUTWARD),
        1,
    )
    (pictures,) = rows
    image_key_own, image_value_own, probe_own, latent_all, image_out_own, *layer_own = own
    query_own, key_own, value_own, out_own = layer_own
    qkv_own = jnp.concatenate([query_own, key_own, value_own], 1)

    slot_range = jnp.arange(image_total, dtype=jnp.int32)
    live = slot_range % IMG_DEV < jnp.repeat(image_count[0], IMG_DEV)
    live_mark = live.astype(jnp.int32)
    block_count = group_rows // LAT
    owner = (image_slot[0][None, :] == jnp.arange(block_count, dtype=jnp.int32)[:, None]) & live[None, :]
    taken = jnp.repeat(jnp.any(owner, 1).astype(f32), LAT)[:, None]
    taken_own = lax.dynamic_slice_in_dim(taken, seq_rank * row_count, row_count, 0)
    image_keys, mixed_placed, probe = image_forward(
        pictures, image_key_own, image_value_own, latent_all, probe_own, image_slot[0], live_mark
    )

    def wide(vector):
        return vector.astype(f32)[None, :]

    def own_part(vector):
        width = vector.shape[0] // PLANE
        return lax.dynamic_slice_in_dim(vector, seq_rank * width, width, 0)

    def begin(total, piece, views, outs):
        text_view, taken_view, gain, shift = views
        embed = total.astype(jnp.bfloat16).astype(jnp.float32)
        mixed = jnp.where(taken_view[...] > 0.5, embed, text_view[...].astype(jnp.float32))
        outs[0][...] = mixed
        return norm_rows(mixed, gain[...], shift[...])[0].astype(jnp.bfloat16)

    rows_wide = jax.ShapeDtypeStruct((row_count, model_width), f32)
    (mixed_in, normed), hidden_blocks = exchange(
        None,
        [
            Stream(
                group_rows,
                mixed_placed,
                image_out_own,
                False,
                (text[0], taken_own, wide(input_gain), wide(input_shift)),
                (ROWS, ROWS, ALL, ALL),
                ((rows_wide, ROWS),),
                begin,
                True,
            )
        ],
        [PlaneWeights((up_weight, down_weight), (INWARD, OUTWARD))],
        3,
    )

    segment_all = segment[0]
    row_index = jnp.arange(group_rows, dtype=jnp.int32)
    earlier = (row_index[None, :] < row_index[:, None]) & (segment_all[None, :] == segment_all[:, None])
    tables = xpos_tables(jnp.sum(earlier.astype(f32), 1), own_width)
    cot_late, _ = lax.optimization_barrier((cotangent[0], normed))
    cot_all = lax.all_gather(cot_late, SEQ, axis=0, tiled=True)
    query_rot, keys_rot, values, attended, log_total, inner_sums = attend_forward(
        normed, query_own, key_own, value_own, tables, segment_all
    )

    inner_gain_own = wide(own_part(inner_gain))
    def middle_step(total, piece, views, outs):
        mixed_view, gain, shift = views
        middle = mixed_view[...] + total
        outs[0][...] = middle
        return norm_rows(middle, gain[...], shift[...])[0].astype(jnp.bfloat16)

    (inner_low, inner_hat, inner_factor), (middle, lifted), hidden_own = exchange(
        InnerFront(attended, inner_sums, inner_gain_own, wide(own_part(inner_shift)), model_width),
        [
            Stream(
                group_rows,
                None,
                out_own,
                False,
                (mixed_in, wide(middle_gain), wide(middle_shift)),
                (ROWS, ALL, ALL),
                ((rows_wide, ROWS),),
                middle_step,
                True,
            )
        ],
        [CrossWeights(hidden_blocks, (INWARD, OUTWARD))],
        5,
    )
    up_own, down_own = hidden_own[0].reshape(model_width, -1), hidden_own[1]
    own_hidden = up_own.shape[1]

    hidden_gain_own = wide(own_part(hidden_gain))
    activated, slope, d_settled, hidden_sums = hidden_forward(
        lifted, up_own, wide(own_part(up_bias)), cot_all, down_own, hidden_gain_own
    )
    def blocks_in(grad):
        return grad.reshape(PLANE, 2, -1, grad.shape[1])

    def last_step(total, piece, views, outs):
        outs[0][...] = (views[0][...] + total).astype(jnp.bfloat16)

    vector_out = jax.ShapeDtypeStruct((1, model_width), f32)

    def norm_back_step(total, piece, views, outs):
        rows_view, carried_view, gain = views
        rows_in = rows_view[...]
        center = rows_in - jnp.mean(rows_in, -1, keepdims=True)
        factor = lax.rsqrt(jnp.mean(center * center, -1, keepdims=True) + EPSILON)
        normal = center * factor
        grad = carried_view[...].astype(jnp.float32) + full_back(total, normal, factor, gain[...])
        outs[0][...] = grad
        if piece == 0:
            outs[1][...] = jnp.zeros_like(outs[1])
            outs[2][...] = jnp.zeros_like(outs[2])
        outs[1][...] += jnp.sum(total * normal, 0, keepdims=True)
        outs[2][...] += jnp.sum(total, 0, keepdims=True)
        return grad.astype(jnp.bfloat16)

    hidden_made, (d_middle, middle_gain_grad, middle_shift_grad, d_branch) = exchange(
        HiddenFront(
            activated,
            slope,
            d_settled,
            hidden_sums,
            hidden_gain_own,
            wide(own_part(hidden_shift)),
            lifted,
            cot_all,
            FF,
        ),
        [
            Stream(
                group_rows,
                None,
                up_own,
                True,
                (middle, cotangent[0], wide(middle_gain)),
                (ROWS, ROWS, ALL),
                ((rows_wide, ROWS), (vector_out, ALL), (vector_out, ALL)),
                norm_back_step,
                True,
            )
        ],
        [],
        8,
    )

    settled, _, hidden_vectors, *hidden_pairs = hidden_made
    attend_made, (d_mixed, input_gain_grad, input_shift_grad, d_rows), (result,) = exchange(
        AttendFront(
            d_branch,
            out_own,
            inner_hat,
            inner_factor,
            inner_gain_own,
            (attended, query_rot, keys_rot, values, log_total),
            tables,
            segment_all,
            normed,
            inner_low,
            model_width,
        ),
        [
            Stream(
                group_rows,
                None,
                qkv_own,
                True,
                (mixed_in, d_middle, wide(input_gain)),
                (ROWS, ROWS, ALL),
                ((rows_wide, ROWS), (vector_out, ALL), (vector_out, ALL)),
                norm_back_step,
                True,
            ),
            Stream(
                group_rows,
                settled,
                down_own,
                False,
                (middle,),
                (ROWS,),
                ((jax.ShapeDtypeStruct((row_count, model_width), low), ROWS),),
                last_step,
                False,
            ),
        ],
        [],
        10,
    )
    inner_vectors, *layer_pairs = attend_made
    text_grad = jnp.where(taken_own > 0.5, 0.0, d_mixed)

    image_key_grad, image_value_grad, image_out_grad, d_probe = image_backward(
        d_rows, pictures, image_keys, probe, mixed_placed, image_out_own, image_slot[0], live_mark
    )

    own_vectors = jnp.concatenate(
        [inner_vectors[0], inner_vectors[1], hidden_vectors[2], hidden_vectors[0], hidden_vectors[1]]
    )
    row_vectors = jnp.concatenate(
        [input_gain_grad[0], input_shift_grad[0], middle_gain_grad[0], middle_shift_grad[0]]
    )
    packed = jnp.concatenate([row_vectors, own_vectors]).reshape(-1, LANES)
    spare = -packed.shape[0] % 8
    packed = jnp.concatenate([d_probe, jnp.pad(packed, ((0, spare), (0, 0)))], 0)
    image_grads = (blocks_in(image_key_grad), blocks_in(image_value_grad), image_out_grad)
    owned, (spread, resample_query_grad, latent_grad) = finale(
        list(zip(hidden_pairs[:2] + layer_pairs[:4], hidden_pairs[2:] + layer_pairs[4:])),
        image_grads,
        (INWARD, OUTWARD, INWARD, INWARD, INWARD, OUTWARD),
        (INWARD, INWARD, OUTWARD),
        packed,
        latents.astype(f32).T,
        resample_query.astype(f32),
        12,
    )
    up_sum, down_sum, query_sum, key_sum, value_sum, out_sum, image_key_sum, image_value_sum, image_out_sum = widened(owned)
    spread = spread.reshape(PLANE, -1)
    first = LAT * own_width
    row_sums = spread[:, first : first + row_vectors.shape[0]].sum(0).reshape(4, model_width)
    own_sums = spread[:, first + row_vectors.shape[0] :]

    def joined(start, width):
        return own_sums[:, start : start + width].reshape(-1)

    inner_gain_sum = joined(0, own_width)
    inner_shift_sum = joined(own_width, own_width)
    up_bias_sum = joined(2 * own_width, own_hidden)
    hidden_gain_sum = joined(2 * own_width + own_hidden, own_hidden)
    hidden_shift_sum = joined(2 * own_width + 2 * own_hidden, own_hidden)

    return (
        result[None],
        text_grad[None],
        row_sums[0],
        row_sums[1],
        query_sum,
        key_sum,
        value_sum,
        inner_gain_sum,
        inner_shift_sum,
        out_sum,
        row_sums[2],
        row_sums[3],
        up_sum,
        up_bias_sum,
        hidden_gain_sum,
        hidden_shift_sum,
        down_sum,
        latent_grad,
        resample_query_grad,
        image_key_sum,
        image_value_sum,
        image_out_sum,
    )


def solution(mesh):
    placed = (
        P(IMG, SEQ, None),
        P(IMG, None),
        P(IMG, SEQ, None, None),
        P(IMG, None),
        P(IMG, None),
        P(IMG, SEQ, None),
        P(),
        P(),
        P((SEQ, IMG), TP),
        P((SEQ, IMG), TP),
        P((SEQ, IMG), TP),
        P(TP),
        P(TP),
        P(TP, (SEQ, IMG)),
        P(),
        P(),
        P((SEQ, IMG), TP),
        P(TP),
        P(TP),
        P(TP),
        P(TP, (SEQ, IMG)),
        P(None, (SEQ, IMG)),
        P((SEQ, IMG), TP),
        P((SEQ, IMG), TP),
        P((SEQ, IMG), TP),
        P(TP, (SEQ, IMG)),
    )
    return jax.shard_map(
        on_device if narrow_heads(mesh) else on_plane,
        mesh=mesh,
        in_specs=placed,
        out_specs=(
            P(IMG, SEQ, None),
            P(IMG, SEQ, None),
            P(),
            P(),
            P((SEQ, IMG), TP),
            P((SEQ, IMG), TP),
            P((SEQ, IMG), TP),
            P(TP),
            P(TP),
            P(TP, (SEQ, IMG)),
            P(),
            P(),
            P((SEQ, IMG), TP),
            P(TP),
            P(TP),
            P(TP),
            P(TP, (SEQ, IMG)),
            P(None, (SEQ, IMG)),
            P((SEQ, IMG), TP),
            P((SEQ, IMG), TP),
            P((SEQ, IMG), TP),
            P(TP, (SEQ, IMG)),
        ),
        check_vma=False,
    )
```

```python
import functools

import jax
import jax.numpy as jnp
from jax import lax
from jax.experimental import pallas as pl
from jax.experimental.pallas import tpu as pltpu
from jax.sharding import PartitionSpec as P

SEQ, TP, IMG = "seq", "tp", "img"
HEAD = 64
FF = 8192
PATCH = 256
LAT = 64
SEQ_MAX = 2048
IMG_DEV = 2


EPSILON = 1e-05
HIGHEST_PRECISION = lax.Precision.HIGHEST


def shortened(x):

    def short(part):
        return part.astype(jnp.bfloat16) if part.dtype == jnp.float32 else part

    return jax.tree.map(short, x)


def xpos_factors(position, half_size):
    ladder = jnp.arange(half_size, dtype=jnp.float32)
    frequency = jnp.exp(ladder * (-2.0 * jnp.log(10000.0) / (2.0 * half_size)))
    decay_base = (ladder / half_size + 0.4) / 1.4
    angles = position[:, None] * frequency[None, :]
    growth = jnp.exp(position[:, None] / 512.0 * jnp.log(decay_base)[None, :])
    return (jnp.cos(angles)[:, None, :], jnp.sin(angles)[:, None, :], growth[:, None, :])


def rotate(inputs, cosine, sine_table, factor):
    half_size = inputs.shape[-1] // 2
    first_half = inputs[..., :half_size]
    second_half = inputs[..., half_size:]
    turned = jnp.concatenate(
        [
            first_half * cosine - second_half * sine_table,
            first_half * sine_table + second_half * cosine,
        ],
        -1,
    )
    return turned * jnp.concatenate([factor, factor], -1)


def rotate_back(gradient, cosine, sine_table, factor):
    half_size = gradient.shape[-1] // 2
    scaled = gradient * jnp.concatenate([factor, factor], -1)
    first_half = scaled[..., :half_size]
    second_half = scaled[..., half_size:]
    return jnp.concatenate(
        [
            first_half * cosine + second_half * sine_table,
            second_half * cosine - first_half * sine_table,
        ],
        -1,
    )


def tp_total(inputs):
    return jax.tree.map(lambda part: part.astype(jnp.float32), lax.psum(shortened(inputs), TP))


def full_norm(inputs, norm_gain, norm_shift):
    center = inputs - jnp.mean(inputs, -1, keepdims=True)
    spread = jnp.mean(center * center, -1, keepdims=True)
    factor = lax.rsqrt(spread + EPSILON)
    normal = center * factor
    return (normal * norm_gain + norm_shift, normal, factor)


def full_back(gradient, normal, factor, norm_gain):
    scaled = gradient * norm_gain
    return factor * (
        scaled
        - jnp.mean(scaled, -1, keepdims=True)
        - normal * jnp.mean(scaled * normal, -1, keepdims=True)
    )


def split_norm(inputs, norm_gain, norm_shift, full_width):
    totals = tp_total(
        (jnp.sum(inputs, -1, keepdims=True), jnp.sum(inputs * inputs, -1, keepdims=True))
    )
    average = totals[0] / full_width
    spread = totals[1] / full_width - average * average
    factor = lax.rsqrt(spread + EPSILON)
    normal = (inputs - average) * factor
    return (normal * norm_gain + norm_shift, normal, factor)


def split_back(gradient, normal, factor, norm_gain, full_width):
    scaled = gradient * norm_gain
    totals = tp_total(
        (jnp.sum(scaled, -1, keepdims=True), jnp.sum(scaled * normal, -1, keepdims=True))
    )
    return factor * (scaled - totals[0] / full_width - normal * (totals[1] / full_width))


def attend_piece(
    running, query_rot, key_piece, value_piece, row_index, row_segment, segment_all, score_scale
):
    heads_local = query_rot.shape[1]
    amount = key_piece.shape[0]
    block_size = 1024

    def step(state_in, number):
        first_row = number * block_size
        key_block = lax.dynamic_slice_in_dim(key_piece, first_row, block_size, 0).reshape(
            block_size, heads_local, -1
        )
        value_block = lax.dynamic_slice_in_dim(value_piece, first_row, block_size, 0).reshape(
            block_size, heads_local, -1
        )
        key_index = first_row + jnp.arange(block_size, dtype=jnp.int32)
        key_segment = lax.dynamic_slice_in_dim(segment_all, first_row, block_size, 0)
        scores = (
            jnp.einsum("qhd,khd->hqk", query_rot, key_block, preferred_element_type=jnp.float32)
            * score_scale
        )
        allowed = (key_index[None, :] <= row_index[:, None]) & (
            key_segment[None, :] == row_segment[:, None]
        )
        scores = jnp.where(allowed[None], scores, -1e30)
        best_old, total_old, accum_old = state_in
        best_new = jnp.maximum(best_old, jnp.max(scores, -1))
        weights = jnp.where(allowed[None], jnp.exp(scores - best_new[..., None]), 0.0)
        shrink = jnp.exp(best_old - best_new)
        total_new = total_old * shrink + jnp.sum(weights, -1)
        added = jnp.einsum(
            "hqk,khd->qhd",
            weights.astype(jnp.bfloat16),
            value_block,
            preferred_element_type=jnp.float32,
        )
        accum_new = accum_old * shrink.T[:, :, None] + added
        return ((best_new, total_new, accum_new), None)

    return lax.scan(step, running, jnp.arange(amount // block_size, dtype=jnp.int32))[0]


def attend_back(
    query_rot,
    key_all,
    value_all,
    grad_attended,
    log_total,
    delta,
    row_index,
    row_segment,
    segment_all,
    score_scale,
):
    heads_local = query_rot.shape[1]
    amount = key_all.shape[0]
    block_size = 1024

    def step(dquery, number):
        first_row = number * block_size
        key_block = lax.dynamic_slice_in_dim(key_all, first_row, block_size, 0).reshape(
            block_size, heads_local, -1
        )
        value_block = lax.dynamic_slice_in_dim(value_all, first_row, block_size, 0).reshape(
            block_size, heads_local, -1
        )
        key_index = first_row + jnp.arange(block_size, dtype=jnp.int32)
        key_segment = lax.dynamic_slice_in_dim(segment_all, first_row, block_size, 0)
        scores = (
            jnp.einsum("qhd,khd->hqk", query_rot, key_block, preferred_element_type=jnp.float32)
            * score_scale
        )
        allowed = (key_index[None, :] <= row_index[:, None]) & (
            key_segment[None, :] == row_segment[:, None]
        )
        weights = jnp.where(
            allowed[None],
            jnp.exp(jnp.where(allowed[None], scores, -1e30) - log_total[..., None]),
            0.0,
        )
        dweights = jnp.einsum(
            "qhd,khd->hqk", grad_attended, value_block, preferred_element_type=jnp.float32
        )
        dscores = (weights * (dweights - delta[..., None])).astype(jnp.bfloat16)
        dquery = (
            dquery
            + jnp.einsum("hqk,khd->qhd", dscores, key_block, preferred_element_type=jnp.float32)
            * score_scale
        )
        dkeys = (
            jnp.einsum("hqk,qhd->khd", dscores, query_rot, preferred_element_type=jnp.float32)
            * score_scale
        )
        dvalues = jnp.einsum(
            "hqk,qhd->khd",
            weights.astype(jnp.bfloat16),
            grad_attended,
            preferred_element_type=jnp.float32,
        )
        return (dquery, (dkeys, dvalues))

    start_grad = jnp.zeros(query_rot.shape, jnp.float32)
    dquery, outputs = lax.scan(step, start_grad, jnp.arange(amount // block_size, dtype=jnp.int32))
    return (dquery, outputs[0].reshape(amount, -1), outputs[1].reshape(amount, -1))


def on_device(
    text,
    segment,
    features,
    image_count,
    image_slot,
    cotangent,
    input_gain,
    input_shift,
    query_weight,
    key_weight,
    value_weight,
    inner_gain,
    inner_shift,
    out_weight,
    middle_gain,
    middle_shift,
    up_weight,
    up_bias,
    hidden_gain,
    hidden_shift,
    down_weight,
    latents,
    resample_query,
    resample_key,
    resample_value,
    resample_out,
):
    row_count = text.shape[1]
    model_width = text.shape[2]
    group_rows = segment.shape[1]
    seq_rank = lax.axis_index(SEQ)
    gathered_in = (
        lax.all_gather(query_weight, (SEQ, IMG), axis=0, tiled=True),
        lax.all_gather(key_weight, (SEQ, IMG), axis=0, tiled=True),
        lax.all_gather(value_weight, (SEQ, IMG), axis=0, tiled=True),
        lax.all_gather(up_weight, (SEQ, IMG), axis=0, tiled=True),
        lax.all_gather(resample_query, (SEQ, IMG), axis=0, tiled=True),
        lax.all_gather(resample_key, (SEQ, IMG), axis=0, tiled=True),
        lax.all_gather(resample_value, (SEQ, IMG), axis=0, tiled=True),
    )
    query_full, key_full, value_full, up_full, probe_full, image_key_full, image_value_full = (
        gathered_in
    )
    gathered_out = (
        lax.all_gather(out_weight, (SEQ, IMG), axis=1, tiled=True),
        lax.all_gather(down_weight, (SEQ, IMG), axis=1, tiled=True),
        lax.all_gather(resample_out, (SEQ, IMG), axis=1, tiled=True),
        lax.all_gather(latents, (SEQ, IMG), axis=1, tiled=True),
    )
    out_full, down_full, image_out_full, latent_full = gathered_out
    half_width = query_full.shape[1]
    heads_local = half_width // HEAD
    score_scale = HEAD ** (-0.5)
    gelu_exact = functools.partial(jax.nn.gelu, approximate=False)
    image_slots = features.shape[1]
    pictures = features[0].reshape(image_slots * PATCH, features.shape[3])
    probe = (
        jnp.dot(latent_full, probe_full, preferred_element_type=jnp.float32)
        .astype(jnp.bfloat16)
        .reshape(LAT, heads_local, HEAD)
    )
    image_keys = (
        jnp.dot(pictures, image_key_full, preferred_element_type=jnp.float32)
        .astype(jnp.bfloat16)
        .reshape(image_slots, PATCH, heads_local, HEAD)
    )
    image_values = (
        jnp.dot(pictures, image_value_full, preferred_element_type=jnp.float32)
        .astype(jnp.bfloat16)
        .reshape(image_slots, PATCH, heads_local, HEAD)
    )
    image_scores = (
        jnp.einsum("qhd,iphd->ihqp", probe, image_keys, preferred_element_type=jnp.float32)
        * score_scale
    )
    image_probs = jax.nn.softmax(image_scores, -1)
    image_mixed = jnp.einsum(
        "ihqp,iphd->iqhd",
        image_probs.astype(jnp.bfloat16),
        image_values,
        preferred_element_type=jnp.float32,
    )
    image_mixed = image_mixed.astype(jnp.bfloat16).reshape(image_slots * LAT, half_width)
    embed = tp_total(jnp.dot(image_mixed, image_out_full, preferred_element_type=jnp.float32))
    embed = embed.astype(jnp.bfloat16).reshape(image_slots, LAT, model_width)
    image_total = image_slot.shape[1]
    slot_range = jnp.arange(image_total, dtype=jnp.int32)
    live = slot_range % IMG_DEV < jnp.repeat(image_count[0], IMG_DEV)
    block_local = row_count // LAT
    block_count = group_rows // LAT
    block_ids = seq_rank * block_local + jnp.arange(block_local, dtype=jnp.int32)
    owner = ((image_slot[0][None, :] == block_ids[:, None]) & live[None, :]).astype(jnp.float32)
    owner_low = owner.astype(jnp.bfloat16)
    taken = jnp.sum(owner, 1) > 0.5
    chosen = owner_low
    placed = jnp.einsum(
        "bi,ild->bld",
        chosen,
        lax.all_gather(embed, SEQ, axis=0, tiled=True),
        preferred_element_type=jnp.float32,
    )
    text_blocks = text[0].astype(jnp.float32).reshape(block_local, LAT, model_width)
    mixed_in = jnp.where(taken[:, None, None], placed, text_blocks).reshape(row_count, model_width)
    segment_all = segment[0]
    docs_count = 3 * (group_rows // min(SEQ_MAX, group_rows))
    marks = (segment_all[:, None] == jnp.arange(docs_count, dtype=jnp.int32)[None, :]).astype(
        jnp.int32
    )
    earlier_rows = jnp.cumsum(marks, 0) - marks
    position_all = jnp.sum(earlier_rows * marks, 1)
    first_local = seq_rank * row_count
    row_index = first_local + jnp.arange(row_count, dtype=jnp.int32)
    row_segment = lax.dynamic_slice_in_dim(segment_all, first_local, row_count, 0)
    position = lax.dynamic_slice_in_dim(position_all, first_local, row_count, 0).astype(jnp.float32)
    cosine, sine_table, growth = xpos_factors(position, HEAD // 2)
    input_out, input_hat, input_factor = full_norm(
        mixed_in, input_gain.astype(jnp.float32), input_shift.astype(jnp.float32)
    )
    normed = input_out.astype(jnp.bfloat16)
    query_lin = jnp.dot(normed, query_full, preferred_element_type=jnp.float32).reshape(
        row_count, heads_local, HEAD
    )
    key_lin = jnp.dot(normed, key_full, preferred_element_type=jnp.float32).reshape(
        row_count, heads_local, HEAD
    )
    value_lin = jnp.dot(normed, value_full, preferred_element_type=jnp.float32)
    query_rot = rotate(query_lin, cosine, sine_table, growth).astype(jnp.bfloat16)
    keys_rot = (
        rotate(key_lin, cosine, sine_table, 1.0 / growth)
        .astype(jnp.bfloat16)
        .reshape(row_count, half_width)
    )
    values_low = value_lin.astype(jnp.bfloat16)
    start_state = (
        jnp.full((heads_local, row_count), -1e30, jnp.float32),
        jnp.zeros((heads_local, row_count), jnp.float32),
        jnp.zeros((row_count, heads_local, HEAD), jnp.float32),
    )
    best, weight_total, accum = attend_piece(
        start_state,
        query_rot,
        lax.all_gather(keys_rot, SEQ, axis=0, tiled=True),
        lax.all_gather(values_low, SEQ, axis=0, tiled=True),
        row_index,
        row_segment,
        segment_all,
        score_scale,
    )
    attended = accum / weight_total.T[:, :, None]
    log_total = best + jnp.log(weight_total)
    inner_out, inner_hat, inner_factor = split_norm(
        attended.reshape(row_count, half_width),
        inner_gain.astype(jnp.float32),
        inner_shift.astype(jnp.float32),
        model_width,
    )
    inner_low = inner_out.astype(jnp.bfloat16)
    middle = mixed_in + tp_total(jnp.dot(inner_low, out_full, preferred_element_type=jnp.float32))
    lifted_out, lifted_hat, lifted_factor = full_norm(
        middle, middle_gain.astype(jnp.float32), middle_shift.astype(jnp.float32)
    )
    lifted = lifted_out.astype(jnp.bfloat16)
    hidden_pre = jnp.dot(lifted, up_full, preferred_element_type=jnp.float32) + up_bias.astype(
        jnp.float32
    )
    activated, gelu_pull = jax.vjp(gelu_exact, hidden_pre)
    settled_out, settled_hat, settled_factor = split_norm(
        activated, hidden_gain.astype(jnp.float32), hidden_shift.astype(jnp.float32), FF
    )
    settled = settled_out.astype(jnp.bfloat16)
    final_rows = middle + tp_total(jnp.dot(settled, down_full, preferred_element_type=jnp.float32))
    result = final_rows.astype(jnp.bfloat16).reshape(1, row_count, model_width)
    grad_low = cotangent[0]
    grad_rows = grad_low.astype(jnp.float32)
    down_grad = jnp.dot(settled.T, grad_low, preferred_element_type=jnp.float32)
    d_settled = jnp.dot(grad_low, down_full.T, preferred_element_type=jnp.float32)
    hidden_gain_grad = jnp.sum(d_settled * settled_hat, 0)
    hidden_shift_grad = jnp.sum(d_settled, 0)
    d_activated = split_back(
        d_settled, settled_hat, settled_factor, hidden_gain.astype(jnp.float32), FF
    )
    d_hidden = gelu_pull(d_activated)[0].astype(jnp.bfloat16)
    up_bias_grad = jnp.sum(d_hidden.astype(jnp.float32), 0)
    up_grad = jnp.dot(lifted.T, d_hidden, preferred_element_type=jnp.float32)
    d_lifted = tp_total(jnp.dot(d_hidden, up_full.T, preferred_element_type=jnp.float32))
    middle_gain_grad = jnp.sum(d_lifted * lifted_hat, 0)
    middle_shift_grad = jnp.sum(d_lifted, 0)
    d_middle = grad_rows + full_back(
        d_lifted, lifted_hat, lifted_factor, middle_gain.astype(jnp.float32)
    )
    d_branch = d_middle.astype(jnp.bfloat16)
    out_grad = jnp.dot(inner_low.T, d_branch, preferred_element_type=jnp.float32)
    d_inner = jnp.dot(d_branch, out_full.T, preferred_element_type=jnp.float32)
    inner_gain_grad = jnp.sum(d_inner * inner_hat, 0)
    inner_shift_grad = jnp.sum(d_inner, 0)
    d_attended = split_back(
        d_inner, inner_hat, inner_factor, inner_gain.astype(jnp.float32), model_width
    )
    d_attended = d_attended.astype(jnp.bfloat16).reshape(row_count, heads_local, HEAD)
    delta = jnp.sum(d_attended.astype(jnp.float32) * attended, -1).T
    key_back, value_back = (
        lax.all_gather(keys_rot, SEQ, axis=0, tiled=True),
        lax.all_gather(values_low, SEQ, axis=0, tiled=True),
    )
    d_query_rot, d_key_term, d_value_term = attend_back(
        query_rot,
        key_back,
        value_back,
        d_attended,
        log_total,
        delta,
        row_index,
        row_segment,
        segment_all,
        score_scale,
    )
    d_key_sum, d_value_sum = (
        lax.psum_scatter(
            d_key_term.astype(jnp.bfloat16), SEQ, scatter_dimension=0, tiled=True
        ).astype(jnp.float32),
        lax.psum_scatter(
            d_value_term.astype(jnp.bfloat16), SEQ, scatter_dimension=0, tiled=True
        ).astype(jnp.float32),
    )
    d_query_lin = (
        rotate_back(d_query_rot, cosine, sine_table, growth)
        .astype(jnp.bfloat16)
        .reshape(row_count, half_width)
    )
    d_key_lin = (
        rotate_back(
            d_key_sum.reshape(row_count, heads_local, HEAD), cosine, sine_table, 1.0 / growth
        )
        .astype(jnp.bfloat16)
        .reshape(row_count, half_width)
    )
    d_value_lin = d_value_sum.astype(jnp.bfloat16)
    query_grad = jnp.dot(normed.T, d_query_lin, preferred_element_type=jnp.float32)
    key_grad = jnp.dot(normed.T, d_key_lin, preferred_element_type=jnp.float32)
    value_grad = jnp.dot(normed.T, d_value_lin, preferred_element_type=jnp.float32)
    d_normed_part = (
        jnp.dot(d_query_lin, query_full.T, preferred_element_type=jnp.float32)
        + jnp.dot(d_key_lin, key_full.T, preferred_element_type=jnp.float32)
        + jnp.dot(d_value_lin, value_full.T, preferred_element_type=jnp.float32)
    )
    d_normed = tp_total(d_normed_part)
    input_gain_grad = jnp.sum(d_normed * input_hat, 0)
    input_shift_grad = jnp.sum(d_normed, 0)
    d_mixed = d_middle + full_back(
        d_normed, input_hat, input_factor, input_gain.astype(jnp.float32)
    )
    d_blocks = d_mixed.reshape(block_local, LAT, model_width)
    text_grad = jnp.where(taken[:, None, None], 0.0, d_blocks).reshape(1, row_count, model_width)
    my_target = lax.dynamic_slice_in_dim(image_slot[0], seq_rank * image_slots, image_slots, 0)
    my_live = lax.dynamic_slice_in_dim(live, seq_rank * image_slots, image_slots, 0)
    owner_mine = (
        (jnp.arange(block_count, dtype=jnp.int32)[:, None] == my_target[None, :]) & my_live[None, :]
    ).astype(jnp.bfloat16)
    chosen = owner_mine
    d_embed = jnp.einsum(
        "bi,bld->ild",
        chosen,
        lax.all_gather(d_blocks.astype(jnp.bfloat16), SEQ, axis=0, tiled=True),
        preferred_element_type=jnp.float32,
    )
    d_embed_low = d_embed.astype(jnp.bfloat16).reshape(image_slots * LAT, model_width)
    resample_out_grad = jnp.dot(image_mixed.T, d_embed_low, preferred_element_type=jnp.float32)
    d_image_mixed = jnp.dot(d_embed_low, image_out_full.T, preferred_element_type=jnp.float32)
    d_image_mixed = d_image_mixed.astype(jnp.bfloat16).reshape(image_slots, LAT, heads_local, HEAD)
    d_image_probs = jnp.einsum(
        "iqhd,iphd->ihqp", d_image_mixed, image_values, preferred_element_type=jnp.float32
    )
    d_image_scores = image_probs * (
        d_image_probs - jnp.sum(image_probs * d_image_probs, -1, keepdims=True)
    )
    d_image_scores = d_image_scores.astype(jnp.bfloat16)
    d_probe = (
        jnp.einsum("ihqp,iphd->qhd", d_image_scores, image_keys, preferred_element_type=jnp.float32)
        * score_scale
    )
    d_image_keys = (
        jnp.einsum("ihqp,qhd->iphd", d_image_scores, probe, preferred_element_type=jnp.float32)
        * score_scale
    ).astype(jnp.bfloat16)
    d_image_values = jnp.einsum(
        "ihqp,iqhd->iphd",
        image_probs.astype(jnp.bfloat16),
        d_image_mixed,
        preferred_element_type=jnp.float32,
    ).astype(jnp.bfloat16)
    resample_key_grad = jnp.dot(
        pictures.T,
        d_image_keys.reshape(image_slots * PATCH, half_width),
        preferred_element_type=jnp.float32,
    )
    resample_value_grad = jnp.dot(
        pictures.T,
        d_image_values.reshape(image_slots * PATCH, half_width),
        preferred_element_type=jnp.float32,
    )
    d_probe_flat = d_probe.reshape(LAT, half_width)
    resample_query_grad = jnp.dot(
        latent_full.astype(jnp.float32).T, d_probe_flat, precision=HIGHEST_PRECISION
    )
    latent_grad = tp_total(
        jnp.dot(d_probe_flat, probe_full.astype(jnp.float32).T, precision=HIGHEST_PRECISION)
    )
    summed_in = (
        lax.psum_scatter(query_grad, (SEQ, IMG), scatter_dimension=0, tiled=True),
        lax.psum_scatter(key_grad, (SEQ, IMG), scatter_dimension=0, tiled=True),
        lax.psum_scatter(value_grad, (SEQ, IMG), scatter_dimension=0, tiled=True),
        lax.psum_scatter(up_grad, (SEQ, IMG), scatter_dimension=0, tiled=True),
        lax.psum_scatter(resample_query_grad, (SEQ, IMG), scatter_dimension=0, tiled=True),
        lax.psum_scatter(resample_key_grad, (SEQ, IMG), scatter_dimension=0, tiled=True),
        lax.psum_scatter(resample_value_grad, (SEQ, IMG), scatter_dimension=0, tiled=True),
    )
    summed_out = (
        lax.psum_scatter(out_grad, (SEQ, IMG), scatter_dimension=1, tiled=True),
        lax.psum_scatter(down_grad, (SEQ, IMG), scatter_dimension=1, tiled=True),
        lax.psum_scatter(resample_out_grad, (SEQ, IMG), scatter_dimension=1, tiled=True),
        lax.psum_scatter(latent_grad, (SEQ, IMG), scatter_dimension=1, tiled=True),
    )
    summed_small = lax.psum(
        (
            input_gain_grad,
            input_shift_grad,
            inner_gain_grad,
            inner_shift_grad,
            middle_gain_grad,
            middle_shift_grad,
            up_bias_grad,
            hidden_gain_grad,
            hidden_shift_grad,
        ),
        (SEQ, IMG),
    )
    return (
        result,
        text_grad,
        summed_small[0],
        summed_small[1],
        summed_in[0],
        summed_in[1],
        summed_in[2],
        summed_small[2],
        summed_small[3],
        summed_out[0],
        summed_small[4],
        summed_small[5],
        summed_in[3],
        summed_small[6],
        summed_small[7],
        summed_small[8],
        summed_out[1],
        summed_out[3],
        summed_in[4],
        summed_in[5],
        summed_in[6],
        summed_out[2],
    )


MESH_IDS = pl.DeviceIdType.MESH
ANYWHERE = pl.BlockSpec(memory_space=pl.ANY)
ON_CHIP = pl.BlockSpec(memory_space=pltpu.VMEM)
IN_SMEM = pl.BlockSpec(memory_space=pltpu.SMEM)
LANES = 128
PLANE = 8
VMEM_BYTES = 60 * 1024 * 1024
PIECE_ROWS = (32, 32, 32, 32)
PIECES = len(PIECE_ROWS)
FRONT, BACK, ALL, ROWS, INWARD, OUTWARD, SHARED = range(7)


def narrow_heads(mesh):
    return mesh.shape[SEQ] != PLANE or mesh.shape[IMG] != 2 or mesh.shape[TP] != 2


def flipped(number, bit):
    step = 2**bit
    return number + step - 2 * step * ((number // step) % 2)


class Places:
    def __init__(self):
        self.seq, self.tp, self.img = (lax.axis_index(name) for name in (SEQ, TP, IMG))
        self.s_core, self.s_x, self.s_y = (flipped(self.seq, bit) for bit in range(3))
        self.s_xy = flipped(self.s_x, 2)
        self.core, self.x, self.y = (self.at(seq) for seq in (self.s_core, self.s_x, self.s_y))
        self.tp_peer = (self.seq, 1 - self.tp, self.img)
        self.img_peer = (self.seq, self.tp, 1 - self.img)

    def at(self, seq):
        return (seq, self.tp, self.img)


def greet(peers):
    barrier = pltpu.get_barrier_semaphore()
    for peer in peers:
        pl.semaphore_signal(barrier, inc=1, device_id=peer, device_id_type=MESH_IDS)
    pl.semaphore_wait(barrier, len(peers))


def remote(src, dst, send, recv, peer):
    return pltpu.make_async_remote_copy(
        src_ref=src, dst_ref=dst, send_sem=send, recv_sem=recv, device_id=peer, device_id_type=MESH_IDS
    )


def rows_at(ref, first, count):
    return ref.at[pl.ds(pl.multiple_of(first, 16), count)]


class Spread:
    def __init__(self, here, out, block, first, count, send, recv):
        self.here, self.out, self.block = here, out, block
        self.first, self.count, self.send, self.recv = first, count, send, recv
        self.half = out.shape[1] // 2
        self.sent = []

    def cut(self, ref, first, which):
        rows = pl.ds(first, self.count)
        if which == ALL:
            return ref.at[rows]
        return ref.at[rows, pl.ds(self.half if which == BACK else 0, self.half)]

    def part(self, seq, which):
        return self.cut(self.out, pl.multiple_of(seq * self.block + self.first, 16), which)

    def copy(self, src, dst, slot, peer):
        return remote(src, dst, self.send.at[slot], self.recv.at[slot], peer)

    def go(self, src, dst, slot, peer):
        made = self.copy(src, dst, slot, peer)
        made.start()
        self.sent.append(made)

    def own(self, src, src_first):
        here, seq = self.here, self.here.seq

        def own_part(which):
            return self.cut(src, src_first, which)

        self.go(own_part(FRONT), self.part(seq, FRONT), 0, here.x)
        self.go(own_part(BACK), self.part(seq, BACK), 1, here.y)
        self.go(own_part(BACK), self.part(seq, BACK), 2, here.x)
        self.go(own_part(FRONT), self.part(seq, FRONT), 3, here.y)
        self.go(own_part(ALL), self.part(seq, ALL), 4, here.core)

    def arrived(self, slot, seq, which):
        target = self.part(seq, which)
        self.copy(target, target, slot, self.here.core).wait_recv()

    def forward(self):
        here = self.here
        self.arrived(0, here.s_x, FRONT)
        self.go(self.part(here.s_x, FRONT), self.part(here.s_x, FRONT), 5, here.y)
        self.arrived(1, here.s_y, BACK)
        self.go(self.part(here.s_y, BACK), self.part(here.s_y, BACK), 6, here.x)
        self.arrived(2, here.s_x, BACK)
        self.go(self.part(here.s_x, ALL), self.part(here.s_x, ALL), 7, here.core)
        self.arrived(3, here.s_y, FRONT)
        self.go(self.part(here.s_y, ALL), self.part(here.s_y, ALL), 8, here.core)

    def corner(self):
        here = self.here
        self.arrived(5, here.s_xy, FRONT)
        self.arrived(6, here.s_xy, BACK)
        self.go(self.part(here.s_xy, ALL), self.part(here.s_xy, ALL), 9, here.core)

    def finish(self):
        core = self.here.s_core
        self.arrived(4, core, ALL)
        self.arrived(7, flipped(core, 1), ALL)
        self.arrived(8, flipped(core, 2), ALL)
        self.arrived(9, flipped(flipped(core, 1), 2), ALL)
        for made in self.sent:
            made.wait_send()


def ticks_of(stages, count):
    def tick_of(tick):
        def run():
            for lag, stage in reversed(stages):
                if 0 <= tick - lag < count:
                    stage(tick - lag)

        return run

    return [tick_of(tick) for tick in range(count + max(lag for lag, _ in stages))]


def take_some(waiting, count):
    for launch in waiting[:count]:
        launch()
    del waiting[:count]


def weight_blocks(weight, side):
    if side == SHARED:
        return weight.shape
    if side == INWARD:
        return (weight.shape[0], weight.shape[1] // PLANE)
    return (weight.shape[0] // PLANE, weight.shape[1])


def intake(gathered, weights, sides, cid):
    n_rows, n_weights = len(gathered), len(weights)
    pieces = PIECES

    def kernel(*refs):
        row_refs, weight_refs = refs[:n_rows], refs[n_rows : n_rows + n_weights]
        refs = refs[n_rows + n_weights :]
        row_outs, weight_outs = refs[:n_rows], refs[n_rows : n_rows + n_weights]
        local, send, recv, w_local, w_send, w_recv, z_send, z_recv = refs[n_rows + n_weights :]
        here = Places()
        seq, tp, img = here.seq, here.tp, here.img
        others = [lax.rem(seq + step, PLANE) for step in range(1, PLANE)]
        greet([(other, tp, img) for other in others] + [here.img_peer])

        def slot_of(out, side, shape, from_seq, from_img):
            number = from_seq * 2 + from_img
            if side == INWARD:
                return out.at[pl.ds(pl.multiple_of(number * shape[0], shape[0]), shape[0])]
            return out.at[:, pl.ds(pl.multiple_of(number * shape[1], shape[1]), shape[1])]

        def block_of(weight, side, shape, to_seq):
            if side == SHARED:
                return weight
            if side == INWARD:
                return weight.at[:, pl.ds(pl.multiple_of(to_seq * shape[1], shape[1]), shape[1])]
            return weight.at[pl.ds(pl.multiple_of(to_seq * shape[0], shape[0]), shape[0])]

        flights, own_copies = [], []

        def begin(index):
            weight, out, side = weight_refs[index], weight_outs[index], sides[index]
            shape = weight_blocks(weight, side)
            mine = pltpu.make_async_copy(
                block_of(weight, side, shape, seq), slot_of(out, side, shape, seq, img), w_local.at[index]
            )
            mine.start()
            crossing = remote(
                block_of(weight, side, shape, seq),
                slot_of(out, side, shape, seq, img),
                z_send.at[index, 0],
                z_recv.at[index, 0],
                here.img_peer,
            )
            crossing.start()
            own_copies.append(mine)
            flights.append(crossing)
            for step, other in enumerate(others, 1):
                made = remote(
                    block_of(weight, side, shape, other),
                    slot_of(out, side, shape, seq, img),
                    w_send.at[index, step],
                    w_recv.at[index, step],
                    here.at(other),
                )
                made.start()
                flights.append(made)

        spreads = []
        for number, (rows, out) in enumerate(zip(row_refs, row_outs)):
            block = rows.shape[0]
            count = block // pieces
            keep = pltpu.make_async_copy(rows, rows_at(out, seq * block, block), local.at[number])
            keep.start()
            own_copies.append(keep)
            for piece in range(pieces):
                at = number * pieces + piece
                spreads.append(
                    (Spread(here, out, block, piece * count, count, send.at[at], recv.at[at]), rows, piece * count)
                )

        def cross(piece):
            for index in range(piece, n_weights, len(spreads)):
                weight, out, side = weight_refs[index], weight_outs[index], sides[index]
                shape = weight_blocks(weight, side)
                for step in range(1, PLANE):
                    source = lax.rem(seq + PLANE - step, PLANE)
                    landed = slot_of(out, side, shape, source, img)
                    remote(landed, landed, w_send.at[index, step], w_recv.at[index, step], here.core).wait_recv()
                    crossing = remote(
                        landed, landed, z_send.at[index, step], z_recv.at[index, step], here.img_peer
                    )
                    crossing.start()
                    flights.append(crossing)

        def own_rows(piece):
            for index in range(piece, n_weights, len(spreads)):
                begin(index)
            spreads[piece][0].own(spreads[piece][1], spreads[piece][2])

        for tick in ticks_of(
            [
                (0, own_rows),
                (2, lambda piece: spreads[piece][0].forward()),
                (3, lambda piece: cross(piece)),
                (4, lambda piece: spreads[piece][0].corner()),
            ],
            len(spreads),
        ):
            tick()
        for index, (weight, out, side) in enumerate(zip(weight_refs, weight_outs, sides)):
            shape = weight_blocks(weight, side)
            for step in range(PLANE):
                source = lax.rem(seq + PLANE - step, PLANE)
                landed = slot_of(out, side, shape, source, 1 - img)
                remote(landed, landed, z_send.at[index, step], z_recv.at[index, step], here.core).wait_recv()
        for spread, _, _ in spreads:
            spread.finish()
        for made in flights:
            made.wait_send()
        for made in own_copies:
            made.wait()

    def whole(weight, side):
        shape = weight_blocks(weight, side)
        if side == INWARD:
            return jax.ShapeDtypeStruct((2 * PLANE * shape[0], shape[1]), weight.dtype)
        return jax.ShapeDtypeStruct((shape[0], 2 * PLANE * shape[1]), weight.dtype)

    dma = pltpu.SemaphoreType.DMA
    outs = [jax.ShapeDtypeStruct((PLANE * rows.shape[0], rows.shape[1]), rows.dtype) for rows in gathered]
    outs += [whole(weight, side) for weight, side in zip(weights, sides)]
    made = pl.pallas_call(
        kernel,
        out_shape=tuple(outs),
        in_specs=[ANYWHERE] * (n_rows + n_weights),
        out_specs=tuple([ANYWHERE] * len(outs)),
        scratch_shapes=[
            dma((n_rows,)),
            dma((n_rows * pieces, 10)),
            dma((n_rows * pieces, 10)),
            dma((n_weights,)),
            dma((n_weights, PLANE)),
            dma((n_weights, PLANE)),
            dma((n_weights, PLANE)),
            dma((n_weights, PLANE)),
        ],
        compiler_params=pltpu.CompilerParams(
            collective_id=cid, has_side_effects=True, vmem_limit_bytes=VMEM_BYTES
        ),
    )(*gathered, *weights)
    return made[:n_rows], made[n_rows:]


LAZY_BYTES = 256 * 1024


class Lazy:
    def __init__(self, src, dst, sem):
        self.copy = pltpu.make_async_copy(src, dst, sem)
        self.copy.start()
        self.dst, self.shape, self.pending = dst, dst.shape, True

    def ready(self):
        if self.pending:
            self.copy.wait()
            self.pending = False
        return self.dst

    @property
    def at(self):
        return self.ready().at

    def __getitem__(self, where):
        return self.ready()[where]


def is_lazy(value, spec):
    return spec is ON_CHIP and value.size * value.dtype.itemsize >= LAZY_BYTES


class Rider:
    inputs, out_shapes, scratch, in_specs = (), (), (), ()

    def bind(self, here, ins, outs, scratch):
        self.here, self.ins, self.outs, self.held = here, ins, outs, scratch
        self.sent, self.kept, self.due, self.launches, self.later = [], [], [], [], []

    def keep(self, src, dst, sem):
        made = pltpu.make_async_copy(src, dst, sem)
        self.launches.append(made.start)
        self.kept.append(made)

    def send(self, src, dst, send, recv, peer):
        made = remote(src, dst, send, recv, peer)
        self.launches.append(made.start)
        self.sent.append(made)

    def finish(self):
        for dst, send, recv in self.due:
            remote(dst, dst, send, recv, self.here.core).wait_recv()
        for made in self.sent:
            made.wait_send()
        for made in self.kept:
            made.wait()


class ChainWeights(Rider):
    def __init__(self, weights, sides, places):
        self.inputs, self.sides, self.places = weights, sides, places
        self.blocks = [weight_blocks(weight, side) for weight, side in zip(weights, sides)]
        shapes = {}
        for (rows, columns), side, (out, first) in zip(self.blocks, sides, places):
            if side == INWARD:
                shapes[out] = (2 * PLANE * rows, first + columns)
            else:
                shapes[out] = (rows, 2 * PLANE * columns)
        self.out_shapes = [jax.ShapeDtypeStruct(shapes[out], weights[0].dtype) for out in range(len(shapes))]
        dma, count = pltpu.SemaphoreType.DMA, len(weights)
        self.scratch = [dma((count, PLANE))] * 4 + [dma((count,))]

    def peers(self, here):
        return [here.at(lax.rem(here.seq + step, PLANE)) for step in range(1, PLANE)]

    def slot(self, index, seq, img):
        out, first = self.places[index]
        (rows, columns), number = self.blocks[index], seq * 2 + img
        if self.sides[index] == INWARD:
            return self.outs[out].at[pl.ds(pl.multiple_of(number * rows, rows), rows), pl.ds(first, columns)]
        return self.outs[out].at[:, pl.ds(pl.multiple_of(number * columns, columns), columns)]

    def start(self):
        here, (send, recv, z_send, z_recv, local) = self.here, self.held
        self.later = []
        for index, (weight, side, (rows, columns)) in enumerate(zip(self.ins, self.sides, self.blocks)):
            for step in range(PLANE):
                target = lax.rem(here.seq + step, PLANE)
                source = lax.rem(here.seq + PLANE - step, PLANE)
                if side == INWARD:
                    part = weight.at[:, pl.ds(pl.multiple_of(target * columns, columns), columns)]
                else:
                    part = weight.at[pl.ds(pl.multiple_of(target * rows, rows), rows)]
                mine = self.slot(index, here.seq, here.img)
                if step == 0:
                    self.keep(part, mine, local.at[index])
                    cross = remote(part, mine, z_send.at[index, 0], z_recv.at[index, 0], here.img_peer)
                    self.launches.append(cross.start)
                    self.sent.append(cross)
                else:
                    self.send(part, mine, send.at[index, step], recv.at[index, step], here.at(target))
                    self.later.append(functools.partial(self.cross, index, step, source))
                there = self.slot(index, source, 1 - here.img)
                self.due.append((there, z_send.at[index, step], z_recv.at[index, step]))

    def cross(self, index, step, source):
        here, (send, recv, z_send, z_recv, _) = self.here, self.held
        landed = self.slot(index, source, here.img)
        remote(landed, landed, send.at[index, step], recv.at[index, step], here.core).wait_recv()
        made = remote(landed, landed, z_send.at[index, step], z_recv.at[index, step], here.img_peer)
        made.start()
        self.sent.append(made)


class CrossGrads(Rider):
    def __init__(self, grads, sides):
        self.inputs, self.sides = grads, sides
        self.out_shapes = []
        for grad, side in zip(grads, sides):
            if side == INWARD:
                shape = (grad.shape[0], grad.shape[2], grad.shape[3])
            else:
                shape = (PLANE, grad.shape[0], grad.shape[1] // (2 * PLANE))
            self.out_shapes.append(jax.ShapeDtypeStruct(shape, grad.dtype))
        dma = pltpu.SemaphoreType.DMA
        self.scratch = [dma((len(grads), PLANE)), dma((len(grads), PLANE))]

    def peers(self, here):
        return [here.img_peer]

    def start(self):
        here, (send, recv) = self.here, self.held
        for index, (grad, out, side) in enumerate(zip(self.ins, self.outs, self.sides)):
            width = out.shape[2]
            for seq in range(PLANE):
                if side == INWARD:
                    part = grad.at[seq, 1 - here.img]
                else:
                    part = grad.at[:, pl.ds(pl.multiple_of((seq * 2 + 1 - here.img) * width, width), width)]
                self.send(part, out.at[seq], send.at[index, seq], recv.at[index, seq], here.img_peer)
                self.due.append((out.at[seq], send.at[index, seq], recv.at[index, seq]))


class Stream:
    in_specs = ()

    def __init__(self, rows_all, left, right, across, row_inputs, row_kinds, row_outs, row_function, gather):
        self.own_left = left is not None
        self.inputs = ([left] if self.own_left else []) + [right] + list(row_inputs)
        self.across, self.row_kinds, self.row_outs = across, row_kinds, row_outs
        self.row_function, self.gather = row_function, gather
        width = right.shape[0] if across else right.shape[1]
        self.width, self.block, self.pieces = width, rows_all // PLANE, PIECES
        self.half = width // 2
        low_type = jnp.bfloat16
        self.out_shapes = [shape for shape, _ in row_outs]
        if gather:
            self.out_shapes.append(jax.ShapeDtypeStruct((rows_all, width), low_type))
        dma = pltpu.SemaphoreType.DMA
        block, pieces, half = self.block, self.pieces, self.half
        self.scratch = [
            pltpu.VMEM((4, block, width), low_type),
            pltpu.VMEM((4, block, width), low_type),
            pltpu.VMEM((4, block, width), jnp.float32),
            pltpu.VMEM((block, half), low_type),
            pltpu.VMEM((block, half), low_type),
            pltpu.VMEM((block, width), low_type),
            pltpu.VMEM((block, width), low_type),
            pltpu.VMEM((block, width), low_type),
            pltpu.VMEM((block, width), low_type),
            pltpu.VMEM((block, width), low_type),
            dma((4,)),
            dma((4,)),
            dma((pieces, 7)),
            dma((pieces, 7)),
            dma((pieces, 10)),
            dma((pieces, 10)),
            dma((pieces,)),
        ]

    def out_specs(self):
        return [ON_CHIP] * len(self.row_outs) + [ANYWHERE] * (len(self.out_shapes) - len(self.row_outs))

    def peers(self, here):
        return [here.core, here.x, here.y, here.tp_peer]

    def bind(self, here, ins, outs, scratch):
        self.here = here
        if self.own_left:
            self.left, ins = ins[0], ins[1:]
        self.right, self.ins = ins[0], ins[1:]
        self.outs = outs
        (self.away, self.core_in, self.near, self.from_xd, self.from_yd, self.from_x, self.from_y) = scratch[:7]
        (self.mine, self.theirs, self.low, self.c_send, self.c_recv) = scratch[7:12]
        (self.send, self.recv, self.g_send, self.g_recv, self.l_sem) = scratch[12:]
        self.sent, self.spreads, self.core_copies = [], [], {}

    def chunk(self, base, kind):
        if kind in (1, 3):
            base = flipped(base, 1)
        if kind in (2, 3):
            base = flipped(base, 2)
        return base

    def product(self, seq, target, low_type):
        first = pl.multiple_of(seq * self.block, self.block)
        rows = self.left[pl.ds(first, self.block), :]
        step = min(512, self.width)
        for column in range(0, self.width, step):
            if self.across:
                part = lax.dot_general(
                    rows,
                    self.right[column : column + step, :],
                    (((1,), (1,)), ((), ())),
                    preferred_element_type=jnp.float32,
                )
            else:
                part = jnp.dot(
                    rows, self.right[:, column : column + step], preferred_element_type=jnp.float32
                )
            target[:, column : column + step] = part.astype(low_type)

    def begin(self):
        here = self.here
        for kind in (3, 1, 2, 0):
            self.product(self.chunk(here.s_core, kind), self.away.at[kind], jnp.bfloat16)
            made = remote(
                self.away.at[kind], self.core_in.at[kind], self.c_send.at[kind], self.c_recv.at[kind], here.core
            )
            made.start()
            self.core_copies[kind] = made
            self.product(self.chunk(here.seq, kind), self.near.at[kind], jnp.float32)

    def go(self, src, dst, piece, slot, peer):
        made = remote(src, dst, self.send.at[piece, slot], self.recv.at[piece, slot], peer)
        made.start()
        self.sent.append(made)

    def landed(self, dst, piece, slot):
        remote(dst, dst, self.send.at[piece, slot], self.recv.at[piece, slot], self.here.core).wait_recv()

    def rows_of(self, piece):
        return pl.ds(sum(PIECE_ROWS[:piece]), PIECE_ROWS[piece])

    def columns_of(self, which):
        return pl.ds(self.half if which == BACK else 0, self.half)

    def held(self, kind, piece, which=ALL):
        if which == ALL:
            return self.core_in.at[kind, self.rows_of(piece)]
        return self.core_in.at[kind, self.rows_of(piece), self.columns_of(which)]

    def halved(self, ref, piece, which):
        return ref.at[self.rows_of(piece), self.columns_of(which)]

    def folded(self, kind, piece):
        if piece == 0:
            self.core_copies[kind].wait_recv()
        near = self.near[kind, self.rows_of(piece), :]
        return self.held(kind, piece)[...].astype(jnp.float32) + near

    def first_sends(self, piece):
        here = self.here
        self.held(3, piece)[...] = self.folded(3, piece).astype(jnp.bfloat16)
        self.go(self.held(3, piece, FRONT), self.from_xd.at[self.rows_of(piece)], piece, 0, here.x)
        self.go(self.held(3, piece, BACK), self.from_yd.at[self.rows_of(piece)], piece, 1, here.y)
        self.held(1, piece)[...] = self.folded(1, piece).astype(jnp.bfloat16)
        self.go(self.held(1, piece, FRONT), self.halved(self.from_x, piece, FRONT), piece, 2, here.x)
        self.held(2, piece)[...] = self.folded(2, piece).astype(jnp.bfloat16)
        self.go(self.held(2, piece, BACK), self.halved(self.from_y, piece, BACK), piece, 3, here.y)

    def second_sends(self, piece):
        here = self.here
        self.landed(self.from_xd.at[self.rows_of(piece)], piece, 0)
        at = self.held(2, piece, FRONT)
        at[...] = (at[...].astype(jnp.float32) + self.from_xd[self.rows_of(piece), :].astype(jnp.float32)).astype(jnp.bfloat16)
        self.go(at, self.halved(self.from_y, piece, FRONT), piece, 4, here.y)
        self.landed(self.from_yd.at[self.rows_of(piece)], piece, 1)
        at = self.held(1, piece, BACK)
        at[...] = (at[...].astype(jnp.float32) + self.from_yd[self.rows_of(piece), :].astype(jnp.float32)).astype(jnp.bfloat16)
        self.go(at, self.halved(self.from_x, piece, BACK), piece, 5, here.x)

    def plane_sum(self, piece):
        self.landed(self.halved(self.from_x, piece, FRONT), piece, 2)
        self.landed(self.halved(self.from_y, piece, BACK), piece, 3)
        self.landed(self.halved(self.from_y, piece, FRONT), piece, 4)
        self.landed(self.halved(self.from_x, piece, BACK), piece, 5)
        total = self.folded(0, piece)
        total = total + self.from_x[self.rows_of(piece), :].astype(jnp.float32) + self.from_y[self.rows_of(piece), :].astype(jnp.float32)
        self.mine[self.rows_of(piece), :] = total.astype(jnp.bfloat16)
        self.go(self.mine.at[self.rows_of(piece)], self.theirs.at[self.rows_of(piece)], piece, 6, self.here.tp_peer)

    def rows_done(self, piece):
        here = self.here
        self.landed(self.theirs.at[self.rows_of(piece)], piece, 6)
        total = self.mine[self.rows_of(piece), :].astype(jnp.float32) + self.theirs[self.rows_of(piece), :].astype(jnp.float32)
        rows = self.rows_of(piece)
        views = [ref.at[rows] if kind == ROWS else ref for ref, kind in zip(self.ins, self.row_kinds)]
        out_views = [ref.at[rows] if kind == ROWS else ref for ref, (_, kind) in zip(self.outs, self.row_outs)]
        given = self.row_function(total, piece, views, out_views)
        if self.gather:
            out = self.outs[-1]
            self.low[rows, :] = given
            first = pl.multiple_of(here.seq * self.block + rows.start, 16)
            keep = pltpu.make_async_copy(self.low.at[rows], out.at[pl.ds(first, rows.size)], self.l_sem.at[piece])
            keep.start()
            spread = Spread(
                here, out, self.block, rows.start, rows.size, self.g_send.at[piece], self.g_recv.at[piece]
            )
            spread.own(self.low, rows.start)
            self.spreads.append((spread, keep))

    def stages(self):
        stages = [(0, self.first_sends), (1, self.second_sends), (2, self.plane_sum), (4, self.rows_done)]
        if self.gather:
            stages.append((5, lambda piece: self.spreads[piece][0].forward()))
            stages.append((6, lambda piece: self.spreads[piece][0].corner()))
        return stages

    def finish(self):
        for spread, keep in self.spreads:
            spread.finish()
            keep.wait()
        for made in self.sent:
            made.wait_send()
        for made in self.core_copies.values():
            made.wait_send()


class Front(Rider):
    def total_scratch(self, count, rows):
        dma = pltpu.SemaphoreType.DMA
        return [
            pltpu.VMEM((PLANE - 1, count, rows), jnp.float32),
            pltpu.VMEM((count, rows), jnp.float32),
            pltpu.VMEM((count, rows), jnp.float32),
            pltpu.VMEM((count, rows), jnp.float32),
            dma((PLANE,)),
            dma((PLANE,)),
        ]

    def peers(self, here):
        return [here.at(lax.rem(here.seq + step, PLANE)) for step in range(1, PLANE)]

    def small_sum(self, scratch):
        here, (plane, own, mine, theirs, send, recv) = self.here, scratch
        made = []
        for step, peer in enumerate(self.peers(here)):
            copy = remote(own, plane.at[step], send.at[step], recv.at[step], peer)
            copy.start()
            made.append(copy)
        total = own[...]
        for step, copy in enumerate(made):
            copy.wait_recv()
            total = total + plane[step]
        mine[...] = total
        last = remote(mine, theirs, send.at[PLANE - 1], recv.at[PLANE - 1], here.tp_peer)
        last.start()
        last.wait()
        for copy in made:
            copy.wait_send()
        total = mine[...] + theirs[...]
        count, rows = total.shape
        return jnp.concatenate([total, jnp.zeros((8 - count, rows), jnp.float32)], 0).T


def chosen_rows(target_rows, first, count):
    row = first + lax.broadcasted_iota(jnp.int32, (count, target_rows.shape[1]), 0)
    return (row == target_rows[...]).astype(jnp.float32).astype(jnp.bfloat16)


class ImageFront(Rider):
    def __init__(self, pictures, key_part, value_part, latent_all, probe_part, target_rows):
        self.inputs = [pictures, key_part, value_part, latent_all, probe_part, target_rows]
        rows, width = pictures.shape[0], key_part.shape[1]
        images = rows // PATCH
        low_type = jnp.bfloat16
        self.out_shapes = [
            jax.ShapeDtypeStruct((rows, 2 * width), low_type),
            jax.ShapeDtypeStruct((images * LAT, width), low_type),
            jax.ShapeDtypeStruct((LAT, width), low_type),
        ]
        self.scratch = [
            pltpu.VMEM((key_part.shape[0], 2 * width), low_type),
            pltpu.VMEM((images * LAT, width), low_type),
        ]

    def run(self):
        pictures, key_w, value_w, latent_all, probe_w, target_rows = self.ins
        keys, placed, probe = self.outs
        both_w, mixed_all = self.held
        width, scale = probe.shape[1], HEAD ** (-0.5)
        both_w[:, :width] = key_w[...]
        both_w[:, width:] = value_w[...]
        probe[...] = jnp.dot(latent_all[...], probe_w[...], preferred_element_type=jnp.float32).astype(jnp.bfloat16)
        yield
        for image in range(pictures.shape[0] // PATCH):
            rows = slice(image * PATCH, (image + 1) * PATCH)
            if image % IMAGES_A_STEP == 0:
                more = slice(image * PATCH, (image + IMAGES_A_STEP) * PATCH)
                keys[more, :] = jnp.dot(
                    pictures[more, :], both_w[...], preferred_element_type=jnp.float32
                ).astype(jnp.bfloat16)
            mixed = []
            for first in range(0, width, HEAD):
                probs = image_probs_of(probe[:, first : first + HEAD], keys[rows, first : first + HEAD], scale)
                values = keys[rows, width + first : width + first + HEAD]
                mixed.append(jnp.dot(probs.astype(jnp.bfloat16), values, preferred_element_type=jnp.float32))
            mixed_all[image * LAT : (image + 1) * LAT, :] = jnp.concatenate(mixed, 1).astype(jnp.bfloat16)
            yield
        for first in range(0, placed.shape[0], PATCH):
            chosen = chosen_rows(target_rows, first, PATCH)
            placed[first : first + PATCH, :] = jnp.dot(
                chosen, mixed_all[...], preferred_element_type=jnp.float32
            ).astype(jnp.bfloat16)
        self.left = placed


class AttendFront(Front):
    def __init__(self, normed, layer_part, tables, segment, gain, shift, full_width):
        self.inputs = [normed, layer_part, *tables, segment[:, None], segment[None, :], gain, shift]
        self.full_width = full_width
        rows, width = normed.shape[0], layer_part.shape[1] // 3
        low_shape = jax.ShapeDtypeStruct((rows, width), jnp.bfloat16)
        wide_shape = jax.ShapeDtypeStruct((rows, width), jnp.float32)
        lse_shape = jax.ShapeDtypeStruct((rows, 8), jnp.float32)
        self.out_shapes = [low_shape, low_shape, low_shape, wide_shape, lse_shape, low_shape, wide_shape, wide_shape]
        self.scratch = self.total_scratch(2, rows)

    def run(self):
        normed, layer_w, cos_ref, sin_ref, grow_ref, column_ref, row_ref, gain, shift = self.ins
        q_out, k_out, v_out, att_out, lse_out, low, hat, factor_out = self.outs
        rows_all, width = att_out.shape
        scale = HEAD ** (-0.5)
        f32, low_type = jnp.float32, jnp.bfloat16
        for first in range(0, rows_all, ATTEND_ROWS):
            at, keys = slice(first, first + ATTEND_ROWS), first + ATTEND_ROWS
            cosine, sine, growth = cos_ref[at, :], sin_ref[at, :], grow_ref[at, :]
            linear = jnp.dot(normed[at, :], layer_w[...], preferred_element_type=f32)
            lin = linear[:, :width]
            q_out[at, :] = ((lin * cosine + halves_swapped(lin) * sine) * growth).astype(low_type)
            lin = linear[:, width : 2 * width]
            k_out[at, :] = ((lin * cosine + halves_swapped(lin) * sine) * (1.0 / growth)).astype(low_type)
            v_out[at, :] = linear[:, 2 * width :].astype(low_type)
            allowed = allowed_part(column_ref, row_ref, first, ATTEND_ROWS, keys)
            for head in range(width // HEAD):
                lanes = slice(head * HEAD, (head + 1) * HEAD)
                scores = lax.dot_general(
                    q_out[at, lanes] * scale,
                    k_out[:keys, lanes],
                    (((1,), (1,)), ((), ())),
                    preferred_element_type=f32,
                )
                scores = jnp.where(allowed, scores, -1e30)
                best = jnp.max(scores, -1, keepdims=True)
                weights = jnp.exp(scores - best)
                total = jnp.sum(weights, -1, keepdims=True)
                probs = (weights * (1.0 / total)).astype(low_type)
                att_out[at, lanes] = jnp.dot(probs, v_out[:keys, lanes], preferred_element_type=f32)
                lse_out[at, head : head + 1] = best + jnp.log(total)
            rows = att_out[at, :]
            sums = [jnp.sum(rows, 1, keepdims=True), jnp.sum(rows * rows, 1, keepdims=True)]
            self.held[1][:, at] = as_lanes(sums)[:2]
            yield
        total = self.small_sum(self.held) / self.full_width
        average = total[:, 0:1]
        factor = lax.rsqrt(total[:, 1:2] - average * average + EPSILON)
        normal = (att_out[...] - average) * factor
        hat[...] = normal
        factor_out[...] = jnp.broadcast_to(factor, normal.shape)
        low[...] = (normal * gain[...] + shift[...]).astype(low_type)
        self.left = low


class GradFront(Front):
    def grads(self, products):
        for seq in range(PLANE):
            for product in products:
                self.launches.append(functools.partial(self.part, *product, seq))

    def part(self, left, right, outs, side, seq):
        span = (left.shape[1] if side == INWARD else right.shape[1]) // PLANE
        at = slice(seq * span, (seq + 1) * span)
        contract = (((0,), (0,)), ((), ()))
        if side == OUTWARD:
            outs[0][:, at] = lax.dot_general(
                left[...], right[:, at], contract, preferred_element_type=jnp.float32
            ).astype(jnp.bfloat16)
            return
        made = lax.dot_general(left[:, at], right[...], contract, preferred_element_type=jnp.float32)
        made = made.astype(jnp.bfloat16)
        half = span // 2
        for number, out in enumerate(outs):
            width = out.shape[3]
            piece = made[:, number * width : (number + 1) * width]
            out[seq, 0], out[seq, 1] = piece[:half], piece[half:]


def grad_shape(model_width, rows, side):
    span = model_width // PLANE
    shape = (PLANE, 2, span // 2, rows) if side == INWARD else (rows, model_width)
    return jax.ShapeDtypeStruct(shape, jnp.bfloat16)


class HiddenFront(GradFront):
    def __init__(self, lifted, up_part, bias, cotangent_all, down_part, gain, shift, full_width):
        self.inputs = [lifted, up_part, bias, cotangent_all, down_part, gain, shift]
        self.full_width = full_width
        rows, width, model_width = lifted.shape[0], up_part.shape[1], lifted.shape[1]
        low_shape = jax.ShapeDtypeStruct((rows, width), jnp.bfloat16)
        self.out_shapes = [
            low_shape,
            low_shape,
            jax.ShapeDtypeStruct((8, width), jnp.float32),
            grad_shape(model_width, width, INWARD),
            grad_shape(model_width, width, OUTWARD),
        ]
        self.scratch = self.total_scratch(4, rows) + [pltpu.VMEM((rows, width), jnp.float32)] * 3

    def run(self):
        lifted, up_w, bias, cotangent_all, down_w, gain, shift = self.ins
        settled, d_hidden, vectors, up, down = self.outs
        activated, slope, d_settled = self.held[6:]
        f32 = jnp.float32
        rows = activated.shape[0]
        step = rows // 4
        for first in range(0, rows, step):
            at = slice(first, first + step)
            pre = jnp.dot(lifted[at, :], up_w[...], preferred_element_type=f32) + bias[...]
            below = 0.5 + 0.5 * lax.erf(pre * (0.5**0.5))
            act = pre * below
            activated[at, :] = act
            slope[at, :] = below + pre * jnp.exp(-0.5 * pre * pre) * (1.0 / (2.0 * jnp.pi) ** 0.5)
            grad = lax.dot_general(
                cotangent_all[at, :], down_w[...], (((1,), (1,)), ((), ())), preferred_element_type=f32
            )
            d_settled[at, :] = grad
            scaled = grad * gain[...]
            sums = [jnp.sum(part, 1, keepdims=True) for part in (act, act * act, scaled, scaled * act)]
            self.held[1][:, at] = as_lanes(sums)[:4]
            yield
        total = self.small_sum(self.held[:6]) / self.full_width
        average = total[:, 0:1]
        factor = lax.rsqrt(total[:, 1:2] - average * average + EPSILON)
        mean_scaled = total[:, 2:3]
        mean_cross = factor * (total[:, 3:4] - average * mean_scaled)
        step = rows // PLANE
        gain_sum = shift_sum = bias_sum = 0.0
        for first in range(0, rows, step):
            at = slice(first, first + step)
            normal = (activated[at, :] - average[at]) * factor[at]
            settled[at, :] = (normal * gain[...] + shift[...]).astype(jnp.bfloat16)
            grad = d_settled[at, :]
            inner = factor[at] * (grad * gain[...] - mean_scaled[at] - normal * mean_cross[at])
            low = (slope[at, :] * inner).astype(jnp.bfloat16)
            d_hidden[at, :] = low
            gain_sum += jnp.sum(grad * normal, 0, keepdims=True)
            shift_sum += jnp.sum(grad, 0, keepdims=True)
            bias_sum += jnp.sum(low.astype(f32), 0, keepdims=True)
        vectors[...] = jnp.zeros_like(vectors)
        vectors[0:1, :], vectors[1:2, :], vectors[2:3, :] = gain_sum, shift_sum, bias_sum
        self.grads([(lifted, d_hidden, [up], INWARD), (settled, cotangent_all, [down], OUTWARD)])
        self.left = d_hidden


class AttendBackFront(GradFront):
    def __init__(self, d_branch, out_part, hat, factor, gain, kept, tables, segment, normed, inner_low, full_width):
        self.inputs = [d_branch, out_part, hat, factor, gain, *kept, *tables]
        self.inputs += [segment[:, None], segment[None, :], normed, inner_low]
        self.full_width = full_width
        rows, width = hat.shape
        model_width = normed.shape[1]
        low_type, f32 = jnp.bfloat16, jnp.float32
        self.out_shapes = [jax.ShapeDtypeStruct((8, width), f32)]
        self.out_shapes += [grad_shape(model_width, width, INWARD)] * 3 + [grad_shape(model_width, width, OUTWARD)]
        self.scratch = self.total_scratch(2, rows)
        self.scratch += [pltpu.VMEM((rows, width), low_type), pltpu.VMEM((rows, 3 * width), low_type)]
        self.scratch += [pltpu.VMEM((rows, width), f32)] * 4

    def run(self):
        d_branch, out_part, hat, factor, gain, attended, q_ref, k_ref, v_ref, lse = self.ins[:10]
        cos_ref, sin_ref, grow_ref, column_ref, row_ref, normed, inner_low = self.ins[10:]
        vectors, *grads = self.outs
        d_att, lin_out, d_inner, d_query, d_key, d_value = self.held[6:]
        rows_all, width = hat.shape
        f32, low_type = jnp.float32, jnp.bfloat16
        gain_sum = shift_sum = 0.0
        for first in range(0, rows_all, ATTEND_ROWS):
            at = slice(first, first + ATTEND_ROWS)
            grad = lax.dot_general(
                d_branch[at, :], out_part[...], (((1,), (1,)), ((), ())), preferred_element_type=f32
            )
            d_inner[at, :] = grad
            gain_sum += jnp.sum(grad * hat[at, :], 0, keepdims=True)
            shift_sum += jnp.sum(grad, 0, keepdims=True)
            scaled = grad * gain[...]
            sums = [jnp.sum(scaled, 1, keepdims=True), jnp.sum(scaled * hat[at, :], 1, keepdims=True)]
            self.held[1][:, at] = as_lanes(sums)[:2]
            yield
        vectors[...] = jnp.zeros_like(vectors)
        vectors[0:1, :], vectors[1:2, :] = gain_sum, shift_sum
        total = self.small_sum(self.held[:6]) / self.full_width
        d_att[...] = (
            factor[...] * (d_inner[...] * gain[...] - total[:, 0:1] - hat[...] * total[:, 1:2])
        ).astype(low_type)
        heads, scale = width // HEAD, HEAD ** (-0.5)
        for first in range(0, rows_all, ATTEND_ROWS):
            at, keys = slice(first, first + ATTEND_ROWS), first + ATTEND_ROWS
            allowed = allowed_part(column_ref, row_ref, first, ATTEND_ROWS, keys)
            for head in range(heads):
                lanes = slice(head * HEAD, (head + 1) * HEAD)
                scores = lax.dot_general(
                    q_ref[at, lanes] * scale,
                    k_ref[:keys, lanes],
                    (((1,), (1,)), ((), ())),
                    preferred_element_type=f32,
                )
                scores = jnp.where(allowed, scores, -1e30)
                probs = jnp.exp(scores - lse[at, head : head + 1])
                d_rows = d_att[at, lanes]
                d_probs = lax.dot_general(
                    d_rows, v_ref[:keys, lanes], (((1,), (1,)), ((), ())), preferred_element_type=f32
                )
                delta = jnp.sum(d_rows.astype(f32) * attended[at, lanes], -1, keepdims=True)
                d_scores = (probs * (d_probs - delta)).astype(low_type)
                d_query[at, lanes] = jnp.dot(d_scores, k_ref[:keys, lanes], preferred_element_type=f32) * scale
                key_part = (
                    lax.dot_general(
                        d_scores, q_ref[at, lanes], (((0,), (0,)), ((), ())), preferred_element_type=f32
                    )
                    * scale
                )
                value_part = lax.dot_general(
                    probs.astype(low_type), d_rows, (((0,), (0,)), ((), ())), preferred_element_type=f32
                )
                if first:
                    d_key[:first, lanes] += key_part[:first]
                    d_value[:first, lanes] += value_part[:first]
                d_key[first:keys, lanes] = key_part[first:]
                d_value[first:keys, lanes] = value_part[first:]
                yield
        for first in range(0, rows_all, ATTEND_ROWS):
            at = slice(first, first + ATTEND_ROWS)
            cosine, sine, growth = cos_ref[at, :], sin_ref[at, :], grow_ref[at, :]
            scaled = d_query[at, :] * growth
            lin_out[at, :width] = (scaled * cosine - halves_swapped(scaled) * sine).astype(low_type)
            scaled = d_key[at, :] * (1.0 / growth)
            lin_out[at, width : 2 * width] = (scaled * cosine - halves_swapped(scaled) * sine).astype(low_type)
            lin_out[at, 2 * width :] = d_value[at, :].astype(low_type)
        self.grads(
            [
                (normed, lin_out, grads[:3], INWARD),
                (inner_low, d_branch, grads[3:], OUTWARD),
            ]
        )
        self.left = lin_out


def lazy_call(kernel, inputs, in_specs, out_shapes, out_specs, scratch, cid):
    late = [is_lazy(value, spec) for value, spec in zip(inputs, in_specs)]
    buffers = [pltpu.VMEM(value.shape, value.dtype) for value, flag in zip(inputs, late) if flag]
    n_in, n_out, n_scratch, n_late = len(inputs), len(out_shapes), len(scratch), len(buffers)

    def body(*refs):
        refs = list(refs)
        ins, outs, held = refs[:n_in], refs[n_in : n_in + n_out], refs[n_in + n_out : n_in + n_out + n_scratch]
        spare, sems = refs[n_in + n_out + n_scratch : -1], refs[-1]
        lazies = []
        for number, flag in enumerate(late):
            if flag:
                ins[number] = Lazy(ins[number], spare[len(lazies)], sems.at[len(lazies)])
                lazies.append(ins[number])
        kernel(ins, outs, held)
        for item in lazies:
            item.ready()

    return pl.pallas_call(
        body,
        out_shape=tuple(out_shapes),
        in_specs=[ANYWHERE if flag else spec for spec, flag in zip(in_specs, late)],
        out_specs=tuple(out_specs),
        scratch_shapes=list(scratch) + buffers + [pltpu.SemaphoreType.DMA((max(n_late, 1),))],
        compiler_params=pltpu.CompilerParams(
            collective_id=cid, has_side_effects=True, vmem_limit_bytes=VMEM_BYTES
        ),
    )(*inputs)


def exchange(front, streams, riders, cid, early=None, pace=1, early_pace=3):
    fronts = [front] if front is not None else []
    earlies = [early] if early is not None else []
    sums = list(streams) + earlies
    parts = fronts + sums + list(riders)

    def kernel(ins, outs, held):
        here = Places()
        ins, outs, held = list(ins), list(outs), list(held)

        def take(refs, count):
            taken = refs[:count]
            del refs[:count]
            return taken

        for part in parts:
            part.bind(
                here, take(ins, len(part.inputs)), take(outs, len(part.out_shapes)), take(held, len(part.scratch))
            )
        wide_parts = [part for part in parts if isinstance(part, (Front, ChainWeights))]
        peers = [here.tp_peer]
        if riders:
            peers.append(here.img_peer)
        if wide_parts:
            peers += wide_parts[0].peers(here)
        else:
            peers += [here.core, here.x, here.y]
        greet(peers)
        waiting, crossing = [], []
        for rider in riders:
            rider.start()
            if rider.later:
                take_some(rider.launches, len(rider.launches))
            waiting += rider.launches + rider.later
        early_ticks = []
        if early is not None:
            early.begin()
            early_ticks = ticks_of(early.stages(), PIECES)
        if front is not None:
            for number, _ in enumerate(front.run()):
                take_some(waiting, pace)
                if number % early_pace == 0:
                    take_some(early_ticks, 1)
            streams[0].left = front.left
            waiting += front.launches
        for stream in streams:
            stream.begin()
        stages = []
        for stream in reversed(streams):
            stages += stream.stages()
        ticks = ticks_of(stages, PIECES)
        share = -(-len(waiting) // max(len(ticks) - 2, 1))
        for tick in ticks:
            tick()
            take_some(early_ticks, 1)
            take_some(waiting, share)
        take_some(early_ticks, len(early_ticks))
        for part in parts:
            part.finish()

    in_specs = []
    for part in fronts + sums:
        in_specs += part.in_specs or [ON_CHIP] * len(part.inputs)
    in_specs += [ANYWHERE] * sum(len(rider.inputs) for rider in riders)
    out_specs = [ON_CHIP for part in fronts for _ in part.out_shapes]
    out_specs += [spec for stream in sums for spec in stream.out_specs()]
    out_specs += [ANYWHERE] * sum(len(rider.out_shapes) for rider in riders)
    made = list(
        lazy_call(
            kernel,
            [value for part in parts for value in part.inputs],
            in_specs,
            [shape for part in parts for shape in part.out_shapes],
            out_specs,
            [item for part in parts for item in part.scratch],
            cid,
        )
    )
    split = []
    for part in parts:
        split.append(made[: len(part.out_shapes)])
        del made[: len(part.out_shapes)]
    return split


def finale(pairs, sides, raw, raw_sides, image, vectors, latents_t, query_rows, cid):
    f32, low_type, dma = jnp.float32, jnp.bfloat16, pltpu.SemaphoreType.DMA
    d_rows, pictures, keys, probe, placed, out_part, target_rows = image
    width, model_width, picture_width = probe.shape[1], d_rows.shape[1], pictures.shape[1]
    images = pictures.shape[0] // PATCH
    image_shapes = [
        grad_shape(picture_width, width, INWARD),
        grad_shape(picture_width, width, INWARD),
        grad_shape(model_width, width, OUTWARD),
    ]
    all_sides = list(sides) + list(raw_sides) + [INWARD, INWARD, OUTWARD]
    n, n_raw, n_image = len(sides), len(raw_sides), len(image_shapes)
    total = n + n_raw + n_image
    shapes = [grad.shape for grad, _ in pairs] + [grad.shape for grad in raw] + [item.shape for item in image_shapes]
    blocks = [
        shape[2:] if side == INWARD else (shape[0], shape[1] // (2 * PLANE)) for shape, side in zip(shapes, all_sides)
    ]
    small_shape = (LAT + vectors.shape[0], LANES)

    def kernel(ins, outs, held):
        refs = list(ins) + list(outs) + list(held)

        def take(count):
            taken = refs[:count]
            del refs[:count]
            return taken

        target_ref, d_ref, pictures_ref, keys_ref, probe_ref, placed_ref, out_w = take(7)
        grad_refs = take(n + n_raw)
        theirs = take(n)
        vectors_ref, latents_ref, query_ref = take(3)
        out_refs = take(total)
        sums_out, query_out, latent_out = take(3)
        grad_refs += take(n_image)
        theirs += take(n_raw + n_image)
        summed = take(total)
        small_own, small_theirs, small_mine, small_all, lat_mine, lat_theirs, d_mixed, d_both = take(8)
        z_send, z_recv, send, recv, local, s_send, s_recv = take(7)
        here = Places()
        seq, img = here.seq, here.img
        ring = [here.at(lax.rem(seq + step, PLANE)) for step in range(1, PLANE)]
        greet(ring + [here.img_peer, here.tp_peer])

        def part_of(index, to_seq, to_img):
            ref, block = grad_refs[index], blocks[index]
            if all_sides[index] == INWARD:
                return ref.at[to_seq, to_img]
            return ref.at[:, pl.ds(pl.multiple_of((to_seq * 2 + to_img) * block[1], block[1]), block[1])]

        def slot_of(index, from_seq):
            ref, block = out_refs[index], blocks[index]
            if all_sides[index] == INWARD:
                return ref.at[:, pl.ds(pl.multiple_of(from_seq * block[1], block[1]), block[1])]
            return ref.at[pl.ds(pl.multiple_of(from_seq * block[0], block[0]), block[0])]

        waits, crossings = [], {}

        def cross(index):
            for step in range(PLANE):
                target = lax.rem(seq + step, PLANE)
                made = remote(
                    part_of(index, target, 1 - img),
                    theirs[index].at[target],
                    z_send.at[index - n, step],
                    z_recv.at[index - n, step],
                    here.img_peer,
                )
                made.start()
                crossings[index, step] = made

        def deliver(index, step):
            target = lax.rem(seq + step, PLANE)
            if index >= n:
                crossings[index, step].wait_recv()
            mine = part_of(index, target, img)[...].astype(f32)
            summed[index][target] = (mine + theirs[index][target].astype(f32)).astype(low_type)
            if step == 0:
                made = pltpu.make_async_copy(summed[index].at[target], slot_of(index, seq), local.at[index])
                made.start()
                waits.append(made.wait)
                return
            made = remote(
                summed[index].at[target], slot_of(index, seq), send.at[index, step], recv.at[index, step], here.at(target)
            )
            made.start()
            waits.append(made.wait_send)

        for index in range(n, n + n_raw):
            cross(index)
        waiting = [functools.partial(deliver, index, step) for index in range(n + n_raw) for step in range(PLANE)]

        scale = HEAD ** (-0.5)
        d_slots = jnp.zeros(d_mixed.shape, f32)
        for first in range(0, d_ref.shape[0], PATCH):
            d_part = lax.dot_general(
                d_ref[first : first + PATCH, :], out_w[...], (((1,), (1,)), ((), ())), preferred_element_type=f32
            ).astype(low_type)
            chosen = chosen_rows(target_ref, first, PATCH)
            d_slots += lax.dot_general(chosen, d_part, (((0,), (0,)), ((), ())), preferred_element_type=f32)
        d_mixed[...] = d_slots.astype(low_type)
        take_some(waiting, 1)
        for first in range(0, model_width, 512):
            at = slice(first, first + 512)
            grad_refs[total - 1][:, at] = lax.dot_general(
                placed_ref[...], d_ref[:, at], (((0,), (0,)), ((), ())), preferred_element_type=f32
            ).astype(low_type)
            take_some(waiting, 1)
        cross(total - 1)
        d_probe_sum = jnp.zeros(probe_ref.shape, f32)
        for number in range(images):
            rows = slice(number * PATCH, (number + 1) * PATCH)
            d_here = d_mixed[number * LAT : (number + 1) * LAT, :]
            d_probe = []
            for first in range(0, width, HEAD):
                at = slice(first, first + HEAD)
                keys_here = keys_ref[rows, at]
                values = keys_ref[rows, width + first : width + first + HEAD]
                probs = image_probs_of(probe_ref[:, at], keys_here, scale)
                d_probs = lax.dot_general(
                    d_here[:, at], values, (((1,), (1,)), ((), ())), preferred_element_type=f32
                )
                d_scores = probs * (d_probs - jnp.sum(probs * d_probs, -1, keepdims=True))
                d_scores = d_scores.astype(low_type)
                d_probe.append(jnp.dot(d_scores, keys_here, preferred_element_type=f32) * scale)
                d_both[rows, at] = (
                    lax.dot_general(
                        d_scores, probe_ref[:, at], (((0,), (0,)), ((), ())), preferred_element_type=f32
                    )
                    * scale
                ).astype(low_type)
                d_both[rows, width + first : width + first + HEAD] = lax.dot_general(
                    probs.astype(low_type), d_here[:, at], (((0,), (0,)), ((), ())), preferred_element_type=f32
                ).astype(low_type)
            d_probe_sum += jnp.concatenate(d_probe, 1)
            take_some(waiting, 2)
        small_own[:LAT, :] = d_probe_sum
        small_own[LAT:, :] = vectors_ref[...]
        small_cross = remote(small_own, small_theirs, s_send.at[0], s_recv.at[0], here.img_peer)
        small_cross.start()
        span = picture_width // PLANE
        for part in range(PLANE):
            made = lax.dot_general(
                pictures_ref[:, part * span : (part + 1) * span],
                d_both[...],
                (((0,), (0,)), ((), ())),
                preferred_element_type=f32,
            ).astype(low_type)
            for kind in range(2):
                piece = made[:, kind * width : (kind + 1) * width]
                grad_refs[n + n_raw + kind][part, 0] = piece[: span // 2]
                grad_refs[n + n_raw + kind][part, 1] = piece[span // 2 :]
            take_some(waiting, 2)
        for kind in range(2):
            cross(n + n_raw + kind)
        small_cross.wait()
        small_mine[...] = small_own[...] + small_theirs[...]
        small_all[seq] = small_mine[...]
        small_copies = []
        for step, peer in enumerate(ring, 1):
            made = remote(small_mine, small_all.at[seq], s_send.at[step], s_recv.at[step], peer)
            made.start()
            small_copies.append(made)
        take_some(waiting, len(waiting))
        for index in (total - 1, total - 3, total - 2):
            for step in range(PLANE):
                deliver(index, step)
        for made in small_copies:
            made.wait()
        sums_out[...] = small_all[...]
        latent_part = jnp.zeros(lat_mine.shape, f32)
        for source in range(PLANE):
            given = small_all[source, :LAT, :]
            at = slice(source * width, (source + 1) * width)
            query_out[:, at] = jnp.dot(
                latents_ref[...], given, precision=HIGHEST_PRECISION, preferred_element_type=f32
            )
            latent_part += lax.dot_general(
                given,
                query_ref[:, at],
                (((1,), (1,)), ((), ())),
                precision=HIGHEST_PRECISION,
                preferred_element_type=f32,
            )
        lat_mine[...] = latent_part
        last = remote(lat_mine, lat_theirs, s_send.at[PLANE], s_recv.at[PLANE], here.tp_peer)
        last.start()
        last.wait()
        latent_out[...] = lat_mine[...] + lat_theirs[...]
        for index in range(total):
            for step in range(1, PLANE):
                source = lax.rem(seq + PLANE - step, PLANE)
                at = slot_of(index, source)
                remote(at, at, send.at[index, step], recv.at[index, step], here.core).wait_recv()
        for wait in waits:
            wait()
        for made in crossings.values():
            made.wait_send()

    outs = []
    for block, side in zip(blocks, all_sides):
        shape = (block[0], PLANE * block[1]) if side == INWARD else (PLANE * block[0], block[1])
        outs.append(jax.ShapeDtypeStruct(shape, low_type))
    lat_shape = (latents_t.shape[1], latents_t.shape[0])
    small_shapes = [
        jax.ShapeDtypeStruct((PLANE,) + small_shape, f32),
        jax.ShapeDtypeStruct(query_rows.shape, f32),
        jax.ShapeDtypeStruct(lat_shape, f32),
    ]
    n_cross = n_raw + n_image
    made = lazy_call(
        kernel,
        [
            target_rows,
            d_rows,
            pictures,
            keys,
            probe,
            placed,
            out_part,
            *[grad for grad, _ in pairs],
            *raw,
            *[given for _, given in pairs],
            vectors,
            latents_t,
            query_rows,
        ],
        [ON_CHIP] * (7 + n + n_raw + n + 3),
        outs + small_shapes,
        [ANYWHERE] * total + [ON_CHIP] * 3,
        [pltpu.VMEM(item.shape, low_type) for item in image_shapes]
        + [pltpu.VMEM((PLANE,) + tuple(block), low_type) for block in blocks[n:]]
        + [pltpu.VMEM((PLANE,) + tuple(block), low_type) for block in blocks]
        + [
            pltpu.VMEM(small_shape, f32),
            pltpu.VMEM(small_shape, f32),
            pltpu.VMEM(small_shape, f32),
            pltpu.VMEM((PLANE,) + small_shape, f32),
            pltpu.VMEM(lat_shape, f32),
            pltpu.VMEM(lat_shape, f32),
            pltpu.VMEM((d_rows.shape[0], width), low_type),
            pltpu.VMEM((images * PATCH, 2 * width), low_type),
            dma((n_cross, PLANE)),
            dma((n_cross, PLANE)),
            dma((total, PLANE)),
            dma((total, PLANE)),
            dma((total,)),
            dma((PLANE + 1,)),
            dma((PLANE + 1,)),
        ],
        cid,
    )
    return made[:total], made[total:]


def widened(arrays):
    def kernel(*refs):
        for src, dst in zip(refs[: len(arrays)], refs[len(arrays) :]):
            dst[...] = src[...].astype(jnp.float32)

    return pl.pallas_call(
        kernel,
        out_shape=tuple(jax.ShapeDtypeStruct(array.shape, jnp.float32) for array in arrays),
        in_specs=[ON_CHIP] * len(arrays),
        out_specs=tuple([ON_CHIP] * len(arrays)),
        compiler_params=pltpu.CompilerParams(vmem_limit_bytes=VMEM_BYTES),
    )(*arrays)


IMAGES_A_STEP = 4


def image_probs_of(probe, keys, scale):
    scores = lax.dot_general(
        probe * scale, keys, (((1,), (1,)), ((), ())), preferred_element_type=jnp.float32
    )
    weights = jnp.exp(scores - jnp.max(scores, -1, keepdims=True))
    return weights * (1.0 / jnp.sum(weights, -1, keepdims=True))


def xpos_tables(position, width):
    cosine, sine, growth = (table[:, 0, :] for table in xpos_factors(position, HEAD // 2))
    repeats = width // HEAD
    return (
        jnp.tile(cosine, (1, 2 * repeats)),
        jnp.tile(jnp.concatenate([-sine, sine], 1), (1, repeats)),
        jnp.tile(growth, (1, 2 * repeats)),
    )


def halves_swapped(rows):
    width, half = rows.shape[1], HEAD // 2
    lane = lax.broadcasted_iota(jnp.int32, rows.shape, 1)
    ahead = pltpu.roll(rows, width - half, 1)
    behind = pltpu.roll(rows, half, 1)
    return jnp.where(lane % HEAD < half, ahead, behind)


def allowed_part(segment_column, segment_row, first, count, keys):
    row = first + lax.broadcasted_iota(jnp.int32, (count, keys), 0)
    column = lax.broadcasted_iota(jnp.int32, (count, keys), 1)
    same = segment_column[pl.ds(first, count), :] == segment_row[:, :keys]
    return same & (column <= row)


ATTEND_ROWS = 256


def as_lanes(columns):
    rows = columns[0].shape[0]
    lane = lax.broadcasted_iota(jnp.int32, (rows, LANES), 1)
    joined = jnp.zeros((rows, LANES), jnp.float32)
    for number, column in enumerate(columns):
        joined = jnp.where(lane == number, column, joined)
    return joined.T[:8, :]


def norm_rows(rows, gain, shift):
    center = rows - jnp.mean(rows, -1, keepdims=True)
    factor = lax.rsqrt(jnp.mean(center * center, -1, keepdims=True) + EPSILON)
    normal = center * factor
    return (normal * gain + shift, normal, factor)


def dot32(left, right):
    return jnp.dot(left, right, preferred_element_type=jnp.float32)


def on_plane(
    text,
    segment,
    features,
    image_count,
    image_slot,
    cotangent,
    input_gain,
    input_shift,
    query_weight,
    key_weight,
    value_weight,
    inner_gain,
    inner_shift,
    out_weight,
    middle_gain,
    middle_shift,
    up_weight,
    up_bias,
    hidden_gain,
    hidden_shift,
    down_weight,
    latents,
    resample_query,
    resample_key,
    resample_value,
    resample_out,
):
    f32, low = jnp.float32, jnp.bfloat16
    row_count, model_width = text.shape[1], text.shape[2]
    group_rows = segment.shape[1]
    seq_rank = lax.axis_index(SEQ)
    image_slots = features.shape[1]
    image_total = image_slot.shape[1]
    half_width = query_weight.shape[1]
    own_width = half_width // PLANE
    own_heads = own_width // HEAD
    score_scale = HEAD ** (-0.5)

    rows, own = intake(
        (features[0].reshape(image_slots * PATCH, features.shape[3]),),
        (
            resample_key,
            resample_value,
            resample_query,
            latents,
            resample_out,
        ),
        (INWARD, INWARD, INWARD, SHARED, OUTWARD),
        1,
    )
    (pictures,) = rows
    image_key_own, image_value_own, probe_own, latent_all, image_out_own = own

    slot_range = jnp.arange(image_total, dtype=jnp.int32)
    live = slot_range % IMG_DEV < jnp.repeat(image_count[0], IMG_DEV)
    block_count = group_rows // LAT
    owner = (image_slot[0][None, :] == jnp.arange(block_count, dtype=jnp.int32)[:, None]) & live[None, :]
    taken = jnp.repeat(jnp.any(owner, 1).astype(f32), LAT)[:, None]
    taken_own = lax.dynamic_slice_in_dim(taken, seq_rank * row_count, row_count, 0)
    first_rows = jnp.where(live, image_slot[0] * LAT, -LAT)
    target_rows = (first_rows[:, None] + jnp.arange(LAT, dtype=jnp.int32)[None, :]).reshape(1, -1)

    def wide(vector):
        return vector.astype(f32)[None, :]

    def own_part(vector):
        width = vector.shape[0] // PLANE
        return lax.dynamic_slice_in_dim(vector, seq_rank * width, width, 0)

    def begin(total, piece, views, outs):
        text_view, taken_view, gain, shift = views
        embed = total.astype(jnp.bfloat16).astype(jnp.float32)
        mixed = jnp.where(taken_view[...] > 0.5, embed, text_view[...].astype(jnp.float32))
        outs[0][...] = mixed
        return norm_rows(mixed, gain[...], shift[...])[0].astype(jnp.bfloat16)

    rows_wide = jax.ShapeDtypeStruct((row_count, model_width), f32)
    (image_keys, mixed_placed, probe), (mixed_in, normed), (qkv_own, out_own) = exchange(
        ImageFront(
            pictures, image_key_own, image_value_own, latent_all, probe_own, target_rows
        ),
        [
            Stream(
                group_rows,
                None,
                image_out_own,
                False,
                (text[0], taken_own, wide(input_gain), wide(input_shift)),
                (ROWS, ROWS, ALL, ALL),
                ((rows_wide, ROWS),),
                begin,
                True,
            )
        ],
        [
            ChainWeights(
                (query_weight, key_weight, value_weight, out_weight),
                (INWARD, INWARD, INWARD, OUTWARD),
                ((0, 0), (0, own_width), (0, 2 * own_width), (1, 0)),
            )
        ],
        3,
    )

    segment_all = segment[0]
    row_index = jnp.arange(group_rows, dtype=jnp.int32)
    earlier = (row_index[None, :] < row_index[:, None]) & (segment_all[None, :] == segment_all[:, None])
    tables = xpos_tables(jnp.sum(earlier.astype(f32), 1), own_width)
    cot_late, _ = lax.optimization_barrier((cotangent[0], normed))
    cot_all = lax.all_gather(cot_late, SEQ, axis=0, tiled=True)
    inner_gain_own = wide(own_part(inner_gain))
    def middle_step(total, piece, views, outs):
        mixed_view, gain, shift = views
        middle = mixed_view[...] + total
        outs[0][...] = middle
        return norm_rows(middle, gain[...], shift[...])[0].astype(jnp.bfloat16)

    attend_made, (middle, lifted), (up_own, down_own) = exchange(
        AttendFront(
            normed, qkv_own, tables, segment_all, inner_gain_own, wide(own_part(inner_shift)), model_width
        ),
        [
            Stream(
                group_rows,
                None,
                out_own,
                False,
                (mixed_in, wide(middle_gain), wide(middle_shift)),
                (ROWS, ALL, ALL),
                ((rows_wide, ROWS),),
                middle_step,
                True,
            )
        ],
        [ChainWeights((up_weight, down_weight), (INWARD, OUTWARD), ((0, 0), (1, 0)))],
        5,
    )
    *attended_kept, inner_low, inner_hat, inner_factor = attend_made
    query_rot, keys_rot, values, attended, log_total = attended_kept
    own_hidden = up_own.shape[1]

    hidden_gain_own = wide(own_part(hidden_gain))
    def last_step(total, piece, views, outs):
        outs[0][...] = (views[0][...] + total).astype(jnp.bfloat16)

    vector_out = jax.ShapeDtypeStruct((1, model_width), f32)

    def norm_back_step(total, piece, views, outs):
        rows_view, carried_view, gain = views
        rows_in = rows_view[...]
        center = rows_in - jnp.mean(rows_in, -1, keepdims=True)
        factor = lax.rsqrt(jnp.mean(center * center, -1, keepdims=True) + EPSILON)
        normal = center * factor
        grad = carried_view[...].astype(jnp.float32) + full_back(total, normal, factor, gain[...])
        outs[0][...] = grad
        if piece == 0:
            outs[1][...] = jnp.zeros_like(outs[1])
            outs[2][...] = jnp.zeros_like(outs[2])
        outs[1][...] += jnp.sum(total * normal, 0, keepdims=True)
        outs[2][...] += jnp.sum(total, 0, keepdims=True)
        return grad.astype(jnp.bfloat16)

    hidden_made, (d_middle, middle_gain_grad, middle_shift_grad, d_branch) = exchange(
        HiddenFront(
            lifted,
            up_own,
            wide(own_part(up_bias)),
            cot_all,
            down_own,
            hidden_gain_own,
            wide(own_part(hidden_shift)),
            FF,
        ),
        [
            Stream(
                group_rows,
                None,
                up_own,
                True,
                (middle, cotangent[0], wide(middle_gain)),
                (ROWS, ROWS, ALL),
                ((rows_wide, ROWS), (vector_out, ALL), (vector_out, ALL)),
                norm_back_step,
                True,
            )
        ],
        [],
        8,
    )

    settled, _, hidden_vectors, *hidden_grads = hidden_made
    back_made, (d_mixed, input_gain_grad, input_shift_grad, d_rows), (result,), hidden_theirs = exchange(
        AttendBackFront(
            d_branch,
            out_own,
            inner_hat,
            inner_factor,
            inner_gain_own,
            (attended, query_rot, keys_rot, values, log_total),
            tables,
            segment_all,
            normed,
            inner_low,
            model_width,
        ),
        [
            Stream(
                group_rows,
                None,
                qkv_own,
                True,
                (mixed_in, d_middle, wide(input_gain)),
                (ROWS, ROWS, ALL),
                ((rows_wide, ROWS), (vector_out, ALL), (vector_out, ALL)),
                norm_back_step,
                True,
            ),
        ],
        [CrossGrads(hidden_grads, (INWARD, OUTWARD))],
        10,
        Stream(
            group_rows,
            settled,
            down_own,
            False,
            (middle,),
            (ROWS,),
            ((jax.ShapeDtypeStruct((row_count, model_width), low), ROWS),),
            last_step,
            False,
        ),
    )
    inner_vectors, *layer_grads = back_made
    text_grad = jnp.where(taken_own > 0.5, 0.0, d_mixed)

    own_vectors = jnp.concatenate(
        [inner_vectors[0], inner_vectors[1], hidden_vectors[2], hidden_vectors[0], hidden_vectors[1]]
    )
    row_vectors = jnp.concatenate(
        [input_gain_grad[0], input_shift_grad[0], middle_gain_grad[0], middle_shift_grad[0]]
    )
    packed = jnp.concatenate([row_vectors, own_vectors]).reshape(-1, LANES)
    spare = -packed.shape[0] % 8
    packed = jnp.pad(packed, ((0, spare), (0, 0)))
    layer_sides = (INWARD, INWARD, INWARD, OUTWARD)
    owned, (spread, resample_query_grad, latent_grad) = finale(
        list(zip(hidden_grads, hidden_theirs)),
        (INWARD, OUTWARD),
        layer_grads,
        layer_sides,
        (d_rows, pictures, image_keys, probe, mixed_placed, image_out_own, target_rows),
        packed,
        latents.astype(f32).T,
        resample_query.astype(f32),
        12,
    )
    up_sum, down_sum, query_sum, key_sum, value_sum, out_sum, image_key_sum, image_value_sum, image_out_sum = widened(owned)
    spread = spread.reshape(PLANE, -1)
    first = LAT * own_width
    row_sums = spread[:, first : first + row_vectors.shape[0]].sum(0).reshape(4, model_width)
    own_sums = spread[:, first + row_vectors.shape[0] :]

    def joined(start, width):
        return own_sums[:, start : start + width].reshape(-1)

    inner_gain_sum = joined(0, own_width)
    inner_shift_sum = joined(own_width, own_width)
    up_bias_sum = joined(2 * own_width, own_hidden)
    hidden_gain_sum = joined(2 * own_width + own_hidden, own_hidden)
    hidden_shift_sum = joined(2 * own_width + 2 * own_hidden, own_hidden)

    return (
        result[None],
        text_grad[None],
        row_sums[0],
        row_sums[1],
        query_sum,
        key_sum,
        value_sum,
        inner_gain_sum,
        inner_shift_sum,
        out_sum,
        row_sums[2],
        row_sums[3],
        up_sum,
        up_bias_sum,
        hidden_gain_sum,
        hidden_shift_sum,
        down_sum,
        latent_grad,
        resample_query_grad,
        image_key_sum,
        image_value_sum,
        image_out_sum,
    )


def solution(mesh):
    placed = (
        P(IMG, SEQ, None),
        P(IMG, None),
        P(IMG, SEQ, None, None),
        P(IMG, None),
        P(IMG, None),
        P(IMG, SEQ, None),
        P(),
        P(),
        P((SEQ, IMG), TP),
        P((SEQ, IMG), TP),
        P((SEQ, IMG), TP),
        P(TP),
        P(TP),
        P(TP, (SEQ, IMG)),
        P(),
        P(),
        P((SEQ, IMG), TP),
        P(TP),
        P(TP),
        P(TP),
        P(TP, (SEQ, IMG)),
        P(None, (SEQ, IMG)),
        P((SEQ, IMG), TP),
        P((SEQ, IMG), TP),
        P((SEQ, IMG), TP),
        P(TP, (SEQ, IMG)),
    )
    return jax.shard_map(
        on_device if narrow_heads(mesh) else on_plane,
        mesh=mesh,
        in_specs=placed,
        out_specs=(
            P(IMG, SEQ, None),
            P(IMG, SEQ, None),
            P(),
            P(),
            P((SEQ, IMG), TP),
            P((SEQ, IMG), TP),
            P((SEQ, IMG), TP),
            P(TP),
            P(TP),
            P(TP, (SEQ, IMG)),
            P(),
            P(),
            P((SEQ, IMG), TP),
            P(TP),
            P(TP),
            P(TP),
            P(TP, (SEQ, IMG)),
            P(None, (SEQ, IMG)),
            P((SEQ, IMG), TP),
            P((SEQ, IMG), TP),
            P((SEQ, IMG), TP),
            P(TP, (SEQ, IMG)),
        ),
        check_vma=False,
    )
```

```python
import functools

import jax
import jax.numpy as jnp
from jax import lax
from jax.experimental import pallas as pl
from jax.experimental.pallas import tpu as pltpu
from jax.sharding import PartitionSpec as P

SEQ, TP, IMG = "seq", "tp", "img"
HEAD = 64
FF = 8192
PATCH = 256
LAT = 64
SEQ_MAX = 2048
IMG_DEV = 2


EPSILON = 1e-05
HIGHEST_PRECISION = lax.Precision.HIGHEST


def shortened(x):

    def short(part):
        return part.astype(jnp.bfloat16) if part.dtype == jnp.float32 else part

    return jax.tree.map(short, x)


def xpos_factors(position, half_size):
    ladder = jnp.arange(half_size, dtype=jnp.float32)
    frequency = jnp.exp(ladder * (-2.0 * jnp.log(10000.0) / (2.0 * half_size)))
    decay_base = (ladder / half_size + 0.4) / 1.4
    angles = position[:, None] * frequency[None, :]
    growth = jnp.exp(position[:, None] / 512.0 * jnp.log(decay_base)[None, :])
    return (jnp.cos(angles)[:, None, :], jnp.sin(angles)[:, None, :], growth[:, None, :])


def rotate(inputs, cosine, sine_table, factor):
    half_size = inputs.shape[-1] // 2
    first_half = inputs[..., :half_size]
    second_half = inputs[..., half_size:]
    turned = jnp.concatenate(
        [
            first_half * cosine - second_half * sine_table,
            first_half * sine_table + second_half * cosine,
        ],
        -1,
    )
    return turned * jnp.concatenate([factor, factor], -1)


def rotate_back(gradient, cosine, sine_table, factor):
    half_size = gradient.shape[-1] // 2
    scaled = gradient * jnp.concatenate([factor, factor], -1)
    first_half = scaled[..., :half_size]
    second_half = scaled[..., half_size:]
    return jnp.concatenate(
        [
            first_half * cosine + second_half * sine_table,
            second_half * cosine - first_half * sine_table,
        ],
        -1,
    )


def tp_total(inputs):
    return jax.tree.map(lambda part: part.astype(jnp.float32), lax.psum(shortened(inputs), TP))


def full_norm(inputs, norm_gain, norm_shift):
    center = inputs - jnp.mean(inputs, -1, keepdims=True)
    spread = jnp.mean(center * center, -1, keepdims=True)
    factor = lax.rsqrt(spread + EPSILON)
    normal = center * factor
    return (normal * norm_gain + norm_shift, normal, factor)


def full_back(gradient, normal, factor, norm_gain):
    scaled = gradient * norm_gain
    return factor * (
        scaled
        - jnp.mean(scaled, -1, keepdims=True)
        - normal * jnp.mean(scaled * normal, -1, keepdims=True)
    )


def split_norm(inputs, norm_gain, norm_shift, full_width):
    totals = tp_total(
        (jnp.sum(inputs, -1, keepdims=True), jnp.sum(inputs * inputs, -1, keepdims=True))
    )
    average = totals[0] / full_width
    spread = totals[1] / full_width - average * average
    factor = lax.rsqrt(spread + EPSILON)
    normal = (inputs - average) * factor
    return (normal * norm_gain + norm_shift, normal, factor)


def split_back(gradient, normal, factor, norm_gain, full_width):
    scaled = gradient * norm_gain
    totals = tp_total(
        (jnp.sum(scaled, -1, keepdims=True), jnp.sum(scaled * normal, -1, keepdims=True))
    )
    return factor * (scaled - totals[0] / full_width - normal * (totals[1] / full_width))


def attend_piece(
    running, query_rot, key_piece, value_piece, row_index, row_segment, segment_all, score_scale
):
    heads_local = query_rot.shape[1]
    amount = key_piece.shape[0]
    block_size = 1024

    def step(state_in, number):
        first_row = number * block_size
        key_block = lax.dynamic_slice_in_dim(key_piece, first_row, block_size, 0).reshape(
            block_size, heads_local, -1
        )
        value_block = lax.dynamic_slice_in_dim(value_piece, first_row, block_size, 0).reshape(
            block_size, heads_local, -1
        )
        key_index = first_row + jnp.arange(block_size, dtype=jnp.int32)
        key_segment = lax.dynamic_slice_in_dim(segment_all, first_row, block_size, 0)
        scores = (
            jnp.einsum("qhd,khd->hqk", query_rot, key_block, preferred_element_type=jnp.float32)
            * score_scale
        )
        allowed = (key_index[None, :] <= row_index[:, None]) & (
            key_segment[None, :] == row_segment[:, None]
        )
        scores = jnp.where(allowed[None], scores, -1e30)
        best_old, total_old, accum_old = state_in
        best_new = jnp.maximum(best_old, jnp.max(scores, -1))
        weights = jnp.where(allowed[None], jnp.exp(scores - best_new[..., None]), 0.0)
        shrink = jnp.exp(best_old - best_new)
        total_new = total_old * shrink + jnp.sum(weights, -1)
        added = jnp.einsum(
            "hqk,khd->qhd",
            weights.astype(jnp.bfloat16),
            value_block,
            preferred_element_type=jnp.float32,
        )
        accum_new = accum_old * shrink.T[:, :, None] + added
        return ((best_new, total_new, accum_new), None)

    return lax.scan(step, running, jnp.arange(amount // block_size, dtype=jnp.int32))[0]


def attend_back(
    query_rot,
    key_all,
    value_all,
    grad_attended,
    log_total,
    delta,
    row_index,
    row_segment,
    segment_all,
    score_scale,
):
    heads_local = query_rot.shape[1]
    amount = key_all.shape[0]
    block_size = 1024

    def step(dquery, number):
        first_row = number * block_size
        key_block = lax.dynamic_slice_in_dim(key_all, first_row, block_size, 0).reshape(
            block_size, heads_local, -1
        )
        value_block = lax.dynamic_slice_in_dim(value_all, first_row, block_size, 0).reshape(
            block_size, heads_local, -1
        )
        key_index = first_row + jnp.arange(block_size, dtype=jnp.int32)
        key_segment = lax.dynamic_slice_in_dim(segment_all, first_row, block_size, 0)
        scores = (
            jnp.einsum("qhd,khd->hqk", query_rot, key_block, preferred_element_type=jnp.float32)
            * score_scale
        )
        allowed = (key_index[None, :] <= row_index[:, None]) & (
            key_segment[None, :] == row_segment[:, None]
        )
        weights = jnp.where(
            allowed[None],
            jnp.exp(jnp.where(allowed[None], scores, -1e30) - log_total[..., None]),
            0.0,
        )
        dweights = jnp.einsum(
            "qhd,khd->hqk", grad_attended, value_block, preferred_element_type=jnp.float32
        )
        dscores = (weights * (dweights - delta[..., None])).astype(jnp.bfloat16)
        dquery = (
            dquery
            + jnp.einsum("hqk,khd->qhd", dscores, key_block, preferred_element_type=jnp.float32)
            * score_scale
        )
        dkeys = (
            jnp.einsum("hqk,qhd->khd", dscores, query_rot, preferred_element_type=jnp.float32)
            * score_scale
        )
        dvalues = jnp.einsum(
            "hqk,qhd->khd",
            weights.astype(jnp.bfloat16),
            grad_attended,
            preferred_element_type=jnp.float32,
        )
        return (dquery, (dkeys, dvalues))

    start_grad = jnp.zeros(query_rot.shape, jnp.float32)
    dquery, outputs = lax.scan(step, start_grad, jnp.arange(amount // block_size, dtype=jnp.int32))
    return (dquery, outputs[0].reshape(amount, -1), outputs[1].reshape(amount, -1))


def on_device(
    text,
    segment,
    features,
    image_count,
    image_slot,
    cotangent,
    input_gain,
    input_shift,
    query_weight,
    key_weight,
    value_weight,
    inner_gain,
    inner_shift,
    out_weight,
    middle_gain,
    middle_shift,
    up_weight,
    up_bias,
    hidden_gain,
    hidden_shift,
    down_weight,
    latents,
    resample_query,
    resample_key,
    resample_value,
    resample_out,
):
    row_count = text.shape[1]
    model_width = text.shape[2]
    group_rows = segment.shape[1]
    seq_rank = lax.axis_index(SEQ)
    gathered_in = (
        lax.all_gather(query_weight, (SEQ, IMG), axis=0, tiled=True),
        lax.all_gather(key_weight, (SEQ, IMG), axis=0, tiled=True),
        lax.all_gather(value_weight, (SEQ, IMG), axis=0, tiled=True),
        lax.all_gather(up_weight, (SEQ, IMG), axis=0, tiled=True),
        lax.all_gather(resample_query, (SEQ, IMG), axis=0, tiled=True),
        lax.all_gather(resample_key, (SEQ, IMG), axis=0, tiled=True),
        lax.all_gather(resample_value, (SEQ, IMG), axis=0, tiled=True),
    )
    query_full, key_full, value_full, up_full, probe_full, image_key_full, image_value_full = (
        gathered_in
    )
    gathered_out = (
        lax.all_gather(out_weight, (SEQ, IMG), axis=1, tiled=True),
        lax.all_gather(down_weight, (SEQ, IMG), axis=1, tiled=True),
        lax.all_gather(resample_out, (SEQ, IMG), axis=1, tiled=True),
        lax.all_gather(latents, (SEQ, IMG), axis=1, tiled=True),
    )
    out_full, down_full, image_out_full, latent_full = gathered_out
    half_width = query_full.shape[1]
    heads_local = half_width // HEAD
    score_scale = HEAD ** (-0.5)
    gelu_exact = functools.partial(jax.nn.gelu, approximate=False)
    image_slots = features.shape[1]
    pictures = features[0].reshape(image_slots * PATCH, features.shape[3])
    probe = (
        jnp.dot(latent_full, probe_full, preferred_element_type=jnp.float32)
        .astype(jnp.bfloat16)
        .reshape(LAT, heads_local, HEAD)
    )
    image_keys = (
        jnp.dot(pictures, image_key_full, preferred_element_type=jnp.float32)
        .astype(jnp.bfloat16)
        .reshape(image_slots, PATCH, heads_local, HEAD)
    )
    image_values = (
        jnp.dot(pictures, image_value_full, preferred_element_type=jnp.float32)
        .astype(jnp.bfloat16)
        .reshape(image_slots, PATCH, heads_local, HEAD)
    )
    image_scores = (
        jnp.einsum("qhd,iphd->ihqp", probe, image_keys, preferred_element_type=jnp.float32)
        * score_scale
    )
    image_probs = jax.nn.softmax(image_scores, -1)
    image_mixed = jnp.einsum(
        "ihqp,iphd->iqhd",
        image_probs.astype(jnp.bfloat16),
        image_values,
        preferred_element_type=jnp.float32,
    )
    image_mixed = image_mixed.astype(jnp.bfloat16).reshape(image_slots * LAT, half_width)
    embed = tp_total(jnp.dot(image_mixed, image_out_full, preferred_element_type=jnp.float32))
    embed = embed.astype(jnp.bfloat16).reshape(image_slots, LAT, model_width)
    image_total = image_slot.shape[1]
    slot_range = jnp.arange(image_total, dtype=jnp.int32)
    live = slot_range % IMG_DEV < jnp.repeat(image_count[0], IMG_DEV)
    block_local = row_count // LAT
    block_count = group_rows // LAT
    block_ids = seq_rank * block_local + jnp.arange(block_local, dtype=jnp.int32)
    owner = ((image_slot[0][None, :] == block_ids[:, None]) & live[None, :]).astype(jnp.float32)
    owner_low = owner.astype(jnp.bfloat16)
    taken = jnp.sum(owner, 1) > 0.5
    chosen = owner_low
    placed = jnp.einsum(
        "bi,ild->bld",
        chosen,
        lax.all_gather(embed, SEQ, axis=0, tiled=True),
        preferred_element_type=jnp.float32,
    )
    text_blocks = text[0].astype(jnp.float32).reshape(block_local, LAT, model_width)
    mixed_in = jnp.where(taken[:, None, None], placed, text_blocks).reshape(row_count, model_width)
    segment_all = segment[0]
    docs_count = 3 * (group_rows // min(SEQ_MAX, group_rows))
    marks = (segment_all[:, None] == jnp.arange(docs_count, dtype=jnp.int32)[None, :]).astype(
        jnp.int32
    )
    earlier_rows = jnp.cumsum(marks, 0) - marks
    position_all = jnp.sum(earlier_rows * marks, 1)
    first_local = seq_rank * row_count
    row_index = first_local + jnp.arange(row_count, dtype=jnp.int32)
    row_segment = lax.dynamic_slice_in_dim(segment_all, first_local, row_count, 0)
    position = lax.dynamic_slice_in_dim(position_all, first_local, row_count, 0).astype(jnp.float32)
    cosine, sine_table, growth = xpos_factors(position, HEAD // 2)
    input_out, input_hat, input_factor = full_norm(
        mixed_in, input_gain.astype(jnp.float32), input_shift.astype(jnp.float32)
    )
    normed = input_out.astype(jnp.bfloat16)
    query_lin = jnp.dot(normed, query_full, preferred_element_type=jnp.float32).reshape(
        row_count, heads_local, HEAD
    )
    key_lin = jnp.dot(normed, key_full, preferred_element_type=jnp.float32).reshape(
        row_count, heads_local, HEAD
    )
    value_lin = jnp.dot(normed, value_full, preferred_element_type=jnp.float32)
    query_rot = rotate(query_lin, cosine, sine_table, growth).astype(jnp.bfloat16)
    keys_rot = (
        rotate(key_lin, cosine, sine_table, 1.0 / growth)
        .astype(jnp.bfloat16)
        .reshape(row_count, half_width)
    )
    values_low = value_lin.astype(jnp.bfloat16)
    start_state = (
        jnp.full((heads_local, row_count), -1e30, jnp.float32),
        jnp.zeros((heads_local, row_count), jnp.float32),
        jnp.zeros((row_count, heads_local, HEAD), jnp.float32),
    )
    best, weight_total, accum = attend_piece(
        start_state,
        query_rot,
        lax.all_gather(keys_rot, SEQ, axis=0, tiled=True),
        lax.all_gather(values_low, SEQ, axis=0, tiled=True),
        row_index,
        row_segment,
        segment_all,
        score_scale,
    )
    attended = accum / weight_total.T[:, :, None]
    log_total = best + jnp.log(weight_total)
    inner_out, inner_hat, inner_factor = split_norm(
        attended.reshape(row_count, half_width),
        inner_gain.astype(jnp.float32),
        inner_shift.astype(jnp.float32),
        model_width,
    )
    inner_low = inner_out.astype(jnp.bfloat16)
    middle = mixed_in + tp_total(jnp.dot(inner_low, out_full, preferred_element_type=jnp.float32))
    lifted_out, lifted_hat, lifted_factor = full_norm(
        middle, middle_gain.astype(jnp.float32), middle_shift.astype(jnp.float32)
    )
    lifted = lifted_out.astype(jnp.bfloat16)
    hidden_pre = jnp.dot(lifted, up_full, preferred_element_type=jnp.float32) + up_bias.astype(
        jnp.float32
    )
    activated, gelu_pull = jax.vjp(gelu_exact, hidden_pre)
    settled_out, settled_hat, settled_factor = split_norm(
        activated, hidden_gain.astype(jnp.float32), hidden_shift.astype(jnp.float32), FF
    )
    settled = settled_out.astype(jnp.bfloat16)
    final_rows = middle + tp_total(jnp.dot(settled, down_full, preferred_element_type=jnp.float32))
    result = final_rows.astype(jnp.bfloat16).reshape(1, row_count, model_width)
    grad_low = cotangent[0]
    grad_rows = grad_low.astype(jnp.float32)
    down_grad = jnp.dot(settled.T, grad_low, preferred_element_type=jnp.float32)
    d_settled = jnp.dot(grad_low, down_full.T, preferred_element_type=jnp.float32)
    hidden_gain_grad = jnp.sum(d_settled * settled_hat, 0)
    hidden_shift_grad = jnp.sum(d_settled, 0)
    d_activated = split_back(
        d_settled, settled_hat, settled_factor, hidden_gain.astype(jnp.float32), FF
    )
    d_hidden = gelu_pull(d_activated)[0].astype(jnp.bfloat16)
    up_bias_grad = jnp.sum(d_hidden.astype(jnp.float32), 0)
    up_grad = jnp.dot(lifted.T, d_hidden, preferred_element_type=jnp.float32)
    d_lifted = tp_total(jnp.dot(d_hidden, up_full.T, preferred_element_type=jnp.float32))
    middle_gain_grad = jnp.sum(d_lifted * lifted_hat, 0)
    middle_shift_grad = jnp.sum(d_lifted, 0)
    d_middle = grad_rows + full_back(
        d_lifted, lifted_hat, lifted_factor, middle_gain.astype(jnp.float32)
    )
    d_branch = d_middle.astype(jnp.bfloat16)
    out_grad = jnp.dot(inner_low.T, d_branch, preferred_element_type=jnp.float32)
    d_inner = jnp.dot(d_branch, out_full.T, preferred_element_type=jnp.float32)
    inner_gain_grad = jnp.sum(d_inner * inner_hat, 0)
    inner_shift_grad = jnp.sum(d_inner, 0)
    d_attended = split_back(
        d_inner, inner_hat, inner_factor, inner_gain.astype(jnp.float32), model_width
    )
    d_attended = d_attended.astype(jnp.bfloat16).reshape(row_count, heads_local, HEAD)
    delta = jnp.sum(d_attended.astype(jnp.float32) * attended, -1).T
    key_back, value_back = (
        lax.all_gather(keys_rot, SEQ, axis=0, tiled=True),
        lax.all_gather(values_low, SEQ, axis=0, tiled=True),
    )
    d_query_rot, d_key_term, d_value_term = attend_back(
        query_rot,
        key_back,
        value_back,
        d_attended,
        log_total,
        delta,
        row_index,
        row_segment,
        segment_all,
        score_scale,
    )
    d_key_sum, d_value_sum = (
        lax.psum_scatter(
            d_key_term.astype(jnp.bfloat16), SEQ, scatter_dimension=0, tiled=True
        ).astype(jnp.float32),
        lax.psum_scatter(
            d_value_term.astype(jnp.bfloat16), SEQ, scatter_dimension=0, tiled=True
        ).astype(jnp.float32),
    )
    d_query_lin = (
        rotate_back(d_query_rot, cosine, sine_table, growth)
        .astype(jnp.bfloat16)
        .reshape(row_count, half_width)
    )
    d_key_lin = (
        rotate_back(
            d_key_sum.reshape(row_count, heads_local, HEAD), cosine, sine_table, 1.0 / growth
        )
        .astype(jnp.bfloat16)
        .reshape(row_count, half_width)
    )
    d_value_lin = d_value_sum.astype(jnp.bfloat16)
    query_grad = jnp.dot(normed.T, d_query_lin, preferred_element_type=jnp.float32)
    key_grad = jnp.dot(normed.T, d_key_lin, preferred_element_type=jnp.float32)
    value_grad = jnp.dot(normed.T, d_value_lin, preferred_element_type=jnp.float32)
    d_normed_part = (
        jnp.dot(d_query_lin, query_full.T, preferred_element_type=jnp.float32)
        + jnp.dot(d_key_lin, key_full.T, preferred_element_type=jnp.float32)
        + jnp.dot(d_value_lin, value_full.T, preferred_element_type=jnp.float32)
    )
    d_normed = tp_total(d_normed_part)
    input_gain_grad = jnp.sum(d_normed * input_hat, 0)
    input_shift_grad = jnp.sum(d_normed, 0)
    d_mixed = d_middle + full_back(
        d_normed, input_hat, input_factor, input_gain.astype(jnp.float32)
    )
    d_blocks = d_mixed.reshape(block_local, LAT, model_width)
    text_grad = jnp.where(taken[:, None, None], 0.0, d_blocks).reshape(1, row_count, model_width)
    my_target = lax.dynamic_slice_in_dim(image_slot[0], seq_rank * image_slots, image_slots, 0)
    my_live = lax.dynamic_slice_in_dim(live, seq_rank * image_slots, image_slots, 0)
    owner_mine = (
        (jnp.arange(block_count, dtype=jnp.int32)[:, None] == my_target[None, :]) & my_live[None, :]
    ).astype(jnp.bfloat16)
    chosen = owner_mine
    d_embed = jnp.einsum(
        "bi,bld->ild",
        chosen,
        lax.all_gather(d_blocks.astype(jnp.bfloat16), SEQ, axis=0, tiled=True),
        preferred_element_type=jnp.float32,
    )
    d_embed_low = d_embed.astype(jnp.bfloat16).reshape(image_slots * LAT, model_width)
    resample_out_grad = jnp.dot(image_mixed.T, d_embed_low, preferred_element_type=jnp.float32)
    d_image_mixed = jnp.dot(d_embed_low, image_out_full.T, preferred_element_type=jnp.float32)
    d_image_mixed = d_image_mixed.astype(jnp.bfloat16).reshape(image_slots, LAT, heads_local, HEAD)
    d_image_probs = jnp.einsum(
        "iqhd,iphd->ihqp", d_image_mixed, image_values, preferred_element_type=jnp.float32
    )
    d_image_scores = image_probs * (
        d_image_probs - jnp.sum(image_probs * d_image_probs, -1, keepdims=True)
    )
    d_image_scores = d_image_scores.astype(jnp.bfloat16)
    d_probe = (
        jnp.einsum("ihqp,iphd->qhd", d_image_scores, image_keys, preferred_element_type=jnp.float32)
        * score_scale
    )
    d_image_keys = (
        jnp.einsum("ihqp,qhd->iphd", d_image_scores, probe, preferred_element_type=jnp.float32)
        * score_scale
    ).astype(jnp.bfloat16)
    d_image_values = jnp.einsum(
        "ihqp,iqhd->iphd",
        image_probs.astype(jnp.bfloat16),
        d_image_mixed,
        preferred_element_type=jnp.float32,
    ).astype(jnp.bfloat16)
    resample_key_grad = jnp.dot(
        pictures.T,
        d_image_keys.reshape(image_slots * PATCH, half_width),
        preferred_element_type=jnp.float32,
    )
    resample_value_grad = jnp.dot(
        pictures.T,
        d_image_values.reshape(image_slots * PATCH, half_width),
        preferred_element_type=jnp.float32,
    )
    d_probe_flat = d_probe.reshape(LAT, half_width)
    resample_query_grad = jnp.dot(
        latent_full.astype(jnp.float32).T, d_probe_flat, precision=HIGHEST_PRECISION
    )
    latent_grad = tp_total(
        jnp.dot(d_probe_flat, probe_full.astype(jnp.float32).T, precision=HIGHEST_PRECISION)
    )
    summed_in = (
        lax.psum_scatter(query_grad, (SEQ, IMG), scatter_dimension=0, tiled=True),
        lax.psum_scatter(key_grad, (SEQ, IMG), scatter_dimension=0, tiled=True),
        lax.psum_scatter(value_grad, (SEQ, IMG), scatter_dimension=0, tiled=True),
        lax.psum_scatter(up_grad, (SEQ, IMG), scatter_dimension=0, tiled=True),
        lax.psum_scatter(resample_query_grad, (SEQ, IMG), scatter_dimension=0, tiled=True),
        lax.psum_scatter(resample_key_grad, (SEQ, IMG), scatter_dimension=0, tiled=True),
        lax.psum_scatter(resample_value_grad, (SEQ, IMG), scatter_dimension=0, tiled=True),
    )
    summed_out = (
        lax.psum_scatter(out_grad, (SEQ, IMG), scatter_dimension=1, tiled=True),
        lax.psum_scatter(down_grad, (SEQ, IMG), scatter_dimension=1, tiled=True),
        lax.psum_scatter(resample_out_grad, (SEQ, IMG), scatter_dimension=1, tiled=True),
        lax.psum_scatter(latent_grad, (SEQ, IMG), scatter_dimension=1, tiled=True),
    )
    summed_small = lax.psum(
        (
            input_gain_grad,
            input_shift_grad,
            inner_gain_grad,
            inner_shift_grad,
            middle_gain_grad,
            middle_shift_grad,
            up_bias_grad,
            hidden_gain_grad,
            hidden_shift_grad,
        ),
        (SEQ, IMG),
    )
    return (
        result,
        text_grad,
        summed_small[0],
        summed_small[1],
        summed_in[0],
        summed_in[1],
        summed_in[2],
        summed_small[2],
        summed_small[3],
        summed_out[0],
        summed_small[4],
        summed_small[5],
        summed_in[3],
        summed_small[6],
        summed_small[7],
        summed_small[8],
        summed_out[1],
        summed_out[3],
        summed_in[4],
        summed_in[5],
        summed_in[6],
        summed_out[2],
    )


MESH_IDS = pl.DeviceIdType.MESH
ANYWHERE = pl.BlockSpec(memory_space=pl.ANY)
ON_CHIP = pl.BlockSpec(memory_space=pltpu.VMEM)
IN_SMEM = pl.BlockSpec(memory_space=pltpu.SMEM)
LANES = 128
PLANE = 8
VMEM_BYTES = 60 * 1024 * 1024
PIECE_ROWS = (32, 32, 32, 32)
PIECES = len(PIECE_ROWS)
SECOND_LAG = 2
FRONT, BACK, ALL, ROWS, INWARD, OUTWARD, SHARED = range(7)


def narrow_heads(mesh):
    return mesh.shape[SEQ] != PLANE or mesh.shape[IMG] != 2 or mesh.shape[TP] != 2


def flipped(number, bit):
    step = 2**bit
    return number + step - 2 * step * ((number // step) % 2)


class Places:
    def __init__(self):
        self.seq, self.tp, self.img = (lax.axis_index(name) for name in (SEQ, TP, IMG))
        self.s_core, self.s_x, self.s_y = (flipped(self.seq, bit) for bit in range(3))
        self.s_xy = flipped(self.s_x, 2)
        self.core, self.x, self.y = (self.at(seq) for seq in (self.s_core, self.s_x, self.s_y))
        self.tp_peer = (self.seq, 1 - self.tp, self.img)
        self.img_peer = (self.seq, self.tp, 1 - self.img)

    def at(self, seq):
        return (seq, self.tp, self.img)


def greet(peers):
    barrier = pltpu.get_barrier_semaphore()
    for peer in peers:
        pl.semaphore_signal(barrier, inc=1, device_id=peer, device_id_type=MESH_IDS)
    pl.semaphore_wait(barrier, len(peers))


def remote(src, dst, send, recv, peer):
    return pltpu.make_async_remote_copy(
        src_ref=src, dst_ref=dst, send_sem=send, recv_sem=recv, device_id=peer, device_id_type=MESH_IDS
    )


def rows_at(ref, first, count):
    return ref.at[pl.ds(pl.multiple_of(first, 16), count)]


class Spread:
    def __init__(self, here, out, block, first, count, send, recv):
        self.here, self.out, self.block = here, out, block
        self.first, self.count, self.send, self.recv = first, count, send, recv
        self.half = out.shape[1] // 2
        self.sent = []

    def cut(self, ref, first, which):
        rows = pl.ds(first, self.count)
        if which == ALL:
            return ref.at[rows]
        return ref.at[rows, pl.ds(self.half if which == BACK else 0, self.half)]

    def part(self, seq, which):
        return self.cut(self.out, pl.multiple_of(seq * self.block + self.first, 16), which)

    def copy(self, src, dst, slot, peer):
        return remote(src, dst, self.send.at[slot], self.recv.at[slot], peer)

    def go(self, src, dst, slot, peer):
        made = self.copy(src, dst, slot, peer)
        made.start()
        self.sent.append(made)

    def own(self, src, src_first):
        here, seq = self.here, self.here.seq

        def own_part(which):
            return self.cut(src, src_first, which)

        self.go(own_part(FRONT), self.part(seq, FRONT), 0, here.x)
        self.go(own_part(BACK), self.part(seq, BACK), 1, here.y)
        self.go(own_part(BACK), self.part(seq, BACK), 2, here.x)
        self.go(own_part(FRONT), self.part(seq, FRONT), 3, here.y)
        self.go(own_part(ALL), self.part(seq, ALL), 4, here.core)

    def arrived(self, slot, seq, which):
        target = self.part(seq, which)
        self.copy(target, target, slot, self.here.core).wait_recv()

    def forward(self):
        here = self.here
        self.arrived(0, here.s_x, FRONT)
        self.go(self.part(here.s_x, FRONT), self.part(here.s_x, FRONT), 5, here.y)
        self.arrived(1, here.s_y, BACK)
        self.go(self.part(here.s_y, BACK), self.part(here.s_y, BACK), 6, here.x)
        self.arrived(2, here.s_x, BACK)
        self.go(self.part(here.s_x, ALL), self.part(here.s_x, ALL), 7, here.core)
        self.arrived(3, here.s_y, FRONT)
        self.go(self.part(here.s_y, ALL), self.part(here.s_y, ALL), 8, here.core)

    def corner(self):
        here = self.here
        self.arrived(5, here.s_xy, FRONT)
        self.arrived(6, here.s_xy, BACK)
        self.go(self.part(here.s_xy, ALL), self.part(here.s_xy, ALL), 9, here.core)

    def finish(self):
        core = self.here.s_core
        self.arrived(4, core, ALL)
        self.arrived(7, flipped(core, 1), ALL)
        self.arrived(8, flipped(core, 2), ALL)
        self.arrived(9, flipped(flipped(core, 1), 2), ALL)
        for made in self.sent:
            made.wait_send()


def ticks_of(stages, count):
    def tick_of(tick):
        def run():
            for lag, stage in reversed(stages):
                if 0 <= tick - lag < count:
                    stage(tick - lag)

        return run

    return [tick_of(tick) for tick in range(count + max(lag for lag, _ in stages))]


def take_some(waiting, count):
    for launch in waiting[:count]:
        launch()
    del waiting[:count]


def weight_blocks(weight, side):
    if side == SHARED:
        return weight.shape
    if side == INWARD:
        return (weight.shape[0], weight.shape[1] // PLANE)
    return (weight.shape[0] // PLANE, weight.shape[1])


def intake(gathered, weights, sides, cid):
    n_rows, n_weights = len(gathered), len(weights)
    pieces = PIECES

    def kernel(*refs):
        row_refs, weight_refs = refs[:n_rows], refs[n_rows : n_rows + n_weights]
        refs = refs[n_rows + n_weights :]
        row_outs, weight_outs = refs[:n_rows], refs[n_rows : n_rows + n_weights]
        refs = refs[n_rows + n_weights :]
        held, (local, send, recv, w_local, w_send, w_recv, z_send, z_recv) = refs[:n_rows], refs[n_rows:]
        here = Places()
        seq, tp, img = here.seq, here.tp, here.img
        others = [lax.rem(seq + step, PLANE) for step in range(1, PLANE)]
        greet([(other, tp, img) for other in others] + [here.img_peer])

        def slot_of(out, side, shape, from_seq, from_img):
            number = from_seq * 2 + from_img
            if side == INWARD:
                return out.at[pl.ds(pl.multiple_of(number * shape[0], shape[0]), shape[0])]
            return out.at[:, pl.ds(pl.multiple_of(number * shape[1], shape[1]), shape[1])]

        def block_of(weight, side, shape, to_seq):
            if side == SHARED:
                return weight
            if side == INWARD:
                return weight.at[:, pl.ds(pl.multiple_of(to_seq * shape[1], shape[1]), shape[1])]
            return weight.at[pl.ds(pl.multiple_of(to_seq * shape[0], shape[0]), shape[0])]

        flights, own_copies = [], []

        def begin(index):
            weight, out, side = weight_refs[index], weight_outs[index], sides[index]
            shape = weight_blocks(weight, side)
            mine = pltpu.make_async_copy(
                block_of(weight, side, shape, seq), slot_of(out, side, shape, seq, img), w_local.at[index]
            )
            mine.start()
            crossing = remote(
                block_of(weight, side, shape, seq),
                slot_of(out, side, shape, seq, img),
                z_send.at[index, 0],
                z_recv.at[index, 0],
                here.img_peer,
            )
            crossing.start()
            own_copies.append(mine)
            flights.append(crossing)
            for step, other in enumerate(others, 1):
                made = remote(
                    block_of(weight, side, shape, other),
                    slot_of(out, side, shape, seq, img),
                    w_send.at[index, step],
                    w_recv.at[index, step],
                    here.at(other),
                )
                made.start()
                flights.append(made)

        spreads, loads, stores = [], [], []
        for number, (rows, out) in enumerate(zip(row_refs, row_outs)):
            block = rows.shape[0]
            count = block // pieces
            loads.append(pltpu.make_async_copy(rows, held[number], local.at[number, 0]))
            loads[-1].start()
            stores.append(pltpu.make_async_copy(held[number], rows_at(out, seq * block, block), local.at[number, 1]))
            for piece in range(pieces):
                at = number * pieces + piece
                spreads.append(
                    (Spread(here, out, block, piece * count, count, send.at[at], recv.at[at]), rows, piece * count)
                )

        def cross(piece):
            for index in range(piece, n_weights, len(spreads)):
                weight, out, side = weight_refs[index], weight_outs[index], sides[index]
                shape = weight_blocks(weight, side)
                for step in range(1, PLANE):
                    source = lax.rem(seq + PLANE - step, PLANE)
                    landed = slot_of(out, side, shape, source, img)
                    remote(landed, landed, w_send.at[index, step], w_recv.at[index, step], here.core).wait_recv()
                    crossing = remote(
                        landed, landed, z_send.at[index, step], z_recv.at[index, step], here.img_peer
                    )
                    crossing.start()
                    flights.append(crossing)

        def own_rows(piece):
            if piece == 1:
                for load, store in zip(loads, stores):
                    load.wait()
                    store.start()
            for index in range(piece, n_weights, len(spreads)):
                begin(index)
            spreads[piece][0].own(spreads[piece][1], spreads[piece][2])

        for tick in ticks_of(
            [
                (0, own_rows),
                (2, lambda piece: spreads[piece][0].forward()),
                (3, lambda piece: cross(piece)),
                (4, lambda piece: spreads[piece][0].corner()),
            ],
            len(spreads),
        ):
            tick()
        for index, (weight, out, side) in enumerate(zip(weight_refs, weight_outs, sides)):
            shape = weight_blocks(weight, side)
            for step in range(PLANE):
                source = lax.rem(seq + PLANE - step, PLANE)
                landed = slot_of(out, side, shape, source, 1 - img)
                remote(landed, landed, z_send.at[index, step], z_recv.at[index, step], here.core).wait_recv()
        for spread, _, _ in spreads:
            spread.finish()
        for made in flights:
            made.wait_send()
        for made in own_copies + stores:
            made.wait()

    def whole(weight, side):
        shape = weight_blocks(weight, side)
        if side == INWARD:
            return jax.ShapeDtypeStruct((2 * PLANE * shape[0], shape[1]), weight.dtype)
        return jax.ShapeDtypeStruct((shape[0], 2 * PLANE * shape[1]), weight.dtype)

    dma = pltpu.SemaphoreType.DMA
    outs = [jax.ShapeDtypeStruct((PLANE * rows.shape[0], rows.shape[1]), rows.dtype) for rows in gathered]
    outs += [whole(weight, side) for weight, side in zip(weights, sides)]
    made = pl.pallas_call(
        kernel,
        out_shape=tuple(outs),
        in_specs=[ANYWHERE] * (n_rows + n_weights),
        out_specs=tuple([ANYWHERE] * len(outs)),
        scratch_shapes=[pltpu.VMEM(rows.shape, rows.dtype) for rows in gathered]
        + [
            dma((n_rows, 2)),
            dma((n_rows * pieces, 10)),
            dma((n_rows * pieces, 10)),
            dma((n_weights,)),
            dma((n_weights, PLANE)),
            dma((n_weights, PLANE)),
            dma((n_weights, PLANE)),
            dma((n_weights, PLANE)),
        ],
        compiler_params=pltpu.CompilerParams(
            collective_id=cid, has_side_effects=True, vmem_limit_bytes=VMEM_BYTES
        ),
    )(*gathered, *weights)
    return made[:n_rows], made[n_rows:]


LAZY_BYTES = 256 * 1024


class Lazy:
    def __init__(self, src, dst, sem):
        self.copy = pltpu.make_async_copy(src, dst, sem)
        self.copy.start()
        self.dst, self.shape, self.pending = dst, dst.shape, True

    def ready(self):
        if self.pending:
            self.copy.wait()
            self.pending = False
        return self.dst

    @property
    def at(self):
        return self.ready().at

    def __getitem__(self, where):
        return self.ready()[where]


def is_lazy(value, spec):
    return spec is ON_CHIP and value.size * value.dtype.itemsize >= LAZY_BYTES


class Rider:
    inputs, out_shapes, scratch, in_specs = (), (), (), ()

    def bind(self, here, ins, outs, scratch):
        self.here, self.ins, self.outs, self.held = here, ins, outs, scratch
        self.sent, self.kept, self.due, self.launches, self.later = [], [], [], [], []

    def keep(self, src, dst, sem):
        made = pltpu.make_async_copy(src, dst, sem)
        self.launches.append(made.start)
        self.kept.append(made)

    def send(self, src, dst, send, recv, peer):
        made = remote(src, dst, send, recv, peer)
        self.launches.append(made.start)
        self.sent.append(made)

    def finish(self):
        for dst, send, recv in self.due:
            remote(dst, dst, send, recv, self.here.core).wait_recv()
        for made in self.sent:
            made.wait_send()
        for made in self.kept:
            made.wait()


class ChainWeights(Rider):
    def __init__(self, weights, sides, places):
        self.inputs, self.sides, self.places = weights, sides, places
        self.blocks = [weight_blocks(weight, side) for weight, side in zip(weights, sides)]
        shapes = {}
        for (rows, columns), side, (out, first) in zip(self.blocks, sides, places):
            if side == INWARD:
                shapes[out] = (2 * PLANE * rows, first + columns)
            else:
                shapes[out] = (rows, 2 * PLANE * columns)
        self.out_shapes = [jax.ShapeDtypeStruct(shapes[out], weights[0].dtype) for out in range(len(shapes))]
        dma, count = pltpu.SemaphoreType.DMA, len(weights)
        self.scratch = [dma((count, PLANE))] * 4 + [dma((count,))]

    def peers(self, here):
        return [here.at(lax.rem(here.seq + step, PLANE)) for step in range(1, PLANE)]

    def slot(self, index, seq, img):
        out, first = self.places[index]
        (rows, columns), number = self.blocks[index], seq * 2 + img
        if self.sides[index] == INWARD:
            return self.outs[out].at[pl.ds(pl.multiple_of(number * rows, rows), rows), pl.ds(first, columns)]
        return self.outs[out].at[:, pl.ds(pl.multiple_of(number * columns, columns), columns)]

    def start(self):
        here, (send, recv, z_send, z_recv, local) = self.here, self.held
        self.later = []
        for index, (weight, side, (rows, columns)) in enumerate(zip(self.ins, self.sides, self.blocks)):
            for step in range(PLANE):
                target = lax.rem(here.seq + step, PLANE)
                source = lax.rem(here.seq + PLANE - step, PLANE)
                if side == INWARD:
                    part = weight.at[:, pl.ds(pl.multiple_of(target * columns, columns), columns)]
                else:
                    part = weight.at[pl.ds(pl.multiple_of(target * rows, rows), rows)]
                mine = self.slot(index, here.seq, here.img)
                if step == 0:
                    self.keep(part, mine, local.at[index])
                    cross = remote(part, mine, z_send.at[index, 0], z_recv.at[index, 0], here.img_peer)
                    self.launches.append(cross.start)
                    self.sent.append(cross)
                else:
                    self.send(part, mine, send.at[index, step], recv.at[index, step], here.at(target))
                    self.later.append(functools.partial(self.cross, index, step, source))
                there = self.slot(index, source, 1 - here.img)
                self.due.append((there, z_send.at[index, step], z_recv.at[index, step]))

    def cross(self, index, step, source):
        here, (send, recv, z_send, z_recv, _) = self.here, self.held
        landed = self.slot(index, source, here.img)
        remote(landed, landed, send.at[index, step], recv.at[index, step], here.core).wait_recv()
        made = remote(landed, landed, z_send.at[index, step], z_recv.at[index, step], here.img_peer)
        made.start()
        self.sent.append(made)


class GatherRows(Rider):
    def __init__(self, rows):
        self.inputs = [rows]
        self.out_shapes = [jax.ShapeDtypeStruct((PLANE * rows.shape[0], rows.shape[1]), rows.dtype)]
        dma = pltpu.SemaphoreType.DMA
        self.scratch = [dma((PIECES, 10)), dma((PIECES, 10)), dma((1,))]

    def start(self):
        (rows,), (out,), (send, recv, local) = self.ins, self.outs, self.held
        block = rows.shape[0]
        self.spreads = []
        for piece, count in enumerate(PIECE_ROWS):
            first = sum(PIECE_ROWS[:piece])
            self.spreads.append(Spread(self.here, out, block, first, count, send.at[piece], recv.at[piece]))
            self.launches.append(functools.partial(self.spreads[piece].own, rows, first))
        self.keep(rows, rows_at(out, self.here.seq * block, block), local.at[0])
        self.later = [spread.forward for spread in self.spreads] + [spread.corner for spread in self.spreads]

    def finish(self):
        for spread in self.spreads:
            spread.finish()
        super().finish()


class CrossGrads(Rider):
    def __init__(self, grads, sides):
        self.inputs, self.sides = grads, sides
        self.out_shapes = []
        for grad, side in zip(grads, sides):
            if side == INWARD:
                shape = (grad.shape[0], grad.shape[2], grad.shape[3])
            else:
                shape = (PLANE, grad.shape[0], grad.shape[1] // (2 * PLANE))
            self.out_shapes.append(jax.ShapeDtypeStruct(shape, grad.dtype))
        dma = pltpu.SemaphoreType.DMA
        self.scratch = [dma((len(grads), PLANE)), dma((len(grads), PLANE))]

    def peers(self, here):
        return [here.img_peer]

    def start(self):
        here, (send, recv) = self.here, self.held
        for index, (grad, out, side) in enumerate(zip(self.ins, self.outs, self.sides)):
            width = out.shape[2]
            for seq in range(PLANE):
                if side == INWARD:
                    part = grad.at[seq, 1 - here.img]
                else:
                    part = grad.at[:, pl.ds(pl.multiple_of((seq * 2 + 1 - here.img) * width, width), width)]
                self.send(part, out.at[seq], send.at[index, seq], recv.at[index, seq], here.img_peer)
                self.due.append((out.at[seq], send.at[index, seq], recv.at[index, seq]))


class Stream:
    in_specs = ()

    def __init__(self, rows_all, left, right, across, row_inputs, row_kinds, row_outs, row_function, gather):
        self.own_left = left is not None
        self.inputs = ([left] if self.own_left else []) + [right] + list(row_inputs)
        self.across, self.row_kinds, self.row_outs = across, row_kinds, row_outs
        self.row_function, self.gather = row_function, gather
        width = right.shape[0] if across else right.shape[1]
        self.width, self.block, self.pieces = width, rows_all // PLANE, PIECES
        self.half = width // 2
        low_type = jnp.bfloat16
        self.out_shapes = [shape for shape, _ in row_outs]
        if gather:
            self.out_shapes.append(jax.ShapeDtypeStruct((rows_all, width), low_type))
        dma = pltpu.SemaphoreType.DMA
        block, pieces, half = self.block, self.pieces, self.half
        self.scratch = [
            pltpu.VMEM((4, block, width), low_type),
            pltpu.VMEM((4, block, width), low_type),
            pltpu.VMEM((4, block, width), jnp.float32),
            pltpu.VMEM((block, half), low_type),
            pltpu.VMEM((block, half), low_type),
            pltpu.VMEM((block, width), low_type),
            pltpu.VMEM((block, width), low_type),
            pltpu.VMEM((block, width), low_type),
            pltpu.VMEM((block, width), low_type),
            pltpu.VMEM((block, width), low_type),
            dma((4,)),
            dma((4,)),
            dma((pieces, 7)),
            dma((pieces, 7)),
            dma((pieces, 10)),
            dma((pieces, 10)),
            dma((pieces,)),
        ]

    def out_specs(self):
        return [ON_CHIP] * len(self.row_outs) + [ANYWHERE] * (len(self.out_shapes) - len(self.row_outs))

    def peers(self, here):
        return [here.core, here.x, here.y, here.tp_peer]

    def bind(self, here, ins, outs, scratch):
        self.here = here
        if self.own_left:
            self.left, ins = ins[0], ins[1:]
        self.right, self.ins = ins[0], ins[1:]
        self.outs = outs
        (self.away, self.core_in, self.near, self.from_xd, self.from_yd, self.from_x, self.from_y) = scratch[:7]
        (self.mine, self.theirs, self.low, self.c_send, self.c_recv) = scratch[7:12]
        (self.send, self.recv, self.g_send, self.g_recv, self.l_sem) = scratch[12:]
        self.sent, self.spreads, self.core_copies = [], [], {}

    def chunk(self, base, kind):
        if kind in (1, 3):
            base = flipped(base, 1)
        if kind in (2, 3):
            base = flipped(base, 2)
        return base

    def product(self, seq, target, low_type):
        first = pl.multiple_of(seq * self.block, self.block)
        rows = self.left[pl.ds(first, self.block), :]
        step = min(512, self.width)
        for column in range(0, self.width, step):
            if self.across:
                part = lax.dot_general(
                    rows,
                    self.right[column : column + step, :],
                    (((1,), (1,)), ((), ())),
                    preferred_element_type=jnp.float32,
                )
            else:
                part = jnp.dot(
                    rows, self.right[:, column : column + step], preferred_element_type=jnp.float32
                )
            target[:, column : column + step] = part.astype(low_type)

    def begin(self):
        here = self.here
        for kind in (3, 1, 2, 0):
            self.product(self.chunk(here.s_core, kind), self.away.at[kind], jnp.bfloat16)
            made = remote(
                self.away.at[kind], self.core_in.at[kind], self.c_send.at[kind], self.c_recv.at[kind], here.core
            )
            made.start()
            self.core_copies[kind] = made
            self.product(self.chunk(here.seq, kind), self.near.at[kind], jnp.float32)

    def go(self, src, dst, piece, slot, peer):
        made = remote(src, dst, self.send.at[piece, slot], self.recv.at[piece, slot], peer)
        made.start()
        self.sent.append(made)

    def landed(self, dst, piece, slot):
        remote(dst, dst, self.send.at[piece, slot], self.recv.at[piece, slot], self.here.core).wait_recv()

    def rows_of(self, piece):
        return pl.ds(sum(PIECE_ROWS[:piece]), PIECE_ROWS[piece])

    def columns_of(self, which):
        return pl.ds(self.half if which == BACK else 0, self.half)

    def held(self, kind, piece, which=ALL):
        if which == ALL:
            return self.core_in.at[kind, self.rows_of(piece)]
        return self.core_in.at[kind, self.rows_of(piece), self.columns_of(which)]

    def halved(self, ref, piece, which):
        return ref.at[self.rows_of(piece), self.columns_of(which)]

    def folded(self, kind, piece):
        if piece == 0:
            self.core_copies[kind].wait_recv()
        near = self.near[kind, self.rows_of(piece), :]
        return self.held(kind, piece)[...].astype(jnp.float32) + near

    def first_sends(self, piece):
        here = self.here
        self.held(3, piece)[...] = self.folded(3, piece).astype(jnp.bfloat16)
        self.go(self.held(3, piece, FRONT), self.from_xd.at[self.rows_of(piece)], piece, 0, here.x)
        self.go(self.held(3, piece, BACK), self.from_yd.at[self.rows_of(piece)], piece, 1, here.y)
        self.held(1, piece)[...] = self.folded(1, piece).astype(jnp.bfloat16)
        self.go(self.held(1, piece, FRONT), self.halved(self.from_x, piece, FRONT), piece, 2, here.x)
        self.held(2, piece)[...] = self.folded(2, piece).astype(jnp.bfloat16)
        self.go(self.held(2, piece, BACK), self.halved(self.from_y, piece, BACK), piece, 3, here.y)

    def second_sends(self, piece):
        here = self.here
        self.landed(self.from_xd.at[self.rows_of(piece)], piece, 0)
        at = self.held(2, piece, FRONT)
        at[...] = (at[...].astype(jnp.float32) + self.from_xd[self.rows_of(piece), :].astype(jnp.float32)).astype(jnp.bfloat16)
        self.go(at, self.halved(self.from_y, piece, FRONT), piece, 4, here.y)
        self.landed(self.from_yd.at[self.rows_of(piece)], piece, 1)
        at = self.held(1, piece, BACK)
        at[...] = (at[...].astype(jnp.float32) + self.from_yd[self.rows_of(piece), :].astype(jnp.float32)).astype(jnp.bfloat16)
        self.go(at, self.halved(self.from_x, piece, BACK), piece, 5, here.x)

    def plane_sum(self, piece):
        self.landed(self.halved(self.from_x, piece, FRONT), piece, 2)
        self.landed(self.halved(self.from_y, piece, BACK), piece, 3)
        self.landed(self.halved(self.from_y, piece, FRONT), piece, 4)
        self.landed(self.halved(self.from_x, piece, BACK), piece, 5)
        total = self.folded(0, piece)
        total = total + self.from_x[self.rows_of(piece), :].astype(jnp.float32) + self.from_y[self.rows_of(piece), :].astype(jnp.float32)
        self.mine[self.rows_of(piece), :] = total.astype(jnp.bfloat16)
        self.go(self.mine.at[self.rows_of(piece)], self.theirs.at[self.rows_of(piece)], piece, 6, self.here.tp_peer)

    def rows_done(self, piece):
        here = self.here
        self.landed(self.theirs.at[self.rows_of(piece)], piece, 6)
        total = self.mine[self.rows_of(piece), :].astype(jnp.float32) + self.theirs[self.rows_of(piece), :].astype(jnp.float32)
        rows = self.rows_of(piece)
        views = [ref.at[rows] if kind == ROWS else ref for ref, kind in zip(self.ins, self.row_kinds)]
        out_views = [ref.at[rows] if kind == ROWS else ref for ref, (_, kind) in zip(self.outs, self.row_outs)]
        given = self.row_function(total, piece, views, out_views)
        if self.gather:
            out = self.outs[-1]
            self.low[rows, :] = given
            first = pl.multiple_of(here.seq * self.block + rows.start, 16)
            keep = pltpu.make_async_copy(self.low.at[rows], out.at[pl.ds(first, rows.size)], self.l_sem.at[piece])
            keep.start()
            spread = Spread(
                here, out, self.block, rows.start, rows.size, self.g_send.at[piece], self.g_recv.at[piece]
            )
            spread.own(self.low, rows.start)
            self.spreads.append((spread, keep))

    def stages(self):
        stages = [(0, self.first_sends), (1, self.second_sends), (2, self.plane_sum), (4, self.rows_done)]
        if self.gather:
            stages.append((5, lambda piece: self.spreads[piece][0].forward()))
            stages.append((6, lambda piece: self.spreads[piece][0].corner()))
        return stages

    def phases(self):
        def phase_of(stage):
            def run():
                for piece in range(PIECES):
                    stage(piece)

            return run

        return [phase_of(stage) for _, stage in self.stages()]

    def finish(self):
        for spread, keep in self.spreads:
            spread.finish()
            keep.wait()
        for made in self.sent:
            made.wait_send()
        for made in self.core_copies.values():
            made.wait_send()


def full_line(rows):
    held = rows[...].astype(jnp.float32)
    return jnp.concatenate([held[number : number + 1, :] for number in range(held.shape[0])], 1)


def own_line(here, rows, width):
    held = rows[...].astype(jnp.float32)
    count = width // LANES
    number = lax.broadcasted_iota(jnp.int32, held.shape, 0)
    parts = [
        jnp.sum(jnp.where(number == here.seq * count + part, held, 0.0), 0, keepdims=True) for part in range(count)
    ]
    return jnp.concatenate(parts, 1)


class Front(Rider):
    def total_scratch(self, count, rows):
        dma = pltpu.SemaphoreType.DMA
        return [
            pltpu.VMEM((PLANE - 1, count, rows), jnp.float32),
            pltpu.VMEM((count, rows), jnp.float32),
            pltpu.VMEM((count, rows), jnp.float32),
            pltpu.VMEM((count, rows), jnp.float32),
            dma((PLANE,)),
            dma((PLANE,)),
        ]

    def peers(self, here):
        return [here.at(lax.rem(here.seq + step, PLANE)) for step in range(1, PLANE)]

    def small_sum(self, scratch):
        here, (plane, own, mine, theirs, send, recv) = self.here, scratch
        made = []
        for step, peer in enumerate(self.peers(here)):
            copy = remote(own, plane.at[step], send.at[step], recv.at[step], peer)
            copy.start()
            made.append(copy)
        total = own[...]
        for step, copy in enumerate(made):
            copy.wait_recv()
            total = total + plane[step]
        mine[...] = total
        last = remote(mine, theirs, send.at[PLANE - 1], recv.at[PLANE - 1], here.tp_peer)
        last.start()
        last.wait()
        for copy in made:
            copy.wait_send()
        total = mine[...] + theirs[...]
        count, rows = total.shape
        return jnp.concatenate([total, jnp.zeros((8 - count, rows), jnp.float32)], 0).T


def chosen_rows(target_rows, first, count):
    row = first + lax.broadcasted_iota(jnp.int32, (count, target_rows.shape[1]), 0)
    return (row == target_rows[...]).astype(jnp.float32).astype(jnp.bfloat16)


class ImageFront(Rider):
    def __init__(self, pictures, key_part, value_part, latent_all, probe_part, target_rows, segment):
        self.inputs = [pictures, key_part, value_part, latent_all, probe_part, target_rows, segment]
        rows, width = pictures.shape[0], key_part.shape[1]
        images = rows // PATCH
        low_type = jnp.bfloat16
        self.out_shapes = [
            jax.ShapeDtypeStruct((rows, 2 * width), low_type),
            jax.ShapeDtypeStruct((images * LAT, width), low_type),
            jax.ShapeDtypeStruct((LAT, width), low_type),
        ]
        self.out_shapes += [jax.ShapeDtypeStruct((segment.shape[1], width), jnp.float32)] * 3
        self.out_shapes.append(jax.ShapeDtypeStruct((segment.shape[1], 8), jnp.float32))
        self.scratch = [
            pltpu.VMEM((key_part.shape[0], 2 * width), low_type),
            pltpu.VMEM((images * LAT, width), low_type),
        ]

    def run(self):
        pictures, key_w, value_w, latent_all, probe_w, target_rows, segment = self.ins
        keys, placed, probe, *tables, column = self.outs
        row = segment[...].astype(jnp.float32)
        column[...] = jnp.broadcast_to(row, (8, row.shape[1])).T
        for first in range(0, segment.shape[1], ATTEND_ROWS):
            self.launches.append(functools.partial(xpos_part, segment, column, tables, first))
        both_w, mixed_all = self.held
        width, scale = probe.shape[1], HEAD ** (-0.5)
        both_w[:, :width] = key_w[...]
        both_w[:, width:] = value_w[...]
        probe[...] = jnp.dot(latent_all[...], probe_w[...], preferred_element_type=jnp.float32).astype(jnp.bfloat16)
        yield
        for image in range(pictures.shape[0] // PATCH):
            rows = slice(image * PATCH, (image + 1) * PATCH)
            if image % IMAGES_A_STEP == 0:
                more = slice(image * PATCH, (image + IMAGES_A_STEP) * PATCH)
                keys[more, :] = jnp.dot(
                    pictures[more, :], both_w[...], preferred_element_type=jnp.float32
                ).astype(jnp.bfloat16)
            mixed = []
            for first in range(0, width, HEAD):
                probs = image_probs_of(probe[:, first : first + HEAD], keys[rows, first : first + HEAD], scale)
                values = keys[rows, width + first : width + first + HEAD]
                mixed.append(jnp.dot(probs.astype(jnp.bfloat16), values, preferred_element_type=jnp.float32))
            mixed_all[image * LAT : (image + 1) * LAT, :] = jnp.concatenate(mixed, 1).astype(jnp.bfloat16)
            yield
        for first in range(0, placed.shape[0], PATCH):
            chosen = chosen_rows(target_rows, first, PATCH)
            placed[first : first + PATCH, :] = jnp.dot(
                chosen, mixed_all[...], preferred_element_type=jnp.float32
            ).astype(jnp.bfloat16)
        self.lefts = [placed]


class AttendFront(Front):
    def __init__(self, normed, layer_part, tables, segment, column, gain, shift, full_width):
        self.inputs = [normed, layer_part, *tables, segment, column, gain, shift]
        self.full_width = full_width
        rows, width = normed.shape[0], layer_part.shape[1] // 3
        low_shape = jax.ShapeDtypeStruct((rows, width), jnp.bfloat16)
        wide_shape = jax.ShapeDtypeStruct((rows, width), jnp.float32)
        lse_shape = jax.ShapeDtypeStruct((rows, 8), jnp.float32)
        self.out_shapes = [low_shape, low_shape, low_shape, wide_shape, lse_shape, low_shape, wide_shape, wide_shape]
        self.scratch = self.total_scratch(2, rows)

    def run(self):
        normed, layer_w, cos_ref, sin_ref, grow_ref, segment, column, gain, shift = self.ins
        q_out, k_out, v_out, att_out, lse_out, low, hat, factor_out = self.outs
        rows_all, width = att_out.shape
        scale = HEAD ** (-0.5)
        f32, low_type = jnp.float32, jnp.bfloat16
        for first in range(0, rows_all, ATTEND_ROWS):
            at, keys = slice(first, first + ATTEND_ROWS), first + ATTEND_ROWS
            cosine, sine, growth = cos_ref[at, :], sin_ref[at, :], grow_ref[at, :]
            linear = jnp.dot(normed[at, :], layer_w[...], preferred_element_type=f32)
            lin = linear[:, :width]
            q_out[at, :] = ((lin * cosine + halves_swapped(lin) * sine) * growth).astype(low_type)
            lin = linear[:, width : 2 * width]
            k_out[at, :] = ((lin * cosine + halves_swapped(lin) * sine) * (1.0 / growth)).astype(low_type)
            v_out[at, :] = linear[:, 2 * width :].astype(low_type)
            allowed = allowed_part(column, segment, first, ATTEND_ROWS, keys)
            for head in range(width // HEAD):
                lanes = slice(head * HEAD, (head + 1) * HEAD)
                scores = lax.dot_general(
                    q_out[at, lanes] * scale,
                    k_out[:keys, lanes],
                    (((1,), (1,)), ((), ())),
                    preferred_element_type=f32,
                )
                scores = jnp.where(allowed, scores, -1e30)
                best = jnp.max(scores, -1, keepdims=True)
                weights = jnp.exp(scores - best)
                total = jnp.sum(weights, -1, keepdims=True)
                probs = (weights * (1.0 / total)).astype(low_type)
                att_out[at, lanes] = jnp.dot(probs, v_out[:keys, lanes], preferred_element_type=f32)
                lse_out[at, head : head + 1] = best + jnp.log(total)
            rows = att_out[at, :]
            sums = [jnp.sum(rows, 1, keepdims=True), jnp.sum(rows * rows, 1, keepdims=True)]
            self.held[1][:, at] = as_lanes(sums)[:2]
            yield
        total = self.small_sum(self.held) / self.full_width
        average = total[:, 0:1]
        factor = lax.rsqrt(total[:, 1:2] - average * average + EPSILON)
        normal = (att_out[...] - average) * factor
        hat[...] = normal
        factor_out[...] = jnp.broadcast_to(factor, normal.shape)
        gain, shift = (own_line(self.here, line, low.shape[1]) for line in (gain, shift))
        low[...] = (normal * gain + shift).astype(low_type)
        self.lefts = [low]


class GradFront(Front):
    def grads(self, products):
        for seq in range(PLANE):
            for product in products:
                self.launches.append(functools.partial(self.part, *product, seq))

    def part(self, left, right, outs, side, seq):
        span = (left.shape[1] if side == INWARD else right.shape[1]) // PLANE
        at = slice(seq * span, (seq + 1) * span)
        contract = (((0,), (0,)), ((), ()))
        if side == OUTWARD:
            outs[0][:, at] = lax.dot_general(
                left[...], right[:, at], contract, preferred_element_type=jnp.float32
            ).astype(jnp.bfloat16)
            return
        made = lax.dot_general(left[:, at], right[...], contract, preferred_element_type=jnp.float32)
        made = made.astype(jnp.bfloat16)
        half = span // 2
        for number, out in enumerate(outs):
            width = out.shape[3]
            piece = made[:, number * width : (number + 1) * width]
            out[seq, 0], out[seq, 1] = piece[:half], piece[half:]


def grad_shape(model_width, rows, side):
    span = model_width // PLANE
    shape = (PLANE, 2, span // 2, rows) if side == INWARD else (rows, model_width)
    return jax.ShapeDtypeStruct(shape, jnp.bfloat16)


class HiddenFront(GradFront):
    def __init__(self, lifted, up_part, bias, cotangent_all, down_part, gain, shift, full_width):
        self.inputs = [lifted, up_part, bias, cotangent_all, down_part, gain, shift]
        self.full_width = full_width
        rows, width, model_width = lifted.shape[0], up_part.shape[1], lifted.shape[1]
        low_shape = jax.ShapeDtypeStruct((rows, width), jnp.bfloat16)
        self.out_shapes = [
            low_shape,
            low_shape,
            jax.ShapeDtypeStruct((8, width), jnp.float32),
            grad_shape(model_width, width, INWARD),
            grad_shape(model_width, width, OUTWARD),
        ]
        self.scratch = self.total_scratch(4, rows) + [pltpu.VMEM((rows, width), jnp.float32)] * 3

    def run(self):
        lifted, up_w, bias, cotangent_all, down_w, gain, shift = self.ins
        settled, d_hidden, vectors, up, down = self.outs
        activated, slope, d_settled = self.held[6:]
        f32 = jnp.float32
        bias, gain, shift = (own_line(self.here, line, settled.shape[1]) for line in (bias, gain, shift))
        rows = activated.shape[0]
        step = rows // 4
        for first in range(0, rows, step):
            at = slice(first, first + step)
            pre = jnp.dot(lifted[at, :], up_w[...], preferred_element_type=f32) + bias
            below = 0.5 + 0.5 * lax.erf(pre * (0.5**0.5))
            act = pre * below
            activated[at, :] = act
            slope[at, :] = below + pre * jnp.exp(-0.5 * pre * pre) * (1.0 / (2.0 * jnp.pi) ** 0.5)
            grad = lax.dot_general(
                cotangent_all[at, :], down_w[...], (((1,), (1,)), ((), ())), preferred_element_type=f32
            )
            d_settled[at, :] = grad
            scaled = grad * gain
            sums = [jnp.sum(part, 1, keepdims=True) for part in (act, act * act, scaled, scaled * act)]
            self.held[1][:, at] = as_lanes(sums)[:4]
            yield
        total = self.small_sum(self.held[:6]) / self.full_width
        average = total[:, 0:1]
        factor = lax.rsqrt(total[:, 1:2] - average * average + EPSILON)
        mean_scaled = total[:, 2:3]
        mean_cross = factor * (total[:, 3:4] - average * mean_scaled)
        step = rows // PLANE
        gain_sum = shift_sum = bias_sum = 0.0
        for first in range(0, rows, step):
            at = slice(first, first + step)
            normal = (activated[at, :] - average[at]) * factor[at]
            settled[at, :] = (normal * gain + shift).astype(jnp.bfloat16)
            grad = d_settled[at, :]
            inner = factor[at] * (grad * gain - mean_scaled[at] - normal * mean_cross[at])
            low = (slope[at, :] * inner).astype(jnp.bfloat16)
            d_hidden[at, :] = low
            gain_sum += jnp.sum(grad * normal, 0, keepdims=True)
            shift_sum += jnp.sum(grad, 0, keepdims=True)
            bias_sum += jnp.sum(low.astype(f32), 0, keepdims=True)
        vectors[...] = jnp.zeros_like(vectors)
        vectors[0:1, :], vectors[1:2, :], vectors[2:3, :] = gain_sum, shift_sum, bias_sum
        self.grads([(lifted, d_hidden, [up], INWARD), (settled, cotangent_all, [down], OUTWARD)])
        self.lefts = [d_hidden, settled]


class AttendBackFront(GradFront):
    def __init__(self, d_branch, out_part, hat, factor, gain, kept, tables, segment, column, normed, inner_low, full_width):
        self.inputs = [d_branch, out_part, hat, factor, gain, *kept, *tables]
        self.inputs += [segment, column, normed, inner_low]
        self.full_width = full_width
        rows, width = hat.shape
        model_width = normed.shape[1]
        low_type, f32 = jnp.bfloat16, jnp.float32
        self.out_shapes = [jax.ShapeDtypeStruct((8, width), f32)]
        self.out_shapes += [grad_shape(model_width, width, INWARD)] * 3 + [grad_shape(model_width, width, OUTWARD)]
        self.scratch = self.total_scratch(2, rows)
        self.scratch += [pltpu.VMEM((rows, width), low_type), pltpu.VMEM((rows, 3 * width), low_type)]
        self.scratch += [pltpu.VMEM((rows, width), f32)] * 4

    def run(self):
        d_branch, out_part, hat, factor, gain, attended, q_ref, k_ref, v_ref, lse = self.ins[:10]
        cos_ref, sin_ref, grow_ref, segment, column, normed, inner_low = self.ins[10:]
        gain = own_line(self.here, gain, hat.shape[1])
        vectors, *grads = self.outs
        d_att, lin_out, d_inner, d_query, d_key, d_value = self.held[6:]
        rows_all, width = hat.shape
        f32, low_type = jnp.float32, jnp.bfloat16
        gain_sum = shift_sum = 0.0
        for first in range(0, rows_all, ATTEND_ROWS):
            at = slice(first, first + ATTEND_ROWS)
            grad = lax.dot_general(
                d_branch[at, :], out_part[...], (((1,), (1,)), ((), ())), preferred_element_type=f32
            )
            d_inner[at, :] = grad
            gain_sum += jnp.sum(grad * hat[at, :], 0, keepdims=True)
            shift_sum += jnp.sum(grad, 0, keepdims=True)
            scaled = grad * gain
            sums = [jnp.sum(scaled, 1, keepdims=True), jnp.sum(scaled * hat[at, :], 1, keepdims=True)]
            self.held[1][:, at] = as_lanes(sums)[:2]
            yield
        vectors[...] = jnp.zeros_like(vectors)
        vectors[0:1, :], vectors[1:2, :] = gain_sum, shift_sum
        total = self.small_sum(self.held[:6]) / self.full_width
        d_att[...] = (
            factor[...] * (d_inner[...] * gain - total[:, 0:1] - hat[...] * total[:, 1:2])
        ).astype(low_type)
        heads, scale = width // HEAD, HEAD ** (-0.5)
        for first in range(0, rows_all, ATTEND_ROWS):
            at, keys = slice(first, first + ATTEND_ROWS), first + ATTEND_ROWS
            allowed = allowed_part(column, segment, first, ATTEND_ROWS, keys)
            for head in range(heads):
                lanes = slice(head * HEAD, (head + 1) * HEAD)
                scores = lax.dot_general(
                    q_ref[at, lanes] * scale,
                    k_ref[:keys, lanes],
                    (((1,), (1,)), ((), ())),
                    preferred_element_type=f32,
                )
                scores = jnp.where(allowed, scores, -1e30)
                probs = jnp.exp(scores - lse[at, head : head + 1])
                d_rows = d_att[at, lanes]
                d_probs = lax.dot_general(
                    d_rows, v_ref[:keys, lanes], (((1,), (1,)), ((), ())), preferred_element_type=f32
                )
                delta = jnp.sum(d_rows.astype(f32) * attended[at, lanes], -1, keepdims=True)
                d_scores = (probs * (d_probs - delta)).astype(low_type)
                d_query[at, lanes] = jnp.dot(d_scores, k_ref[:keys, lanes], preferred_element_type=f32) * scale
                key_part = (
                    lax.dot_general(
                        d_scores, q_ref[at, lanes], (((0,), (0,)), ((), ())), preferred_element_type=f32
                    )
                    * scale
                )
                value_part = lax.dot_general(
                    probs.astype(low_type), d_rows, (((0,), (0,)), ((), ())), preferred_element_type=f32
                )
                if first:
                    d_key[:first, lanes] += key_part[:first]
                    d_value[:first, lanes] += value_part[:first]
                d_key[first:keys, lanes] = key_part[first:]
                d_value[first:keys, lanes] = value_part[first:]
                yield
        for first in range(0, rows_all, ATTEND_ROWS):
            at = slice(first, first + ATTEND_ROWS)
            cosine, sine, growth = cos_ref[at, :], sin_ref[at, :], grow_ref[at, :]
            scaled = d_query[at, :] * growth
            lin_out[at, :width] = (scaled * cosine - halves_swapped(scaled) * sine).astype(low_type)
            scaled = d_key[at, :] * (1.0 / growth)
            lin_out[at, width : 2 * width] = (scaled * cosine - halves_swapped(scaled) * sine).astype(low_type)
            lin_out[at, 2 * width :] = d_value[at, :].astype(low_type)
        self.grads(
            [
                (normed, lin_out, grads[:3], INWARD),
                (inner_low, d_branch, grads[3:], OUTWARD),
            ]
        )
        self.lefts = [lin_out]


def lazy_call(kernel, inputs, in_specs, out_shapes, out_specs, scratch, cid):
    late = [is_lazy(value, spec) for value, spec in zip(inputs, in_specs)]
    buffers = [pltpu.VMEM(value.shape, value.dtype) for value, flag in zip(inputs, late) if flag]
    n_in, n_out, n_scratch, n_late = len(inputs), len(out_shapes), len(scratch), len(buffers)

    def body(*refs):
        refs = list(refs)
        ins, outs, held = refs[:n_in], refs[n_in : n_in + n_out], refs[n_in + n_out : n_in + n_out + n_scratch]
        spare, sems = refs[n_in + n_out + n_scratch : -1], refs[-1]
        lazies = []
        for number, flag in enumerate(late):
            if flag:
                ins[number] = Lazy(ins[number], spare[len(lazies)], sems.at[len(lazies)])
                lazies.append(ins[number])
        kernel(ins, outs, held)
        for item in lazies:
            item.ready()

    return pl.pallas_call(
        body,
        out_shape=tuple(out_shapes),
        in_specs=[ANYWHERE if flag else spec for spec, flag in zip(in_specs, late)],
        out_specs=tuple(out_specs),
        scratch_shapes=list(scratch) + buffers + [pltpu.SemaphoreType.DMA((max(n_late, 1),))],
        compiler_params=pltpu.CompilerParams(
            collective_id=cid, has_side_effects=True, vmem_limit_bytes=VMEM_BYTES
        ),
    )(*inputs)


def exchange(front, streams, riders, cid, early=None, pace=1, early_pace=5):
    fronts = [front] if front is not None else []
    earlies = [early] if early is not None else []
    sums = list(streams) + earlies
    parts = fronts + sums + list(riders)

    def kernel(ins, outs, held):
        here = Places()
        ins, outs, held = list(ins), list(outs), list(held)

        def take(refs, count):
            taken = refs[:count]
            del refs[:count]
            return taken

        for part in parts:
            part.bind(
                here, take(ins, len(part.inputs)), take(outs, len(part.out_shapes)), take(held, len(part.scratch))
            )
        wide_parts = [part for part in parts if isinstance(part, (Front, ChainWeights))]
        peers = [here.tp_peer]
        if riders:
            peers.append(here.img_peer)
        if wide_parts:
            peers += wide_parts[0].peers(here)
        else:
            peers += [here.core, here.x, here.y]
        greet(peers)
        waiting, crossing = [], []
        for rider in riders:
            rider.start()
            if rider.later:
                take_some(rider.launches, len(rider.launches))
            waiting += rider.launches + rider.later
        early_steps = []
        if early is not None:
            early.begin()
            early_steps = early.phases()
            take_some(early_steps, 1)
        if front is not None:
            for number, _ in enumerate(front.run(), 1):
                take_some(waiting, pace)
                if number % early_pace == 0 and len(early_steps) > 1:
                    take_some(early_steps, 1)
            for stream, left in zip(streams, front.lefts):
                stream.left = left
            waiting += front.launches
        for stream in streams:
            stream.begin()
        stages = []
        for number, stream in reversed(list(enumerate(streams))):
            stages += [(lag + number * SECOND_LAG, stage) for lag, stage in stream.stages()]
        ticks = ticks_of(stages, PIECES)
        share = -(-len(waiting) // max(len(ticks) - 2, 1))
        for number, tick in enumerate(ticks):
            tick()
            if number >= PIECES:
                take_some(early_steps, 1)
            take_some(waiting, share)
        take_some(early_steps, len(early_steps))
        for part in parts:
            part.finish()

    in_specs = []
    for part in fronts + sums:
        in_specs += part.in_specs or [ON_CHIP] * len(part.inputs)
    in_specs += [ANYWHERE] * sum(len(rider.inputs) for rider in riders)
    out_specs = [ON_CHIP for part in fronts for _ in part.out_shapes]
    out_specs += [spec for stream in sums for spec in stream.out_specs()]
    out_specs += [ANYWHERE] * sum(len(rider.out_shapes) for rider in riders)
    made = list(
        lazy_call(
            kernel,
            [value for part in parts for value in part.inputs],
            in_specs,
            [shape for part in parts for shape in part.out_shapes],
            out_specs,
            [item for part in parts for item in part.scratch],
            cid,
        )
    )
    split = []
    for part in parts:
        split.append(made[: len(part.out_shapes)])
        del made[: len(part.out_shapes)]
    return split


def finale(pairs, sides, raw, raw_sides, image, row_vectors, own_vectors, latents, query_rows, result_parts, cid):
    f32, low_type, dma = jnp.float32, jnp.bfloat16, pltpu.SemaphoreType.DMA
    d_rows, pictures, keys, probe, placed, out_part, target_rows = image
    width, model_width, picture_width = probe.shape[1], d_rows.shape[1], pictures.shape[1]
    images = pictures.shape[0] // PATCH
    image_shapes = [
        grad_shape(picture_width, width, INWARD),
        grad_shape(picture_width, width, INWARD),
        grad_shape(model_width, width, OUTWARD),
    ]
    all_sides = list(sides) + list(raw_sides) + [INWARD, INWARD, OUTWARD]
    n, n_raw, n_image = len(sides), len(raw_sides), len(image_shapes)
    total = n + n_raw + n_image
    shapes = [grad.shape for grad, _ in pairs] + [grad.shape for grad in raw] + [item.shape for item in image_shapes]
    blocks = [
        shape[2:] if side == INWARD else (shape[0], shape[1] // (2 * PLANE)) for shape, side in zip(shapes, all_sides)
    ]
    vectors = list(row_vectors) + [array for array, _ in own_vectors]
    picked = [0] * len(row_vectors) + [row for _, row in own_vectors]
    vector_rows = sum(vector.shape[1] // LANES for vector in vectors)
    small_shape = (LAT + vector_rows + -vector_rows % 8, LANES)
    result_shape = result_parts[0].shape

    def kernel(ins, outs, held):
        refs = list(ins) + list(outs) + list(held)

        def take(count):
            taken = refs[:count]
            del refs[:count]
            return taken

        target_ref, d_ref, pictures_ref, keys_ref, probe_ref, placed_ref, out_w = take(7)
        grad_refs = take(n + n_raw)
        theirs = take(n)
        vector_refs = take(len(vectors))
        latents_ref, query_ref, result_ref, result_here, middle_ref = take(5)
        out_refs = take(total)
        sums_out, query_out, latent_out, result_out = take(4)
        grad_refs += take(n_image)
        theirs += take(n_raw + n_image)
        summed = take(total)
        small_own, small_theirs, small_mine, small_all, lat_mine, lat_theirs, d_mixed, d_both, result_theirs = take(9)
        z_send, z_recv, send, recv, local, s_send, s_recv, r_send, r_recv = take(9)
        here = Places()
        seq, img = here.seq, here.img
        ring = [here.at(lax.rem(seq + step, PLANE)) for step in range(1, PLANE)]
        greet(ring + [here.img_peer, here.tp_peer])

        def part_of(index, to_seq, to_img):
            ref, block = grad_refs[index], blocks[index]
            if all_sides[index] == INWARD:
                return ref.at[to_seq, to_img]
            return ref.at[:, pl.ds(pl.multiple_of((to_seq * 2 + to_img) * block[1], block[1]), block[1])]

        def slot_of(index, from_seq):
            ref, block = out_refs[index], blocks[index]
            if all_sides[index] == INWARD:
                return ref.at[:, pl.ds(pl.multiple_of(from_seq * block[1], block[1]), block[1])]
            return ref.at[pl.ds(pl.multiple_of(from_seq * block[0], block[0]), block[0])]

        waits, crossings = [], {}

        def cross(index):
            for step in range(PLANE):
                target = lax.rem(seq + step, PLANE)
                made = remote(
                    part_of(index, target, 1 - img),
                    theirs[index].at[target],
                    z_send.at[index - n, step],
                    z_recv.at[index - n, step],
                    here.img_peer,
                )
                made.start()
                crossings[index, step] = made

        def deliver(index, step):
            target = lax.rem(seq + step, PLANE)
            if index >= n:
                crossings[index, step].wait_recv()
            mine = part_of(index, target, img)[...].astype(f32)
            summed[index][target] = (mine + theirs[index][target].astype(f32)).astype(low_type)
            if step == 0:
                made = pltpu.make_async_copy(summed[index].at[target], slot_of(index, seq), local.at[index])
                made.start()
                waits.append(made.wait)
                return
            made = remote(
                summed[index].at[target], slot_of(index, seq), send.at[index, step], recv.at[index, step], here.at(target)
            )
            made.start()
            waits.append(made.wait_send)

        result_copy = remote(result_ref, result_theirs, r_send.at[0], r_recv.at[0], here.tp_peer)
        result_copy.start()
        for index in range(n, n + n_raw):
            cross(index)
        at_row = LAT
        for vector, row in zip(vector_refs, picked):
            for first in range(0, vector.shape[1], LANES):
                small_own[at_row : at_row + 1, :] = vector[row : row + 1, first : first + LANES]
                at_row += 1
        if at_row < small_shape[0]:
            small_own[at_row:, :] = jnp.zeros((small_shape[0] - at_row, LANES), f32)
        waiting = [functools.partial(deliver, index, step) for index in range(n + n_raw) for step in range(PLANE)]

        scale = HEAD ** (-0.5)
        d_slots = jnp.zeros(d_mixed.shape, f32)
        for first in range(0, d_ref.shape[0], PATCH):
            d_part = lax.dot_general(
                d_ref[first : first + PATCH, :], out_w[...], (((1,), (1,)), ((), ())), preferred_element_type=f32
            ).astype(low_type)
            chosen = chosen_rows(target_ref, first, PATCH)
            d_slots += lax.dot_general(chosen, d_part, (((0,), (0,)), ((), ())), preferred_element_type=f32)
        d_mixed[...] = d_slots.astype(low_type)
        take_some(waiting, 1)
        for first in range(0, model_width, 512):
            at = slice(first, first + 512)
            grad_refs[total - 1][:, at] = lax.dot_general(
                placed_ref[...], d_ref[:, at], (((0,), (0,)), ((), ())), preferred_element_type=f32
            ).astype(low_type)
            take_some(waiting, 1)
        cross(total - 1)
        d_probe_sum = jnp.zeros(probe_ref.shape, f32)
        for number in range(images):
            rows = slice(number * PATCH, (number + 1) * PATCH)
            d_here = d_mixed[number * LAT : (number + 1) * LAT, :]
            d_probe = []
            for first in range(0, width, HEAD):
                at = slice(first, first + HEAD)
                keys_here = keys_ref[rows, at]
                values = keys_ref[rows, width + first : width + first + HEAD]
                probs = image_probs_of(probe_ref[:, at], keys_here, scale)
                d_probs = lax.dot_general(
                    d_here[:, at], values, (((1,), (1,)), ((), ())), preferred_element_type=f32
                )
                d_scores = probs * (d_probs - jnp.sum(probs * d_probs, -1, keepdims=True))
                d_scores = d_scores.astype(low_type)
                d_probe.append(jnp.dot(d_scores, keys_here, preferred_element_type=f32) * scale)
                d_both[rows, at] = (
                    lax.dot_general(
                        d_scores, probe_ref[:, at], (((0,), (0,)), ((), ())), preferred_element_type=f32
                    )
                    * scale
                ).astype(low_type)
                d_both[rows, width + first : width + first + HEAD] = lax.dot_general(
                    probs.astype(low_type), d_here[:, at], (((0,), (0,)), ((), ())), preferred_element_type=f32
                ).astype(low_type)
            d_probe_sum += jnp.concatenate(d_probe, 1)
            take_some(waiting, 2)
        small_own[:LAT, :] = d_probe_sum
        small_cross = remote(small_own, small_theirs, s_send.at[0], s_recv.at[0], here.img_peer)
        small_cross.start()
        span = picture_width // PLANE
        for part in range(PLANE):
            made = lax.dot_general(
                pictures_ref[:, part * span : (part + 1) * span],
                d_both[...],
                (((0,), (0,)), ((), ())),
                preferred_element_type=f32,
            ).astype(low_type)
            for kind in range(2):
                piece = made[:, kind * width : (kind + 1) * width]
                grad_refs[n + n_raw + kind][part, 0] = piece[: span // 2]
                grad_refs[n + n_raw + kind][part, 1] = piece[span // 2 :]
            take_some(waiting, 2)
        for kind in range(2):
            cross(n + n_raw + kind)
        small_cross.wait()
        small_mine[...] = small_own[...] + small_theirs[...]
        small_all[seq] = small_mine[...]
        small_copies = []
        for step, peer in enumerate(ring, 1):
            made = remote(small_mine, small_all.at[seq], s_send.at[step], s_recv.at[step], peer)
            made.start()
            small_copies.append(made)
        take_some(waiting, len(waiting))
        for index in (total - 1, total - 3, total - 2):
            for step in range(PLANE):
                deliver(index, step)
        for made in small_copies:
            made.wait()
        sums_out[...] = small_all[...]
        latent_part = jnp.zeros(lat_mine.shape, f32)
        for source in range(PLANE):
            given = small_all[source, :LAT, :]
            at = slice(source * width, (source + 1) * width)
            query_out[:, at] = lax.dot_general(
                latents_ref[...].astype(f32),
                given,
                (((0,), (0,)), ((), ())),
                precision=HIGHEST_PRECISION,
                preferred_element_type=f32,
            )
            latent_part += lax.dot_general(
                given,
                query_ref[:, at].astype(f32),
                (((1,), (1,)), ((), ())),
                precision=HIGHEST_PRECISION,
                preferred_element_type=f32,
            )
        lat_mine[...] = latent_part
        last = remote(lat_mine, lat_theirs, s_send.at[PLANE], s_recv.at[PLANE], here.tp_peer)
        last.start()
        last.wait()
        latent_out[...] = lat_mine[...] + lat_theirs[...]
        result_copy.wait()
        result_sum = result_here[...].astype(f32) + result_theirs[...].astype(f32)
        result_out[...] = (middle_ref[...] + result_sum).astype(low_type)
        for index in range(total):
            for step in range(1, PLANE):
                source = lax.rem(seq + PLANE - step, PLANE)
                at = slot_of(index, source)
                remote(at, at, send.at[index, step], recv.at[index, step], here.core).wait_recv()
        for wait in waits:
            wait()
        for made in crossings.values():
            made.wait_send()

    outs = []
    for block, side in zip(blocks, all_sides):
        shape = (block[0], PLANE * block[1]) if side == INWARD else (PLANE * block[0], block[1])
        outs.append(jax.ShapeDtypeStruct(shape, low_type))
    lat_shape = latents.shape
    small_shapes = [
        jax.ShapeDtypeStruct((PLANE,) + small_shape, f32),
        jax.ShapeDtypeStruct(query_rows.shape, f32),
        jax.ShapeDtypeStruct(lat_shape, f32),
        jax.ShapeDtypeStruct(result_shape, low_type),
    ]
    n_cross = n_raw + n_image
    made = lazy_call(
        kernel,
        [
            target_rows,
            d_rows,
            pictures,
            keys,
            probe,
            placed,
            out_part,
            *[grad for grad, _ in pairs],
            *raw,
            *[given for _, given in pairs],
            *vectors,
            latents,
            query_rows,
            result_parts[0],
            *result_parts,
        ],
        [ON_CHIP] * (7 + n + n_raw + n + len(vectors)) + [ON_CHIP] * 2 + [ANYWHERE, ON_CHIP, ON_CHIP],
        outs + small_shapes,
        [ANYWHERE] * total + [ON_CHIP] * 4,
        [pltpu.VMEM(item.shape, low_type) for item in image_shapes]
        + [pltpu.VMEM((PLANE,) + tuple(block), low_type) for block in blocks[n:]]
        + [pltpu.VMEM((PLANE,) + tuple(block), low_type) for block in blocks]
        + [
            pltpu.VMEM(small_shape, f32),
            pltpu.VMEM(small_shape, f32),
            pltpu.VMEM(small_shape, f32),
            pltpu.VMEM((PLANE,) + small_shape, f32),
            pltpu.VMEM(lat_shape, f32),
            pltpu.VMEM(lat_shape, f32),
            pltpu.VMEM((d_rows.shape[0], width), low_type),
            pltpu.VMEM((images * PATCH, 2 * width), low_type),
            pltpu.VMEM(result_shape, low_type),
            dma((n_cross, PLANE)),
            dma((n_cross, PLANE)),
            dma((total, PLANE)),
            dma((total, PLANE)),
            dma((total,)),
            dma((PLANE + 1,)),
            dma((PLANE + 1,)),
            dma((1,)),
            dma((1,)),
        ],
        cid,
    )
    return made[:total], made[total:]


def widened(grads, passed, spread, model_width, n_rows, widths):
    f32, dma = jnp.float32, pltpu.SemaphoreType.DMA
    n, n_passed = len(grads), len(passed)

    def kernel(*refs):
        refs = list(refs)

        def take(count):
            taken = refs[:count]
            del refs[:count]
            return taken

        ins, passed_ins, (spread_ref,) = take(n), take(n_passed), take(1)
        outs, passed_outs, row_outs, own_outs = take(n), take(n_passed), take(n_rows), take(len(widths))
        narrow, wide, held, (in_sems, out_sems, passed_sems) = take(n), take(n), take(n_passed), take(3)
        copies_in = [pltpu.make_async_copy(src, dst, in_sems.at[i]) for i, (src, dst) in enumerate(zip(ins, narrow))]
        copies_out = [pltpu.make_async_copy(src, dst, out_sems.at[i]) for i, (src, dst) in enumerate(zip(wide, outs))]
        held_in = [pltpu.make_async_copy(src, dst, passed_sems.at[0, i]) for i, (src, dst) in enumerate(zip(passed_ins, held))]
        held_out = [pltpu.make_async_copy(src, dst, passed_sems.at[1, i]) for i, (src, dst) in enumerate(zip(held, passed_outs))]
        for copy in copies_in + held_in:
            copy.start()
        for i in range(n):
            copies_in[i].wait()
            wide[i][...] = narrow[i][...].astype(f32)
            copies_out[i].start()
        for arrive, leave in zip(held_in, held_out):
            arrive.wait()
            leave.start()
        first = LAT
        for out in row_outs:
            count = model_width // LANES
            total = jnp.sum(spread_ref[:, first : first + count, :], 0)
            for part in range(count):
                out[:, part * LANES : (part + 1) * LANES] = total[part : part + 1, :]
            first += count
        for out, width in zip(own_outs, widths):
            for seq in range(PLANE):
                for part in range(width // LANES):
                    at = seq * width + part * LANES
                    out[:, at : at + LANES] = spread_ref[seq, first + part : first + part + 1, :]
            first += width // LANES
        for copy in copies_out + held_out:
            copy.wait()

    shapes = [jax.ShapeDtypeStruct(array.shape, f32) for array in grads]
    shapes += [jax.ShapeDtypeStruct(array.shape, array.dtype) for array in passed]
    shapes += [jax.ShapeDtypeStruct((1, model_width), f32)] * n_rows
    shapes += [jax.ShapeDtypeStruct((1, PLANE * width), f32) for width in widths]
    small = n_rows + len(widths)
    made = pl.pallas_call(
        kernel,
        out_shape=tuple(shapes),
        in_specs=[ANYWHERE] * (n + n_passed) + [ON_CHIP],
        out_specs=tuple([ANYWHERE] * (n + n_passed) + [ON_CHIP] * small),
        scratch_shapes=[pltpu.VMEM(array.shape, array.dtype) for array in grads]
        + [pltpu.VMEM(array.shape, f32) for array in grads]
        + [pltpu.VMEM(array.shape, array.dtype) for array in passed]
        + [dma((n,)), dma((n,)), dma((2, n_passed))],
        compiler_params=pltpu.CompilerParams(vmem_limit_bytes=VMEM_BYTES),
    )(*grads, *passed, spread)
    made = list(made)
    cut = [made[:n], made[n : n + n_passed], made[n + n_passed : n + n_passed + n_rows]]
    return (*cut, made[n + n_passed + n_rows :])


IMAGES_A_STEP = 4


def image_probs_of(probe, keys, scale):
    scores = lax.dot_general(
        probe * scale, keys, (((1,), (1,)), ((), ())), preferred_element_type=jnp.float32
    )
    weights = jnp.exp(scores - jnp.max(scores, -1, keepdims=True))
    return weights * (1.0 / jnp.sum(weights, -1, keepdims=True))


def xpos_part(segment, column, tables, first):
    at, half = slice(first, first + ATTEND_ROWS), HEAD // 2
    f32 = jnp.float32
    rows = segment.shape[1]
    here = segment[:, at].astype(f32)
    earlier = lax.broadcasted_iota(jnp.int32, (rows, ATTEND_ROWS), 0)
    now = first + lax.broadcasted_iota(jnp.int32, (rows, ATTEND_ROWS), 1)
    counted = (column[:, 0:1] == here) & (earlier < now)
    position = jnp.sum(counted.astype(f32), 0, keepdims=True)
    ladder = lax.broadcasted_iota(jnp.int32, (half, ATTEND_ROWS), 0).astype(f32)
    angles = position * jnp.exp(ladder * (-2.0 * jnp.log(f32(10000.0)) / (2.0 * half)))
    growth = jnp.exp(position / 512.0 * jnp.log((ladder / half + 0.4) / 1.4))
    cosine, sine = jnp.cos(angles), jnp.sin(angles)
    repeats = tables[0].shape[1] // HEAD
    tables[0][at, :] = jnp.concatenate([cosine, cosine] * repeats, 0).T
    tables[1][at, :] = jnp.concatenate([-sine, sine] * repeats, 0).T
    tables[2][at, :] = jnp.concatenate([growth, growth] * repeats, 0).T


def halves_swapped(rows):
    width, half = rows.shape[1], HEAD // 2
    lane = lax.broadcasted_iota(jnp.int32, rows.shape, 1)
    ahead = pltpu.roll(rows, width - half, 1)
    behind = pltpu.roll(rows, half, 1)
    return jnp.where(lane % HEAD < half, ahead, behind)


def allowed_part(column, segment, first, count, keys):
    row = first + lax.broadcasted_iota(jnp.int32, (count, keys), 0)
    later = lax.broadcasted_iota(jnp.int32, (count, keys), 1)
    same = column[first : first + count, 0:1] == segment[:, :keys].astype(jnp.float32)
    return same & (later <= row)


ATTEND_ROWS = 256


def as_lanes(columns):
    rows = columns[0].shape[0]
    lane = lax.broadcasted_iota(jnp.int32, (rows, LANES), 1)
    joined = jnp.zeros((rows, LANES), jnp.float32)
    for number, column in enumerate(columns):
        joined = jnp.where(lane == number, column, joined)
    return joined.T[:8, :]


def norm_rows(rows, gain, shift):
    center = rows - jnp.mean(rows, -1, keepdims=True)
    factor = lax.rsqrt(jnp.mean(center * center, -1, keepdims=True) + EPSILON)
    normal = center * factor
    return (normal * gain + shift, normal, factor)


def dot32(left, right):
    return jnp.dot(left, right, preferred_element_type=jnp.float32)


def on_plane(
    text,
    segment,
    features,
    image_count,
    image_slot,
    cotangent,
    input_gain,
    input_shift,
    query_weight,
    key_weight,
    value_weight,
    inner_gain,
    inner_shift,
    out_weight,
    middle_gain,
    middle_shift,
    up_weight,
    up_bias,
    hidden_gain,
    hidden_shift,
    down_weight,
    latents,
    resample_query,
    resample_key,
    resample_value,
    resample_out,
):
    f32, low = jnp.float32, jnp.bfloat16
    row_count, model_width = text.shape[1], text.shape[2]
    group_rows = segment.shape[1]
    image_slots = features.shape[1]
    half_width = query_weight.shape[1]
    own_width = half_width // PLANE

    rows, own = intake(
        (features[0].reshape(image_slots * PATCH, features.shape[3]),),
        (
            resample_key,
            resample_value,
            resample_query,
            latents,
            resample_out,
        ),
        (INWARD, INWARD, INWARD, SHARED, OUTWARD),
        1,
    )
    (pictures,) = rows
    image_key_own, image_value_own, probe_own, latent_all, image_out_own = own

    counts = image_count.reshape(-1, 1)
    live = jnp.arange(IMG_DEV, dtype=jnp.int32)[None, :] < counts
    first_rows = jnp.where(live, image_slot.reshape(live.shape) * LAT, -LAT)
    target_rows = (first_rows[:, :, None] + jnp.arange(LAT, dtype=jnp.int32)).reshape(1, -1)

    def line(vector):
        return vector.reshape(-1, LANES)

    def taken_in(targets, piece, rows):
        first = lax.axis_index(SEQ) * row_count + sum(PIECE_ROWS[:piece])
        row = first + lax.broadcasted_iota(jnp.int32, (rows, targets.shape[1]), 0)
        return jnp.max((row == targets[...]).astype(jnp.float32), 1, keepdims=True) > 0.5

    def begin(total, piece, views, outs):
        text_view, targets, gain, shift = views
        embed = total.astype(jnp.bfloat16).astype(jnp.float32)
        taken = taken_in(targets, piece, total.shape[0])
        mixed = jnp.where(taken, embed, text_view[...].astype(jnp.float32))
        outs[0][...] = mixed
        return norm_rows(mixed, full_line(gain), full_line(shift))[0].astype(jnp.bfloat16)

    rows_wide = jax.ShapeDtypeStruct((row_count, model_width), f32)
    (image_keys, mixed_placed, probe, *tables, column), (mixed_in, normed), (qkv_own, out_own, up_own) = exchange(
        ImageFront(
            pictures, image_key_own, image_value_own, latent_all, probe_own, target_rows, segment
        ),
        [
            Stream(
                group_rows,
                None,
                image_out_own,
                False,
                (text[0], target_rows, line(input_gain), line(input_shift)),
                (ROWS, ALL, ALL, ALL),
                ((rows_wide, ROWS),),
                begin,
                True,
            )
        ],
        [
            ChainWeights(
                (query_weight, key_weight, value_weight, out_weight, up_weight),
                (INWARD, INWARD, INWARD, OUTWARD, INWARD),
                ((0, 0), (0, own_width), (0, 2 * own_width), (1, 0), (2, 0)),
            )
        ],
        3,
    )

    def middle_step(total, piece, views, outs):
        mixed_view, gain, shift = views
        middle = mixed_view[...] + total
        outs[0][...] = middle
        return norm_rows(middle, full_line(gain), full_line(shift))[0].astype(jnp.bfloat16)

    attend_made, (middle, lifted), (down_own,), (cot_all,) = exchange(
        AttendFront(
            normed, qkv_own, tables, segment, column, line(inner_gain), line(inner_shift), model_width
        ),
        [
            Stream(
                group_rows,
                None,
                out_own,
                False,
                (mixed_in, line(middle_gain), line(middle_shift)),
                (ROWS, ALL, ALL),
                ((rows_wide, ROWS),),
                middle_step,
                True,
            )
        ],
        [ChainWeights((down_weight,), (OUTWARD,), ((0, 0),)), GatherRows(cotangent[0])],
        5,
        pace=2,
    )
    *attended_kept, inner_low, inner_hat, inner_factor = attend_made
    query_rot, keys_rot, values, attended, log_total = attended_kept
    own_hidden = up_own.shape[1]

    vector_out = jax.ShapeDtypeStruct((1, model_width), f32)

    def norm_back_step(total, piece, views, outs):
        rows_view, carried_view, gain, *targets = views
        rows_in = rows_view[...]
        center = rows_in - jnp.mean(rows_in, -1, keepdims=True)
        factor = lax.rsqrt(jnp.mean(center * center, -1, keepdims=True) + EPSILON)
        normal = center * factor
        grad = carried_view[...].astype(jnp.float32) + full_back(total, normal, factor, full_line(gain))
        if targets:
            outs[0][...] = jnp.where(taken_in(targets[0], piece, total.shape[0]), 0.0, grad)
        else:
            outs[0][...] = grad
        if piece == 0:
            outs[1][...] = jnp.zeros_like(outs[1])
            outs[2][...] = jnp.zeros_like(outs[2])
        outs[1][...] += jnp.sum(total * normal, 0, keepdims=True)
        outs[2][...] += jnp.sum(total, 0, keepdims=True)
        return grad.astype(jnp.bfloat16)

    hidden_made, (d_middle, middle_gain_grad, middle_shift_grad, d_branch) = exchange(
        HiddenFront(
            lifted,
            up_own,
            line(up_bias),
            cot_all,
            down_own,
            line(hidden_gain),
            line(hidden_shift),
            FF,
        ),
        [
            Stream(
                group_rows,
                None,
                up_own,
                True,
                (middle, cotangent[0], line(middle_gain)),
                (ROWS, ROWS, ALL),
                ((rows_wide, ROWS), (vector_out, ALL), (vector_out, ALL)),
                norm_back_step,
                True,
            ),
        ],
        [],
        8,
    )

    settled, _, hidden_vectors, *hidden_grads = hidden_made
    result_part, d_branch = lax.optimization_barrier((dot32(settled, down_own).astype(low), d_branch))
    result_rows = lax.psum_scatter(result_part, SEQ, scatter_dimension=0, tiled=True)
    back_made, (text_grad, input_gain_grad, input_shift_grad, d_rows), hidden_theirs = exchange(
        AttendBackFront(
            d_branch,
            out_own,
            inner_hat,
            inner_factor,
            line(inner_gain),
            (attended, query_rot, keys_rot, values, log_total),
            tables,
            segment,
            column,
            normed,
            inner_low,
            model_width,
        ),
        [
            Stream(
                group_rows,
                None,
                qkv_own,
                True,
                (mixed_in, d_middle, line(input_gain), target_rows),
                (ROWS, ROWS, ALL, ALL),
                ((rows_wide, ROWS), (vector_out, ALL), (vector_out, ALL)),
                norm_back_step,
                True,
            ),
        ],
        [CrossGrads(hidden_grads, (INWARD, OUTWARD))],
        10,
    )
    inner_vectors, *layer_grads = back_made
    row_vectors = (input_gain_grad, input_shift_grad, middle_gain_grad, middle_shift_grad)
    own_vectors = (
        (inner_vectors, 0),
        (inner_vectors, 1),
        (hidden_vectors, 2),
        (hidden_vectors, 0),
        (hidden_vectors, 1),
    )
    layer_sides = (INWARD, INWARD, INWARD, OUTWARD)
    owned, (spread, resample_query_grad, latent_grad, result) = finale(
        list(zip(hidden_grads, hidden_theirs)),
        (INWARD, OUTWARD),
        layer_grads,
        layer_sides,
        (d_rows, pictures, image_keys, probe, mixed_placed, image_out_own, target_rows),
        row_vectors,
        own_vectors,
        latents,
        resample_query,
        (result_rows, middle),
        12,
    )
    widths = (own_width, own_width, own_hidden, own_hidden, own_hidden)
    grads, passed, row_sums, own_sums = widened(
        owned, (result, text_grad, resample_query_grad, latent_grad), spread, model_width, len(row_vectors), widths
    )
    up_sum, down_sum, query_sum, key_sum, value_sum, out_sum, image_key_sum, image_value_sum, image_out_sum = grads
    result, text_grad, resample_query_grad, latent_grad = passed
    row_sums = [vector.reshape(-1) for vector in row_sums]
    inner_gain_sum, inner_shift_sum, up_bias_sum, hidden_gain_sum, hidden_shift_sum = (
        vector.reshape(-1) for vector in own_sums
    )

    return (
        result[None],
        text_grad[None],
        row_sums[0],
        row_sums[1],
        query_sum,
        key_sum,
        value_sum,
        inner_gain_sum,
        inner_shift_sum,
        out_sum,
        row_sums[2],
        row_sums[3],
        up_sum,
        up_bias_sum,
        hidden_gain_sum,
        hidden_shift_sum,
        down_sum,
        latent_grad,
        resample_query_grad,
        image_key_sum,
        image_value_sum,
        image_out_sum,
    )


def solution(mesh):
    placed = (
        P(IMG, SEQ, None),
        P(IMG, None),
        P(IMG, SEQ, None, None),
        P(IMG, None),
        P(IMG, None),
        P(IMG, SEQ, None),
        P(),
        P(),
        P((SEQ, IMG), TP),
        P((SEQ, IMG), TP),
        P((SEQ, IMG), TP),
        P(TP),
        P(TP),
        P(TP, (SEQ, IMG)),
        P(),
        P(),
        P((SEQ, IMG), TP),
        P(TP),
        P(TP),
        P(TP),
        P(TP, (SEQ, IMG)),
        P(None, (SEQ, IMG)),
        P((SEQ, IMG), TP),
        P((SEQ, IMG), TP),
        P((SEQ, IMG), TP),
        P(TP, (SEQ, IMG)),
    )
    return jax.shard_map(
        on_device if narrow_heads(mesh) else on_plane,
        mesh=mesh,
        in_specs=placed,
        out_specs=(
            P(IMG, SEQ, None),
            P(IMG, SEQ, None),
            P(),
            P(),
            P((SEQ, IMG), TP),
            P((SEQ, IMG), TP),
            P((SEQ, IMG), TP),
            P(TP),
            P(TP),
            P(TP, (SEQ, IMG)),
            P(),
            P(),
            P((SEQ, IMG), TP),
            P(TP),
            P(TP),
            P(TP),
            P(TP, (SEQ, IMG)),
            P(None, (SEQ, IMG)),
            P((SEQ, IMG), TP),
            P((SEQ, IMG), TP),
            P((SEQ, IMG), TP),
            P(TP, (SEQ, IMG)),
        ),
        check_vma=False,
    )
```

```python
import functools

import jax
import jax.numpy as jnp
from jax import lax
from jax.experimental import pallas as pl
from jax.experimental.pallas import tpu as pltpu
from jax.sharding import PartitionSpec as P

SEQ, TP, IMG = "seq", "tp", "img"
HEAD = 64
FF = 8192
PATCH = 256
LAT = 64
SEQ_MAX = 2048
IMG_DEV = 2


EPSILON = 1e-05
HIGHEST_PRECISION = lax.Precision.HIGHEST


def shortened(x):

    def short(part):
        return part.astype(jnp.bfloat16) if part.dtype == jnp.float32 else part

    return jax.tree.map(short, x)


def xpos_factors(position, half_size):
    ladder = jnp.arange(half_size, dtype=jnp.float32)
    frequency = jnp.exp(ladder * (-2.0 * jnp.log(10000.0) / (2.0 * half_size)))
    decay_base = (ladder / half_size + 0.4) / 1.4
    angles = position[:, None] * frequency[None, :]
    growth = jnp.exp(position[:, None] / 512.0 * jnp.log(decay_base)[None, :])
    return (jnp.cos(angles)[:, None, :], jnp.sin(angles)[:, None, :], growth[:, None, :])


def rotate(inputs, cosine, sine_table, factor):
    half_size = inputs.shape[-1] // 2
    first_half = inputs[..., :half_size]
    second_half = inputs[..., half_size:]
    turned = jnp.concatenate(
        [
            first_half * cosine - second_half * sine_table,
            first_half * sine_table + second_half * cosine,
        ],
        -1,
    )
    return turned * jnp.concatenate([factor, factor], -1)


def rotate_back(gradient, cosine, sine_table, factor):
    half_size = gradient.shape[-1] // 2
    scaled = gradient * jnp.concatenate([factor, factor], -1)
    first_half = scaled[..., :half_size]
    second_half = scaled[..., half_size:]
    return jnp.concatenate(
        [
            first_half * cosine + second_half * sine_table,
            second_half * cosine - first_half * sine_table,
        ],
        -1,
    )


def tp_total(inputs):
    return jax.tree.map(lambda part: part.astype(jnp.float32), lax.psum(shortened(inputs), TP))


def full_norm(inputs, norm_gain, norm_shift):
    center = inputs - jnp.mean(inputs, -1, keepdims=True)
    spread = jnp.mean(center * center, -1, keepdims=True)
    factor = lax.rsqrt(spread + EPSILON)
    normal = center * factor
    return (normal * norm_gain + norm_shift, normal, factor)


def full_back(gradient, normal, factor, norm_gain):
    scaled = gradient * norm_gain
    return factor * (
        scaled
        - jnp.mean(scaled, -1, keepdims=True)
        - normal * jnp.mean(scaled * normal, -1, keepdims=True)
    )


def split_norm(inputs, norm_gain, norm_shift, full_width):
    totals = tp_total(
        (jnp.sum(inputs, -1, keepdims=True), jnp.sum(inputs * inputs, -1, keepdims=True))
    )
    average = totals[0] / full_width
    spread = totals[1] / full_width - average * average
    factor = lax.rsqrt(spread + EPSILON)
    normal = (inputs - average) * factor
    return (normal * norm_gain + norm_shift, normal, factor)


def split_back(gradient, normal, factor, norm_gain, full_width):
    scaled = gradient * norm_gain
    totals = tp_total(
        (jnp.sum(scaled, -1, keepdims=True), jnp.sum(scaled * normal, -1, keepdims=True))
    )
    return factor * (scaled - totals[0] / full_width - normal * (totals[1] / full_width))


def attend_piece(
    running, query_rot, key_piece, value_piece, row_index, row_segment, segment_all, score_scale
):
    heads_local = query_rot.shape[1]
    amount = key_piece.shape[0]
    block_size = 1024

    def step(state_in, number):
        first_row = number * block_size
        key_block = lax.dynamic_slice_in_dim(key_piece, first_row, block_size, 0).reshape(
            block_size, heads_local, -1
        )
        value_block = lax.dynamic_slice_in_dim(value_piece, first_row, block_size, 0).reshape(
            block_size, heads_local, -1
        )
        key_index = first_row + jnp.arange(block_size, dtype=jnp.int32)
        key_segment = lax.dynamic_slice_in_dim(segment_all, first_row, block_size, 0)
        scores = (
            jnp.einsum("qhd,khd->hqk", query_rot, key_block, preferred_element_type=jnp.float32)
            * score_scale
        )
        allowed = (key_index[None, :] <= row_index[:, None]) & (
            key_segment[None, :] == row_segment[:, None]
        )
        scores = jnp.where(allowed[None], scores, -1e30)
        best_old, total_old, accum_old = state_in
        best_new = jnp.maximum(best_old, jnp.max(scores, -1))
        weights = jnp.where(allowed[None], jnp.exp(scores - best_new[..., None]), 0.0)
        shrink = jnp.exp(best_old - best_new)
        total_new = total_old * shrink + jnp.sum(weights, -1)
        added = jnp.einsum(
            "hqk,khd->qhd",
            weights.astype(jnp.bfloat16),
            value_block,
            preferred_element_type=jnp.float32,
        )
        accum_new = accum_old * shrink.T[:, :, None] + added
        return ((best_new, total_new, accum_new), None)

    return lax.scan(step, running, jnp.arange(amount // block_size, dtype=jnp.int32))[0]


def attend_back(
    query_rot,
    key_all,
    value_all,
    grad_attended,
    log_total,
    delta,
    row_index,
    row_segment,
    segment_all,
    score_scale,
):
    heads_local = query_rot.shape[1]
    amount = key_all.shape[0]
    block_size = 1024

    def step(dquery, number):
        first_row = number * block_size
        key_block = lax.dynamic_slice_in_dim(key_all, first_row, block_size, 0).reshape(
            block_size, heads_local, -1
        )
        value_block = lax.dynamic_slice_in_dim(value_all, first_row, block_size, 0).reshape(
            block_size, heads_local, -1
        )
        key_index = first_row + jnp.arange(block_size, dtype=jnp.int32)
        key_segment = lax.dynamic_slice_in_dim(segment_all, first_row, block_size, 0)
        scores = (
            jnp.einsum("qhd,khd->hqk", query_rot, key_block, preferred_element_type=jnp.float32)
            * score_scale
        )
        allowed = (key_index[None, :] <= row_index[:, None]) & (
            key_segment[None, :] == row_segment[:, None]
        )
        weights = jnp.where(
            allowed[None],
            jnp.exp(jnp.where(allowed[None], scores, -1e30) - log_total[..., None]),
            0.0,
        )
        dweights = jnp.einsum(
            "qhd,khd->hqk", grad_attended, value_block, preferred_element_type=jnp.float32
        )
        dscores = (weights * (dweights - delta[..., None])).astype(jnp.bfloat16)
        dquery = (
            dquery
            + jnp.einsum("hqk,khd->qhd", dscores, key_block, preferred_element_type=jnp.float32)
            * score_scale
        )
        dkeys = (
            jnp.einsum("hqk,qhd->khd", dscores, query_rot, preferred_element_type=jnp.float32)
            * score_scale
        )
        dvalues = jnp.einsum(
            "hqk,qhd->khd",
            weights.astype(jnp.bfloat16),
            grad_attended,
            preferred_element_type=jnp.float32,
        )
        return (dquery, (dkeys, dvalues))

    start_grad = jnp.zeros(query_rot.shape, jnp.float32)
    dquery, outputs = lax.scan(step, start_grad, jnp.arange(amount // block_size, dtype=jnp.int32))
    return (dquery, outputs[0].reshape(amount, -1), outputs[1].reshape(amount, -1))


def on_device(
    text,
    segment,
    features,
    image_count,
    image_slot,
    cotangent,
    input_gain,
    input_shift,
    query_weight,
    key_weight,
    value_weight,
    inner_gain,
    inner_shift,
    out_weight,
    middle_gain,
    middle_shift,
    up_weight,
    up_bias,
    hidden_gain,
    hidden_shift,
    down_weight,
    latents,
    resample_query,
    resample_key,
    resample_value,
    resample_out,
):
    row_count = text.shape[1]
    model_width = text.shape[2]
    group_rows = segment.shape[1]
    seq_rank = lax.axis_index(SEQ)
    gathered_in = (
        lax.all_gather(query_weight, (SEQ, IMG), axis=0, tiled=True),
        lax.all_gather(key_weight, (SEQ, IMG), axis=0, tiled=True),
        lax.all_gather(value_weight, (SEQ, IMG), axis=0, tiled=True),
        lax.all_gather(up_weight, (SEQ, IMG), axis=0, tiled=True),
        lax.all_gather(resample_query, (SEQ, IMG), axis=0, tiled=True),
        lax.all_gather(resample_key, (SEQ, IMG), axis=0, tiled=True),
        lax.all_gather(resample_value, (SEQ, IMG), axis=0, tiled=True),
    )
    query_full, key_full, value_full, up_full, probe_full, image_key_full, image_value_full = (
        gathered_in
    )
    gathered_out = (
        lax.all_gather(out_weight, (SEQ, IMG), axis=1, tiled=True),
        lax.all_gather(down_weight, (SEQ, IMG), axis=1, tiled=True),
        lax.all_gather(resample_out, (SEQ, IMG), axis=1, tiled=True),
        lax.all_gather(latents, (SEQ, IMG), axis=1, tiled=True),
    )
    out_full, down_full, image_out_full, latent_full = gathered_out
    half_width = query_full.shape[1]
    heads_local = half_width // HEAD
    score_scale = HEAD ** (-0.5)
    gelu_exact = functools.partial(jax.nn.gelu, approximate=False)
    image_slots = features.shape[1]
    pictures = features[0].reshape(image_slots * PATCH, features.shape[3])
    probe = (
        jnp.dot(latent_full, probe_full, preferred_element_type=jnp.float32)
        .astype(jnp.bfloat16)
        .reshape(LAT, heads_local, HEAD)
    )
    image_keys = (
        jnp.dot(pictures, image_key_full, preferred_element_type=jnp.float32)
        .astype(jnp.bfloat16)
        .reshape(image_slots, PATCH, heads_local, HEAD)
    )
    image_values = (
        jnp.dot(pictures, image_value_full, preferred_element_type=jnp.float32)
        .astype(jnp.bfloat16)
        .reshape(image_slots, PATCH, heads_local, HEAD)
    )
    image_scores = (
        jnp.einsum("qhd,iphd->ihqp", probe, image_keys, preferred_element_type=jnp.float32)
        * score_scale
    )
    image_probs = jax.nn.softmax(image_scores, -1)
    image_mixed = jnp.einsum(
        "ihqp,iphd->iqhd",
        image_probs.astype(jnp.bfloat16),
        image_values,
        preferred_element_type=jnp.float32,
    )
    image_mixed = image_mixed.astype(jnp.bfloat16).reshape(image_slots * LAT, half_width)
    embed = tp_total(jnp.dot(image_mixed, image_out_full, preferred_element_type=jnp.float32))
    embed = embed.astype(jnp.bfloat16).reshape(image_slots, LAT, model_width)
    image_total = image_slot.shape[1]
    slot_range = jnp.arange(image_total, dtype=jnp.int32)
    live = slot_range % IMG_DEV < jnp.repeat(image_count[0], IMG_DEV)
    block_local = row_count // LAT
    block_count = group_rows // LAT
    block_ids = seq_rank * block_local + jnp.arange(block_local, dtype=jnp.int32)
    owner = ((image_slot[0][None, :] == block_ids[:, None]) & live[None, :]).astype(jnp.float32)
    owner_low = owner.astype(jnp.bfloat16)
    taken = jnp.sum(owner, 1) > 0.5
    chosen = owner_low
    placed = jnp.einsum(
        "bi,ild->bld",
        chosen,
        lax.all_gather(embed, SEQ, axis=0, tiled=True),
        preferred_element_type=jnp.float32,
    )
    text_blocks = text[0].astype(jnp.float32).reshape(block_local, LAT, model_width)
    mixed_in = jnp.where(taken[:, None, None], placed, text_blocks).reshape(row_count, model_width)
    segment_all = segment[0]
    docs_count = 3 * (group_rows // min(SEQ_MAX, group_rows))
    marks = (segment_all[:, None] == jnp.arange(docs_count, dtype=jnp.int32)[None, :]).astype(
        jnp.int32
    )
    earlier_rows = jnp.cumsum(marks, 0) - marks
    position_all = jnp.sum(earlier_rows * marks, 1)
    first_local = seq_rank * row_count
    row_index = first_local + jnp.arange(row_count, dtype=jnp.int32)
    row_segment = lax.dynamic_slice_in_dim(segment_all, first_local, row_count, 0)
    position = lax.dynamic_slice_in_dim(position_all, first_local, row_count, 0).astype(jnp.float32)
    cosine, sine_table, growth = xpos_factors(position, HEAD // 2)
    input_out, input_hat, input_factor = full_norm(
        mixed_in, input_gain.astype(jnp.float32), input_shift.astype(jnp.float32)
    )
    normed = input_out.astype(jnp.bfloat16)
    query_lin = jnp.dot(normed, query_full, preferred_element_type=jnp.float32).reshape(
        row_count, heads_local, HEAD
    )
    key_lin = jnp.dot(normed, key_full, preferred_element_type=jnp.float32).reshape(
        row_count, heads_local, HEAD
    )
    value_lin = jnp.dot(normed, value_full, preferred_element_type=jnp.float32)
    query_rot = rotate(query_lin, cosine, sine_table, growth).astype(jnp.bfloat16)
    keys_rot = (
        rotate(key_lin, cosine, sine_table, 1.0 / growth)
        .astype(jnp.bfloat16)
        .reshape(row_count, half_width)
    )
    values_low = value_lin.astype(jnp.bfloat16)
    start_state = (
        jnp.full((heads_local, row_count), -1e30, jnp.float32),
        jnp.zeros((heads_local, row_count), jnp.float32),
        jnp.zeros((row_count, heads_local, HEAD), jnp.float32),
    )
    best, weight_total, accum = attend_piece(
        start_state,
        query_rot,
        lax.all_gather(keys_rot, SEQ, axis=0, tiled=True),
        lax.all_gather(values_low, SEQ, axis=0, tiled=True),
        row_index,
        row_segment,
        segment_all,
        score_scale,
    )
    attended = accum / weight_total.T[:, :, None]
    log_total = best + jnp.log(weight_total)
    inner_out, inner_hat, inner_factor = split_norm(
        attended.reshape(row_count, half_width),
        inner_gain.astype(jnp.float32),
        inner_shift.astype(jnp.float32),
        model_width,
    )
    inner_low = inner_out.astype(jnp.bfloat16)
    middle = mixed_in + tp_total(jnp.dot(inner_low, out_full, preferred_element_type=jnp.float32))
    lifted_out, lifted_hat, lifted_factor = full_norm(
        middle, middle_gain.astype(jnp.float32), middle_shift.astype(jnp.float32)
    )
    lifted = lifted_out.astype(jnp.bfloat16)
    hidden_pre = jnp.dot(lifted, up_full, preferred_element_type=jnp.float32) + up_bias.astype(
        jnp.float32
    )
    activated, gelu_pull = jax.vjp(gelu_exact, hidden_pre)
    settled_out, settled_hat, settled_factor = split_norm(
        activated, hidden_gain.astype(jnp.float32), hidden_shift.astype(jnp.float32), FF
    )
    settled = settled_out.astype(jnp.bfloat16)
    final_rows = middle + tp_total(jnp.dot(settled, down_full, preferred_element_type=jnp.float32))
    result = final_rows.astype(jnp.bfloat16).reshape(1, row_count, model_width)
    grad_low = cotangent[0]
    grad_rows = grad_low.astype(jnp.float32)
    down_grad = jnp.dot(settled.T, grad_low, preferred_element_type=jnp.float32)
    d_settled = jnp.dot(grad_low, down_full.T, preferred_element_type=jnp.float32)
    hidden_gain_grad = jnp.sum(d_settled * settled_hat, 0)
    hidden_shift_grad = jnp.sum(d_settled, 0)
    d_activated = split_back(
        d_settled, settled_hat, settled_factor, hidden_gain.astype(jnp.float32), FF
    )
    d_hidden = gelu_pull(d_activated)[0].astype(jnp.bfloat16)
    up_bias_grad = jnp.sum(d_hidden.astype(jnp.float32), 0)
    up_grad = jnp.dot(lifted.T, d_hidden, preferred_element_type=jnp.float32)
    d_lifted = tp_total(jnp.dot(d_hidden, up_full.T, preferred_element_type=jnp.float32))
    middle_gain_grad = jnp.sum(d_lifted * lifted_hat, 0)
    middle_shift_grad = jnp.sum(d_lifted, 0)
    d_middle = grad_rows + full_back(
        d_lifted, lifted_hat, lifted_factor, middle_gain.astype(jnp.float32)
    )
    d_branch = d_middle.astype(jnp.bfloat16)
    out_grad = jnp.dot(inner_low.T, d_branch, preferred_element_type=jnp.float32)
    d_inner = jnp.dot(d_branch, out_full.T, preferred_element_type=jnp.float32)
    inner_gain_grad = jnp.sum(d_inner * inner_hat, 0)
    inner_shift_grad = jnp.sum(d_inner, 0)
    d_attended = split_back(
        d_inner, inner_hat, inner_factor, inner_gain.astype(jnp.float32), model_width
    )
    d_attended = d_attended.astype(jnp.bfloat16).reshape(row_count, heads_local, HEAD)
    delta = jnp.sum(d_attended.astype(jnp.float32) * attended, -1).T
    key_back, value_back = (
        lax.all_gather(keys_rot, SEQ, axis=0, tiled=True),
        lax.all_gather(values_low, SEQ, axis=0, tiled=True),
    )
    d_query_rot, d_key_term, d_value_term = attend_back(
        query_rot,
        key_back,
        value_back,
        d_attended,
        log_total,
        delta,
        row_index,
        row_segment,
        segment_all,
        score_scale,
    )
    d_key_sum, d_value_sum = (
        lax.psum_scatter(
            d_key_term.astype(jnp.bfloat16), SEQ, scatter_dimension=0, tiled=True
        ).astype(jnp.float32),
        lax.psum_scatter(
            d_value_term.astype(jnp.bfloat16), SEQ, scatter_dimension=0, tiled=True
        ).astype(jnp.float32),
    )
    d_query_lin = (
        rotate_back(d_query_rot, cosine, sine_table, growth)
        .astype(jnp.bfloat16)
        .reshape(row_count, half_width)
    )
    d_key_lin = (
        rotate_back(
            d_key_sum.reshape(row_count, heads_local, HEAD), cosine, sine_table, 1.0 / growth
        )
        .astype(jnp.bfloat16)
        .reshape(row_count, half_width)
    )
    d_value_lin = d_value_sum.astype(jnp.bfloat16)
    query_grad = jnp.dot(normed.T, d_query_lin, preferred_element_type=jnp.float32)
    key_grad = jnp.dot(normed.T, d_key_lin, preferred_element_type=jnp.float32)
    value_grad = jnp.dot(normed.T, d_value_lin, preferred_element_type=jnp.float32)
    d_normed_part = (
        jnp.dot(d_query_lin, query_full.T, preferred_element_type=jnp.float32)
        + jnp.dot(d_key_lin, key_full.T, preferred_element_type=jnp.float32)
        + jnp.dot(d_value_lin, value_full.T, preferred_element_type=jnp.float32)
    )
    d_normed = tp_total(d_normed_part)
    input_gain_grad = jnp.sum(d_normed * input_hat, 0)
    input_shift_grad = jnp.sum(d_normed, 0)
    d_mixed = d_middle + full_back(
        d_normed, input_hat, input_factor, input_gain.astype(jnp.float32)
    )
    d_blocks = d_mixed.reshape(block_local, LAT, model_width)
    text_grad = jnp.where(taken[:, None, None], 0.0, d_blocks).reshape(1, row_count, model_width)
    my_target = lax.dynamic_slice_in_dim(image_slot[0], seq_rank * image_slots, image_slots, 0)
    my_live = lax.dynamic_slice_in_dim(live, seq_rank * image_slots, image_slots, 0)
    owner_mine = (
        (jnp.arange(block_count, dtype=jnp.int32)[:, None] == my_target[None, :]) & my_live[None, :]
    ).astype(jnp.bfloat16)
    chosen = owner_mine
    d_embed = jnp.einsum(
        "bi,bld->ild",
        chosen,
        lax.all_gather(d_blocks.astype(jnp.bfloat16), SEQ, axis=0, tiled=True),
        preferred_element_type=jnp.float32,
    )
    d_embed_low = d_embed.astype(jnp.bfloat16).reshape(image_slots * LAT, model_width)
    resample_out_grad = jnp.dot(image_mixed.T, d_embed_low, preferred_element_type=jnp.float32)
    d_image_mixed = jnp.dot(d_embed_low, image_out_full.T, preferred_element_type=jnp.float32)
    d_image_mixed = d_image_mixed.astype(jnp.bfloat16).reshape(image_slots, LAT, heads_local, HEAD)
    d_image_probs = jnp.einsum(
        "iqhd,iphd->ihqp", d_image_mixed, image_values, preferred_element_type=jnp.float32
    )
    d_image_scores = image_probs * (
        d_image_probs - jnp.sum(image_probs * d_image_probs, -1, keepdims=True)
    )
    d_image_scores = d_image_scores.astype(jnp.bfloat16)
    d_probe = (
        jnp.einsum("ihqp,iphd->qhd", d_image_scores, image_keys, preferred_element_type=jnp.float32)
        * score_scale
    )
    d_image_keys = (
        jnp.einsum("ihqp,qhd->iphd", d_image_scores, probe, preferred_element_type=jnp.float32)
        * score_scale
    ).astype(jnp.bfloat16)
    d_image_values = jnp.einsum(
        "ihqp,iqhd->iphd",
        image_probs.astype(jnp.bfloat16),
        d_image_mixed,
        preferred_element_type=jnp.float32,
    ).astype(jnp.bfloat16)
    resample_key_grad = jnp.dot(
        pictures.T,
        d_image_keys.reshape(image_slots * PATCH, half_width),
        preferred_element_type=jnp.float32,
    )
    resample_value_grad = jnp.dot(
        pictures.T,
        d_image_values.reshape(image_slots * PATCH, half_width),
        preferred_element_type=jnp.float32,
    )
    d_probe_flat = d_probe.reshape(LAT, half_width)
    resample_query_grad = jnp.dot(
        latent_full.astype(jnp.float32).T, d_probe_flat, precision=HIGHEST_PRECISION
    )
    latent_grad = tp_total(
        jnp.dot(d_probe_flat, probe_full.astype(jnp.float32).T, precision=HIGHEST_PRECISION)
    )
    summed_in = (
        lax.psum_scatter(query_grad, (SEQ, IMG), scatter_dimension=0, tiled=True),
        lax.psum_scatter(key_grad, (SEQ, IMG), scatter_dimension=0, tiled=True),
        lax.psum_scatter(value_grad, (SEQ, IMG), scatter_dimension=0, tiled=True),
        lax.psum_scatter(up_grad, (SEQ, IMG), scatter_dimension=0, tiled=True),
        lax.psum_scatter(resample_query_grad, (SEQ, IMG), scatter_dimension=0, tiled=True),
        lax.psum_scatter(resample_key_grad, (SEQ, IMG), scatter_dimension=0, tiled=True),
        lax.psum_scatter(resample_value_grad, (SEQ, IMG), scatter_dimension=0, tiled=True),
    )
    summed_out = (
        lax.psum_scatter(out_grad, (SEQ, IMG), scatter_dimension=1, tiled=True),
        lax.psum_scatter(down_grad, (SEQ, IMG), scatter_dimension=1, tiled=True),
        lax.psum_scatter(resample_out_grad, (SEQ, IMG), scatter_dimension=1, tiled=True),
        lax.psum_scatter(latent_grad, (SEQ, IMG), scatter_dimension=1, tiled=True),
    )
    summed_small = lax.psum(
        (
            input_gain_grad,
            input_shift_grad,
            inner_gain_grad,
            inner_shift_grad,
            middle_gain_grad,
            middle_shift_grad,
            up_bias_grad,
            hidden_gain_grad,
            hidden_shift_grad,
        ),
        (SEQ, IMG),
    )
    return (
        result,
        text_grad,
        summed_small[0],
        summed_small[1],
        summed_in[0],
        summed_in[1],
        summed_in[2],
        summed_small[2],
        summed_small[3],
        summed_out[0],
        summed_small[4],
        summed_small[5],
        summed_in[3],
        summed_small[6],
        summed_small[7],
        summed_small[8],
        summed_out[1],
        summed_out[3],
        summed_in[4],
        summed_in[5],
        summed_in[6],
        summed_out[2],
    )


MESH_IDS = pl.DeviceIdType.MESH
ANYWHERE = pl.BlockSpec(memory_space=pl.ANY)
ON_CHIP = pl.BlockSpec(memory_space=pltpu.VMEM)
IN_SMEM = pl.BlockSpec(memory_space=pltpu.SMEM)
LANES = 128
PLANE = 8
VMEM_BYTES = 60 * 1024 * 1024
PIECE_ROWS = (32, 32, 32, 32)
PIECES = len(PIECE_ROWS)
SECOND_LAG = 2
PACE_IMAGE = (0, 7, 7, 7, 7)
PACE_ATTEND = (0, 1, 1, 0)
WORK_FROM = 0
PACE_BACK = (1, 0, 0, 0, 2, 2, 2, 2)
FRONT, BACK, ALL, ROWS, INWARD, OUTWARD, SHARED = range(7)


def narrow_heads(mesh):
    return mesh.shape[SEQ] != PLANE or mesh.shape[IMG] != 2 or mesh.shape[TP] != 2


def flipped(number, bit):
    step = 2**bit
    return number + step - 2 * step * ((number // step) % 2)


class Places:
    def __init__(self):
        self.seq, self.tp, self.img = (lax.axis_index(name) for name in (SEQ, TP, IMG))
        self.s_core, self.s_x, self.s_y = (flipped(self.seq, bit) for bit in range(3))
        self.s_xy = flipped(self.s_x, 2)
        self.core, self.x, self.y = (self.at(seq) for seq in (self.s_core, self.s_x, self.s_y))
        self.tp_peer = (self.seq, 1 - self.tp, self.img)
        self.img_peer = (self.seq, self.tp, 1 - self.img)

    def at(self, seq):
        return (seq, self.tp, self.img)


def greet(peers):
    barrier = pltpu.get_barrier_semaphore()
    for peer in peers:
        pl.semaphore_signal(barrier, inc=1, device_id=peer, device_id_type=MESH_IDS)
    pl.semaphore_wait(barrier, len(peers))


def remote(src, dst, send, recv, peer):
    return pltpu.make_async_remote_copy(
        src_ref=src, dst_ref=dst, send_sem=send, recv_sem=recv, device_id=peer, device_id_type=MESH_IDS
    )


def rows_at(ref, first, count):
    return ref.at[pl.ds(pl.multiple_of(first, 16), count)]


class Spread:
    def __init__(self, here, out, block, first, count, send, recv):
        self.here, self.out, self.block = here, out, block
        self.first, self.count, self.send, self.recv = first, count, send, recv
        self.half = out.shape[1] // 2
        self.sent = []

    def cut(self, ref, first, which):
        rows = pl.ds(first, self.count)
        if which == ALL:
            return ref.at[rows]
        return ref.at[rows, pl.ds(self.half if which == BACK else 0, self.half)]

    def part(self, seq, which):
        return self.cut(self.out, pl.multiple_of(seq * self.block + self.first, 16), which)

    def copy(self, src, dst, slot, peer):
        return remote(src, dst, self.send.at[slot], self.recv.at[slot], peer)

    def go(self, src, dst, slot, peer):
        made = self.copy(src, dst, slot, peer)
        made.start()
        self.sent.append(made)

    def own(self, src, src_first):
        here, seq = self.here, self.here.seq

        def own_part(which):
            return self.cut(src, src_first, which)

        self.go(own_part(FRONT), self.part(seq, FRONT), 0, here.x)
        self.go(own_part(BACK), self.part(seq, BACK), 1, here.y)
        self.go(own_part(BACK), self.part(seq, BACK), 2, here.x)
        self.go(own_part(FRONT), self.part(seq, FRONT), 3, here.y)
        self.go(own_part(ALL), self.part(seq, ALL), 4, here.core)

    def arrived(self, slot, seq, which):
        target = self.part(seq, which)
        self.copy(target, target, slot, self.here.core).wait_recv()

    def forward(self):
        here = self.here
        self.arrived(0, here.s_x, FRONT)
        self.go(self.part(here.s_x, FRONT), self.part(here.s_x, FRONT), 5, here.y)
        self.arrived(1, here.s_y, BACK)
        self.go(self.part(here.s_y, BACK), self.part(here.s_y, BACK), 6, here.x)
        self.arrived(2, here.s_x, BACK)
        self.go(self.part(here.s_x, ALL), self.part(here.s_x, ALL), 7, here.core)
        self.arrived(3, here.s_y, FRONT)
        self.go(self.part(here.s_y, ALL), self.part(here.s_y, ALL), 8, here.core)

    def corner(self):
        here = self.here
        self.arrived(5, here.s_xy, FRONT)
        self.arrived(6, here.s_xy, BACK)
        self.go(self.part(here.s_xy, ALL), self.part(here.s_xy, ALL), 9, here.core)

    def finish(self):
        core = self.here.s_core
        self.arrived(4, core, ALL)
        self.arrived(7, flipped(core, 1), ALL)
        self.arrived(8, flipped(core, 2), ALL)
        self.arrived(9, flipped(flipped(core, 1), 2), ALL)
        for made in self.sent:
            made.wait_send()


def ticks_of(stages, count):
    def tick_of(tick):
        def run():
            for lag, stage in reversed(stages):
                if 0 <= tick - lag < count:
                    stage(tick - lag)

        return run

    return [tick_of(tick) for tick in range(count + max(lag for lag, _ in stages))]


def take_some(waiting, count):
    for launch in waiting[:count]:
        launch()
    del waiting[:count]


def weight_blocks(weight, side):
    if side == SHARED:
        return weight.shape
    if side == INWARD:
        return (weight.shape[0], weight.shape[1] // PLANE)
    return (weight.shape[0] // PLANE, weight.shape[1])


def intake(gathered, weights, sides, cid):
    n_rows, n_weights = len(gathered), len(weights)
    pieces = PIECES

    def kernel(*refs):
        row_refs, weight_refs = refs[:n_rows], refs[n_rows : n_rows + n_weights]
        refs = refs[n_rows + n_weights :]
        row_outs, weight_outs = refs[:n_rows], refs[n_rows : n_rows + n_weights]
        refs = refs[n_rows + n_weights :]
        held, (local, send, recv, w_local, w_send, w_recv, z_send, z_recv) = refs[:n_rows], refs[n_rows:]
        here = Places()
        seq, tp, img = here.seq, here.tp, here.img
        others = [lax.rem(seq + step, PLANE) for step in range(1, PLANE)]
        greet([(other, tp, img) for other in others] + [here.img_peer])

        def slot_of(out, side, shape, from_seq, from_img):
            number = from_seq * 2 + from_img
            if side == INWARD:
                return out.at[pl.ds(pl.multiple_of(number * shape[0], shape[0]), shape[0])]
            return out.at[:, pl.ds(pl.multiple_of(number * shape[1], shape[1]), shape[1])]

        def block_of(weight, side, shape, to_seq):
            if side == SHARED:
                return weight
            if side == INWARD:
                return weight.at[:, pl.ds(pl.multiple_of(to_seq * shape[1], shape[1]), shape[1])]
            return weight.at[pl.ds(pl.multiple_of(to_seq * shape[0], shape[0]), shape[0])]

        flights, own_copies = [], []

        def begin(index):
            weight, out, side = weight_refs[index], weight_outs[index], sides[index]
            shape = weight_blocks(weight, side)
            mine = pltpu.make_async_copy(
                block_of(weight, side, shape, seq), slot_of(out, side, shape, seq, img), w_local.at[index]
            )
            mine.start()
            crossing = remote(
                block_of(weight, side, shape, seq),
                slot_of(out, side, shape, seq, img),
                z_send.at[index, 0],
                z_recv.at[index, 0],
                here.img_peer,
            )
            crossing.start()
            own_copies.append(mine)
            flights.append(crossing)
            for step, other in enumerate(others, 1):
                made = remote(
                    block_of(weight, side, shape, other),
                    slot_of(out, side, shape, seq, img),
                    w_send.at[index, step],
                    w_recv.at[index, step],
                    here.at(other),
                )
                made.start()
                flights.append(made)

        spreads, loads, stores = [], [], []
        for number, (rows, out) in enumerate(zip(row_refs, row_outs)):
            block = rows.shape[0]
            count = block // pieces
            loads.append(pltpu.make_async_copy(rows, held[number], local.at[number, 0]))
            loads[-1].start()
            stores.append(pltpu.make_async_copy(held[number], rows_at(out, seq * block, block), local.at[number, 1]))
            for piece in range(pieces):
                at = number * pieces + piece
                spreads.append(
                    (Spread(here, out, block, piece * count, count, send.at[at], recv.at[at]), rows, piece * count)
                )

        def cross(piece):
            for index in range(piece, n_weights, len(spreads)):
                weight, out, side = weight_refs[index], weight_outs[index], sides[index]
                shape = weight_blocks(weight, side)
                for step in range(1, PLANE):
                    source = lax.rem(seq + PLANE - step, PLANE)
                    landed = slot_of(out, side, shape, source, img)
                    remote(landed, landed, w_send.at[index, step], w_recv.at[index, step], here.core).wait_recv()
                    crossing = remote(
                        landed, landed, z_send.at[index, step], z_recv.at[index, step], here.img_peer
                    )
                    crossing.start()
                    flights.append(crossing)

        def own_rows(piece):
            if piece == 1:
                for load, store in zip(loads, stores):
                    load.wait()
                    store.start()
            for index in range(piece, n_weights, len(spreads)):
                begin(index)
            spreads[piece][0].own(spreads[piece][1], spreads[piece][2])

        for tick in ticks_of(
            [
                (0, own_rows),
                (2, lambda piece: spreads[piece][0].forward()),
                (3, lambda piece: cross(piece)),
                (4, lambda piece: spreads[piece][0].corner()),
            ],
            len(spreads),
        ):
            tick()
        for index, (weight, out, side) in enumerate(zip(weight_refs, weight_outs, sides)):
            shape = weight_blocks(weight, side)
            for step in range(PLANE):
                source = lax.rem(seq + PLANE - step, PLANE)
                landed = slot_of(out, side, shape, source, 1 - img)
                remote(landed, landed, z_send.at[index, step], z_recv.at[index, step], here.core).wait_recv()
        for spread, _, _ in spreads:
            spread.finish()
        for made in flights:
            made.wait_send()
        for made in own_copies + stores:
            made.wait()

    def whole(weight, side):
        shape = weight_blocks(weight, side)
        if side == INWARD:
            return jax.ShapeDtypeStruct((2 * PLANE * shape[0], shape[1]), weight.dtype)
        return jax.ShapeDtypeStruct((shape[0], 2 * PLANE * shape[1]), weight.dtype)

    dma = pltpu.SemaphoreType.DMA
    outs = [jax.ShapeDtypeStruct((PLANE * rows.shape[0], rows.shape[1]), rows.dtype) for rows in gathered]
    outs += [whole(weight, side) for weight, side in zip(weights, sides)]
    made = pl.pallas_call(
        kernel,
        out_shape=tuple(outs),
        in_specs=[ANYWHERE] * (n_rows + n_weights),
        out_specs=tuple([ANYWHERE] * len(outs)),
        scratch_shapes=[pltpu.VMEM(rows.shape, rows.dtype) for rows in gathered]
        + [
            dma((n_rows, 2)),
            dma((n_rows * pieces, 10)),
            dma((n_rows * pieces, 10)),
            dma((n_weights,)),
            dma((n_weights, PLANE)),
            dma((n_weights, PLANE)),
            dma((n_weights, PLANE)),
            dma((n_weights, PLANE)),
        ],
        compiler_params=pltpu.CompilerParams(
            collective_id=cid, has_side_effects=True, vmem_limit_bytes=VMEM_BYTES
        ),
    )(*gathered, *weights)
    return made[:n_rows], made[n_rows:]


LAZY_BYTES = 256 * 1024


class Lazy:
    def __init__(self, src, dst, sem):
        self.copy = pltpu.make_async_copy(src, dst, sem)
        self.copy.start()
        self.dst, self.shape, self.pending = dst, dst.shape, True

    def ready(self):
        if self.pending:
            self.copy.wait()
            self.pending = False
        return self.dst

    @property
    def at(self):
        return self.ready().at

    def __getitem__(self, where):
        return self.ready()[where]


def is_lazy(value, spec):
    return spec is ON_CHIP and value.size * value.dtype.itemsize >= LAZY_BYTES


class Rider:
    inputs, out_shapes, scratch, in_specs = (), (), (), ()

    def bind(self, here, ins, outs, scratch):
        self.here, self.ins, self.outs, self.held = here, ins, outs, scratch
        self.sent, self.kept, self.due, self.launches, self.later = [], [], [], [], []

    def keep(self, src, dst, sem):
        made = pltpu.make_async_copy(src, dst, sem)
        self.launches.append(made.start)
        self.kept.append(made)

    def send(self, src, dst, send, recv, peer):
        made = remote(src, dst, send, recv, peer)
        self.launches.append(made.start)
        self.sent.append(made)

    def finish(self):
        for dst, send, recv in self.due:
            remote(dst, dst, send, recv, self.here.core).wait_recv()
        for made in self.sent:
            made.wait_send()
        for made in self.kept:
            made.wait()


class ChainWeights(Rider):
    def __init__(self, weights, sides, places):
        self.inputs, self.sides, self.places = weights, sides, places
        self.blocks = [weight_blocks(weight, side) for weight, side in zip(weights, sides)]
        shapes = {}
        for (rows, columns), side, (out, first) in zip(self.blocks, sides, places):
            if side == INWARD:
                shapes[out] = (2 * PLANE * rows, first + columns)
            else:
                shapes[out] = (rows, 2 * PLANE * columns)
        self.out_shapes = [jax.ShapeDtypeStruct(shapes[out], weights[0].dtype) for out in range(len(shapes))]
        dma, count = pltpu.SemaphoreType.DMA, len(weights)
        self.scratch = [dma((count, PLANE))] * 4 + [dma((count,))]

    def peers(self, here):
        return [here.at(lax.rem(here.seq + step, PLANE)) for step in range(1, PLANE)]

    def slot(self, index, seq, img):
        out, first = self.places[index]
        (rows, columns), number = self.blocks[index], seq * 2 + img
        if self.sides[index] == INWARD:
            return self.outs[out].at[pl.ds(pl.multiple_of(number * rows, rows), rows), pl.ds(first, columns)]
        return self.outs[out].at[:, pl.ds(pl.multiple_of(number * columns, columns), columns)]

    def start(self):
        here, (send, recv, z_send, z_recv, local) = self.here, self.held
        self.later = []
        for index, (weight, side, (rows, columns)) in enumerate(zip(self.ins, self.sides, self.blocks)):
            for step in range(PLANE):
                target = lax.rem(here.seq + step, PLANE)
                source = lax.rem(here.seq + PLANE - step, PLANE)
                if side == INWARD:
                    part = weight.at[:, pl.ds(pl.multiple_of(target * columns, columns), columns)]
                else:
                    part = weight.at[pl.ds(pl.multiple_of(target * rows, rows), rows)]
                mine = self.slot(index, here.seq, here.img)
                if step == 0:
                    self.keep(part, mine, local.at[index])
                    cross = remote(part, mine, z_send.at[index, 0], z_recv.at[index, 0], here.img_peer)
                    self.launches.append(cross.start)
                    self.sent.append(cross)
                else:
                    self.send(part, mine, send.at[index, step], recv.at[index, step], here.at(target))
                    self.later.append(functools.partial(self.cross, index, step, source))
                there = self.slot(index, source, 1 - here.img)
                self.due.append((there, z_send.at[index, step], z_recv.at[index, step]))

    def cross(self, index, step, source):
        here, (send, recv, z_send, z_recv, _) = self.here, self.held
        landed = self.slot(index, source, here.img)
        remote(landed, landed, send.at[index, step], recv.at[index, step], here.core).wait_recv()
        made = remote(landed, landed, z_send.at[index, step], z_recv.at[index, step], here.img_peer)
        made.start()
        self.sent.append(made)


class GatherRows(Rider):
    def __init__(self, rows):
        self.inputs = [rows]
        self.out_shapes = [jax.ShapeDtypeStruct((PLANE * rows.shape[0], rows.shape[1]), rows.dtype)]
        dma = pltpu.SemaphoreType.DMA
        self.scratch = [dma((PIECES, 10)), dma((PIECES, 10)), dma((1,))]

    def start(self):
        (rows,), (out,), (send, recv, local) = self.ins, self.outs, self.held
        block = rows.shape[0]
        self.spreads = []
        for piece, count in enumerate(PIECE_ROWS):
            first = sum(PIECE_ROWS[:piece])
            self.spreads.append(Spread(self.here, out, block, first, count, send.at[piece], recv.at[piece]))
            self.launches.append(functools.partial(self.spreads[piece].own, rows, first))
        self.keep(rows, rows_at(out, self.here.seq * block, block), local.at[0])
        self.later = [spread.forward for spread in self.spreads] + [spread.corner for spread in self.spreads]

    def finish(self):
        for spread in self.spreads:
            spread.finish()
        super().finish()


class CrossGrads(Rider):
    def __init__(self, grads, sides):
        self.inputs, self.sides = grads, sides
        self.out_shapes = []
        for grad, side in zip(grads, sides):
            if side == INWARD:
                shape = (grad.shape[0], grad.shape[2], grad.shape[3])
            else:
                shape = (PLANE, grad.shape[0], grad.shape[1] // (2 * PLANE))
            self.out_shapes.append(jax.ShapeDtypeStruct(shape, grad.dtype))
        dma = pltpu.SemaphoreType.DMA
        self.scratch = [dma((len(grads), PLANE)), dma((len(grads), PLANE))]

    def peers(self, here):
        return [here.img_peer]

    def start(self):
        here, (send, recv) = self.here, self.held
        for index, (grad, out, side) in enumerate(zip(self.ins, self.outs, self.sides)):
            width = out.shape[2]
            for seq in range(PLANE):
                if side == INWARD:
                    part = grad.at[seq, 1 - here.img]
                else:
                    part = grad.at[:, pl.ds(pl.multiple_of((seq * 2 + 1 - here.img) * width, width), width)]
                self.send(part, out.at[seq], send.at[index, seq], recv.at[index, seq], here.img_peer)
                self.due.append((out.at[seq], send.at[index, seq], recv.at[index, seq]))


class Stream:
    in_specs = ()

    def __init__(self, rows_all, left, right, across, row_inputs, row_kinds, row_outs, row_function, gather):
        self.own_left = left is not None
        self.inputs = ([left] if self.own_left else []) + [right] + list(row_inputs)
        self.across, self.row_kinds, self.row_outs = across, row_kinds, row_outs
        self.row_function, self.gather = row_function, gather
        width = right.shape[0] if across else right.shape[1]
        self.width, self.block, self.pieces = width, rows_all // PLANE, PIECES
        self.half = width // 2
        low_type = jnp.bfloat16
        self.out_shapes = [shape for shape, _ in row_outs]
        if gather:
            self.out_shapes.append(jax.ShapeDtypeStruct((rows_all, width), low_type))
        dma = pltpu.SemaphoreType.DMA
        block, pieces, half = self.block, self.pieces, self.half
        self.scratch = [
            pltpu.VMEM((4, block, width), low_type),
            pltpu.VMEM((4, block, width), low_type),
            pltpu.VMEM((4, block, width), jnp.float32),
            pltpu.VMEM((block, half), low_type),
            pltpu.VMEM((block, half), low_type),
            pltpu.VMEM((block, width), low_type),
            pltpu.VMEM((block, width), low_type),
            pltpu.VMEM((block, width), low_type),
            pltpu.VMEM((block, width), low_type),
            pltpu.VMEM((block, width), low_type),
            dma((4,)),
            dma((4,)),
            dma((pieces, 7)),
            dma((pieces, 7)),
            dma((pieces, 10)),
            dma((pieces, 10)),
            dma((pieces,)),
        ]

    def out_specs(self):
        return [ON_CHIP] * len(self.row_outs) + [ANYWHERE] * (len(self.out_shapes) - len(self.row_outs))

    def peers(self, here):
        return [here.core, here.x, here.y, here.tp_peer]

    def bind(self, here, ins, outs, scratch):
        self.here = here
        if self.own_left:
            self.left, ins = ins[0], ins[1:]
        self.right, self.ins = ins[0], ins[1:]
        self.outs = outs
        (self.away, self.core_in, self.near, self.from_xd, self.from_yd, self.from_x, self.from_y) = scratch[:7]
        (self.mine, self.theirs, self.low, self.c_send, self.c_recv) = scratch[7:12]
        (self.send, self.recv, self.g_send, self.g_recv, self.l_sem) = scratch[12:]
        self.sent, self.spreads, self.core_copies = [], [], {}

    def chunk(self, base, kind):
        if kind in (1, 3):
            base = flipped(base, 1)
        if kind in (2, 3):
            base = flipped(base, 2)
        return base

    def product(self, seq, target, low_type):
        first = pl.multiple_of(seq * self.block, self.block)
        rows = self.left[pl.ds(first, self.block), :]
        step = min(512, self.width)
        for column in range(0, self.width, step):
            if self.across:
                part = lax.dot_general(
                    rows,
                    self.right[column : column + step, :],
                    (((1,), (1,)), ((), ())),
                    preferred_element_type=jnp.float32,
                )
            else:
                part = jnp.dot(
                    rows, self.right[:, column : column + step], preferred_element_type=jnp.float32
                )
            target[:, column : column + step] = part.astype(low_type)

    def begin(self):
        here = self.here
        for kind in (3, 1, 2, 0):
            self.product(self.chunk(here.s_core, kind), self.away.at[kind], jnp.bfloat16)
            made = remote(
                self.away.at[kind], self.core_in.at[kind], self.c_send.at[kind], self.c_recv.at[kind], here.core
            )
            made.start()
            self.core_copies[kind] = made
            self.product(self.chunk(here.seq, kind), self.near.at[kind], jnp.float32)

    def go(self, src, dst, piece, slot, peer):
        made = remote(src, dst, self.send.at[piece, slot], self.recv.at[piece, slot], peer)
        made.start()
        self.sent.append(made)

    def landed(self, dst, piece, slot):
        remote(dst, dst, self.send.at[piece, slot], self.recv.at[piece, slot], self.here.core).wait_recv()

    def rows_of(self, piece):
        return pl.ds(sum(PIECE_ROWS[:piece]), PIECE_ROWS[piece])

    def columns_of(self, which):
        return pl.ds(self.half if which == BACK else 0, self.half)

    def held(self, kind, piece, which=ALL):
        if which == ALL:
            return self.core_in.at[kind, self.rows_of(piece)]
        return self.core_in.at[kind, self.rows_of(piece), self.columns_of(which)]

    def halved(self, ref, piece, which):
        return ref.at[self.rows_of(piece), self.columns_of(which)]

    def folded(self, kind, piece):
        if piece == 0:
            self.core_copies[kind].wait_recv()
        near = self.near[kind, self.rows_of(piece), :]
        return self.held(kind, piece)[...].astype(jnp.float32) + near

    def first_sends(self, piece):
        here = self.here
        self.held(3, piece)[...] = self.folded(3, piece).astype(jnp.bfloat16)
        self.go(self.held(3, piece, FRONT), self.from_xd.at[self.rows_of(piece)], piece, 0, here.x)
        self.go(self.held(3, piece, BACK), self.from_yd.at[self.rows_of(piece)], piece, 1, here.y)
        self.held(1, piece)[...] = self.folded(1, piece).astype(jnp.bfloat16)
        self.go(self.held(1, piece, FRONT), self.halved(self.from_x, piece, FRONT), piece, 2, here.x)
        self.held(2, piece)[...] = self.folded(2, piece).astype(jnp.bfloat16)
        self.go(self.held(2, piece, BACK), self.halved(self.from_y, piece, BACK), piece, 3, here.y)

    def second_sends(self, piece):
        here = self.here
        self.landed(self.from_xd.at[self.rows_of(piece)], piece, 0)
        at = self.held(2, piece, FRONT)
        at[...] = (at[...].astype(jnp.float32) + self.from_xd[self.rows_of(piece), :].astype(jnp.float32)).astype(jnp.bfloat16)
        self.go(at, self.halved(self.from_y, piece, FRONT), piece, 4, here.y)
        self.landed(self.from_yd.at[self.rows_of(piece)], piece, 1)
        at = self.held(1, piece, BACK)
        at[...] = (at[...].astype(jnp.float32) + self.from_yd[self.rows_of(piece), :].astype(jnp.float32)).astype(jnp.bfloat16)
        self.go(at, self.halved(self.from_x, piece, BACK), piece, 5, here.x)

    def plane_sum(self, piece):
        self.landed(self.halved(self.from_x, piece, FRONT), piece, 2)
        self.landed(self.halved(self.from_y, piece, BACK), piece, 3)
        self.landed(self.halved(self.from_y, piece, FRONT), piece, 4)
        self.landed(self.halved(self.from_x, piece, BACK), piece, 5)
        total = self.folded(0, piece)
        total = total + self.from_x[self.rows_of(piece), :].astype(jnp.float32) + self.from_y[self.rows_of(piece), :].astype(jnp.float32)
        self.mine[self.rows_of(piece), :] = total.astype(jnp.bfloat16)
        self.go(self.mine.at[self.rows_of(piece)], self.theirs.at[self.rows_of(piece)], piece, 6, self.here.tp_peer)

    def rows_done(self, piece):
        here = self.here
        self.landed(self.theirs.at[self.rows_of(piece)], piece, 6)
        total = self.mine[self.rows_of(piece), :].astype(jnp.float32) + self.theirs[self.rows_of(piece), :].astype(jnp.float32)
        rows = self.rows_of(piece)
        views = [ref.at[rows] if kind == ROWS else ref for ref, kind in zip(self.ins, self.row_kinds)]
        out_views = [ref.at[rows] if kind == ROWS else ref for ref, (_, kind) in zip(self.outs, self.row_outs)]
        given = self.row_function(total, piece, views, out_views)
        if self.gather:
            out = self.outs[-1]
            self.low[rows, :] = given
            first = pl.multiple_of(here.seq * self.block + rows.start, 16)
            keep = pltpu.make_async_copy(self.low.at[rows], out.at[pl.ds(first, rows.size)], self.l_sem.at[piece])
            keep.start()
            spread = Spread(
                here, out, self.block, rows.start, rows.size, self.g_send.at[piece], self.g_recv.at[piece]
            )
            spread.own(self.low, rows.start)
            self.spreads.append((spread, keep))

    def stages(self):
        stages = [(0, self.first_sends), (1, self.second_sends), (2, self.plane_sum), (4, self.rows_done)]
        if self.gather:
            stages.append((5, lambda piece: self.spreads[piece][0].forward()))
            stages.append((6, lambda piece: self.spreads[piece][0].corner()))
        return stages

    def phases(self):
        def phase_of(stage):
            def run():
                for piece in range(PIECES):
                    stage(piece)

            return run

        return [phase_of(stage) for _, stage in self.stages()]

    def finish(self):
        for spread, keep in self.spreads:
            spread.finish()
            keep.wait()
        for made in self.sent:
            made.wait_send()
        for made in self.core_copies.values():
            made.wait_send()


def full_line(rows):
    held = rows[...].astype(jnp.float32)
    return jnp.concatenate([held[number : number + 1, :] for number in range(held.shape[0])], 1)


def own_line(here, rows, width):
    held = rows[...].astype(jnp.float32)
    count = width // LANES
    number = lax.broadcasted_iota(jnp.int32, held.shape, 0)
    parts = [
        jnp.sum(jnp.where(number == here.seq * count + part, held, 0.0), 0, keepdims=True) for part in range(count)
    ]
    return jnp.concatenate(parts, 1)


class Front(Rider):
    def total_scratch(self, count, rows):
        dma = pltpu.SemaphoreType.DMA
        return [
            pltpu.VMEM((PLANE - 1, count, rows), jnp.float32),
            pltpu.VMEM((count, rows), jnp.float32),
            pltpu.VMEM((count, rows), jnp.float32),
            pltpu.VMEM((count, rows), jnp.float32),
            dma((PLANE,)),
            dma((PLANE,)),
        ]

    def peers(self, here):
        return [here.at(lax.rem(here.seq + step, PLANE)) for step in range(1, PLANE)]

    def small_sum(self, scratch):
        here, (plane, own, mine, theirs, send, recv) = self.here, scratch
        made = []
        for step, peer in enumerate(self.peers(here)):
            copy = remote(own, plane.at[step], send.at[step], recv.at[step], peer)
            copy.start()
            made.append(copy)
        total = own[...]
        for step, copy in enumerate(made):
            copy.wait_recv()
            total = total + plane[step]
        mine[...] = total
        last = remote(mine, theirs, send.at[PLANE - 1], recv.at[PLANE - 1], here.tp_peer)
        last.start()
        last.wait()
        for copy in made:
            copy.wait_send()
        total = mine[...] + theirs[...]
        count, rows = total.shape
        return jnp.concatenate([total, jnp.zeros((8 - count, rows), jnp.float32)], 0).T


def chosen_rows(target_rows, first, count):
    row = first + lax.broadcasted_iota(jnp.int32, (count, target_rows.shape[1]), 0)
    return (row == target_rows[...]).astype(jnp.float32).astype(jnp.bfloat16)


class ImageFront(Rider):
    def __init__(self, pictures, key_part, value_part, latent_all, probe_part, target_rows, segment):
        self.inputs = [pictures, key_part, value_part, latent_all, probe_part, target_rows, segment]
        rows, width = pictures.shape[0], key_part.shape[1]
        images = rows // PATCH
        low_type = jnp.bfloat16
        self.out_shapes = [
            jax.ShapeDtypeStruct((rows, 2 * width), low_type),
            jax.ShapeDtypeStruct((images * LAT, width), low_type),
            jax.ShapeDtypeStruct((LAT, width), low_type),
        ]
        self.out_shapes += [jax.ShapeDtypeStruct((segment.shape[1], width), jnp.float32)] * 3
        self.out_shapes.append(jax.ShapeDtypeStruct((segment.shape[1], 8), jnp.float32))
        self.scratch = [
            pltpu.VMEM((key_part.shape[0], 2 * width), low_type),
            pltpu.VMEM((images * LAT, width), low_type),
        ]

    def run(self):
        pictures, key_w, value_w, latent_all, probe_w, target_rows, segment = self.ins
        keys, placed, probe, *tables, column = self.outs
        row = segment[...].astype(jnp.float32)
        column[...] = jnp.broadcast_to(row, (8, row.shape[1])).T
        for first in range(0, segment.shape[1], ATTEND_ROWS):
            self.launches.append(functools.partial(xpos_part, segment, column, tables, first))
        both_w, mixed_all = self.held
        width, scale = probe.shape[1], HEAD ** (-0.5)
        both_w[:, :width] = key_w[...]
        both_w[:, width:] = value_w[...]
        probe[...] = jnp.dot(latent_all[...], probe_w[...], preferred_element_type=jnp.float32).astype(jnp.bfloat16)
        yield
        heads = range(0, width, HEAD)
        for group in range(0, pictures.shape[0] // PATCH, IMAGES_A_STEP):
            more = slice(group * PATCH, (group + IMAGES_A_STEP) * PATCH)
            both = jnp.dot(pictures[more, :], both_w[...], preferred_element_type=jnp.float32).astype(jnp.bfloat16)
            keys[more, :] = both
            scores = [
                lax.dot_general(
                    probe[:, first : first + HEAD] * scale,
                    both[:, first : first + HEAD],
                    (((1,), (1,)), ((), ())),
                    preferred_element_type=jnp.float32,
                )
                for first in heads
            ]
            parts = [(image, head) for image in range(IMAGES_A_STEP) for head in range(len(heads))]
            rows = [slice(image * PATCH, (image + 1) * PATCH) for image in range(IMAGES_A_STEP)]
            cut = [scores[head][:, rows[image]] for image, head in parts]
            best = [jnp.max(part, -1, keepdims=True) for part in cut]
            weights = [jnp.exp(part - top) for part, top in zip(cut, best)]
            totals = [jnp.sum(part, -1, keepdims=True) for part in weights]
            probs = [(part * (1.0 / total)).astype(jnp.bfloat16) for part, total in zip(weights, totals)]
            mixed = [
                jnp.dot(
                    part,
                    both[rows[image], width + head * HEAD : width + (head + 1) * HEAD],
                    preferred_element_type=jnp.float32,
                ).astype(jnp.bfloat16)
                for part, (image, head) in zip(probs, parts)
            ]
            for image in range(IMAGES_A_STEP):
                at = slice((group + image) * LAT, (group + image + 1) * LAT)
                mixed_all[at, :] = jnp.concatenate(mixed[image * len(heads) : (image + 1) * len(heads)], 1)
            yield
        for first in range(0, placed.shape[0], PATCH):
            chosen = chosen_rows(target_rows, first, PATCH)
            placed[first : first + PATCH, :] = jnp.dot(
                chosen, mixed_all[...], preferred_element_type=jnp.float32
            ).astype(jnp.bfloat16)
        self.lefts = [placed]


class AttendFront(Front):
    def __init__(self, normed, layer_part, tables, segment, column, gain, shift, full_width):
        self.inputs = [normed, layer_part, *tables, segment, column, gain, shift]
        self.full_width = full_width
        rows, width = normed.shape[0], layer_part.shape[1] // 3
        low_shape = jax.ShapeDtypeStruct((rows, width), jnp.bfloat16)
        wide_shape = jax.ShapeDtypeStruct((rows, width), jnp.float32)
        lse_shape = jax.ShapeDtypeStruct((rows, 8), jnp.float32)
        self.out_shapes = [low_shape, low_shape, low_shape, wide_shape, lse_shape, low_shape, wide_shape, wide_shape]
        self.scratch = self.total_scratch(2, rows)

    def run(self):
        normed, layer_w, cos_ref, sin_ref, grow_ref, segment, column, gain, shift = self.ins
        q_out, k_out, v_out, att_out, lse_out, low, hat, factor_out = self.outs
        rows_all, width = att_out.shape
        scale = HEAD ** (-0.5)
        f32, low_type = jnp.float32, jnp.bfloat16
        for first in range(0, rows_all, ATTEND_ROWS):
            at, keys = slice(first, first + ATTEND_ROWS), first + ATTEND_ROWS
            cosine, sine, growth = cos_ref[at, :], sin_ref[at, :], grow_ref[at, :]
            linear = jnp.dot(normed[at, :], layer_w[...], preferred_element_type=f32)
            lin = linear[:, :width]
            q_out[at, :] = ((lin * cosine + halves_swapped(lin) * sine) * growth).astype(low_type)
            lin = linear[:, width : 2 * width]
            k_out[at, :] = ((lin * cosine + halves_swapped(lin) * sine) * (1.0 / growth)).astype(low_type)
            v_out[at, :] = linear[:, 2 * width :].astype(low_type)
            allowed = allowed_part(column, segment, first, ATTEND_ROWS, keys)
            heads = [slice(start, start + HEAD) for start in range(0, width, HEAD)]
            scores = [
                lax.dot_general(
                    q_out[at, lanes] * scale,
                    k_out[:keys, lanes],
                    (((1,), (1,)), ((), ())),
                    preferred_element_type=f32,
                )
                for lanes in heads
            ]
            scores = [jnp.where(allowed, part, -1e30) for part in scores]
            best = [jnp.max(part, -1, keepdims=True) for part in scores]
            weights = [jnp.exp(part - top) for part, top in zip(scores, best)]
            totals = [jnp.sum(part, -1, keepdims=True) for part in weights]
            probs = [(part * (1.0 / total)).astype(low_type) for part, total in zip(weights, totals)]
            mixed = [
                jnp.dot(part, v_out[:keys, lanes], preferred_element_type=f32) for part, lanes in zip(probs, heads)
            ]
            for head, lanes in enumerate(heads):
                att_out[at, lanes] = mixed[head]
                lse_out[at, head : head + 1] = best[head] + jnp.log(totals[head])
            rows = att_out[at, :]
            sums = [jnp.sum(rows, 1, keepdims=True), jnp.sum(rows * rows, 1, keepdims=True)]
            self.held[1][:, at] = as_lanes(sums)[:2]
            yield
        total = self.small_sum(self.held) / self.full_width
        average = total[:, 0:1]
        factor = lax.rsqrt(total[:, 1:2] - average * average + EPSILON)
        normal = (att_out[...] - average) * factor
        hat[...] = normal
        factor_out[...] = jnp.broadcast_to(factor, normal.shape)
        gain, shift = (own_line(self.here, line, low.shape[1]) for line in (gain, shift))
        low[...] = (normal * gain + shift).astype(low_type)
        self.lefts = [low]


class GradFront(Front):
    def grads(self, products):
        for seq in range(PLANE):
            for product in products:
                self.launches.append(functools.partial(self.part, *product, seq))

    def part(self, left, right, out, side, seq):
        span = (left.shape[1] if side == INWARD else right.shape[1]) // PLANE
        at = slice(seq * span, (seq + 1) * span)
        contract = (((0,), (0,)), ((), ()))
        half = span // 2
        if side == OUTWARD:
            out[:, at] = lax.dot_general(
                left[...], right[:, at], contract, preferred_element_type=jnp.float32
            ).astype(jnp.bfloat16)
        else:
            made = lax.dot_general(left[:, at], right[...], contract, preferred_element_type=jnp.float32)
            made = made.astype(jnp.bfloat16)
            out[seq, 0], out[seq, 1] = made[:half], made[half:]


def grad_shape(model_width, rows, side):
    span = model_width // PLANE
    shape = (PLANE, 2, span // 2, rows) if side == INWARD else (rows, model_width)
    return jax.ShapeDtypeStruct(shape, jnp.bfloat16)


class HiddenFront(GradFront):
    def __init__(self, lifted, up_part, bias, cotangent_all, down_part, gain, shift, full_width):
        self.inputs = [lifted, up_part, bias, cotangent_all, down_part, gain, shift]
        self.full_width = full_width
        rows, width, model_width = lifted.shape[0], up_part.shape[1], lifted.shape[1]
        low_shape = jax.ShapeDtypeStruct((rows, width), jnp.bfloat16)
        self.out_shapes = [
            low_shape,
            low_shape,
            jax.ShapeDtypeStruct((8, width), jnp.float32),
            grad_shape(model_width, width, INWARD),
            grad_shape(model_width, width, OUTWARD),
            jax.ShapeDtypeStruct((rows, model_width), jnp.bfloat16),
        ]
        self.scratch = self.total_scratch(4, rows) + [pltpu.VMEM((rows, width), jnp.float32)] * 3

    def run(self):
        lifted, up_w, bias, cotangent_all, down_w, gain, shift = self.ins
        settled, d_hidden, vectors, up, down, result = self.outs
        activated, slope, d_settled = self.held[6:]
        f32 = jnp.float32
        bias, gain, shift = (own_line(self.here, line, settled.shape[1]) for line in (bias, gain, shift))
        rows = activated.shape[0]
        step = rows // 4
        for first in range(0, rows, step):
            at = slice(first, first + step)
            pre = jnp.dot(lifted[at, :], up_w[...], preferred_element_type=f32) + bias
            below = 0.5 + 0.5 * lax.erf(pre * (0.5**0.5))
            act = pre * below
            activated[at, :] = act
            slope[at, :] = below + pre * jnp.exp(-0.5 * pre * pre) * (1.0 / (2.0 * jnp.pi) ** 0.5)
            grad = lax.dot_general(
                cotangent_all[at, :], down_w[...], (((1,), (1,)), ((), ())), preferred_element_type=f32
            )
            d_settled[at, :] = grad
            scaled = grad * gain
            sums = [jnp.sum(part, 1, keepdims=True) for part in (act, act * act, scaled, scaled * act)]
            self.held[1][:, at] = as_lanes(sums)[:4]
            yield
        total = self.small_sum(self.held[:6]) / self.full_width
        average = total[:, 0:1]
        factor = lax.rsqrt(total[:, 1:2] - average * average + EPSILON)
        mean_scaled = total[:, 2:3]
        mean_cross = factor * (total[:, 3:4] - average * mean_scaled)
        step = rows // PLANE
        gain_sum = shift_sum = bias_sum = 0.0
        for first in range(0, rows, step):
            at = slice(first, first + step)
            normal = (activated[at, :] - average[at]) * factor[at]
            settled[at, :] = (normal * gain + shift).astype(jnp.bfloat16)
            grad = d_settled[at, :]
            inner = factor[at] * (grad * gain - mean_scaled[at] - normal * mean_cross[at])
            low = (slope[at, :] * inner).astype(jnp.bfloat16)
            d_hidden[at, :] = low
            gain_sum += jnp.sum(grad * normal, 0, keepdims=True)
            shift_sum += jnp.sum(grad, 0, keepdims=True)
            bias_sum += jnp.sum(low.astype(f32), 0, keepdims=True)
        vectors[...] = jnp.zeros_like(vectors)
        vectors[0:1, :], vectors[1:2, :], vectors[2:3, :] = gain_sum, shift_sum, bias_sum
        def result_part(first):
            at = slice(first, first + step)
            result[at, :] = jnp.dot(settled[at, :], down_w[...], preferred_element_type=f32).astype(jnp.bfloat16)

        for first in range(0, rows, step):
            self.launches.append(functools.partial(result_part, first))
        self.grads([(lifted, d_hidden, up, INWARD), (settled, cotangent_all, down, OUTWARD)])
        self.lefts = [d_hidden, settled]


class AttendBackFront(GradFront):
    def __init__(self, d_branch, out_part, hat, factor, gain, kept, tables, segment, column, normed, inner_low, full_width):
        self.inputs = [d_branch, out_part, hat, factor, gain, *kept, *tables]
        self.inputs += [segment, column, normed, inner_low]
        self.full_width = full_width
        rows, width = hat.shape
        model_width = normed.shape[1]
        low_type, f32 = jnp.bfloat16, jnp.float32
        self.out_shapes = [jax.ShapeDtypeStruct((8, width), f32)]
        self.out_shapes += [grad_shape(model_width, 3 * width, INWARD), grad_shape(model_width, width, OUTWARD)]
        self.scratch = self.total_scratch(2, rows)
        self.scratch += [pltpu.VMEM((rows, width), low_type), pltpu.VMEM((rows, 3 * width), low_type)]
        self.scratch += [pltpu.VMEM((rows, width), f32)] * 4

    def run(self):
        d_branch, out_part, hat, factor, gain, attended, q_ref, k_ref, v_ref, lse = self.ins[:10]
        cos_ref, sin_ref, grow_ref, segment, column, normed, inner_low = self.ins[10:]
        gain = own_line(self.here, gain, hat.shape[1])
        vectors, lin_grad, out_grad = self.outs
        d_att, lin_out, d_inner, d_query, d_key, d_value = self.held[6:]
        rows_all, width = hat.shape
        f32, low_type = jnp.float32, jnp.bfloat16
        gain_sum = shift_sum = 0.0
        for first in range(0, rows_all, ATTEND_ROWS):
            at = slice(first, first + ATTEND_ROWS)
            grad = lax.dot_general(
                d_branch[at, :], out_part[...], (((1,), (1,)), ((), ())), preferred_element_type=f32
            )
            d_inner[at, :] = grad
            gain_sum += jnp.sum(grad * hat[at, :], 0, keepdims=True)
            shift_sum += jnp.sum(grad, 0, keepdims=True)
            scaled = grad * gain
            sums = [jnp.sum(scaled, 1, keepdims=True), jnp.sum(scaled * hat[at, :], 1, keepdims=True)]
            self.held[1][:, at] = as_lanes(sums)[:2]
            yield
        vectors[...] = jnp.zeros_like(vectors)
        vectors[0:1, :], vectors[1:2, :] = gain_sum, shift_sum
        total = self.small_sum(self.held[:6]) / self.full_width
        d_att[...] = (
            factor[...] * (d_inner[...] * gain - total[:, 0:1] - hat[...] * total[:, 1:2])
        ).astype(low_type)
        heads, scale = width // HEAD, HEAD ** (-0.5)
        for first in range(0, rows_all, ATTEND_ROWS):
            at, keys = slice(first, first + ATTEND_ROWS), first + ATTEND_ROWS
            allowed = allowed_part(column, segment, first, ATTEND_ROWS, keys)
            contract_last, contract_first = (((1,), (1,)), ((), ())), (((0,), (0,)), ((), ()))
            lanes_of = [slice(head * HEAD, (head + 1) * HEAD) for head in range(heads)]
            d_rows = [d_att[at, lanes] for lanes in lanes_of]
            scores = [
                lax.dot_general(
                    q_ref[at, lanes] * scale, k_ref[:keys, lanes], contract_last, preferred_element_type=f32
                )
                for lanes in lanes_of
            ]
            d_probs = [
                lax.dot_general(d, v_ref[:keys, lanes], contract_last, preferred_element_type=f32)
                for d, lanes in zip(d_rows, lanes_of)
            ]
            deltas = [
                jnp.sum(d.astype(f32) * attended[at, lanes], -1, keepdims=True) for d, lanes in zip(d_rows, lanes_of)
            ]
            probs = [
                jnp.exp(jnp.where(allowed, part, -1e30) - lse[at, head : head + 1])
                for head, part in enumerate(scores)
            ]
            d_scores = [(p * (d - delta)).astype(low_type) for p, d, delta in zip(probs, d_probs, deltas)]
            for head, lanes in enumerate(lanes_of):
                d_query[at, lanes] = (
                    jnp.dot(d_scores[head], k_ref[:keys, lanes], preferred_element_type=f32) * scale
                )
                key_part = (
                    lax.dot_general(d_scores[head], q_ref[at, lanes], contract_first, preferred_element_type=f32)
                    * scale
                )
                value_part = lax.dot_general(
                    probs[head].astype(low_type), d_rows[head], contract_first, preferred_element_type=f32
                )
                if first:
                    d_key[:first, lanes] += key_part[:first]
                    d_value[:first, lanes] += value_part[:first]
                d_key[first:keys, lanes] = key_part[first:]
                d_value[first:keys, lanes] = value_part[first:]
            yield
        for first in range(0, rows_all, ATTEND_ROWS):
            at = slice(first, first + ATTEND_ROWS)
            cosine, sine, growth = cos_ref[at, :], sin_ref[at, :], grow_ref[at, :]
            scaled = d_query[at, :] * growth
            lin_out[at, :width] = (scaled * cosine - halves_swapped(scaled) * sine).astype(low_type)
            scaled = d_key[at, :] * (1.0 / growth)
            lin_out[at, width : 2 * width] = (scaled * cosine - halves_swapped(scaled) * sine).astype(low_type)
            lin_out[at, 2 * width :] = d_value[at, :].astype(low_type)
        self.grads(
            [
                (normed, lin_out, lin_grad, INWARD),
                (inner_low, d_branch, out_grad, OUTWARD),
            ]
        )
        self.lefts = [lin_out]


def lazy_call(kernel, inputs, in_specs, out_shapes, out_specs, scratch, cid):
    late = [is_lazy(value, spec) for value, spec in zip(inputs, in_specs)]
    buffers = [pltpu.VMEM(value.shape, value.dtype) for value, flag in zip(inputs, late) if flag]
    n_in, n_out, n_scratch, n_late = len(inputs), len(out_shapes), len(scratch), len(buffers)

    def body(*refs):
        refs = list(refs)
        ins, outs, held = refs[:n_in], refs[n_in : n_in + n_out], refs[n_in + n_out : n_in + n_out + n_scratch]
        spare, sems = refs[n_in + n_out + n_scratch : -1], refs[-1]
        lazies = []
        for number, flag in enumerate(late):
            if flag:
                ins[number] = Lazy(ins[number], spare[len(lazies)], sems.at[len(lazies)])
                lazies.append(ins[number])
        kernel(ins, outs, held)
        for item in lazies:
            item.ready()

    return pl.pallas_call(
        body,
        out_shape=tuple(out_shapes),
        in_specs=[ANYWHERE if flag else spec for spec, flag in zip(in_specs, late)],
        out_specs=tuple(out_specs),
        scratch_shapes=list(scratch) + buffers + [pltpu.SemaphoreType.DMA((max(n_late, 1),))],
        compiler_params=pltpu.CompilerParams(
            collective_id=cid, has_side_effects=True, vmem_limit_bytes=VMEM_BYTES
        ),
    )(*inputs)


def exchange(front, streams, riders, cid, pace=(), between=0, work_from=0):
    fronts = [front] if front is not None else []
    sums = list(streams)
    parts = fronts + sums + list(riders)

    def kernel(ins, outs, held):
        here = Places()
        ins, outs, held = list(ins), list(outs), list(held)

        def take(refs, count):
            taken = refs[:count]
            del refs[:count]
            return taken

        for part in parts:
            part.bind(
                here, take(ins, len(part.inputs)), take(outs, len(part.out_shapes)), take(held, len(part.scratch))
            )
        wide_parts = [part for part in parts if isinstance(part, (Front, ChainWeights))]
        peers = [here.tp_peer]
        if riders:
            peers.append(here.img_peer)
        if wide_parts:
            peers += wide_parts[0].peers(here)
        else:
            peers += [here.core, here.x, here.y]
        greet(peers)
        waiting, work = [], []
        for rider in riders:
            rider.start()
            if rider.later:
                take_some(rider.launches, len(rider.launches))
            waiting += rider.launches + rider.later
        if front is not None:
            allowed = list(pace)
            for _ in front.run():
                take_some(waiting, allowed.pop(0) if allowed else 0)
            for stream, left in zip(streams, front.lefts):
                stream.left = left
            work = front.launches
        for stream in streams:
            stream.begin()
        stages = []
        for number, stream in reversed(list(enumerate(streams))):
            stages += [(lag + number * SECOND_LAG, stage) for lag, stage in stream.stages()]
        ticks = ticks_of(stages, PIECES)
        share, last = -(-len(work) // max(len(ticks) - 2 - work_from, 1)), PIECES + 1
        for number, tick in enumerate(ticks):
            tick()
            if number >= work_from:
                take_some(work, share)
            if number < 2:
                take_some(waiting, between)
            if number >= last:
                take_some(waiting, -(-len(waiting) // max(len(ticks) - 1 - number, 1)))
        take_some(work, len(work))
        take_some(waiting, len(waiting))
        for part in parts:
            part.finish()

    in_specs = []
    for part in fronts + sums:
        in_specs += part.in_specs or [ON_CHIP] * len(part.inputs)
    in_specs += [ANYWHERE] * sum(len(rider.inputs) for rider in riders)
    out_specs = [ON_CHIP for part in fronts for _ in part.out_shapes]
    out_specs += [spec for stream in sums for spec in stream.out_specs()]
    out_specs += [ANYWHERE] * sum(len(rider.out_shapes) for rider in riders)
    made = list(
        lazy_call(
            kernel,
            [value for part in parts for value in part.inputs],
            in_specs,
            [shape for part in parts for shape in part.out_shapes],
            out_specs,
            [item for part in parts for item in part.scratch],
            cid,
        )
    )
    split = []
    for part in parts:
        split.append(made[: len(part.out_shapes)])
        del made[: len(part.out_shapes)]
    return split


def finale(pairs, sides, raw, raw_sides, image, row_vectors, own_vectors, latents, query_rows, result_parts, cid):
    f32, low_type, dma = jnp.float32, jnp.bfloat16, pltpu.SemaphoreType.DMA
    d_rows, pictures, keys, probe, placed, out_part, target_rows = image
    width, model_width, picture_width = probe.shape[1], d_rows.shape[1], pictures.shape[1]
    images = pictures.shape[0] // PATCH
    image_shapes = [
        grad_shape(picture_width, width, INWARD),
        grad_shape(picture_width, width, INWARD),
        grad_shape(model_width, width, OUTWARD),
    ]
    all_sides = list(sides) + list(raw_sides) + [INWARD, INWARD, OUTWARD]
    n, n_raw, n_image = len(sides), len(raw_sides), len(image_shapes)
    total = n + n_raw + n_image
    shapes = [grad.shape for grad, _ in pairs] + [grad.shape for grad in raw] + [item.shape for item in image_shapes]
    blocks = [
        shape[2:] if side == INWARD else (shape[0], shape[1] // (2 * PLANE)) for shape, side in zip(shapes, all_sides)
    ]
    vectors = list(row_vectors) + [array for array, _ in own_vectors]
    picked = [0] * len(row_vectors) + [row for _, row in own_vectors]
    vector_rows = sum(vector.shape[1] // LANES for vector in vectors)
    small_shape = (LAT + vector_rows + -vector_rows % 8, LANES)
    result_shape = result_parts[0].shape

    def kernel(ins, outs, held):
        refs = list(ins) + list(outs) + list(held)

        def take(count):
            taken = refs[:count]
            del refs[:count]
            return taken

        target_ref, d_ref, pictures_ref, keys_ref, probe_ref, placed_ref, out_w = take(7)
        grad_refs = take(n + n_raw)
        theirs = take(n)
        vector_refs = take(len(vectors))
        latents_ref, query_ref, result_ref, result_here, middle_ref = take(5)
        out_refs = take(total)
        sums_out, query_out, latent_out, result_out = take(4)
        grad_refs += take(n_image)
        theirs += take(n_raw + n_image)
        summed = take(total)
        small_own, small_theirs, small_mine, small_all, lat_mine, lat_theirs, d_mixed, d_both, result_theirs = take(9)
        z_send, z_recv, send, recv, local, s_send, s_recv, r_send, r_recv = take(9)
        here = Places()
        seq, img = here.seq, here.img
        ring = [here.at(lax.rem(seq + step, PLANE)) for step in range(1, PLANE)]
        greet(ring + [here.img_peer, here.tp_peer])

        def part_of(index, to_seq, to_img):
            ref, block = grad_refs[index], blocks[index]
            if all_sides[index] == INWARD:
                return ref.at[to_seq, to_img]
            return ref.at[:, pl.ds(pl.multiple_of((to_seq * 2 + to_img) * block[1], block[1]), block[1])]

        def slot_of(index, from_seq):
            ref, block = out_refs[index], blocks[index]
            if all_sides[index] == INWARD:
                return ref.at[:, pl.ds(pl.multiple_of(from_seq * block[1], block[1]), block[1])]
            return ref.at[pl.ds(pl.multiple_of(from_seq * block[0], block[0]), block[0])]

        waits, crossings = [], {}

        def cross(index):
            for step in range(PLANE):
                target = lax.rem(seq + step, PLANE)
                made = remote(
                    part_of(index, target, 1 - img),
                    theirs[index].at[target],
                    z_send.at[index - n, step],
                    z_recv.at[index - n, step],
                    here.img_peer,
                )
                made.start()
                crossings[index, step] = made

        def deliver(index, step):
            target = lax.rem(seq + step, PLANE)
            if index >= n:
                crossings[index, step].wait_recv()
            mine = part_of(index, target, img)[...].astype(f32)
            summed[index][target] = (mine + theirs[index][target].astype(f32)).astype(low_type)
            if step == 0:
                made = pltpu.make_async_copy(summed[index].at[target], slot_of(index, seq), local.at[index])
                made.start()
                waits.append(made.wait)
                return
            made = remote(
                summed[index].at[target], slot_of(index, seq), send.at[index, step], recv.at[index, step], here.at(target)
            )
            made.start()
            waits.append(made.wait_send)

        result_copy = remote(result_ref, result_theirs, r_send.at[0], r_recv.at[0], here.tp_peer)
        result_copy.start()
        for index in range(n, n + n_raw):
            cross(index)
        at_row = LAT
        for vector, row in zip(vector_refs, picked):
            for first in range(0, vector.shape[1], LANES):
                small_own[at_row : at_row + 1, :] = vector[row : row + 1, first : first + LANES]
                at_row += 1
        if at_row < small_shape[0]:
            small_own[at_row:, :] = jnp.zeros((small_shape[0] - at_row, LANES), f32)
        waiting = [functools.partial(deliver, index, step) for index in range(n + n_raw) for step in range(PLANE)]

        scale = HEAD ** (-0.5)
        d_slots = jnp.zeros(d_mixed.shape, f32)
        for first in range(0, d_ref.shape[0], PATCH):
            d_part = lax.dot_general(
                d_ref[first : first + PATCH, :], out_w[...], (((1,), (1,)), ((), ())), preferred_element_type=f32
            ).astype(low_type)
            chosen = chosen_rows(target_ref, first, PATCH)
            d_slots += lax.dot_general(chosen, d_part, (((0,), (0,)), ((), ())), preferred_element_type=f32)
        d_mixed[...] = d_slots.astype(low_type)
        take_some(waiting, 1)
        for first in range(0, model_width, 512):
            at = slice(first, first + 512)
            grad_refs[total - 1][:, at] = lax.dot_general(
                placed_ref[...], d_ref[:, at], (((0,), (0,)), ((), ())), preferred_element_type=f32
            ).astype(low_type)
            take_some(waiting, 1)
        cross(total - 1)
        d_probe_sum = jnp.zeros(probe_ref.shape, f32)
        heads = range(0, width, HEAD)
        for group in range(0, images, IMAGES_A_STEP):
            parts = [(image, first) for image in range(group, group + IMAGES_A_STEP) for first in heads]
            contract_last, contract_first = (((1,), (1,)), ((), ())), (((0,), (0,)), ((), ()))
            keys_of = [keys_ref[i * PATCH : (i + 1) * PATCH, f : f + HEAD] for i, f in parts]
            values_of = [keys_ref[i * PATCH : (i + 1) * PATCH, width + f : width + f + HEAD] for i, f in parts]
            probe_of = [probe_ref[:, f : f + HEAD] for _, f in parts]
            d_of = [d_mixed[i * LAT : (i + 1) * LAT, f : f + HEAD] for i, f in parts]
            scores = [
                lax.dot_general(p * scale, k, contract_last, preferred_element_type=f32)
                for p, k in zip(probe_of, keys_of)
            ]
            d_probs = [
                lax.dot_general(d, v, contract_last, preferred_element_type=f32) for d, v in zip(d_of, values_of)
            ]
            best = [jnp.max(part, -1, keepdims=True) for part in scores]
            weights = [jnp.exp(part - top) for part, top in zip(scores, best)]
            totals = [jnp.sum(part, -1, keepdims=True) for part in weights]
            probs = [part * (1.0 / whole) for part, whole in zip(weights, totals)]
            deltas = [jnp.sum(p * d, -1, keepdims=True) for p, d in zip(probs, d_probs)]
            d_scores = [(p * (d - delta)).astype(low_type) for p, d, delta in zip(probs, d_probs, deltas)]
            d_probe = [jnp.dot(d, k, preferred_element_type=f32) for d, k in zip(d_scores, keys_of)]
            d_keys = [
                lax.dot_general(d, p, contract_first, preferred_element_type=f32) for d, p in zip(d_scores, probe_of)
            ]
            d_values = [
                lax.dot_general(p.astype(low_type), d, contract_first, preferred_element_type=f32)
                for p, d in zip(probs, d_of)
            ]
            for number, (image, first) in enumerate(parts):
                rows = slice(image * PATCH, (image + 1) * PATCH)
                d_both[rows, first : first + HEAD] = (d_keys[number] * scale).astype(low_type)
                d_both[rows, width + first : width + first + HEAD] = d_values[number].astype(low_type)
            for number in range(0, len(parts), len(heads)):
                d_probe_sum += jnp.concatenate(d_probe[number : number + len(heads)], 1) * scale
            take_some(waiting, 8)
        small_own[:LAT, :] = d_probe_sum
        small_cross = remote(small_own, small_theirs, s_send.at[0], s_recv.at[0], here.img_peer)
        small_cross.start()
        span = picture_width // PLANE
        for part in range(PLANE):
            made = lax.dot_general(
                pictures_ref[:, part * span : (part + 1) * span],
                d_both[...],
                (((0,), (0,)), ((), ())),
                preferred_element_type=f32,
            ).astype(low_type)
            for kind in range(2):
                piece = made[:, kind * width : (kind + 1) * width]
                grad_refs[n + n_raw + kind][part, 0] = piece[: span // 2]
                grad_refs[n + n_raw + kind][part, 1] = piece[span // 2 :]
            take_some(waiting, 2)
        for kind in range(2):
            cross(n + n_raw + kind)
        small_cross.wait()
        small_mine[...] = small_own[...] + small_theirs[...]
        small_all[seq] = small_mine[...]
        small_copies = []
        for step, peer in enumerate(ring, 1):
            made = remote(small_mine, small_all.at[seq], s_send.at[step], s_recv.at[step], peer)
            made.start()
            small_copies.append(made)
        take_some(waiting, len(waiting))
        for index in (total - 1, total - 3, total - 2):
            for step in range(PLANE):
                deliver(index, step)
        for made in small_copies:
            made.wait()
        sums_out[...] = small_all[...]
        latent_part = jnp.zeros(lat_mine.shape, f32)
        for source in range(PLANE):
            given = small_all[source, :LAT, :]
            at = slice(source * width, (source + 1) * width)
            query_out[:, at] = lax.dot_general(
                latents_ref[...].astype(f32),
                given,
                (((0,), (0,)), ((), ())),
                precision=HIGHEST_PRECISION,
                preferred_element_type=f32,
            )
            latent_part += lax.dot_general(
                given,
                query_ref[:, at].astype(f32),
                (((1,), (1,)), ((), ())),
                precision=HIGHEST_PRECISION,
                preferred_element_type=f32,
            )
        lat_mine[...] = latent_part
        last = remote(lat_mine, lat_theirs, s_send.at[PLANE], s_recv.at[PLANE], here.tp_peer)
        last.start()
        last.wait()
        latent_out[...] = lat_mine[...] + lat_theirs[...]
        result_copy.wait()
        result_sum = result_here[...].astype(f32) + result_theirs[...].astype(f32)
        result_out[...] = (middle_ref[...] + result_sum).astype(low_type)
        for index in range(total):
            for step in range(1, PLANE):
                source = lax.rem(seq + PLANE - step, PLANE)
                at = slot_of(index, source)
                remote(at, at, send.at[index, step], recv.at[index, step], here.core).wait_recv()
        for wait in waits:
            wait()
        for made in crossings.values():
            made.wait_send()

    outs = []
    for block, side in zip(blocks, all_sides):
        shape = (block[0], PLANE * block[1]) if side == INWARD else (PLANE * block[0], block[1])
        outs.append(jax.ShapeDtypeStruct(shape, low_type))
    lat_shape = latents.shape
    small_shapes = [
        jax.ShapeDtypeStruct((PLANE,) + small_shape, f32),
        jax.ShapeDtypeStruct(query_rows.shape, f32),
        jax.ShapeDtypeStruct(lat_shape, f32),
        jax.ShapeDtypeStruct(result_shape, low_type),
    ]
    n_cross = n_raw + n_image
    made = lazy_call(
        kernel,
        [
            target_rows,
            d_rows,
            pictures,
            keys,
            probe,
            placed,
            out_part,
            *[grad for grad, _ in pairs],
            *raw,
            *[given for _, given in pairs],
            *vectors,
            latents,
            query_rows,
            result_parts[0],
            *result_parts,
        ],
        [ON_CHIP] * (7 + n + n_raw + n + len(vectors)) + [ON_CHIP] * 2 + [ANYWHERE, ON_CHIP, ON_CHIP],
        outs + small_shapes,
        [ANYWHERE] * total + [ON_CHIP] * 4,
        [pltpu.VMEM(item.shape, low_type) for item in image_shapes]
        + [pltpu.VMEM((PLANE,) + tuple(block), low_type) for block in blocks[n:]]
        + [pltpu.VMEM((PLANE,) + tuple(block), low_type) for block in blocks]
        + [
            pltpu.VMEM(small_shape, f32),
            pltpu.VMEM(small_shape, f32),
            pltpu.VMEM(small_shape, f32),
            pltpu.VMEM((PLANE,) + small_shape, f32),
            pltpu.VMEM(lat_shape, f32),
            pltpu.VMEM(lat_shape, f32),
            pltpu.VMEM((d_rows.shape[0], width), low_type),
            pltpu.VMEM((images * PATCH, 2 * width), low_type),
            pltpu.VMEM(result_shape, low_type),
            dma((n_cross, PLANE)),
            dma((n_cross, PLANE)),
            dma((total, PLANE)),
            dma((total, PLANE)),
            dma((total,)),
            dma((PLANE + 1,)),
            dma((PLANE + 1,)),
            dma((1,)),
            dma((1,)),
        ],
        cid,
    )
    return made[:total], made[total:]


def widened(grads, splits, passed, spread, model_width, n_rows, widths):
    f32, dma = jnp.float32, pltpu.SemaphoreType.DMA
    n, n_passed, n_wide = len(grads), len(passed), sum(splits)
    wide_shapes = []
    for array, split in zip(grads, splits):
        wide_shapes += [jax.ShapeDtypeStruct((array.shape[0], array.shape[1] // split), f32)] * split

    def kernel(*refs):
        refs = list(refs)

        def take(count):
            taken = refs[:count]
            del refs[:count]
            return taken

        ins, passed_ins, (spread_ref,) = take(n), take(n_passed), take(1)
        outs, passed_outs, row_outs, own_outs = take(n_wide), take(n_passed), take(n_rows), take(len(widths))
        narrow, wide, held, (in_sems, out_sems, passed_sems) = take(n), take(n_wide), take(n_passed), take(3)
        copies_in = [pltpu.make_async_copy(src, dst, in_sems.at[i]) for i, (src, dst) in enumerate(zip(ins, narrow))]
        copies_out = [pltpu.make_async_copy(src, dst, out_sems.at[i]) for i, (src, dst) in enumerate(zip(wide, outs))]
        held_in = [pltpu.make_async_copy(src, dst, passed_sems.at[0, i]) for i, (src, dst) in enumerate(zip(passed_ins, held))]
        held_out = [pltpu.make_async_copy(src, dst, passed_sems.at[1, i]) for i, (src, dst) in enumerate(zip(held, passed_outs))]
        for copy in copies_in + held_in:
            copy.start()
        made = 0
        for i, split in enumerate(splits):
            copies_in[i].wait()
            if split == 1:
                wide[made][...] = narrow[i][...].astype(f32)
            else:
                width = narrow[i].shape[1] // (split * PLANE)
                for seq in range(PLANE):
                    for part in range(split):
                        at = (seq * split + part) * width
                        wide[made + part][:, seq * width : (seq + 1) * width] = narrow[i][:, at : at + width].astype(f32)
            for part in range(split):
                copies_out[made + part].start()
            made += split
        for arrive, leave in zip(held_in, held_out):
            arrive.wait()
            leave.start()
        first = LAT
        for out in row_outs:
            count = model_width // LANES
            total = jnp.sum(spread_ref[:, first : first + count, :], 0)
            for part in range(count):
                out[:, part * LANES : (part + 1) * LANES] = total[part : part + 1, :]
            first += count
        for out, width in zip(own_outs, widths):
            for seq in range(PLANE):
                for part in range(width // LANES):
                    at = seq * width + part * LANES
                    out[:, at : at + LANES] = spread_ref[seq, first + part : first + part + 1, :]
            first += width // LANES
        for copy in copies_out + held_out:
            copy.wait()

    shapes = list(wide_shapes)
    shapes += [jax.ShapeDtypeStruct(array.shape, array.dtype) for array in passed]
    shapes += [jax.ShapeDtypeStruct((1, model_width), f32)] * n_rows
    shapes += [jax.ShapeDtypeStruct((1, PLANE * width), f32) for width in widths]
    small = n_rows + len(widths)
    made = pl.pallas_call(
        kernel,
        out_shape=tuple(shapes),
        in_specs=[ANYWHERE] * (n + n_passed) + [ON_CHIP],
        out_specs=tuple([ANYWHERE] * (n_wide + n_passed) + [ON_CHIP] * small),
        scratch_shapes=[pltpu.VMEM(array.shape, array.dtype) for array in grads]
        + [pltpu.VMEM(item.shape, f32) for item in wide_shapes]
        + [pltpu.VMEM(array.shape, array.dtype) for array in passed]
        + [dma((n,)), dma((n_wide,)), dma((2, n_passed))],
        compiler_params=pltpu.CompilerParams(vmem_limit_bytes=VMEM_BYTES),
    )(*grads, *passed, spread)
    made = list(made)
    n = n_wide
    cut = [made[:n], made[n : n + n_passed], made[n + n_passed : n + n_passed + n_rows]]
    return (*cut, made[n + n_passed + n_rows :])


IMAGES_A_STEP = 4


def image_probs_of(probe, keys, scale):
    scores = lax.dot_general(
        probe * scale, keys, (((1,), (1,)), ((), ())), preferred_element_type=jnp.float32
    )
    weights = jnp.exp(scores - jnp.max(scores, -1, keepdims=True))
    return weights * (1.0 / jnp.sum(weights, -1, keepdims=True))


def xpos_part(segment, column, tables, first):
    at, half = slice(first, first + ATTEND_ROWS), HEAD // 2
    f32 = jnp.float32
    rows = segment.shape[1]
    here = segment[:, at].astype(f32)
    earlier = lax.broadcasted_iota(jnp.int32, (rows, ATTEND_ROWS), 0)
    now = first + lax.broadcasted_iota(jnp.int32, (rows, ATTEND_ROWS), 1)
    counted = (column[:, 0:1] == here) & (earlier < now)
    position = jnp.sum(counted.astype(f32), 0, keepdims=True)
    ladder = lax.broadcasted_iota(jnp.int32, (half, ATTEND_ROWS), 0).astype(f32)
    angles = position * jnp.exp(ladder * (-2.0 * jnp.log(f32(10000.0)) / (2.0 * half)))
    growth = jnp.exp(position / 512.0 * jnp.log((ladder / half + 0.4) / 1.4))
    cosine, sine = jnp.cos(angles), jnp.sin(angles)
    repeats = tables[0].shape[1] // HEAD
    tables[0][at, :] = jnp.concatenate([cosine, cosine] * repeats, 0).T
    tables[1][at, :] = jnp.concatenate([-sine, sine] * repeats, 0).T
    tables[2][at, :] = jnp.concatenate([growth, growth] * repeats, 0).T


def halves_swapped(rows):
    width, half = rows.shape[1], HEAD // 2
    lane = lax.broadcasted_iota(jnp.int32, rows.shape, 1)
    ahead = pltpu.roll(rows, width - half, 1)
    behind = pltpu.roll(rows, half, 1)
    return jnp.where(lane % HEAD < half, ahead, behind)


def allowed_part(column, segment, first, count, keys):
    row = first + lax.broadcasted_iota(jnp.int32, (count, keys), 0)
    later = lax.broadcasted_iota(jnp.int32, (count, keys), 1)
    same = column[first : first + count, 0:1] == segment[:, :keys].astype(jnp.float32)
    return same & (later <= row)


ATTEND_ROWS = 256


def as_lanes(columns):
    rows = columns[0].shape[0]
    lane = lax.broadcasted_iota(jnp.int32, (rows, LANES), 1)
    joined = jnp.zeros((rows, LANES), jnp.float32)
    for number, column in enumerate(columns):
        joined = jnp.where(lane == number, column, joined)
    return joined.T[:8, :]


def norm_rows(rows, gain, shift):
    center = rows - jnp.mean(rows, -1, keepdims=True)
    factor = lax.rsqrt(jnp.mean(center * center, -1, keepdims=True) + EPSILON)
    normal = center * factor
    return (normal * gain + shift, normal, factor)


def dot32(left, right):
    return jnp.dot(left, right, preferred_element_type=jnp.float32)


def on_plane(
    text,
    segment,
    features,
    image_count,
    image_slot,
    cotangent,
    input_gain,
    input_shift,
    query_weight,
    key_weight,
    value_weight,
    inner_gain,
    inner_shift,
    out_weight,
    middle_gain,
    middle_shift,
    up_weight,
    up_bias,
    hidden_gain,
    hidden_shift,
    down_weight,
    latents,
    resample_query,
    resample_key,
    resample_value,
    resample_out,
):
    f32, low = jnp.float32, jnp.bfloat16
    row_count, model_width = text.shape[1], text.shape[2]
    group_rows = segment.shape[1]
    image_slots = features.shape[1]
    half_width = query_weight.shape[1]
    own_width = half_width // PLANE

    rows, own = intake(
        (features[0].reshape(image_slots * PATCH, features.shape[3]),),
        (
            resample_key,
            resample_value,
            resample_query,
            latents,
            resample_out,
        ),
        (INWARD, INWARD, INWARD, SHARED, OUTWARD),
        1,
    )
    (pictures,) = rows
    image_key_own, image_value_own, probe_own, latent_all, image_out_own = own

    counts = image_count.reshape(-1, 1)
    live = jnp.arange(IMG_DEV, dtype=jnp.int32)[None, :] < counts
    first_rows = jnp.where(live, image_slot.reshape(live.shape) * LAT, -LAT)
    target_rows = (first_rows[:, :, None] + jnp.arange(LAT, dtype=jnp.int32)).reshape(1, -1)

    def line(vector):
        return vector.reshape(-1, LANES)

    def taken_in(targets, piece, rows):
        first = lax.axis_index(SEQ) * row_count + sum(PIECE_ROWS[:piece])
        row = first + lax.broadcasted_iota(jnp.int32, (rows, targets.shape[1]), 0)
        return jnp.max((row == targets[...]).astype(jnp.float32), 1, keepdims=True) > 0.5

    def begin(total, piece, views, outs):
        text_view, targets, gain, shift = views
        embed = total.astype(jnp.bfloat16).astype(jnp.float32)
        taken = taken_in(targets, piece, total.shape[0])
        mixed = jnp.where(taken, embed, text_view[...].astype(jnp.float32))
        outs[0][...] = mixed
        return norm_rows(mixed, full_line(gain), full_line(shift))[0].astype(jnp.bfloat16)

    rows_wide = jax.ShapeDtypeStruct((row_count, model_width), f32)
    (image_keys, mixed_placed, probe, *tables, column), (mixed_in, normed), (qkv_own, out_own, up_own) = exchange(
        ImageFront(
            pictures, image_key_own, image_value_own, latent_all, probe_own, target_rows, segment
        ),
        [
            Stream(
                group_rows,
                None,
                image_out_own,
                False,
                (text[0], target_rows, line(input_gain), line(input_shift)),
                (ROWS, ALL, ALL, ALL),
                ((rows_wide, ROWS),),
                begin,
                True,
            )
        ],
        [
            ChainWeights(
                (query_weight, key_weight, value_weight, out_weight, up_weight),
                (INWARD, INWARD, INWARD, OUTWARD, INWARD),
                ((0, 0), (0, own_width), (0, 2 * own_width), (1, 0), (2, 0)),
            )
        ],
        3,
        PACE_IMAGE,
    )

    def middle_step(total, piece, views, outs):
        mixed_view, gain, shift = views
        middle = mixed_view[...] + total
        outs[0][...] = middle
        return norm_rows(middle, full_line(gain), full_line(shift))[0].astype(jnp.bfloat16)

    attend_made, (middle, lifted), (down_own,), (cot_all,) = exchange(
        AttendFront(
            normed, qkv_own, tables, segment, column, line(inner_gain), line(inner_shift), model_width
        ),
        [
            Stream(
                group_rows,
                None,
                out_own,
                False,
                (mixed_in, line(middle_gain), line(middle_shift)),
                (ROWS, ALL, ALL),
                ((rows_wide, ROWS),),
                middle_step,
                True,
            )
        ],
        [ChainWeights((down_weight,), (OUTWARD,), ((0, 0),)), GatherRows(cotangent[0])],
        5,
        PACE_ATTEND,
    )
    *attended_kept, inner_low, inner_hat, inner_factor = attend_made
    query_rot, keys_rot, values, attended, log_total = attended_kept
    own_hidden = up_own.shape[1]

    vector_out = jax.ShapeDtypeStruct((1, model_width), f32)

    def norm_back_step(total, piece, views, outs):
        rows_view, carried_view, gain, *targets = views
        rows_in = rows_view[...]
        center = rows_in - jnp.mean(rows_in, -1, keepdims=True)
        factor = lax.rsqrt(jnp.mean(center * center, -1, keepdims=True) + EPSILON)
        normal = center * factor
        grad = carried_view[...].astype(jnp.float32) + full_back(total, normal, factor, full_line(gain))
        if targets:
            outs[0][...] = jnp.where(taken_in(targets[0], piece, total.shape[0]), 0.0, grad)
        else:
            outs[0][...] = grad
        if piece == 0:
            outs[1][...] = jnp.zeros_like(outs[1])
            outs[2][...] = jnp.zeros_like(outs[2])
        outs[1][...] += jnp.sum(total * normal, 0, keepdims=True)
        outs[2][...] += jnp.sum(total, 0, keepdims=True)
        return grad.astype(jnp.bfloat16)

    hidden_made, (d_middle, middle_gain_grad, middle_shift_grad, d_branch) = exchange(
        HiddenFront(
            lifted,
            up_own,
            line(up_bias),
            cot_all,
            down_own,
            line(hidden_gain),
            line(hidden_shift),
            FF,
        ),
        [
            Stream(
                group_rows,
                None,
                up_own,
                True,
                (middle, cotangent[0], line(middle_gain)),
                (ROWS, ROWS, ALL),
                ((rows_wide, ROWS), (vector_out, ALL), (vector_out, ALL)),
                norm_back_step,
                True,
            ),
        ],
        [],
        8,
    )

    _, _, hidden_vectors, *hidden_grads, result_part = hidden_made
    result_rows = lax.psum_scatter(result_part, SEQ, scatter_dimension=0, tiled=True)
    back_made, (text_grad, input_gain_grad, input_shift_grad, d_rows), hidden_theirs = exchange(
        AttendBackFront(
            d_branch,
            out_own,
            inner_hat,
            inner_factor,
            line(inner_gain),
            (attended, query_rot, keys_rot, values, log_total),
            tables,
            segment,
            column,
            normed,
            inner_low,
            model_width,
        ),
        [
            Stream(
                group_rows,
                None,
                qkv_own,
                True,
                (mixed_in, d_middle, line(input_gain), target_rows),
                (ROWS, ROWS, ALL, ALL),
                ((rows_wide, ROWS), (vector_out, ALL), (vector_out, ALL)),
                norm_back_step,
                True,
            ),
        ],
        [CrossGrads(hidden_grads, (INWARD, OUTWARD))],
        10,
        PACE_BACK,
        1,
        WORK_FROM,
    )
    inner_vectors, *layer_grads = back_made
    row_vectors = (input_gain_grad, input_shift_grad, middle_gain_grad, middle_shift_grad)
    own_vectors = (
        (inner_vectors, 0),
        (inner_vectors, 1),
        (hidden_vectors, 2),
        (hidden_vectors, 0),
        (hidden_vectors, 1),
    )
    owned, (spread, resample_query_grad, latent_grad, result) = finale(
        list(zip(hidden_grads, hidden_theirs)),
        (INWARD, OUTWARD),
        layer_grads,
        (INWARD, OUTWARD),
        (d_rows, pictures, image_keys, probe, mixed_placed, image_out_own, target_rows),
        row_vectors,
        own_vectors,
        latents,
        resample_query,
        (result_rows, middle),
        12,
    )
    widths = (own_width, own_width, own_hidden, own_hidden, own_hidden)
    grads, passed, row_sums, own_sums = widened(
        owned,
        (1, 1, 3, 1, 1, 1, 1),
        (result, text_grad, resample_query_grad, latent_grad),
        spread,
        model_width,
        len(row_vectors),
        widths,
    )
    up_sum, down_sum, query_sum, key_sum, value_sum, out_sum, image_key_sum, image_value_sum, image_out_sum = grads
    result, text_grad, resample_query_grad, latent_grad = passed
    row_sums = [vector.reshape(-1) for vector in row_sums]
    inner_gain_sum, inner_shift_sum, up_bias_sum, hidden_gain_sum, hidden_shift_sum = (
        vector.reshape(-1) for vector in own_sums
    )

    return (
        result[None],
        text_grad[None],
        row_sums[0],
        row_sums[1],
        query_sum,
        key_sum,
        value_sum,
        inner_gain_sum,
        inner_shift_sum,
        out_sum,
        row_sums[2],
        row_sums[3],
        up_sum,
        up_bias_sum,
        hidden_gain_sum,
        hidden_shift_sum,
        down_sum,
        latent_grad,
        resample_query_grad,
        image_key_sum,
        image_value_sum,
        image_out_sum,
    )


def solution(mesh):
    placed = (
        P(IMG, SEQ, None),
        P(IMG, None),
        P(IMG, SEQ, None, None),
        P(IMG, None),
        P(IMG, None),
        P(IMG, SEQ, None),
        P(),
        P(),
        P((SEQ, IMG), TP),
        P((SEQ, IMG), TP),
        P((SEQ, IMG), TP),
        P(TP),
        P(TP),
        P(TP, (SEQ, IMG)),
        P(),
        P(),
        P((SEQ, IMG), TP),
        P(TP),
        P(TP),
        P(TP),
        P(TP, (SEQ, IMG)),
        P(None, (SEQ, IMG)),
        P((SEQ, IMG), TP),
        P((SEQ, IMG), TP),
        P((SEQ, IMG), TP),
        P(TP, (SEQ, IMG)),
    )
    return jax.shard_map(
        on_device if narrow_heads(mesh) else on_plane,
        mesh=mesh,
        in_specs=placed,
        out_specs=(
            P(IMG, SEQ, None),
            P(IMG, SEQ, None),
            P(),
            P(),
            P((SEQ, IMG), TP),
            P((SEQ, IMG), TP),
            P((SEQ, IMG), TP),
            P(TP),
            P(TP),
            P(TP, (SEQ, IMG)),
            P(),
            P(),
            P((SEQ, IMG), TP),
            P(TP),
            P(TP),
            P(TP),
            P(TP, (SEQ, IMG)),
            P(None, (SEQ, IMG)),
            P((SEQ, IMG), TP),
            P((SEQ, IMG), TP),
            P((SEQ, IMG), TP),
            P(TP, (SEQ, IMG)),
        ),
        check_vma=False,
    )
```

```python
import functools

import jax
import jax.numpy as jnp
from jax import lax
from jax.experimental import pallas as pl
from jax.experimental.pallas import tpu as pltpu
from jax.sharding import PartitionSpec as P

SEQ, TP, IMG = "seq", "tp", "img"
HEAD = 64
FF = 8192
PATCH = 256
LAT = 64
SEQ_MAX = 2048
IMG_DEV = 2


EPSILON = 1e-05
HIGHEST_PRECISION = lax.Precision.HIGHEST


def shortened(x):

    def short(part):
        return part.astype(jnp.bfloat16) if part.dtype == jnp.float32 else part

    return jax.tree.map(short, x)


def xpos_factors(position, half_size):
    ladder = jnp.arange(half_size, dtype=jnp.float32)
    frequency = jnp.exp(ladder * (-2.0 * jnp.log(10000.0) / (2.0 * half_size)))
    decay_base = (ladder / half_size + 0.4) / 1.4
    angles = position[:, None] * frequency[None, :]
    growth = jnp.exp(position[:, None] / 512.0 * jnp.log(decay_base)[None, :])
    return (jnp.cos(angles)[:, None, :], jnp.sin(angles)[:, None, :], growth[:, None, :])


def rotate(inputs, cosine, sine_table, factor):
    half_size = inputs.shape[-1] // 2
    first_half = inputs[..., :half_size]
    second_half = inputs[..., half_size:]
    turned = jnp.concatenate(
        [
            first_half * cosine - second_half * sine_table,
            first_half * sine_table + second_half * cosine,
        ],
        -1,
    )
    return turned * jnp.concatenate([factor, factor], -1)


def rotate_back(gradient, cosine, sine_table, factor):
    half_size = gradient.shape[-1] // 2
    scaled = gradient * jnp.concatenate([factor, factor], -1)
    first_half = scaled[..., :half_size]
    second_half = scaled[..., half_size:]
    return jnp.concatenate(
        [
            first_half * cosine + second_half * sine_table,
            second_half * cosine - first_half * sine_table,
        ],
        -1,
    )


def tp_total(inputs):
    return jax.tree.map(lambda part: part.astype(jnp.float32), lax.psum(shortened(inputs), TP))


def full_norm(inputs, norm_gain, norm_shift):
    center = inputs - jnp.mean(inputs, -1, keepdims=True)
    spread = jnp.mean(center * center, -1, keepdims=True)
    factor = lax.rsqrt(spread + EPSILON)
    normal = center * factor
    return (normal * norm_gain + norm_shift, normal, factor)


def full_back(gradient, normal, factor, norm_gain):
    scaled = gradient * norm_gain
    return factor * (
        scaled
        - jnp.mean(scaled, -1, keepdims=True)
        - normal * jnp.mean(scaled * normal, -1, keepdims=True)
    )


def split_norm(inputs, norm_gain, norm_shift, full_width):
    totals = tp_total(
        (jnp.sum(inputs, -1, keepdims=True), jnp.sum(inputs * inputs, -1, keepdims=True))
    )
    average = totals[0] / full_width
    spread = totals[1] / full_width - average * average
    factor = lax.rsqrt(spread + EPSILON)
    normal = (inputs - average) * factor
    return (normal * norm_gain + norm_shift, normal, factor)


def split_back(gradient, normal, factor, norm_gain, full_width):
    scaled = gradient * norm_gain
    totals = tp_total(
        (jnp.sum(scaled, -1, keepdims=True), jnp.sum(scaled * normal, -1, keepdims=True))
    )
    return factor * (scaled - totals[0] / full_width - normal * (totals[1] / full_width))


def attend_piece(
    running, query_rot, key_piece, value_piece, row_index, row_segment, segment_all, score_scale
):
    heads_local = query_rot.shape[1]
    amount = key_piece.shape[0]
    block_size = 1024

    def step(state_in, number):
        first_row = number * block_size
        key_block = lax.dynamic_slice_in_dim(key_piece, first_row, block_size, 0).reshape(
            block_size, heads_local, -1
        )
        value_block = lax.dynamic_slice_in_dim(value_piece, first_row, block_size, 0).reshape(
            block_size, heads_local, -1
        )
        key_index = first_row + jnp.arange(block_size, dtype=jnp.int32)
        key_segment = lax.dynamic_slice_in_dim(segment_all, first_row, block_size, 0)
        scores = (
            jnp.einsum("qhd,khd->hqk", query_rot, key_block, preferred_element_type=jnp.float32)
            * score_scale
        )
        allowed = (key_index[None, :] <= row_index[:, None]) & (
            key_segment[None, :] == row_segment[:, None]
        )
        scores = jnp.where(allowed[None], scores, -1e30)
        best_old, total_old, accum_old = state_in
        best_new = jnp.maximum(best_old, jnp.max(scores, -1))
        weights = jnp.where(allowed[None], jnp.exp(scores - best_new[..., None]), 0.0)
        shrink = jnp.exp(best_old - best_new)
        total_new = total_old * shrink + jnp.sum(weights, -1)
        added = jnp.einsum(
            "hqk,khd->qhd",
            weights.astype(jnp.bfloat16),
            value_block,
            preferred_element_type=jnp.float32,
        )
        accum_new = accum_old * shrink.T[:, :, None] + added
        return ((best_new, total_new, accum_new), None)

    return lax.scan(step, running, jnp.arange(amount // block_size, dtype=jnp.int32))[0]


def attend_back(
    query_rot,
    key_all,
    value_all,
    grad_attended,
    log_total,
    delta,
    row_index,
    row_segment,
    segment_all,
    score_scale,
):
    heads_local = query_rot.shape[1]
    amount = key_all.shape[0]
    block_size = 1024

    def step(dquery, number):
        first_row = number * block_size
        key_block = lax.dynamic_slice_in_dim(key_all, first_row, block_size, 0).reshape(
            block_size, heads_local, -1
        )
        value_block = lax.dynamic_slice_in_dim(value_all, first_row, block_size, 0).reshape(
            block_size, heads_local, -1
        )
        key_index = first_row + jnp.arange(block_size, dtype=jnp.int32)
        key_segment = lax.dynamic_slice_in_dim(segment_all, first_row, block_size, 0)
        scores = (
            jnp.einsum("qhd,khd->hqk", query_rot, key_block, preferred_element_type=jnp.float32)
            * score_scale
        )
        allowed = (key_index[None, :] <= row_index[:, None]) & (
            key_segment[None, :] == row_segment[:, None]
        )
        weights = jnp.where(
            allowed[None],
            jnp.exp(jnp.where(allowed[None], scores, -1e30) - log_total[..., None]),
            0.0,
        )
        dweights = jnp.einsum(
            "qhd,khd->hqk", grad_attended, value_block, preferred_element_type=jnp.float32
        )
        dscores = (weights * (dweights - delta[..., None])).astype(jnp.bfloat16)
        dquery = (
            dquery
            + jnp.einsum("hqk,khd->qhd", dscores, key_block, preferred_element_type=jnp.float32)
            * score_scale
        )
        dkeys = (
            jnp.einsum("hqk,qhd->khd", dscores, query_rot, preferred_element_type=jnp.float32)
            * score_scale
        )
        dvalues = jnp.einsum(
            "hqk,qhd->khd",
            weights.astype(jnp.bfloat16),
            grad_attended,
            preferred_element_type=jnp.float32,
        )
        return (dquery, (dkeys, dvalues))

    start_grad = jnp.zeros(query_rot.shape, jnp.float32)
    dquery, outputs = lax.scan(step, start_grad, jnp.arange(amount // block_size, dtype=jnp.int32))
    return (dquery, outputs[0].reshape(amount, -1), outputs[1].reshape(amount, -1))


def on_device(
    text,
    segment,
    features,
    image_count,
    image_slot,
    cotangent,
    input_gain,
    input_shift,
    query_weight,
    key_weight,
    value_weight,
    inner_gain,
    inner_shift,
    out_weight,
    middle_gain,
    middle_shift,
    up_weight,
    up_bias,
    hidden_gain,
    hidden_shift,
    down_weight,
    latents,
    resample_query,
    resample_key,
    resample_value,
    resample_out,
):
    row_count = text.shape[1]
    model_width = text.shape[2]
    group_rows = segment.shape[1]
    seq_rank = lax.axis_index(SEQ)
    gathered_in = (
        lax.all_gather(query_weight, (SEQ, IMG), axis=0, tiled=True),
        lax.all_gather(key_weight, (SEQ, IMG), axis=0, tiled=True),
        lax.all_gather(value_weight, (SEQ, IMG), axis=0, tiled=True),
        lax.all_gather(up_weight, (SEQ, IMG), axis=0, tiled=True),
        lax.all_gather(resample_query, (SEQ, IMG), axis=0, tiled=True),
        lax.all_gather(resample_key, (SEQ, IMG), axis=0, tiled=True),
        lax.all_gather(resample_value, (SEQ, IMG), axis=0, tiled=True),
    )
    query_full, key_full, value_full, up_full, probe_full, image_key_full, image_value_full = (
        gathered_in
    )
    gathered_out = (
        lax.all_gather(out_weight, (SEQ, IMG), axis=1, tiled=True),
        lax.all_gather(down_weight, (SEQ, IMG), axis=1, tiled=True),
        lax.all_gather(resample_out, (SEQ, IMG), axis=1, tiled=True),
        lax.all_gather(latents, (SEQ, IMG), axis=1, tiled=True),
    )
    out_full, down_full, image_out_full, latent_full = gathered_out
    half_width = query_full.shape[1]
    heads_local = half_width // HEAD
    score_scale = HEAD ** (-0.5)
    gelu_exact = functools.partial(jax.nn.gelu, approximate=False)
    image_slots = features.shape[1]
    pictures = features[0].reshape(image_slots * PATCH, features.shape[3])
    probe = (
        jnp.dot(latent_full, probe_full, preferred_element_type=jnp.float32)
        .astype(jnp.bfloat16)
        .reshape(LAT, heads_local, HEAD)
    )
    image_keys = (
        jnp.dot(pictures, image_key_full, preferred_element_type=jnp.float32)
        .astype(jnp.bfloat16)
        .reshape(image_slots, PATCH, heads_local, HEAD)
    )
    image_values = (
        jnp.dot(pictures, image_value_full, preferred_element_type=jnp.float32)
        .astype(jnp.bfloat16)
        .reshape(image_slots, PATCH, heads_local, HEAD)
    )
    image_scores = (
        jnp.einsum("qhd,iphd->ihqp", probe, image_keys, preferred_element_type=jnp.float32)
        * score_scale
    )
    image_probs = jax.nn.softmax(image_scores, -1)
    image_mixed = jnp.einsum(
        "ihqp,iphd->iqhd",
        image_probs.astype(jnp.bfloat16),
        image_values,
        preferred_element_type=jnp.float32,
    )
    image_mixed = image_mixed.astype(jnp.bfloat16).reshape(image_slots * LAT, half_width)
    embed = tp_total(jnp.dot(image_mixed, image_out_full, preferred_element_type=jnp.float32))
    embed = embed.astype(jnp.bfloat16).reshape(image_slots, LAT, model_width)
    image_total = image_slot.shape[1]
    slot_range = jnp.arange(image_total, dtype=jnp.int32)
    live = slot_range % IMG_DEV < jnp.repeat(image_count[0], IMG_DEV)
    block_local = row_count // LAT
    block_count = group_rows // LAT
    block_ids = seq_rank * block_local + jnp.arange(block_local, dtype=jnp.int32)
    owner = ((image_slot[0][None, :] == block_ids[:, None]) & live[None, :]).astype(jnp.float32)
    owner_low = owner.astype(jnp.bfloat16)
    taken = jnp.sum(owner, 1) > 0.5
    chosen = owner_low
    placed = jnp.einsum(
        "bi,ild->bld",
        chosen,
        lax.all_gather(embed, SEQ, axis=0, tiled=True),
        preferred_element_type=jnp.float32,
    )
    text_blocks = text[0].astype(jnp.float32).reshape(block_local, LAT, model_width)
    mixed_in = jnp.where(taken[:, None, None], placed, text_blocks).reshape(row_count, model_width)
    segment_all = segment[0]
    docs_count = 3 * (group_rows // min(SEQ_MAX, group_rows))
    marks = (segment_all[:, None] == jnp.arange(docs_count, dtype=jnp.int32)[None, :]).astype(
        jnp.int32
    )
    earlier_rows = jnp.cumsum(marks, 0) - marks
    position_all = jnp.sum(earlier_rows * marks, 1)
    first_local = seq_rank * row_count
    row_index = first_local + jnp.arange(row_count, dtype=jnp.int32)
    row_segment = lax.dynamic_slice_in_dim(segment_all, first_local, row_count, 0)
    position = lax.dynamic_slice_in_dim(position_all, first_local, row_count, 0).astype(jnp.float32)
    cosine, sine_table, growth = xpos_factors(position, HEAD // 2)
    input_out, input_hat, input_factor = full_norm(
        mixed_in, input_gain.astype(jnp.float32), input_shift.astype(jnp.float32)
    )
    normed = input_out.astype(jnp.bfloat16)
    query_lin = jnp.dot(normed, query_full, preferred_element_type=jnp.float32).reshape(
        row_count, heads_local, HEAD
    )
    key_lin = jnp.dot(normed, key_full, preferred_element_type=jnp.float32).reshape(
        row_count, heads_local, HEAD
    )
    value_lin = jnp.dot(normed, value_full, preferred_element_type=jnp.float32)
    query_rot = rotate(query_lin, cosine, sine_table, growth).astype(jnp.bfloat16)
    keys_rot = (
        rotate(key_lin, cosine, sine_table, 1.0 / growth)
        .astype(jnp.bfloat16)
        .reshape(row_count, half_width)
    )
    values_low = value_lin.astype(jnp.bfloat16)
    start_state = (
        jnp.full((heads_local, row_count), -1e30, jnp.float32),
        jnp.zeros((heads_local, row_count), jnp.float32),
        jnp.zeros((row_count, heads_local, HEAD), jnp.float32),
    )
    best, weight_total, accum = attend_piece(
        start_state,
        query_rot,
        lax.all_gather(keys_rot, SEQ, axis=0, tiled=True),
        lax.all_gather(values_low, SEQ, axis=0, tiled=True),
        row_index,
        row_segment,
        segment_all,
        score_scale,
    )
    attended = accum / weight_total.T[:, :, None]
    log_total = best + jnp.log(weight_total)
    inner_out, inner_hat, inner_factor = split_norm(
        attended.reshape(row_count, half_width),
        inner_gain.astype(jnp.float32),
        inner_shift.astype(jnp.float32),
        model_width,
    )
    inner_low = inner_out.astype(jnp.bfloat16)
    middle = mixed_in + tp_total(jnp.dot(inner_low, out_full, preferred_element_type=jnp.float32))
    lifted_out, lifted_hat, lifted_factor = full_norm(
        middle, middle_gain.astype(jnp.float32), middle_shift.astype(jnp.float32)
    )
    lifted = lifted_out.astype(jnp.bfloat16)
    hidden_pre = jnp.dot(lifted, up_full, preferred_element_type=jnp.float32) + up_bias.astype(
        jnp.float32
    )
    activated, gelu_pull = jax.vjp(gelu_exact, hidden_pre)
    settled_out, settled_hat, settled_factor = split_norm(
        activated, hidden_gain.astype(jnp.float32), hidden_shift.astype(jnp.float32), FF
    )
    settled = settled_out.astype(jnp.bfloat16)
    final_rows = middle + tp_total(jnp.dot(settled, down_full, preferred_element_type=jnp.float32))
    result = final_rows.astype(jnp.bfloat16).reshape(1, row_count, model_width)
    grad_low = cotangent[0]
    grad_rows = grad_low.astype(jnp.float32)
    down_grad = jnp.dot(settled.T, grad_low, preferred_element_type=jnp.float32)
    d_settled = jnp.dot(grad_low, down_full.T, preferred_element_type=jnp.float32)
    hidden_gain_grad = jnp.sum(d_settled * settled_hat, 0)
    hidden_shift_grad = jnp.sum(d_settled, 0)
    d_activated = split_back(
        d_settled, settled_hat, settled_factor, hidden_gain.astype(jnp.float32), FF
    )
    d_hidden = gelu_pull(d_activated)[0].astype(jnp.bfloat16)
    up_bias_grad = jnp.sum(d_hidden.astype(jnp.float32), 0)
    up_grad = jnp.dot(lifted.T, d_hidden, preferred_element_type=jnp.float32)
    d_lifted = tp_total(jnp.dot(d_hidden, up_full.T, preferred_element_type=jnp.float32))
    middle_gain_grad = jnp.sum(d_lifted * lifted_hat, 0)
    middle_shift_grad = jnp.sum(d_lifted, 0)
    d_middle = grad_rows + full_back(
        d_lifted, lifted_hat, lifted_factor, middle_gain.astype(jnp.float32)
    )
    d_branch = d_middle.astype(jnp.bfloat16)
    out_grad = jnp.dot(inner_low.T, d_branch, preferred_element_type=jnp.float32)
    d_inner = jnp.dot(d_branch, out_full.T, preferred_element_type=jnp.float32)
    inner_gain_grad = jnp.sum(d_inner * inner_hat, 0)
    inner_shift_grad = jnp.sum(d_inner, 0)
    d_attended = split_back(
        d_inner, inner_hat, inner_factor, inner_gain.astype(jnp.float32), model_width
    )
    d_attended = d_attended.astype(jnp.bfloat16).reshape(row_count, heads_local, HEAD)
    delta = jnp.sum(d_attended.astype(jnp.float32) * attended, -1).T
    key_back, value_back = (
        lax.all_gather(keys_rot, SEQ, axis=0, tiled=True),
        lax.all_gather(values_low, SEQ, axis=0, tiled=True),
    )
    d_query_rot, d_key_term, d_value_term = attend_back(
        query_rot,
        key_back,
        value_back,
        d_attended,
        log_total,
        delta,
        row_index,
        row_segment,
        segment_all,
        score_scale,
    )
    d_key_sum, d_value_sum = (
        lax.psum_scatter(
            d_key_term.astype(jnp.bfloat16), SEQ, scatter_dimension=0, tiled=True
        ).astype(jnp.float32),
        lax.psum_scatter(
            d_value_term.astype(jnp.bfloat16), SEQ, scatter_dimension=0, tiled=True
        ).astype(jnp.float32),
    )
    d_query_lin = (
        rotate_back(d_query_rot, cosine, sine_table, growth)
        .astype(jnp.bfloat16)
        .reshape(row_count, half_width)
    )
    d_key_lin = (
        rotate_back(
            d_key_sum.reshape(row_count, heads_local, HEAD), cosine, sine_table, 1.0 / growth
        )
        .astype(jnp.bfloat16)
        .reshape(row_count, half_width)
    )
    d_value_lin = d_value_sum.astype(jnp.bfloat16)
    query_grad = jnp.dot(normed.T, d_query_lin, preferred_element_type=jnp.float32)
    key_grad = jnp.dot(normed.T, d_key_lin, preferred_element_type=jnp.float32)
    value_grad = jnp.dot(normed.T, d_value_lin, preferred_element_type=jnp.float32)
    d_normed_part = (
        jnp.dot(d_query_lin, query_full.T, preferred_element_type=jnp.float32)
        + jnp.dot(d_key_lin, key_full.T, preferred_element_type=jnp.float32)
        + jnp.dot(d_value_lin, value_full.T, preferred_element_type=jnp.float32)
    )
    d_normed = tp_total(d_normed_part)
    input_gain_grad = jnp.sum(d_normed * input_hat, 0)
    input_shift_grad = jnp.sum(d_normed, 0)
    d_mixed = d_middle + full_back(
        d_normed, input_hat, input_factor, input_gain.astype(jnp.float32)
    )
    d_blocks = d_mixed.reshape(block_local, LAT, model_width)
    text_grad = jnp.where(taken[:, None, None], 0.0, d_blocks).reshape(1, row_count, model_width)
    my_target = lax.dynamic_slice_in_dim(image_slot[0], seq_rank * image_slots, image_slots, 0)
    my_live = lax.dynamic_slice_in_dim(live, seq_rank * image_slots, image_slots, 0)
    owner_mine = (
        (jnp.arange(block_count, dtype=jnp.int32)[:, None] == my_target[None, :]) & my_live[None, :]
    ).astype(jnp.bfloat16)
    chosen = owner_mine
    d_embed = jnp.einsum(
        "bi,bld->ild",
        chosen,
        lax.all_gather(d_blocks.astype(jnp.bfloat16), SEQ, axis=0, tiled=True),
        preferred_element_type=jnp.float32,
    )
    d_embed_low = d_embed.astype(jnp.bfloat16).reshape(image_slots * LAT, model_width)
    resample_out_grad = jnp.dot(image_mixed.T, d_embed_low, preferred_element_type=jnp.float32)
    d_image_mixed = jnp.dot(d_embed_low, image_out_full.T, preferred_element_type=jnp.float32)
    d_image_mixed = d_image_mixed.astype(jnp.bfloat16).reshape(image_slots, LAT, heads_local, HEAD)
    d_image_probs = jnp.einsum(
        "iqhd,iphd->ihqp", d_image_mixed, image_values, preferred_element_type=jnp.float32
    )
    d_image_scores = image_probs * (
        d_image_probs - jnp.sum(image_probs * d_image_probs, -1, keepdims=True)
    )
    d_image_scores = d_image_scores.astype(jnp.bfloat16)
    d_probe = (
        jnp.einsum("ihqp,iphd->qhd", d_image_scores, image_keys, preferred_element_type=jnp.float32)
        * score_scale
    )
    d_image_keys = (
        jnp.einsum("ihqp,qhd->iphd", d_image_scores, probe, preferred_element_type=jnp.float32)
        * score_scale
    ).astype(jnp.bfloat16)
    d_image_values = jnp.einsum(
        "ihqp,iqhd->iphd",
        image_probs.astype(jnp.bfloat16),
        d_image_mixed,
        preferred_element_type=jnp.float32,
    ).astype(jnp.bfloat16)
    resample_key_grad = jnp.dot(
        pictures.T,
        d_image_keys.reshape(image_slots * PATCH, half_width),
        preferred_element_type=jnp.float32,
    )
    resample_value_grad = jnp.dot(
        pictures.T,
        d_image_values.reshape(image_slots * PATCH, half_width),
        preferred_element_type=jnp.float32,
    )
    d_probe_flat = d_probe.reshape(LAT, half_width)
    resample_query_grad = jnp.dot(
        latent_full.astype(jnp.float32).T, d_probe_flat, precision=HIGHEST_PRECISION
    )
    latent_grad = tp_total(
        jnp.dot(d_probe_flat, probe_full.astype(jnp.float32).T, precision=HIGHEST_PRECISION)
    )
    summed_in = (
        lax.psum_scatter(query_grad, (SEQ, IMG), scatter_dimension=0, tiled=True),
        lax.psum_scatter(key_grad, (SEQ, IMG), scatter_dimension=0, tiled=True),
        lax.psum_scatter(value_grad, (SEQ, IMG), scatter_dimension=0, tiled=True),
        lax.psum_scatter(up_grad, (SEQ, IMG), scatter_dimension=0, tiled=True),
        lax.psum_scatter(resample_query_grad, (SEQ, IMG), scatter_dimension=0, tiled=True),
        lax.psum_scatter(resample_key_grad, (SEQ, IMG), scatter_dimension=0, tiled=True),
        lax.psum_scatter(resample_value_grad, (SEQ, IMG), scatter_dimension=0, tiled=True),
    )
    summed_out = (
        lax.psum_scatter(out_grad, (SEQ, IMG), scatter_dimension=1, tiled=True),
        lax.psum_scatter(down_grad, (SEQ, IMG), scatter_dimension=1, tiled=True),
        lax.psum_scatter(resample_out_grad, (SEQ, IMG), scatter_dimension=1, tiled=True),
        lax.psum_scatter(latent_grad, (SEQ, IMG), scatter_dimension=1, tiled=True),
    )
    summed_small = lax.psum(
        (
            input_gain_grad,
            input_shift_grad,
            inner_gain_grad,
            inner_shift_grad,
            middle_gain_grad,
            middle_shift_grad,
            up_bias_grad,
            hidden_gain_grad,
            hidden_shift_grad,
        ),
        (SEQ, IMG),
    )
    return (
        result,
        text_grad,
        summed_small[0],
        summed_small[1],
        summed_in[0],
        summed_in[1],
        summed_in[2],
        summed_small[2],
        summed_small[3],
        summed_out[0],
        summed_small[4],
        summed_small[5],
        summed_in[3],
        summed_small[6],
        summed_small[7],
        summed_small[8],
        summed_out[1],
        summed_out[3],
        summed_in[4],
        summed_in[5],
        summed_in[6],
        summed_out[2],
    )


MESH_IDS = pl.DeviceIdType.MESH
ANYWHERE = pl.BlockSpec(memory_space=pl.ANY)
ON_CHIP = pl.BlockSpec(memory_space=pltpu.VMEM)
IN_SMEM = pl.BlockSpec(memory_space=pltpu.SMEM)
LANES = 128
PLANE = 8
VMEM_BYTES = 60 * 1024 * 1024
PIECE_ROWS = (32, 32, 32, 32)
PIECES = len(PIECE_ROWS)
SECOND_LAG = 2
PACE_IMAGE = (0, 7, 7, 7, 7)
PACE_ATTEND = (0, 2, 2, 0)
WORK_FROM = 0
PACE_BACK = (1, 0, 0, 0, 2, 2, 2, 2)
FRONT, BACK, ALL, ROWS, INWARD, OUTWARD, SHARED = range(7)


def narrow_heads(mesh):
    return mesh.shape[SEQ] != PLANE or mesh.shape[IMG] != 2 or mesh.shape[TP] != 2


def flipped(number, bit):
    step = 2**bit
    return number + step - 2 * step * ((number // step) % 2)


class Places:
    def __init__(self):
        self.seq, self.tp, self.img = (lax.axis_index(name) for name in (SEQ, TP, IMG))
        self.s_core, self.s_x, self.s_y = (flipped(self.seq, bit) for bit in range(3))
        self.s_xy = flipped(self.s_x, 2)
        self.core, self.x, self.y = (self.at(seq) for seq in (self.s_core, self.s_x, self.s_y))
        self.tp_peer = (self.seq, 1 - self.tp, self.img)
        self.img_peer = (self.seq, self.tp, 1 - self.img)

    def at(self, seq):
        return (seq, self.tp, self.img)


def greet(peers):
    barrier = pltpu.get_barrier_semaphore()
    for peer in peers:
        pl.semaphore_signal(barrier, inc=1, device_id=peer, device_id_type=MESH_IDS)
    pl.semaphore_wait(barrier, len(peers))


def remote(src, dst, send, recv, peer):
    return pltpu.make_async_remote_copy(
        src_ref=src, dst_ref=dst, send_sem=send, recv_sem=recv, device_id=peer, device_id_type=MESH_IDS
    )


def rows_at(ref, first, count):
    return ref.at[pl.ds(pl.multiple_of(first, 16), count)]


class Spread:
    def __init__(self, here, out, block, first, count, send, recv):
        self.here, self.out, self.block = here, out, block
        self.first, self.count, self.send, self.recv = first, count, send, recv
        self.half = out.shape[1] // 2
        self.sent = []

    def cut(self, ref, first, which):
        rows = pl.ds(first, self.count)
        if which == ALL:
            return ref.at[rows]
        return ref.at[rows, pl.ds(self.half if which == BACK else 0, self.half)]

    def part(self, seq, which):
        return self.cut(self.out, pl.multiple_of(seq * self.block + self.first, 16), which)

    def copy(self, src, dst, slot, peer):
        return remote(src, dst, self.send.at[slot], self.recv.at[slot], peer)

    def go(self, src, dst, slot, peer):
        made = self.copy(src, dst, slot, peer)
        made.start()
        self.sent.append(made)

    def own(self, src, src_first):
        here, seq = self.here, self.here.seq

        def own_part(which):
            return self.cut(src, src_first, which)

        self.go(own_part(FRONT), self.part(seq, FRONT), 0, here.x)
        self.go(own_part(BACK), self.part(seq, BACK), 1, here.y)
        self.go(own_part(BACK), self.part(seq, BACK), 2, here.x)
        self.go(own_part(FRONT), self.part(seq, FRONT), 3, here.y)
        self.go(own_part(ALL), self.part(seq, ALL), 4, here.core)

    def arrived(self, slot, seq, which):
        target = self.part(seq, which)
        self.copy(target, target, slot, self.here.core).wait_recv()

    def forward(self):
        here = self.here
        self.arrived(0, here.s_x, FRONT)
        self.go(self.part(here.s_x, FRONT), self.part(here.s_x, FRONT), 5, here.y)
        self.arrived(1, here.s_y, BACK)
        self.go(self.part(here.s_y, BACK), self.part(here.s_y, BACK), 6, here.x)
        self.arrived(2, here.s_x, BACK)
        self.go(self.part(here.s_x, ALL), self.part(here.s_x, ALL), 7, here.core)
        self.arrived(3, here.s_y, FRONT)
        self.go(self.part(here.s_y, ALL), self.part(here.s_y, ALL), 8, here.core)

    def corner(self):
        here = self.here
        self.arrived(5, here.s_xy, FRONT)
        self.arrived(6, here.s_xy, BACK)
        self.go(self.part(here.s_xy, ALL), self.part(here.s_xy, ALL), 9, here.core)

    def finish(self):
        core = self.here.s_core
        self.arrived(4, core, ALL)
        self.arrived(7, flipped(core, 1), ALL)
        self.arrived(8, flipped(core, 2), ALL)
        self.arrived(9, flipped(flipped(core, 1), 2), ALL)
        for made in self.sent:
            made.wait_send()


def ticks_of(stages, count):
    def tick_of(tick):
        def run():
            for lag, stage in reversed(stages):
                if 0 <= tick - lag < count:
                    stage(tick - lag)

        return run

    return [tick_of(tick) for tick in range(count + max(lag for lag, _ in stages))]


def take_some(waiting, count):
    for launch in waiting[:count]:
        launch()
    del waiting[:count]


def weight_blocks(weight, side):
    if side == SHARED:
        return weight.shape
    if side == INWARD:
        return (weight.shape[0], weight.shape[1] // PLANE)
    return (weight.shape[0] // PLANE, weight.shape[1])


def intake(gathered, weights, sides, cid):
    n_rows, n_weights = len(gathered), len(weights)
    pieces = PIECES

    def kernel(*refs):
        row_refs, weight_refs = refs[:n_rows], refs[n_rows : n_rows + n_weights]
        refs = refs[n_rows + n_weights :]
        row_outs, weight_outs = refs[:n_rows], refs[n_rows : n_rows + n_weights]
        refs = refs[n_rows + n_weights :]
        held, (local, send, recv, w_local, w_send, w_recv, z_send, z_recv) = refs[:n_rows], refs[n_rows:]
        here = Places()
        seq, tp, img = here.seq, here.tp, here.img
        others = [lax.rem(seq + step, PLANE) for step in range(1, PLANE)]
        greet([(other, tp, img) for other in others] + [here.img_peer])

        def slot_of(out, side, shape, from_seq, from_img):
            number = from_seq * 2 + from_img
            if side == INWARD:
                return out.at[pl.ds(pl.multiple_of(number * shape[0], shape[0]), shape[0])]
            return out.at[:, pl.ds(pl.multiple_of(number * shape[1], shape[1]), shape[1])]

        def block_of(weight, side, shape, to_seq):
            if side == SHARED:
                return weight
            if side == INWARD:
                return weight.at[:, pl.ds(pl.multiple_of(to_seq * shape[1], shape[1]), shape[1])]
            return weight.at[pl.ds(pl.multiple_of(to_seq * shape[0], shape[0]), shape[0])]

        flights, own_copies = [], []

        def begin(index):
            weight, out, side = weight_refs[index], weight_outs[index], sides[index]
            shape = weight_blocks(weight, side)
            mine = pltpu.make_async_copy(
                block_of(weight, side, shape, seq), slot_of(out, side, shape, seq, img), w_local.at[index]
            )
            mine.start()
            crossing = remote(
                block_of(weight, side, shape, seq),
                slot_of(out, side, shape, seq, img),
                z_send.at[index, 0],
                z_recv.at[index, 0],
                here.img_peer,
            )
            crossing.start()
            own_copies.append(mine)
            flights.append(crossing)
            for step, other in enumerate(others, 1):
                made = remote(
                    block_of(weight, side, shape, other),
                    slot_of(out, side, shape, seq, img),
                    w_send.at[index, step],
                    w_recv.at[index, step],
                    here.at(other),
                )
                made.start()
                flights.append(made)

        spreads, loads, stores = [], [], []
        for number, (rows, out) in enumerate(zip(row_refs, row_outs)):
            block = rows.shape[0]
            count = block // pieces
            loads.append(pltpu.make_async_copy(rows, held[number], local.at[number, 0]))
            loads[-1].start()
            stores.append(pltpu.make_async_copy(held[number], rows_at(out, seq * block, block), local.at[number, 1]))
            for piece in range(pieces):
                at = number * pieces + piece
                spreads.append(
                    (Spread(here, out, block, piece * count, count, send.at[at], recv.at[at]), rows, piece * count)
                )

        def cross(piece):
            for index in range(piece, n_weights, len(spreads)):
                weight, out, side = weight_refs[index], weight_outs[index], sides[index]
                shape = weight_blocks(weight, side)
                for step in range(1, PLANE):
                    source = lax.rem(seq + PLANE - step, PLANE)
                    landed = slot_of(out, side, shape, source, img)
                    remote(landed, landed, w_send.at[index, step], w_recv.at[index, step], here.core).wait_recv()
                    crossing = remote(
                        landed, landed, z_send.at[index, step], z_recv.at[index, step], here.img_peer
                    )
                    crossing.start()
                    flights.append(crossing)

        def own_rows(piece):
            if piece == 1:
                for load, store in zip(loads, stores):
                    load.wait()
                    store.start()
            for index in range(piece, n_weights, len(spreads)):
                begin(index)
            spreads[piece][0].own(spreads[piece][1], spreads[piece][2])

        for tick in ticks_of(
            [
                (0, own_rows),
                (2, lambda piece: spreads[piece][0].forward()),
                (3, lambda piece: cross(piece)),
                (4, lambda piece: spreads[piece][0].corner()),
            ],
            len(spreads),
        ):
            tick()
        for index, (weight, out, side) in enumerate(zip(weight_refs, weight_outs, sides)):
            shape = weight_blocks(weight, side)
            for step in range(PLANE):
                source = lax.rem(seq + PLANE - step, PLANE)
                landed = slot_of(out, side, shape, source, 1 - img)
                remote(landed, landed, z_send.at[index, step], z_recv.at[index, step], here.core).wait_recv()
        for spread, _, _ in spreads:
            spread.finish()
        for made in flights:
            made.wait_send()
        for made in own_copies + stores:
            made.wait()

    def whole(weight, side):
        shape = weight_blocks(weight, side)
        if side == INWARD:
            return jax.ShapeDtypeStruct((2 * PLANE * shape[0], shape[1]), weight.dtype)
        return jax.ShapeDtypeStruct((shape[0], 2 * PLANE * shape[1]), weight.dtype)

    dma = pltpu.SemaphoreType.DMA
    outs = [jax.ShapeDtypeStruct((PLANE * rows.shape[0], rows.shape[1]), rows.dtype) for rows in gathered]
    outs += [whole(weight, side) for weight, side in zip(weights, sides)]
    made = pl.pallas_call(
        kernel,
        out_shape=tuple(outs),
        in_specs=[ANYWHERE] * (n_rows + n_weights),
        out_specs=tuple([ANYWHERE] * len(outs)),
        scratch_shapes=[pltpu.VMEM(rows.shape, rows.dtype) for rows in gathered]
        + [
            dma((n_rows, 2)),
            dma((n_rows * pieces, 10)),
            dma((n_rows * pieces, 10)),
            dma((n_weights,)),
            dma((n_weights, PLANE)),
            dma((n_weights, PLANE)),
            dma((n_weights, PLANE)),
            dma((n_weights, PLANE)),
        ],
        compiler_params=pltpu.CompilerParams(
            collective_id=cid, has_side_effects=True, vmem_limit_bytes=VMEM_BYTES
        ),
    )(*gathered, *weights)
    return made[:n_rows], made[n_rows:]


LAZY_BYTES = 256 * 1024


class Lazy:
    def __init__(self, src, dst, sem):
        self.copy = pltpu.make_async_copy(src, dst, sem)
        self.copy.start()
        self.dst, self.shape, self.pending = dst, dst.shape, True

    def ready(self):
        if self.pending:
            self.copy.wait()
            self.pending = False
        return self.dst

    @property
    def at(self):
        return self.ready().at

    def __getitem__(self, where):
        return self.ready()[where]


def is_lazy(value, spec):
    return spec is ON_CHIP and value.size * value.dtype.itemsize >= LAZY_BYTES


class Rider:
    inputs, out_shapes, scratch, in_specs = (), (), (), ()

    def bind(self, here, ins, outs, scratch):
        self.here, self.ins, self.outs, self.held = here, ins, outs, scratch
        self.sent, self.kept, self.due, self.launches, self.later = [], [], [], [], []

    def keep(self, src, dst, sem):
        made = pltpu.make_async_copy(src, dst, sem)
        self.launches.append(made.start)
        self.kept.append(made)

    def send(self, src, dst, send, recv, peer):
        made = remote(src, dst, send, recv, peer)
        self.launches.append(made.start)
        self.sent.append(made)

    def finish(self):
        for dst, send, recv in self.due:
            remote(dst, dst, send, recv, self.here.core).wait_recv()
        for made in self.sent:
            made.wait_send()
        for made in self.kept:
            made.wait()


class ChainWeights(Rider):
    def __init__(self, weights, sides, places):
        self.inputs, self.sides, self.places = weights, sides, places
        self.blocks = [weight_blocks(weight, side) for weight, side in zip(weights, sides)]
        shapes = {}
        for (rows, columns), side, (out, first) in zip(self.blocks, sides, places):
            if side == INWARD:
                shapes[out] = (2 * PLANE * rows, first + columns)
            else:
                shapes[out] = (rows, 2 * PLANE * columns)
        self.out_shapes = [jax.ShapeDtypeStruct(shapes[out], weights[0].dtype) for out in range(len(shapes))]
        dma, count = pltpu.SemaphoreType.DMA, len(weights)
        self.scratch = [dma((count, PLANE))] * 4 + [dma((count,))]

    def peers(self, here):
        return [here.at(lax.rem(here.seq + step, PLANE)) for step in range(1, PLANE)]

    def slot(self, index, seq, img):
        out, first = self.places[index]
        (rows, columns), number = self.blocks[index], seq * 2 + img
        if self.sides[index] == INWARD:
            return self.outs[out].at[pl.ds(pl.multiple_of(number * rows, rows), rows), pl.ds(first, columns)]
        return self.outs[out].at[:, pl.ds(pl.multiple_of(number * columns, columns), columns)]

    def start(self):
        here, (send, recv, z_send, z_recv, local) = self.here, self.held
        self.later = []
        for index, (weight, side, (rows, columns)) in enumerate(zip(self.ins, self.sides, self.blocks)):
            for step in range(PLANE):
                target = lax.rem(here.seq + step, PLANE)
                source = lax.rem(here.seq + PLANE - step, PLANE)
                if side == INWARD:
                    part = weight.at[:, pl.ds(pl.multiple_of(target * columns, columns), columns)]
                else:
                    part = weight.at[pl.ds(pl.multiple_of(target * rows, rows), rows)]
                mine = self.slot(index, here.seq, here.img)
                if step == 0:
                    self.keep(part, mine, local.at[index])
                    cross = remote(part, mine, z_send.at[index, 0], z_recv.at[index, 0], here.img_peer)
                    self.launches.append(cross.start)
                    self.sent.append(cross)
                else:
                    self.send(part, mine, send.at[index, step], recv.at[index, step], here.at(target))
                    self.later.append(functools.partial(self.cross, index, step, source))
                there = self.slot(index, source, 1 - here.img)
                self.due.append((there, z_send.at[index, step], z_recv.at[index, step]))

    def cross(self, index, step, source):
        here, (send, recv, z_send, z_recv, _) = self.here, self.held
        landed = self.slot(index, source, here.img)
        remote(landed, landed, send.at[index, step], recv.at[index, step], here.core).wait_recv()
        made = remote(landed, landed, z_send.at[index, step], z_recv.at[index, step], here.img_peer)
        made.start()
        self.sent.append(made)


class GatherRows(Rider):
    def __init__(self, rows):
        self.inputs = [rows]
        self.out_shapes = [jax.ShapeDtypeStruct((PLANE * rows.shape[0], rows.shape[1]), rows.dtype)]
        dma = pltpu.SemaphoreType.DMA
        self.scratch = [dma((PIECES, 10)), dma((PIECES, 10)), dma((1,))]

    def start(self):
        (rows,), (out,), (send, recv, local) = self.ins, self.outs, self.held
        block = rows.shape[0]
        self.spreads = []
        for piece, count in enumerate(PIECE_ROWS):
            first = sum(PIECE_ROWS[:piece])
            self.spreads.append(Spread(self.here, out, block, first, count, send.at[piece], recv.at[piece]))
            self.launches.append(functools.partial(self.spreads[piece].own, rows, first))
        self.keep(rows, rows_at(out, self.here.seq * block, block), local.at[0])
        self.later = [spread.forward for spread in self.spreads] + [spread.corner for spread in self.spreads]

    def finish(self):
        for spread in self.spreads:
            spread.finish()
        super().finish()


class CrossGrads(Rider):
    def __init__(self, grads, sides):
        self.inputs, self.sides = grads, sides
        self.out_shapes = []
        for grad, side in zip(grads, sides):
            if side == INWARD:
                shape = (grad.shape[0], grad.shape[2], grad.shape[3])
            else:
                shape = (PLANE, grad.shape[0], grad.shape[1] // (2 * PLANE))
            self.out_shapes.append(jax.ShapeDtypeStruct(shape, grad.dtype))
        dma = pltpu.SemaphoreType.DMA
        self.scratch = [dma((len(grads), PLANE)), dma((len(grads), PLANE))]

    def peers(self, here):
        return [here.img_peer]

    def start(self):
        here, (send, recv) = self.here, self.held
        for index, (grad, out, side) in enumerate(zip(self.ins, self.outs, self.sides)):
            width = out.shape[2]
            for seq in range(PLANE):
                if side == INWARD:
                    part = grad.at[seq, 1 - here.img]
                else:
                    part = grad.at[:, pl.ds(pl.multiple_of((seq * 2 + 1 - here.img) * width, width), width)]
                self.send(part, out.at[seq], send.at[index, seq], recv.at[index, seq], here.img_peer)
                self.due.append((out.at[seq], send.at[index, seq], recv.at[index, seq]))


class Stream:
    in_specs = ()

    def __init__(self, rows_all, left, right, across, row_inputs, row_kinds, row_outs, row_function, gather):
        self.own_left = left is not None
        self.inputs = ([left] if self.own_left else []) + [right] + list(row_inputs)
        self.across, self.row_kinds, self.row_outs = across, row_kinds, row_outs
        self.row_function, self.gather = row_function, gather
        width = right.shape[0] if across else right.shape[1]
        self.width, self.block, self.pieces = width, rows_all // PLANE, PIECES
        self.half = width // 2
        low_type = jnp.bfloat16
        self.out_shapes = [shape for shape, _ in row_outs]
        if gather:
            self.out_shapes.append(jax.ShapeDtypeStruct((rows_all, width), low_type))
        dma = pltpu.SemaphoreType.DMA
        block, pieces, half = self.block, self.pieces, self.half
        self.scratch = [
            pltpu.VMEM((4, block, width), low_type),
            pltpu.VMEM((4, block, width), low_type),
            pltpu.VMEM((4, block, width), jnp.float32),
            pltpu.VMEM((block, half), low_type),
            pltpu.VMEM((block, half), low_type),
            pltpu.VMEM((block, width), low_type),
            pltpu.VMEM((block, width), low_type),
            pltpu.VMEM((block, width), low_type),
            pltpu.VMEM((block, width), low_type),
            pltpu.VMEM((block, width), low_type),
            dma((4,)),
            dma((4,)),
            dma((pieces, 7)),
            dma((pieces, 7)),
            dma((pieces, 10)),
            dma((pieces, 10)),
            dma((pieces,)),
        ]

    def out_specs(self):
        return [ON_CHIP] * len(self.row_outs) + [ANYWHERE] * (len(self.out_shapes) - len(self.row_outs))

    def peers(self, here):
        return [here.core, here.x, here.y, here.tp_peer]

    def bind(self, here, ins, outs, scratch):
        self.here = here
        if self.own_left:
            self.left, ins = ins[0], ins[1:]
        self.right, self.ins = ins[0], ins[1:]
        self.outs = outs
        (self.away, self.core_in, self.near, self.from_xd, self.from_yd, self.from_x, self.from_y) = scratch[:7]
        (self.mine, self.theirs, self.low, self.c_send, self.c_recv) = scratch[7:12]
        (self.send, self.recv, self.g_send, self.g_recv, self.l_sem) = scratch[12:]
        self.sent, self.spreads, self.core_copies = [], [], {}

    def chunk(self, base, kind):
        if kind in (1, 3):
            base = flipped(base, 1)
        if kind in (2, 3):
            base = flipped(base, 2)
        return base

    def product(self, seq, target, low_type):
        first = pl.multiple_of(seq * self.block, self.block)
        rows = self.left[pl.ds(first, self.block), :]
        step = min(512, self.width)
        for column in range(0, self.width, step):
            if self.across:
                part = lax.dot_general(
                    rows,
                    self.right[column : column + step, :],
                    (((1,), (1,)), ((), ())),
                    preferred_element_type=jnp.float32,
                )
            else:
                part = jnp.dot(
                    rows, self.right[:, column : column + step], preferred_element_type=jnp.float32
                )
            target[:, column : column + step] = part.astype(low_type)

    def begin(self):
        here = self.here
        for kind in (3, 1, 2, 0):
            self.product(self.chunk(here.s_core, kind), self.away.at[kind], jnp.bfloat16)
            made = remote(
                self.away.at[kind], self.core_in.at[kind], self.c_send.at[kind], self.c_recv.at[kind], here.core
            )
            made.start()
            self.core_copies[kind] = made
            self.product(self.chunk(here.seq, kind), self.near.at[kind], jnp.float32)

    def go(self, src, dst, piece, slot, peer):
        made = remote(src, dst, self.send.at[piece, slot], self.recv.at[piece, slot], peer)
        made.start()
        self.sent.append(made)

    def landed(self, dst, piece, slot):
        remote(dst, dst, self.send.at[piece, slot], self.recv.at[piece, slot], self.here.core).wait_recv()

    def rows_of(self, piece):
        return pl.ds(sum(PIECE_ROWS[:piece]), PIECE_ROWS[piece])

    def columns_of(self, which):
        return pl.ds(self.half if which == BACK else 0, self.half)

    def held(self, kind, piece, which=ALL):
        if which == ALL:
            return self.core_in.at[kind, self.rows_of(piece)]
        return self.core_in.at[kind, self.rows_of(piece), self.columns_of(which)]

    def halved(self, ref, piece, which):
        return ref.at[self.rows_of(piece), self.columns_of(which)]

    def folded(self, kind, piece):
        if piece == 0:
            self.core_copies[kind].wait_recv()
        near = self.near[kind, self.rows_of(piece), :]
        return self.held(kind, piece)[...].astype(jnp.float32) + near

    def first_sends(self, piece):
        here = self.here
        self.held(3, piece)[...] = self.folded(3, piece).astype(jnp.bfloat16)
        self.go(self.held(3, piece, FRONT), self.from_xd.at[self.rows_of(piece)], piece, 0, here.x)
        self.go(self.held(3, piece, BACK), self.from_yd.at[self.rows_of(piece)], piece, 1, here.y)
        self.held(1, piece)[...] = self.folded(1, piece).astype(jnp.bfloat16)
        self.go(self.held(1, piece, FRONT), self.halved(self.from_x, piece, FRONT), piece, 2, here.x)
        self.held(2, piece)[...] = self.folded(2, piece).astype(jnp.bfloat16)
        self.go(self.held(2, piece, BACK), self.halved(self.from_y, piece, BACK), piece, 3, here.y)

    def second_sends(self, piece):
        here = self.here
        self.landed(self.from_xd.at[self.rows_of(piece)], piece, 0)
        at = self.held(2, piece, FRONT)
        at[...] = (at[...].astype(jnp.float32) + self.from_xd[self.rows_of(piece), :].astype(jnp.float32)).astype(jnp.bfloat16)
        self.go(at, self.halved(self.from_y, piece, FRONT), piece, 4, here.y)
        self.landed(self.from_yd.at[self.rows_of(piece)], piece, 1)
        at = self.held(1, piece, BACK)
        at[...] = (at[...].astype(jnp.float32) + self.from_yd[self.rows_of(piece), :].astype(jnp.float32)).astype(jnp.bfloat16)
        self.go(at, self.halved(self.from_x, piece, BACK), piece, 5, here.x)

    def plane_sum(self, piece):
        self.landed(self.halved(self.from_x, piece, FRONT), piece, 2)
        self.landed(self.halved(self.from_y, piece, BACK), piece, 3)
        self.landed(self.halved(self.from_y, piece, FRONT), piece, 4)
        self.landed(self.halved(self.from_x, piece, BACK), piece, 5)
        total = self.folded(0, piece)
        total = total + self.from_x[self.rows_of(piece), :].astype(jnp.float32) + self.from_y[self.rows_of(piece), :].astype(jnp.float32)
        self.mine[self.rows_of(piece), :] = total.astype(jnp.bfloat16)
        self.go(self.mine.at[self.rows_of(piece)], self.theirs.at[self.rows_of(piece)], piece, 6, self.here.tp_peer)

    def rows_done(self, piece):
        here = self.here
        self.landed(self.theirs.at[self.rows_of(piece)], piece, 6)
        total = self.mine[self.rows_of(piece), :].astype(jnp.float32) + self.theirs[self.rows_of(piece), :].astype(jnp.float32)
        rows = self.rows_of(piece)
        views = [ref.at[rows] if kind == ROWS else ref for ref, kind in zip(self.ins, self.row_kinds)]
        out_views = [ref.at[rows] if kind == ROWS else ref for ref, (_, kind) in zip(self.outs, self.row_outs)]
        given = self.row_function(total, piece, views, out_views)
        if self.gather:
            out = self.outs[-1]
            self.low[rows, :] = given
            first = pl.multiple_of(here.seq * self.block + rows.start, 16)
            keep = pltpu.make_async_copy(self.low.at[rows], out.at[pl.ds(first, rows.size)], self.l_sem.at[piece])
            keep.start()
            spread = Spread(
                here, out, self.block, rows.start, rows.size, self.g_send.at[piece], self.g_recv.at[piece]
            )
            spread.own(self.low, rows.start)
            self.spreads.append((spread, keep))

    def stages(self):
        stages = [(0, self.first_sends), (1, self.second_sends), (2, self.plane_sum), (4, self.rows_done)]
        if self.gather:
            stages.append((5, lambda piece: self.spreads[piece][0].forward()))
            stages.append((6, lambda piece: self.spreads[piece][0].corner()))
        return stages

    def phases(self):
        def phase_of(stage):
            def run():
                for piece in range(PIECES):
                    stage(piece)

            return run

        return [phase_of(stage) for _, stage in self.stages()]

    def finish(self):
        for spread, keep in self.spreads:
            spread.finish()
            keep.wait()
        for made in self.sent:
            made.wait_send()
        for made in self.core_copies.values():
            made.wait_send()


def full_line(rows):
    held = rows[...].astype(jnp.float32)
    return jnp.concatenate([held[number : number + 1, :] for number in range(held.shape[0])], 1)


def own_line(here, rows, width):
    held = rows[...].astype(jnp.float32)
    count = width // LANES
    number = lax.broadcasted_iota(jnp.int32, held.shape, 0)
    parts = [
        jnp.sum(jnp.where(number == here.seq * count + part, held, 0.0), 0, keepdims=True) for part in range(count)
    ]
    return jnp.concatenate(parts, 1)


class Front(Rider):
    def total_scratch(self, count, rows):
        dma = pltpu.SemaphoreType.DMA
        return [
            pltpu.VMEM((PLANE - 1, count, rows), jnp.float32),
            pltpu.VMEM((count, rows), jnp.float32),
            pltpu.VMEM((count, rows), jnp.float32),
            pltpu.VMEM((count, rows), jnp.float32),
            dma((PLANE,)),
            dma((PLANE,)),
        ]

    def peers(self, here):
        return [here.at(lax.rem(here.seq + step, PLANE)) for step in range(1, PLANE)]

    def small_sum(self, scratch):
        here, (plane, own, mine, theirs, send, recv) = self.here, scratch
        made = []
        for step, peer in enumerate(self.peers(here)):
            copy = remote(own, plane.at[step], send.at[step], recv.at[step], peer)
            copy.start()
            made.append(copy)
        total = own[...]
        for step, copy in enumerate(made):
            copy.wait_recv()
            total = total + plane[step]
        mine[...] = total
        last = remote(mine, theirs, send.at[PLANE - 1], recv.at[PLANE - 1], here.tp_peer)
        last.start()
        last.wait()
        for copy in made:
            copy.wait_send()
        total = mine[...] + theirs[...]
        count, rows = total.shape
        return jnp.concatenate([total, jnp.zeros((8 - count, rows), jnp.float32)], 0).T


def chosen_rows(target_rows, first, count):
    row = first + lax.broadcasted_iota(jnp.int32, (count, target_rows.shape[1]), 0)
    return (row == target_rows[...]).astype(jnp.float32).astype(jnp.bfloat16)


class ImageFront(Rider):
    def __init__(self, pictures, key_part, value_part, latent_all, probe_part, target_rows, segment):
        self.inputs = [pictures, key_part, value_part, latent_all, probe_part, target_rows, segment]
        rows, width = pictures.shape[0], key_part.shape[1]
        images = rows // PATCH
        low_type = jnp.bfloat16
        self.out_shapes = [
            jax.ShapeDtypeStruct((rows, 2 * width), low_type),
            jax.ShapeDtypeStruct((images * LAT, width), low_type),
            jax.ShapeDtypeStruct((LAT, width), low_type),
        ]
        self.out_shapes += [jax.ShapeDtypeStruct((segment.shape[1], width), jnp.float32)] * 3
        self.out_shapes.append(jax.ShapeDtypeStruct((segment.shape[1], 8), jnp.float32))
        self.scratch = [
            pltpu.VMEM((key_part.shape[0], 2 * width), low_type),
            pltpu.VMEM((images * LAT, width), low_type),
        ]

    def run(self):
        pictures, key_w, value_w, latent_all, probe_w, target_rows, segment = self.ins
        keys, placed, probe, *tables, column = self.outs
        row = segment[...].astype(jnp.float32)
        column[...] = jnp.broadcast_to(row, (8, row.shape[1])).T
        for first in range(0, segment.shape[1], ATTEND_ROWS):
            self.launches.append(functools.partial(xpos_part, segment, column, tables, first))
        both_w, mixed_all = self.held
        width, scale = probe.shape[1], HEAD ** (-0.5)
        both_w[:, :width] = key_w[...]
        both_w[:, width:] = value_w[...]
        probe[...] = jnp.dot(latent_all[...], probe_w[...], preferred_element_type=jnp.float32).astype(jnp.bfloat16)
        yield
        heads = range(0, width, HEAD)
        for group in range(0, pictures.shape[0] // PATCH, IMAGES_A_STEP):
            more = slice(group * PATCH, (group + IMAGES_A_STEP) * PATCH)
            both = jnp.dot(pictures[more, :], both_w[...], preferred_element_type=jnp.float32).astype(jnp.bfloat16)
            keys[more, :] = both
            scores = [
                lax.dot_general(
                    probe[:, first : first + HEAD] * scale,
                    both[:, first : first + HEAD],
                    (((1,), (1,)), ((), ())),
                    preferred_element_type=jnp.float32,
                )
                for first in heads
            ]
            parts = [(image, head) for image in range(IMAGES_A_STEP) for head in range(len(heads))]
            rows = [slice(image * PATCH, (image + 1) * PATCH) for image in range(IMAGES_A_STEP)]
            cut = [scores[head][:, rows[image]] for image, head in parts]
            best = [jnp.max(part, -1, keepdims=True) for part in cut]
            weights = [jnp.exp(part - top) for part, top in zip(cut, best)]
            totals = [jnp.sum(part, -1, keepdims=True) for part in weights]
            probs = [(part * (1.0 / total)).astype(jnp.bfloat16) for part, total in zip(weights, totals)]
            mixed = [
                jnp.dot(
                    part,
                    both[rows[image], width + head * HEAD : width + (head + 1) * HEAD],
                    preferred_element_type=jnp.float32,
                ).astype(jnp.bfloat16)
                for part, (image, head) in zip(probs, parts)
            ]
            for image in range(IMAGES_A_STEP):
                at = slice((group + image) * LAT, (group + image + 1) * LAT)
                mixed_all[at, :] = jnp.concatenate(mixed[image * len(heads) : (image + 1) * len(heads)], 1)
            yield
        for first in range(0, placed.shape[0], PATCH):
            chosen = chosen_rows(target_rows, first, PATCH)
            placed[first : first + PATCH, :] = jnp.dot(
                chosen, mixed_all[...], preferred_element_type=jnp.float32
            ).astype(jnp.bfloat16)
        self.lefts = [placed]


class AttendFront(Front):
    def __init__(self, normed, layer_part, tables, segment, column, gain, shift, full_width):
        self.inputs = [normed, layer_part, *tables, segment, column, gain, shift]
        self.full_width = full_width
        rows, width = normed.shape[0], layer_part.shape[1] // 3
        low_shape = jax.ShapeDtypeStruct((rows, width), jnp.bfloat16)
        wide_shape = jax.ShapeDtypeStruct((rows, width), jnp.float32)
        lse_shape = jax.ShapeDtypeStruct((rows, 8), jnp.float32)
        self.out_shapes = [low_shape, low_shape, low_shape, wide_shape, lse_shape, low_shape, wide_shape, wide_shape]
        self.scratch = self.total_scratch(2, rows)

    def run(self):
        normed, layer_w, cos_ref, sin_ref, grow_ref, segment, column, gain, shift = self.ins
        q_out, k_out, v_out, att_out, lse_out, low, hat, factor_out = self.outs
        rows_all, width = att_out.shape
        scale = HEAD ** (-0.5)
        f32, low_type = jnp.float32, jnp.bfloat16
        for first in range(0, rows_all, ATTEND_ROWS):
            at, keys = slice(first, first + ATTEND_ROWS), first + ATTEND_ROWS
            cosine, sine, growth = cos_ref[at, :], sin_ref[at, :], grow_ref[at, :]
            linear = jnp.dot(normed[at, :], layer_w[...], preferred_element_type=f32)
            lin = linear[:, :width]
            q_out[at, :] = ((lin * cosine + halves_swapped(lin) * sine) * growth).astype(low_type)
            lin = linear[:, width : 2 * width]
            k_out[at, :] = ((lin * cosine + halves_swapped(lin) * sine) * (1.0 / growth)).astype(low_type)
            v_out[at, :] = linear[:, 2 * width :].astype(low_type)
            allowed = allowed_part(column, segment, first, ATTEND_ROWS, keys)
            heads = [slice(start, start + HEAD) for start in range(0, width, HEAD)]
            scores = [
                lax.dot_general(
                    q_out[at, lanes] * scale,
                    k_out[:keys, lanes],
                    (((1,), (1,)), ((), ())),
                    preferred_element_type=f32,
                )
                for lanes in heads
            ]
            scores = [jnp.where(allowed, part, -1e30) for part in scores]
            best = [jnp.max(part, -1, keepdims=True) for part in scores]
            weights = [jnp.exp(part - top) for part, top in zip(scores, best)]
            totals = [jnp.sum(part, -1, keepdims=True) for part in weights]
            probs = [(part * (1.0 / total)).astype(low_type) for part, total in zip(weights, totals)]
            mixed = [
                jnp.dot(part, v_out[:keys, lanes], preferred_element_type=f32) for part, lanes in zip(probs, heads)
            ]
            for head, lanes in enumerate(heads):
                att_out[at, lanes] = mixed[head]
                lse_out[at, head : head + 1] = best[head] + jnp.log(totals[head])
            rows = att_out[at, :]
            sums = [jnp.sum(rows, 1, keepdims=True), jnp.sum(rows * rows, 1, keepdims=True)]
            self.held[1][:, at] = as_lanes(sums)[:2]
            yield
        total = self.small_sum(self.held) / self.full_width
        average = total[:, 0:1]
        factor = lax.rsqrt(total[:, 1:2] - average * average + EPSILON)
        normal = (att_out[...] - average) * factor
        hat[...] = normal
        factor_out[...] = jnp.broadcast_to(factor, normal.shape)
        gain, shift = (own_line(self.here, line, low.shape[1]) for line in (gain, shift))
        low[...] = (normal * gain + shift).astype(low_type)
        self.lefts = [low]


class GradFront(Front):
    def grads(self, products):
        for seq in range(PLANE):
            for product in products:
                self.launches.append(functools.partial(self.part, *product, seq))

    def part(self, left, right, out, side, seq):
        span = (left.shape[1] if side == INWARD else right.shape[1]) // PLANE
        at = slice(seq * span, (seq + 1) * span)
        contract = (((0,), (0,)), ((), ()))
        half = span // 2
        if side == OUTWARD:
            out[:, at] = lax.dot_general(
                left[...], right[:, at], contract, preferred_element_type=jnp.float32
            ).astype(jnp.bfloat16)
        else:
            made = lax.dot_general(left[:, at], right[...], contract, preferred_element_type=jnp.float32)
            made = made.astype(jnp.bfloat16)
            out[seq, 0], out[seq, 1] = made[:half], made[half:]


def grad_shape(model_width, rows, side):
    span = model_width // PLANE
    shape = (PLANE, 2, span // 2, rows) if side == INWARD else (rows, model_width)
    return jax.ShapeDtypeStruct(shape, jnp.bfloat16)


class HiddenFront(GradFront):
    def __init__(self, lifted, up_part, bias, cotangent_all, down_part, gain, shift, full_width):
        self.inputs = [lifted, up_part, bias, cotangent_all, down_part, gain, shift]
        self.full_width = full_width
        rows, width, model_width = lifted.shape[0], up_part.shape[1], lifted.shape[1]
        low_shape = jax.ShapeDtypeStruct((rows, width), jnp.bfloat16)
        self.out_shapes = [
            low_shape,
            low_shape,
            jax.ShapeDtypeStruct((8, width), jnp.float32),
            grad_shape(model_width, width, INWARD),
            grad_shape(model_width, width, OUTWARD),
            jax.ShapeDtypeStruct((rows, model_width), jnp.bfloat16),
        ]
        self.scratch = self.total_scratch(4, rows) + [pltpu.VMEM((rows, width), jnp.float32)] * 3

    def run(self):
        lifted, up_w, bias, cotangent_all, down_w, gain, shift = self.ins
        settled, d_hidden, vectors, up, down, result = self.outs
        activated, slope, d_settled = self.held[6:]
        f32 = jnp.float32
        bias, gain, shift = (own_line(self.here, line, settled.shape[1]) for line in (bias, gain, shift))
        rows = activated.shape[0]
        step = rows // 4
        for first in range(0, rows, step):
            at = slice(first, first + step)
            pre = jnp.dot(lifted[at, :], up_w[...], preferred_element_type=f32) + bias
            below = 0.5 + 0.5 * lax.erf(pre * (0.5**0.5))
            act = pre * below
            activated[at, :] = act
            slope[at, :] = below + pre * jnp.exp(-0.5 * pre * pre) * (1.0 / (2.0 * jnp.pi) ** 0.5)
            grad = lax.dot_general(
                cotangent_all[at, :], down_w[...], (((1,), (1,)), ((), ())), preferred_element_type=f32
            )
            d_settled[at, :] = grad
            scaled = grad * gain
            sums = [jnp.sum(part, 1, keepdims=True) for part in (act, act * act, scaled, scaled * act)]
            self.held[1][:, at] = as_lanes(sums)[:4]
            yield
        total = self.small_sum(self.held[:6]) / self.full_width
        average = total[:, 0:1]
        factor = lax.rsqrt(total[:, 1:2] - average * average + EPSILON)
        mean_scaled = total[:, 2:3]
        mean_cross = factor * (total[:, 3:4] - average * mean_scaled)
        step = rows // PLANE
        gain_sum = shift_sum = bias_sum = 0.0
        for first in range(0, rows, step):
            at = slice(first, first + step)
            normal = (activated[at, :] - average[at]) * factor[at]
            settled[at, :] = (normal * gain + shift).astype(jnp.bfloat16)
            grad = d_settled[at, :]
            inner = factor[at] * (grad * gain - mean_scaled[at] - normal * mean_cross[at])
            low = (slope[at, :] * inner).astype(jnp.bfloat16)
            d_hidden[at, :] = low
            gain_sum += jnp.sum(grad * normal, 0, keepdims=True)
            shift_sum += jnp.sum(grad, 0, keepdims=True)
            bias_sum += jnp.sum(low.astype(f32), 0, keepdims=True)
        vectors[...] = jnp.zeros_like(vectors)
        vectors[0:1, :], vectors[1:2, :], vectors[2:3, :] = gain_sum, shift_sum, bias_sum
        def result_part(first):
            at = slice(first, first + step)
            result[at, :] = jnp.dot(settled[at, :], down_w[...], preferred_element_type=f32).astype(jnp.bfloat16)

        for first in range(0, rows, step):
            self.launches.append(functools.partial(result_part, first))
        self.grads([(lifted, d_hidden, up, INWARD), (settled, cotangent_all, down, OUTWARD)])
        self.lefts = [d_hidden, settled]


class AttendBackFront(GradFront):
    def __init__(self, d_branch, out_part, hat, factor, gain, kept, tables, segment, column, normed, inner_low, full_width):
        self.inputs = [d_branch, out_part, hat, factor, gain, *kept, *tables]
        self.inputs += [segment, column, normed, inner_low]
        self.full_width = full_width
        rows, width = hat.shape
        model_width = normed.shape[1]
        low_type, f32 = jnp.bfloat16, jnp.float32
        self.out_shapes = [jax.ShapeDtypeStruct((8, width), f32)]
        self.out_shapes += [grad_shape(model_width, 3 * width, INWARD), grad_shape(model_width, width, OUTWARD)]
        self.scratch = self.total_scratch(2, rows)
        self.scratch += [pltpu.VMEM((rows, width), low_type), pltpu.VMEM((rows, 3 * width), low_type)]
        self.scratch += [pltpu.VMEM((rows, width), f32)] * 4

    def run(self):
        d_branch, out_part, hat, factor, gain, attended, q_ref, k_ref, v_ref, lse = self.ins[:10]
        cos_ref, sin_ref, grow_ref, segment, column, normed, inner_low = self.ins[10:]
        gain = own_line(self.here, gain, hat.shape[1])
        vectors, lin_grad, out_grad = self.outs
        d_att, lin_out, d_inner, d_query, d_key, d_value = self.held[6:]
        rows_all, width = hat.shape
        f32, low_type = jnp.float32, jnp.bfloat16
        gain_sum = shift_sum = 0.0
        for first in range(0, rows_all, ATTEND_ROWS):
            at = slice(first, first + ATTEND_ROWS)
            grad = lax.dot_general(
                d_branch[at, :], out_part[...], (((1,), (1,)), ((), ())), preferred_element_type=f32
            )
            d_inner[at, :] = grad
            gain_sum += jnp.sum(grad * hat[at, :], 0, keepdims=True)
            shift_sum += jnp.sum(grad, 0, keepdims=True)
            scaled = grad * gain
            sums = [jnp.sum(scaled, 1, keepdims=True), jnp.sum(scaled * hat[at, :], 1, keepdims=True)]
            self.held[1][:, at] = as_lanes(sums)[:2]
            yield
        vectors[...] = jnp.zeros_like(vectors)
        vectors[0:1, :], vectors[1:2, :] = gain_sum, shift_sum
        total = self.small_sum(self.held[:6]) / self.full_width
        d_att[...] = (
            factor[...] * (d_inner[...] * gain - total[:, 0:1] - hat[...] * total[:, 1:2])
        ).astype(low_type)
        heads, scale = width // HEAD, HEAD ** (-0.5)
        for first in range(0, rows_all, ATTEND_ROWS):
            at, keys = slice(first, first + ATTEND_ROWS), first + ATTEND_ROWS
            allowed = allowed_part(column, segment, first, ATTEND_ROWS, keys)
            contract_last, contract_first = (((1,), (1,)), ((), ())), (((0,), (0,)), ((), ()))
            lanes_of = [slice(head * HEAD, (head + 1) * HEAD) for head in range(heads)]
            d_rows = [d_att[at, lanes] for lanes in lanes_of]
            scores = [
                lax.dot_general(
                    q_ref[at, lanes] * scale, k_ref[:keys, lanes], contract_last, preferred_element_type=f32
                )
                for lanes in lanes_of
            ]
            d_probs = [
                lax.dot_general(d, v_ref[:keys, lanes], contract_last, preferred_element_type=f32)
                for d, lanes in zip(d_rows, lanes_of)
            ]
            deltas = [
                jnp.sum(d.astype(f32) * attended[at, lanes], -1, keepdims=True) for d, lanes in zip(d_rows, lanes_of)
            ]
            probs = [
                jnp.exp(jnp.where(allowed, part, -1e30) - lse[at, head : head + 1])
                for head, part in enumerate(scores)
            ]
            d_scores = [(p * (d - delta)).astype(low_type) for p, d, delta in zip(probs, d_probs, deltas)]
            for head, lanes in enumerate(lanes_of):
                d_query[at, lanes] = (
                    jnp.dot(d_scores[head], k_ref[:keys, lanes], preferred_element_type=f32) * scale
                )
                key_part = (
                    lax.dot_general(d_scores[head], q_ref[at, lanes], contract_first, preferred_element_type=f32)
                    * scale
                )
                value_part = lax.dot_general(
                    probs[head].astype(low_type), d_rows[head], contract_first, preferred_element_type=f32
                )
                if first:
                    d_key[:first, lanes] += key_part[:first]
                    d_value[:first, lanes] += value_part[:first]
                d_key[first:keys, lanes] = key_part[first:]
                d_value[first:keys, lanes] = value_part[first:]
            yield
        for first in range(0, rows_all, ATTEND_ROWS):
            at = slice(first, first + ATTEND_ROWS)
            cosine, sine, growth = cos_ref[at, :], sin_ref[at, :], grow_ref[at, :]
            scaled = d_query[at, :] * growth
            lin_out[at, :width] = (scaled * cosine - halves_swapped(scaled) * sine).astype(low_type)
            scaled = d_key[at, :] * (1.0 / growth)
            lin_out[at, width : 2 * width] = (scaled * cosine - halves_swapped(scaled) * sine).astype(low_type)
            lin_out[at, 2 * width :] = d_value[at, :].astype(low_type)
        self.grads(
            [
                (normed, lin_out, lin_grad, INWARD),
                (inner_low, d_branch, out_grad, OUTWARD),
            ]
        )
        self.lefts = [lin_out]


def lazy_call(kernel, inputs, in_specs, out_shapes, out_specs, scratch, cid):
    late = [is_lazy(value, spec) for value, spec in zip(inputs, in_specs)]
    buffers = [pltpu.VMEM(value.shape, value.dtype) for value, flag in zip(inputs, late) if flag]
    n_in, n_out, n_scratch, n_late = len(inputs), len(out_shapes), len(scratch), len(buffers)

    def body(*refs):
        refs = list(refs)
        ins, outs, held = refs[:n_in], refs[n_in : n_in + n_out], refs[n_in + n_out : n_in + n_out + n_scratch]
        spare, sems = refs[n_in + n_out + n_scratch : -1], refs[-1]
        lazies = []
        for number, flag in enumerate(late):
            if flag:
                ins[number] = Lazy(ins[number], spare[len(lazies)], sems.at[len(lazies)])
                lazies.append(ins[number])
        kernel(ins, outs, held)
        for item in lazies:
            item.ready()

    return pl.pallas_call(
        body,
        out_shape=tuple(out_shapes),
        in_specs=[ANYWHERE if flag else spec for spec, flag in zip(in_specs, late)],
        out_specs=tuple(out_specs),
        scratch_shapes=list(scratch) + buffers + [pltpu.SemaphoreType.DMA((max(n_late, 1),))],
        compiler_params=pltpu.CompilerParams(
            collective_id=cid, has_side_effects=True, vmem_limit_bytes=VMEM_BYTES
        ),
    )(*inputs)


def exchange(front, streams, riders, cid, pace=(), between=0, work_from=0):
    fronts = [front] if front is not None else []
    sums = list(streams)
    parts = fronts + sums + list(riders)

    def kernel(ins, outs, held):
        here = Places()
        ins, outs, held = list(ins), list(outs), list(held)

        def take(refs, count):
            taken = refs[:count]
            del refs[:count]
            return taken

        for part in parts:
            part.bind(
                here, take(ins, len(part.inputs)), take(outs, len(part.out_shapes)), take(held, len(part.scratch))
            )
        wide_parts = [part for part in parts if isinstance(part, (Front, ChainWeights))]
        peers = [here.tp_peer]
        if riders:
            peers.append(here.img_peer)
        if wide_parts:
            peers += wide_parts[0].peers(here)
        else:
            peers += [here.core, here.x, here.y]
        greet(peers)
        waiting, work = [], []
        for rider in riders:
            rider.start()
            if rider.later:
                take_some(rider.launches, len(rider.launches))
            waiting += rider.launches + rider.later
        if front is not None:
            allowed = list(pace)
            for _ in front.run():
                take_some(waiting, allowed.pop(0) if allowed else 0)
            for stream, left in zip(streams, front.lefts):
                stream.left = left
            work = front.launches
        for stream in streams:
            stream.begin()
        stages = []
        for number, stream in reversed(list(enumerate(streams))):
            stages += [(lag + number * SECOND_LAG, stage) for lag, stage in stream.stages()]
        ticks = ticks_of(stages, PIECES)
        share, last = -(-len(work) // max(len(ticks) - 2 - work_from, 1)), PIECES - 2
        for number, tick in enumerate(ticks):
            tick()
            if number >= work_from:
                take_some(work, share)
            if number < 2:
                take_some(waiting, between)
            if number >= last:
                take_some(waiting, -(-len(waiting) // max(len(ticks) - 1 - number, 1)))
        take_some(work, len(work))
        take_some(waiting, len(waiting))
        for part in parts:
            part.finish()

    in_specs = []
    for part in fronts + sums:
        in_specs += part.in_specs or [ON_CHIP] * len(part.inputs)
    in_specs += [ANYWHERE] * sum(len(rider.inputs) for rider in riders)
    out_specs = [ON_CHIP for part in fronts for _ in part.out_shapes]
    out_specs += [spec for stream in sums for spec in stream.out_specs()]
    out_specs += [ANYWHERE] * sum(len(rider.out_shapes) for rider in riders)
    made = list(
        lazy_call(
            kernel,
            [value for part in parts for value in part.inputs],
            in_specs,
            [shape for part in parts for shape in part.out_shapes],
            out_specs,
            [item for part in parts for item in part.scratch],
            cid,
        )
    )
    split = []
    for part in parts:
        split.append(made[: len(part.out_shapes)])
        del made[: len(part.out_shapes)]
    return split


def finale(pairs, sides, raw, raw_sides, image, row_vectors, own_vectors, latents, query_rows, result_parts, cid):
    f32, low_type, dma = jnp.float32, jnp.bfloat16, pltpu.SemaphoreType.DMA
    d_rows, pictures, keys, probe, placed, out_part, target_rows = image
    width, model_width, picture_width = probe.shape[1], d_rows.shape[1], pictures.shape[1]
    images = pictures.shape[0] // PATCH
    image_shapes = [
        grad_shape(picture_width, width, INWARD),
        grad_shape(picture_width, width, INWARD),
        grad_shape(model_width, width, OUTWARD),
    ]
    all_sides = list(sides) + list(raw_sides) + [INWARD, INWARD, OUTWARD]
    n, n_raw, n_image = len(sides), len(raw_sides), len(image_shapes)
    total = n + n_raw + n_image
    shapes = [grad.shape for grad, _ in pairs] + [grad.shape for grad in raw] + [item.shape for item in image_shapes]
    blocks = [
        shape[2:] if side == INWARD else (shape[0], shape[1] // (2 * PLANE)) for shape, side in zip(shapes, all_sides)
    ]
    vectors = list(row_vectors) + [array for array, _ in own_vectors]
    picked = [0] * len(row_vectors) + [row for _, row in own_vectors]
    vector_rows = sum(vector.shape[1] // LANES for vector in vectors)
    small_shape = (LAT + vector_rows + -vector_rows % 8, LANES)
    result_shape = result_parts[0].shape

    def kernel(ins, outs, held):
        refs = list(ins) + list(outs) + list(held)

        def take(count):
            taken = refs[:count]
            del refs[:count]
            return taken

        target_ref, d_ref, pictures_ref, keys_ref, probe_ref, placed_ref, out_w = take(7)
        grad_refs = take(n + n_raw)
        theirs = take(n)
        vector_refs = take(len(vectors))
        latents_ref, query_ref, result_ref, result_here, middle_ref = take(5)
        out_refs = take(total)
        sums_out, query_out, latent_out, result_out = take(4)
        grad_refs += take(n_image)
        theirs += take(n_raw + n_image)
        summed = take(total)
        small_own, small_theirs, small_mine, small_all, lat_mine, lat_theirs, d_mixed, d_both, result_theirs = take(9)
        z_send, z_recv, send, recv, local, s_send, s_recv, r_send, r_recv = take(9)
        here = Places()
        seq, img = here.seq, here.img
        ring = [here.at(lax.rem(seq + step, PLANE)) for step in range(1, PLANE)]
        greet(ring + [here.img_peer, here.tp_peer])

        def part_of(index, to_seq, to_img):
            ref, block = grad_refs[index], blocks[index]
            if all_sides[index] == INWARD:
                return ref.at[to_seq, to_img]
            return ref.at[:, pl.ds(pl.multiple_of((to_seq * 2 + to_img) * block[1], block[1]), block[1])]

        def slot_of(index, from_seq):
            ref, block = out_refs[index], blocks[index]
            if all_sides[index] == INWARD:
                return ref.at[:, pl.ds(pl.multiple_of(from_seq * block[1], block[1]), block[1])]
            return ref.at[pl.ds(pl.multiple_of(from_seq * block[0], block[0]), block[0])]

        waits, crossings = [], {}

        def cross(index):
            for step in range(PLANE):
                target = lax.rem(seq + step, PLANE)
                made = remote(
                    part_of(index, target, 1 - img),
                    theirs[index].at[target],
                    z_send.at[index - n, step],
                    z_recv.at[index - n, step],
                    here.img_peer,
                )
                made.start()
                crossings[index, step] = made

        def deliver(index, step):
            target = lax.rem(seq + step, PLANE)
            if index >= n:
                crossings[index, step].wait_recv()
            mine = part_of(index, target, img)[...].astype(f32)
            summed[index][target] = (mine + theirs[index][target].astype(f32)).astype(low_type)
            if step == 0:
                made = pltpu.make_async_copy(summed[index].at[target], slot_of(index, seq), local.at[index])
                made.start()
                waits.append(made.wait)
                return
            made = remote(
                summed[index].at[target], slot_of(index, seq), send.at[index, step], recv.at[index, step], here.at(target)
            )
            made.start()
            waits.append(made.wait_send)

        result_copy = remote(result_ref, result_theirs, r_send.at[0], r_recv.at[0], here.tp_peer)
        result_copy.start()
        for index in range(n, n + n_raw):
            cross(index)
        at_row = LAT
        for vector, row in zip(vector_refs, picked):
            for first in range(0, vector.shape[1], LANES):
                small_own[at_row : at_row + 1, :] = vector[row : row + 1, first : first + LANES]
                at_row += 1
        if at_row < small_shape[0]:
            small_own[at_row:, :] = jnp.zeros((small_shape[0] - at_row, LANES), f32)
        waiting = [functools.partial(deliver, index, step) for index in range(n + n_raw) for step in range(PLANE)]

        scale = HEAD ** (-0.5)
        d_slots = jnp.zeros(d_mixed.shape, f32)
        for first in range(0, d_ref.shape[0], PATCH):
            d_part = lax.dot_general(
                d_ref[first : first + PATCH, :], out_w[...], (((1,), (1,)), ((), ())), preferred_element_type=f32
            ).astype(low_type)
            chosen = chosen_rows(target_ref, first, PATCH)
            d_slots += lax.dot_general(chosen, d_part, (((0,), (0,)), ((), ())), preferred_element_type=f32)
        d_mixed[...] = d_slots.astype(low_type)
        take_some(waiting, 1)
        for first in range(0, model_width, 512):
            at = slice(first, first + 512)
            grad_refs[total - 1][:, at] = lax.dot_general(
                placed_ref[...], d_ref[:, at], (((0,), (0,)), ((), ())), preferred_element_type=f32
            ).astype(low_type)
            take_some(waiting, 1)
        cross(total - 1)
        d_probe_sum = jnp.zeros(probe_ref.shape, f32)
        heads = range(0, width, HEAD)
        for group in range(0, images, IMAGES_A_STEP):
            parts = [(image, first) for image in range(group, group + IMAGES_A_STEP) for first in heads]
            contract_last, contract_first = (((1,), (1,)), ((), ())), (((0,), (0,)), ((), ()))
            keys_of = [keys_ref[i * PATCH : (i + 1) * PATCH, f : f + HEAD] for i, f in parts]
            values_of = [keys_ref[i * PATCH : (i + 1) * PATCH, width + f : width + f + HEAD] for i, f in parts]
            probe_of = [probe_ref[:, f : f + HEAD] for _, f in parts]
            d_of = [d_mixed[i * LAT : (i + 1) * LAT, f : f + HEAD] for i, f in parts]
            scores = [
                lax.dot_general(p * scale, k, contract_last, preferred_element_type=f32)
                for p, k in zip(probe_of, keys_of)
            ]
            d_probs = [
                lax.dot_general(d, v, contract_last, preferred_element_type=f32) for d, v in zip(d_of, values_of)
            ]
            best = [jnp.max(part, -1, keepdims=True) for part in scores]
            weights = [jnp.exp(part - top) for part, top in zip(scores, best)]
            totals = [jnp.sum(part, -1, keepdims=True) for part in weights]
            probs = [part * (1.0 / whole) for part, whole in zip(weights, totals)]
            deltas = [jnp.sum(p * d, -1, keepdims=True) for p, d in zip(probs, d_probs)]
            d_scores = [(p * (d - delta)).astype(low_type) for p, d, delta in zip(probs, d_probs, deltas)]
            d_probe = [jnp.dot(d, k, preferred_element_type=f32) for d, k in zip(d_scores, keys_of)]
            d_keys = [
                lax.dot_general(d, p, contract_first, preferred_element_type=f32) for d, p in zip(d_scores, probe_of)
            ]
            d_values = [
                lax.dot_general(p.astype(low_type), d, contract_first, preferred_element_type=f32)
                for p, d in zip(probs, d_of)
            ]
            for number, (image, first) in enumerate(parts):
                rows = slice(image * PATCH, (image + 1) * PATCH)
                d_both[rows, first : first + HEAD] = (d_keys[number] * scale).astype(low_type)
                d_both[rows, width + first : width + first + HEAD] = d_values[number].astype(low_type)
            for number in range(0, len(parts), len(heads)):
                d_probe_sum += jnp.concatenate(d_probe[number : number + len(heads)], 1) * scale
            take_some(waiting, 8)
        small_own[:LAT, :] = d_probe_sum
        small_cross = remote(small_own, small_theirs, s_send.at[0], s_recv.at[0], here.img_peer)
        small_cross.start()
        span = picture_width // PLANE
        for part in range(PLANE):
            made = lax.dot_general(
                pictures_ref[:, part * span : (part + 1) * span],
                d_both[...],
                (((0,), (0,)), ((), ())),
                preferred_element_type=f32,
            ).astype(low_type)
            for kind in range(2):
                piece = made[:, kind * width : (kind + 1) * width]
                grad_refs[n + n_raw + kind][part, 0] = piece[: span // 2]
                grad_refs[n + n_raw + kind][part, 1] = piece[span // 2 :]
            take_some(waiting, 2)
        for kind in range(2):
            cross(n + n_raw + kind)
        small_cross.wait()
        small_mine[...] = small_own[...] + small_theirs[...]
        small_all[seq] = small_mine[...]
        small_copies = []
        for step, peer in enumerate(ring, 1):
            made = remote(small_mine, small_all.at[seq], s_send.at[step], s_recv.at[step], peer)
            made.start()
            small_copies.append(made)
        take_some(waiting, len(waiting))
        for index in (total - 1, total - 3, total - 2):
            for step in range(PLANE):
                deliver(index, step)
        for made in small_copies:
            made.wait()
        sums_out[...] = small_all[...]
        latent_part = jnp.zeros(lat_mine.shape, f32)
        for source in range(PLANE):
            given = small_all[source, :LAT, :]
            at = slice(source * width, (source + 1) * width)
            query_out[:, at] = lax.dot_general(
                latents_ref[...].astype(f32),
                given,
                (((0,), (0,)), ((), ())),
                precision=HIGHEST_PRECISION,
                preferred_element_type=f32,
            )
            latent_part += lax.dot_general(
                given,
                query_ref[:, at].astype(f32),
                (((1,), (1,)), ((), ())),
                precision=HIGHEST_PRECISION,
                preferred_element_type=f32,
            )
        lat_mine[...] = latent_part
        last = remote(lat_mine, lat_theirs, s_send.at[PLANE], s_recv.at[PLANE], here.tp_peer)
        last.start()
        last.wait()
        latent_out[...] = lat_mine[...] + lat_theirs[...]
        result_copy.wait()
        result_sum = result_here[...].astype(f32) + result_theirs[...].astype(f32)
        result_out[...] = (middle_ref[...] + result_sum).astype(low_type)
        for index in range(total):
            for step in range(1, PLANE):
                source = lax.rem(seq + PLANE - step, PLANE)
                at = slot_of(index, source)
                remote(at, at, send.at[index, step], recv.at[index, step], here.core).wait_recv()
        for wait in waits:
            wait()
        for made in crossings.values():
            made.wait_send()

    outs = []
    for block, side in zip(blocks, all_sides):
        shape = (block[0], PLANE * block[1]) if side == INWARD else (PLANE * block[0], block[1])
        outs.append(jax.ShapeDtypeStruct(shape, low_type))
    lat_shape = latents.shape
    small_shapes = [
        jax.ShapeDtypeStruct((PLANE,) + small_shape, f32),
        jax.ShapeDtypeStruct(query_rows.shape, f32),
        jax.ShapeDtypeStruct(lat_shape, f32),
        jax.ShapeDtypeStruct(result_shape, low_type),
    ]
    n_cross = n_raw + n_image
    made = lazy_call(
        kernel,
        [
            target_rows,
            d_rows,
            pictures,
            keys,
            probe,
            placed,
            out_part,
            *[grad for grad, _ in pairs],
            *raw,
            *[given for _, given in pairs],
            *vectors,
            latents,
            query_rows,
            result_parts[0],
            *result_parts,
        ],
        [ON_CHIP] * (7 + n + n_raw + n + len(vectors)) + [ON_CHIP] * 2 + [ANYWHERE, ON_CHIP, ON_CHIP],
        outs + small_shapes,
        [ANYWHERE] * total + [ON_CHIP] * 4,
        [pltpu.VMEM(item.shape, low_type) for item in image_shapes]
        + [pltpu.VMEM((PLANE,) + tuple(block), low_type) for block in blocks[n:]]
        + [pltpu.VMEM((PLANE,) + tuple(block), low_type) for block in blocks]
        + [
            pltpu.VMEM(small_shape, f32),
            pltpu.VMEM(small_shape, f32),
            pltpu.VMEM(small_shape, f32),
            pltpu.VMEM((PLANE,) + small_shape, f32),
            pltpu.VMEM(lat_shape, f32),
            pltpu.VMEM(lat_shape, f32),
            pltpu.VMEM((d_rows.shape[0], width), low_type),
            pltpu.VMEM((images * PATCH, 2 * width), low_type),
            pltpu.VMEM(result_shape, low_type),
            dma((n_cross, PLANE)),
            dma((n_cross, PLANE)),
            dma((total, PLANE)),
            dma((total, PLANE)),
            dma((total,)),
            dma((PLANE + 1,)),
            dma((PLANE + 1,)),
            dma((1,)),
            dma((1,)),
        ],
        cid,
    )
    return made[:total], made[total:]


def widened(grads, splits, passed, spread, model_width, n_rows, widths):
    f32, dma = jnp.float32, pltpu.SemaphoreType.DMA
    n, n_passed, n_wide = len(grads), len(passed), sum(splits)
    wide_shapes = []
    for array, split in zip(grads, splits):
        wide_shapes += [jax.ShapeDtypeStruct((array.shape[0], array.shape[1] // split), f32)] * split

    def kernel(*refs):
        refs = list(refs)

        def take(count):
            taken = refs[:count]
            del refs[:count]
            return taken

        ins, passed_ins, (spread_ref,) = take(n), take(n_passed), take(1)
        outs, passed_outs, row_outs, own_outs = take(n_wide), take(n_passed), take(n_rows), take(len(widths))
        narrow, wide, held, (in_sems, out_sems, passed_sems) = take(n), take(n_wide), take(n_passed), take(3)
        copies_in = [pltpu.make_async_copy(src, dst, in_sems.at[i]) for i, (src, dst) in enumerate(zip(ins, narrow))]
        copies_out = [pltpu.make_async_copy(src, dst, out_sems.at[i]) for i, (src, dst) in enumerate(zip(wide, outs))]
        held_in = [pltpu.make_async_copy(src, dst, passed_sems.at[0, i]) for i, (src, dst) in enumerate(zip(passed_ins, held))]
        held_out = [pltpu.make_async_copy(src, dst, passed_sems.at[1, i]) for i, (src, dst) in enumerate(zip(held, passed_outs))]
        for copy in copies_in + held_in:
            copy.start()
        made = 0
        for i, split in enumerate(splits):
            copies_in[i].wait()
            if split == 1:
                wide[made][...] = narrow[i][...].astype(f32)
            else:
                width = narrow[i].shape[1] // (split * PLANE)
                for seq in range(PLANE):
                    for part in range(split):
                        at = (seq * split + part) * width
                        wide[made + part][:, seq * width : (seq + 1) * width] = narrow[i][:, at : at + width].astype(f32)
            for part in range(split):
                copies_out[made + part].start()
            made += split
        for arrive, leave in zip(held_in, held_out):
            arrive.wait()
            leave.start()
        first = LAT
        for out in row_outs:
            count = model_width // LANES
            total = jnp.sum(spread_ref[:, first : first + count, :], 0)
            for part in range(count):
                out[:, part * LANES : (part + 1) * LANES] = total[part : part + 1, :]
            first += count
        for out, width in zip(own_outs, widths):
            for seq in range(PLANE):
                for part in range(width // LANES):
                    at = seq * width + part * LANES
                    out[:, at : at + LANES] = spread_ref[seq, first + part : first + part + 1, :]
            first += width // LANES
        for copy in copies_out + held_out:
            copy.wait()

    shapes = list(wide_shapes)
    shapes += [jax.ShapeDtypeStruct(array.shape, array.dtype) for array in passed]
    shapes += [jax.ShapeDtypeStruct((1, model_width), f32)] * n_rows
    shapes += [jax.ShapeDtypeStruct((1, PLANE * width), f32) for width in widths]
    small = n_rows + len(widths)
    made = pl.pallas_call(
        kernel,
        out_shape=tuple(shapes),
        in_specs=[ANYWHERE] * (n + n_passed) + [ON_CHIP],
        out_specs=tuple([ANYWHERE] * (n_wide + n_passed) + [ON_CHIP] * small),
        scratch_shapes=[pltpu.VMEM(array.shape, array.dtype) for array in grads]
        + [pltpu.VMEM(item.shape, f32) for item in wide_shapes]
        + [pltpu.VMEM(array.shape, array.dtype) for array in passed]
        + [dma((n,)), dma((n_wide,)), dma((2, n_passed))],
        compiler_params=pltpu.CompilerParams(vmem_limit_bytes=VMEM_BYTES),
    )(*grads, *passed, spread)
    made = list(made)
    n = n_wide
    cut = [made[:n], made[n : n + n_passed], made[n + n_passed : n + n_passed + n_rows]]
    return (*cut, made[n + n_passed + n_rows :])


IMAGES_A_STEP = 4


def image_probs_of(probe, keys, scale):
    scores = lax.dot_general(
        probe * scale, keys, (((1,), (1,)), ((), ())), preferred_element_type=jnp.float32
    )
    weights = jnp.exp(scores - jnp.max(scores, -1, keepdims=True))
    return weights * (1.0 / jnp.sum(weights, -1, keepdims=True))


def xpos_part(segment, column, tables, first):
    at, half = slice(first, first + ATTEND_ROWS), HEAD // 2
    f32 = jnp.float32
    rows = segment.shape[1]
    here = segment[:, at].astype(f32)
    earlier = lax.broadcasted_iota(jnp.int32, (rows, ATTEND_ROWS), 0)
    now = first + lax.broadcasted_iota(jnp.int32, (rows, ATTEND_ROWS), 1)
    counted = (column[:, 0:1] == here) & (earlier < now)
    position = jnp.sum(counted.astype(f32), 0, keepdims=True)
    ladder = lax.broadcasted_iota(jnp.int32, (half, ATTEND_ROWS), 0).astype(f32)
    angles = position * jnp.exp(ladder * (-2.0 * jnp.log(f32(10000.0)) / (2.0 * half)))
    growth = jnp.exp(position / 512.0 * jnp.log((ladder / half + 0.4) / 1.4))
    cosine, sine = jnp.cos(angles), jnp.sin(angles)
    repeats = tables[0].shape[1] // HEAD
    tables[0][at, :] = jnp.concatenate([cosine, cosine] * repeats, 0).T
    tables[1][at, :] = jnp.concatenate([-sine, sine] * repeats, 0).T
    tables[2][at, :] = jnp.concatenate([growth, growth] * repeats, 0).T


def halves_swapped(rows):
    width, half = rows.shape[1], HEAD // 2
    lane = lax.broadcasted_iota(jnp.int32, rows.shape, 1)
    ahead = pltpu.roll(rows, width - half, 1)
    behind = pltpu.roll(rows, half, 1)
    return jnp.where(lane % HEAD < half, ahead, behind)


def allowed_part(column, segment, first, count, keys):
    row = first + lax.broadcasted_iota(jnp.int32, (count, keys), 0)
    later = lax.broadcasted_iota(jnp.int32, (count, keys), 1)
    same = column[first : first + count, 0:1] == segment[:, :keys].astype(jnp.float32)
    return same & (later <= row)


ATTEND_ROWS = 256


def as_lanes(columns):
    rows = columns[0].shape[0]
    lane = lax.broadcasted_iota(jnp.int32, (rows, LANES), 1)
    joined = jnp.zeros((rows, LANES), jnp.float32)
    for number, column in enumerate(columns):
        joined = jnp.where(lane == number, column, joined)
    return joined.T[:8, :]


def norm_rows(rows, gain, shift):
    center = rows - jnp.mean(rows, -1, keepdims=True)
    factor = lax.rsqrt(jnp.mean(center * center, -1, keepdims=True) + EPSILON)
    normal = center * factor
    return (normal * gain + shift, normal, factor)


def dot32(left, right):
    return jnp.dot(left, right, preferred_element_type=jnp.float32)


def on_plane(
    text,
    segment,
    features,
    image_count,
    image_slot,
    cotangent,
    input_gain,
    input_shift,
    query_weight,
    key_weight,
    value_weight,
    inner_gain,
    inner_shift,
    out_weight,
    middle_gain,
    middle_shift,
    up_weight,
    up_bias,
    hidden_gain,
    hidden_shift,
    down_weight,
    latents,
    resample_query,
    resample_key,
    resample_value,
    resample_out,
):
    f32, low = jnp.float32, jnp.bfloat16
    row_count, model_width = text.shape[1], text.shape[2]
    group_rows = segment.shape[1]
    image_slots = features.shape[1]
    half_width = query_weight.shape[1]
    own_width = half_width // PLANE

    rows, own = intake(
        (features[0].reshape(image_slots * PATCH, features.shape[3]),),
        (
            resample_key,
            resample_value,
            resample_query,
            latents,
            resample_out,
        ),
        (INWARD, INWARD, INWARD, SHARED, OUTWARD),
        1,
    )
    (pictures,) = rows
    image_key_own, image_value_own, probe_own, latent_all, image_out_own = own

    counts = image_count.reshape(-1, 1)
    live = jnp.arange(IMG_DEV, dtype=jnp.int32)[None, :] < counts
    first_rows = jnp.where(live, image_slot.reshape(live.shape) * LAT, -LAT)
    target_rows = (first_rows[:, :, None] + jnp.arange(LAT, dtype=jnp.int32)).reshape(1, -1)

    def line(vector):
        return vector.reshape(-1, LANES)

    def taken_in(targets, piece, rows):
        first = lax.axis_index(SEQ) * row_count + sum(PIECE_ROWS[:piece])
        row = first + lax.broadcasted_iota(jnp.int32, (rows, targets.shape[1]), 0)
        return jnp.max((row == targets[...]).astype(jnp.float32), 1, keepdims=True) > 0.5

    def begin(total, piece, views, outs):
        text_view, targets, gain, shift = views
        embed = total.astype(jnp.bfloat16).astype(jnp.float32)
        taken = taken_in(targets, piece, total.shape[0])
        mixed = jnp.where(taken, embed, text_view[...].astype(jnp.float32))
        outs[0][...] = mixed
        return norm_rows(mixed, full_line(gain), full_line(shift))[0].astype(jnp.bfloat16)

    rows_wide = jax.ShapeDtypeStruct((row_count, model_width), f32)
    (image_keys, mixed_placed, probe, *tables, column), (mixed_in, normed), (qkv_own, out_own, up_own) = exchange(
        ImageFront(
            pictures, image_key_own, image_value_own, latent_all, probe_own, target_rows, segment
        ),
        [
            Stream(
                group_rows,
                None,
                image_out_own,
                False,
                (text[0], target_rows, line(input_gain), line(input_shift)),
                (ROWS, ALL, ALL, ALL),
                ((rows_wide, ROWS),),
                begin,
                True,
            )
        ],
        [
            ChainWeights(
                (query_weight, key_weight, value_weight, out_weight, up_weight),
                (INWARD, INWARD, INWARD, OUTWARD, INWARD),
                ((0, 0), (0, own_width), (0, 2 * own_width), (1, 0), (2, 0)),
            )
        ],
        3,
        PACE_IMAGE,
    )

    def middle_step(total, piece, views, outs):
        mixed_view, gain, shift = views
        middle = mixed_view[...] + total
        outs[0][...] = middle
        return norm_rows(middle, full_line(gain), full_line(shift))[0].astype(jnp.bfloat16)

    attend_made, (middle, lifted), (down_own,), (cot_all,) = exchange(
        AttendFront(
            normed, qkv_own, tables, segment, column, line(inner_gain), line(inner_shift), model_width
        ),
        [
            Stream(
                group_rows,
                None,
                out_own,
                False,
                (mixed_in, line(middle_gain), line(middle_shift)),
                (ROWS, ALL, ALL),
                ((rows_wide, ROWS),),
                middle_step,
                True,
            )
        ],
        [ChainWeights((down_weight,), (OUTWARD,), ((0, 0),)), GatherRows(cotangent[0])],
        5,
        PACE_ATTEND,
    )
    *attended_kept, inner_low, inner_hat, inner_factor = attend_made
    query_rot, keys_rot, values, attended, log_total = attended_kept
    own_hidden = up_own.shape[1]

    vector_out = jax.ShapeDtypeStruct((1, model_width), f32)

    def norm_back_step(total, piece, views, outs):
        rows_view, carried_view, gain, *targets = views
        rows_in = rows_view[...]
        center = rows_in - jnp.mean(rows_in, -1, keepdims=True)
        factor = lax.rsqrt(jnp.mean(center * center, -1, keepdims=True) + EPSILON)
        normal = center * factor
        grad = carried_view[...].astype(jnp.float32) + full_back(total, normal, factor, full_line(gain))
        if targets:
            outs[0][...] = jnp.where(taken_in(targets[0], piece, total.shape[0]), 0.0, grad)
        else:
            outs[0][...] = grad
        if piece == 0:
            outs[1][...] = jnp.zeros_like(outs[1])
            outs[2][...] = jnp.zeros_like(outs[2])
        outs[1][...] += jnp.sum(total * normal, 0, keepdims=True)
        outs[2][...] += jnp.sum(total, 0, keepdims=True)
        return grad.astype(jnp.bfloat16)

    hidden_made, (d_middle, middle_gain_grad, middle_shift_grad, d_branch) = exchange(
        HiddenFront(
            lifted,
            up_own,
            line(up_bias),
            cot_all,
            down_own,
            line(hidden_gain),
            line(hidden_shift),
            FF,
        ),
        [
            Stream(
                group_rows,
                None,
                up_own,
                True,
                (middle, cotangent[0], line(middle_gain)),
                (ROWS, ROWS, ALL),
                ((rows_wide, ROWS), (vector_out, ALL), (vector_out, ALL)),
                norm_back_step,
                True,
            ),
        ],
        [],
        8,
    )

    _, _, hidden_vectors, *hidden_grads, result_part = hidden_made
    result_rows = lax.psum_scatter(result_part, SEQ, scatter_dimension=0, tiled=True)
    back_made, (text_grad, input_gain_grad, input_shift_grad, d_rows), hidden_theirs = exchange(
        AttendBackFront(
            d_branch,
            out_own,
            inner_hat,
            inner_factor,
            line(inner_gain),
            (attended, query_rot, keys_rot, values, log_total),
            tables,
            segment,
            column,
            normed,
            inner_low,
            model_width,
        ),
        [
            Stream(
                group_rows,
                None,
                qkv_own,
                True,
                (mixed_in, d_middle, line(input_gain), target_rows),
                (ROWS, ROWS, ALL, ALL),
                ((rows_wide, ROWS), (vector_out, ALL), (vector_out, ALL)),
                norm_back_step,
                True,
            ),
        ],
        [CrossGrads(hidden_grads, (INWARD, OUTWARD))],
        10,
        PACE_BACK,
        1,
        WORK_FROM,
    )
    inner_vectors, *layer_grads = back_made
    row_vectors = (input_gain_grad, input_shift_grad, middle_gain_grad, middle_shift_grad)
    own_vectors = (
        (inner_vectors, 0),
        (inner_vectors, 1),
        (hidden_vectors, 2),
        (hidden_vectors, 0),
        (hidden_vectors, 1),
    )
    owned, (spread, resample_query_grad, latent_grad, result) = finale(
        list(zip(hidden_grads, hidden_theirs)),
        (INWARD, OUTWARD),
        layer_grads,
        (INWARD, OUTWARD),
        (d_rows, pictures, image_keys, probe, mixed_placed, image_out_own, target_rows),
        row_vectors,
        own_vectors,
        latents,
        resample_query,
        (result_rows, middle),
        12,
    )
    widths = (own_width, own_width, own_hidden, own_hidden, own_hidden)
    grads, passed, row_sums, own_sums = widened(
        owned,
        (1, 1, 3, 1, 1, 1, 1),
        (result, text_grad, resample_query_grad, latent_grad),
        spread,
        model_width,
        len(row_vectors),
        widths,
    )
    up_sum, down_sum, query_sum, key_sum, value_sum, out_sum, image_key_sum, image_value_sum, image_out_sum = grads
    result, text_grad, resample_query_grad, latent_grad = passed
    row_sums = [vector.reshape(-1) for vector in row_sums]
    inner_gain_sum, inner_shift_sum, up_bias_sum, hidden_gain_sum, hidden_shift_sum = (
        vector.reshape(-1) for vector in own_sums
    )

    return (
        result[None],
        text_grad[None],
        row_sums[0],
        row_sums[1],
        query_sum,
        key_sum,
        value_sum,
        inner_gain_sum,
        inner_shift_sum,
        out_sum,
        row_sums[2],
        row_sums[3],
        up_sum,
        up_bias_sum,
        hidden_gain_sum,
        hidden_shift_sum,
        down_sum,
        latent_grad,
        resample_query_grad,
        image_key_sum,
        image_value_sum,
        image_out_sum,
    )


def solution(mesh):
    placed = (
        P(IMG, SEQ, None),
        P(IMG, None),
        P(IMG, SEQ, None, None),
        P(IMG, None),
        P(IMG, None),
        P(IMG, SEQ, None),
        P(),
        P(),
        P((SEQ, IMG), TP),
        P((SEQ, IMG), TP),
        P((SEQ, IMG), TP),
        P(TP),
        P(TP),
        P(TP, (SEQ, IMG)),
        P(),
        P(),
        P((SEQ, IMG), TP),
        P(TP),
        P(TP),
        P(TP),
        P(TP, (SEQ, IMG)),
        P(None, (SEQ, IMG)),
        P((SEQ, IMG), TP),
        P((SEQ, IMG), TP),
        P((SEQ, IMG), TP),
        P(TP, (SEQ, IMG)),
    )
    return jax.shard_map(
        on_device if narrow_heads(mesh) else on_plane,
        mesh=mesh,
        in_specs=placed,
        out_specs=(
            P(IMG, SEQ, None),
            P(IMG, SEQ, None),
            P(),
            P(),
            P((SEQ, IMG), TP),
            P((SEQ, IMG), TP),
            P((SEQ, IMG), TP),
            P(TP),
            P(TP),
            P(TP, (SEQ, IMG)),
            P(),
            P(),
            P((SEQ, IMG), TP),
            P(TP),
            P(TP),
            P(TP),
            P(TP, (SEQ, IMG)),
            P(None, (SEQ, IMG)),
            P((SEQ, IMG), TP),
            P((SEQ, IMG), TP),
            P((SEQ, IMG), TP),
            P(TP, (SEQ, IMG)),
        ),
        check_vma=False,
    )
```
